32 devices in a mesh: groups: 2 (over y), px: 4 (over z), py: 4 (over x, core).
Axes of the slice: x: 2, y: 2, z: 4, core: 2. Of those that a mesh axis runs over, the one named last changes fastest.
Arguments:
- nodes: bfloat16 [12288, 256], P(('groups', 'px', 'py')), parts along dimension 0, may hold values from -6 to 6
- edges: bfloat16 [36864, 256], P(('groups', 'px', 'py')), parts along dimension 0, may hold values from -6 to 6
- edge_grads: bfloat16 [36864, 256], P(('groups', 'px', 'py')), parts along dimension 0, may hold values from -6 to 6
- node_grads: bfloat16 [12288, 256], P(('groups', 'px', 'py')), parts along dimension 0, may hold values from -6 to 6
- send_list: int32 [256, 32], P(('groups', 'px', 'py')), parts along dimension 0, may hold values from 0 to 383
- senders: int32 [288, 128], P(('groups', 'px', 'py')), parts along dimension 0, may hold values from 0 to 639
- receivers: int32 [288, 128], P(('groups', 'px', 'py')), parts along dimension 0, may hold values from 0 to 383
- tile_count: int32 [32], P(('groups', 'px', 'py')), parts along dimension 0, may hold values from 2 to 9, as said below
- w_edge_in: bfloat16 [768, 256], replicated, may hold values from -0.21875 to 0.21875
- w_edge_out: bfloat16 [256, 256], replicated, may hold values from -0.375 to 0.375
- gain_edge: bfloat16 [256], replicated, may hold values from 0.099609375 to 1.8984375
- w_node_in: bfloat16 [512, 256], replicated, may hold values from -0.25 to 0.25
- w_node_out: bfloat16 [256, 256], replicated, may hold values from -0.375 to 0.375
- gain_node: bfloat16 [256], replicated, may hold values from 0.099609375 to 1.8984375
Outputs:
- nodes_grad: bfloat16 [12288, 256], P(('groups', 'px', 'py')), parts along dimension 0
- edges_grad: bfloat16 [36864, 256], P(('groups', 'px', 'py')), parts along dimension 0
- w_edge_in_grad: bfloat16 [1536, 256], P('groups'), parts along dimension 0
- w_edge_out_grad: bfloat16 [512, 256], P('groups'), parts along dimension 0
- gain_edge_grad: bfloat16 [512], P('groups'), parts along dimension 0
- w_node_in_grad: bfloat16 [1024, 256], P('groups'), parts along dimension 0
- w_node_out_grad: bfloat16 [512, 256], P('groups'), parts along dimension 0
- gain_node_grad: bfloat16 [512], P('groups'), parts along dimension 0
The draws below stay inside these ranges and needn't reach their ends.
There are 2 independent parts, one for each index of `groups`. The reference program is written for one: setup_inputs(seed, part) draws one part's arguments, and reference() takes and returns one part's arrays. A program takes and returns all parts, laid end to end along the dimension named above; an argument that names none is the same for every part. Nothing has to cross between parts.
Inputs may be any that keep to these rules, and one draw needn't show every extreme that they name: `tile_count`: some patch has all 9 tiles live.
All inputs are finite; a program needn't handle non-finite values.
Results may differ from the reference program's by a relative error of at most 0.0075.
Values may be sent and summed in bfloat16 or wider, within the bound.
No kernel may reach another device: no remote copies, remote signals or barrier semaphores. Data moves between devices by JAX's collectives and lax.ppermute only.
A program may use at most 64 MiB of HBM per device.

```python
import jax
import jax.numpy as jnp
from jax import lax

D = 256
NODES_DEV = 384
SLOT = 32
TILE = 128
TILES = 9
PATCHES = 16
NODES = 6144
EDGES = 18432
N_PX = 4
N_PY = 4


def draw_tile_count(key, part):
    key = jax.random.fold_in(key, 7)
    first_key, second_key = jax.random.split(key)
    counts = jax.random.randint(first_key, (PATCHES,), max(1, TILES // 4), TILES + 1, dtype=jnp.int32)
    chosen = jax.random.randint(second_key, (), 0, PATCHES, dtype=jnp.int32)
    return counts.at[chosen].set(TILES).astype(jnp.int32)


def plant(array, key, least, largest):
    dims = array.shape
    place = [jax.random.randint(jax.random.fold_in(key, axis), (), 0, dims[axis]) for axis in range(len(dims))]
    array = array.at[tuple(place)].set(least)
    longest = dims.index(max(dims))
    place[longest] = (place[longest] + 1) % dims[longest]
    return array.at[tuple(place)].set(largest)


def block_scale(key, shape, cuts, low, top_value):
    level = 1.0
    for axis_at, shards_of in cuts:
        heights = jax.random.uniform(jax.random.fold_in(jax.random.fold_in(key, 6), axis_at), (shards_of,), jnp.float32, low / len(cuts), top_value / len(cuts))
        level = level * jnp.repeat(jnp.exp(heights), shape[axis_at] // shards_of).reshape((-1,) + (1,) * (len(shape) - 1 - axis_at))
    return level


def bell_draw(key, extent, scale, limit, pieces=(), held_as=jnp.bfloat16):
    result = scale * jax.random.normal(key, extent, jnp.float32)
    if pieces:
        result = result * block_scale(key, extent, pieces, -0.22, 0.18)
    return jnp.clip(result, -limit, limit).astype(held_as)


def setup_inputs(seed: int = 0, part: int = 0) -> dict:
    streams_of = jax.random.split(jax.random.key(seed), 15)
    part_splits = jax.random.split(jax.random.fold_in(streams_of[14], part), 15)
    nodes = bell_draw(part_splits[0], (NODES, D), 1.0, 6.0, ((0, 16),))
    edges = bell_draw(part_splits[1], (EDGES, D), 1.0, 6.0, ((0, 16),))
    edge_grads = bell_draw(part_splits[2], (EDGES, D), 1.0, 6.0, ((0, 16),))
    node_grads = bell_draw(part_splits[3], (NODES, D), 1.0, 6.0, ((0, 16),))
    send_list = plant(jax.random.randint(part_splits[4], (8 * PATCHES, SLOT), 0, NODES_DEV), jax.random.fold_in(part_splits[4], 1), 0, NODES_DEV - 1).astype(jnp.int32)
    senders = plant(jax.random.randint(part_splits[5], (TILES * PATCHES, TILE), 0, NODES_DEV + 8 * SLOT), jax.random.fold_in(part_splits[5], 1), 0, (NODES_DEV + 8 * SLOT) - 1).astype(jnp.int32)
    receivers = plant(jax.random.randint(part_splits[6], (TILES * PATCHES, TILE), 0, NODES_DEV), jax.random.fold_in(part_splits[6], 1), 0, NODES_DEV - 1).astype(jnp.int32)
    tile_count = draw_tile_count(jax.random.fold_in(jax.random.fold_in(streams_of[14], part), 71), part)
    w_edge_in = bell_draw(streams_of[8], (3 * D, D), (3 * D) ** -0.5, 0.21875)
    w_edge_out = bell_draw(streams_of[9], (D, D), D ** -0.5, 0.375)
    gain_edge = jnp.clip(1.0 + 0.18 * jax.random.normal(streams_of[10], (D,), jnp.float32), 0.099609375, 1.8984375).astype(jnp.bfloat16)
    w_node_in = bell_draw(streams_of[11], (2 * D, D), (2 * D) ** -0.5, 0.25)
    w_node_out = bell_draw(streams_of[12], (D, D), D ** -0.5, 0.375)
    gain_node = jnp.clip(1.0 + 0.18 * jax.random.normal(streams_of[13], (D,), jnp.float32), 0.099609375, 1.8984375).astype(jnp.bfloat16)
    return {"nodes": nodes, "edges": edges, "edge_grads": edge_grads, "node_grads": node_grads, "send_list": send_list, "senders": senders, "receivers": receivers, "tile_count": tile_count, "w_edge_in": w_edge_in, "w_edge_out": w_edge_out, "gain_edge": gain_edge, "w_node_in": w_node_in, "w_node_out": w_node_out, "gain_node": gain_node}


EPS = 1e-05
OFFSETS = [(-1, -1), (-1, 0), (-1, 1), (0, -1), (0, 1), (1, -1), (1, 0), (1, 1)]

def matmul(left, right):
    return jnp.dot(left, right, preferred_element_type=jnp.float32)

def matmul_tn(left, right):
    return lax.dot_general(left, right, (((0,), (0,)), ((), ())), preferred_element_type=jnp.float32)

def matmul_nt(left, right):
    return lax.dot_general(left, right, (((1,), (1,)), ((), ())), preferred_element_type=jnp.float32)

def silu_slope(value):
    sigma = jax.nn.sigmoid(value)
    return sigma * (1.0 + value * (1.0 - sigma))

def normalize(value):
    centered = value - lax.optimization_barrier(jnp.mean(value, axis=-1, keepdims=True))
    scale_inv = lax.rsqrt(lax.optimization_barrier(jnp.mean(centered * centered, axis=-1, keepdims=True)) + EPS)
    return (centered * scale_inv, scale_inv)

def norm_back(normed, scale_inv, gain, upstream):
    scaled = upstream * gain
    inner = scaled - lax.optimization_barrier(jnp.mean(scaled, axis=-1, keepdims=True)) - normed * lax.optimization_barrier(jnp.mean(scaled * normed, axis=-1, keepdims=True))
    return (inner * scale_inv, lax.optimization_barrier(jnp.sum(upstream * normed, axis=0)))

def one_hot(ids, count):
    return (ids[:, None] == jnp.arange(count, dtype=jnp.int32)[None, :]).astype(jnp.bfloat16)

def edge_forward(extended, local_nodes, edge_tile, sender_ids, receiver_ids, w_edge_in, w_edge_out):
    inputs = jnp.concatenate([edge_tile, jnp.take(extended, sender_ids, axis=0), jnp.take(local_nodes, receiver_ids, axis=0)], axis=1)
    pre_act = matmul(inputs, w_edge_in)
    hidden = jax.nn.silu(pre_act).astype(jnp.bfloat16)
    normed, scale_inv = normalize(matmul(hidden, w_edge_out))
    return (inputs, pre_act, hidden, normed, scale_inv)

def aggregate(extended, local_nodes, edge_tiles, sender_tiles, receiver_tiles, live_tiles, w_edge_in, w_edge_out, gain_edge):
    node_count = local_nodes.shape[0]

    def visit(total, items):
        edge_tile, sender_ids, receiver_ids, tile_live = items
        inputs, pre_act, hidden, normed, scale_inv = edge_forward(extended, local_nodes, edge_tile, sender_ids, receiver_ids, w_edge_in, w_edge_out)
        message = (tile_live * gain_edge * normed).astype(jnp.bfloat16)
        return (total + matmul_tn(one_hot(receiver_ids, node_count), message), None)
    start = jnp.zeros((node_count, local_nodes.shape[1]), jnp.float32)
    total, _ = lax.scan(visit, start, (edge_tiles, sender_tiles, receiver_tiles, live_tiles))
    return total

def node_backward(local_nodes, aggregated, node_grads, w_node_in, w_node_out, gain_node):
    width = local_nodes.shape[1]
    node_inputs = jnp.concatenate([local_nodes, aggregated.astype(jnp.bfloat16)], axis=1)
    node_pre = matmul(node_inputs, w_node_in)
    node_hidden = jax.nn.silu(node_pre).astype(jnp.bfloat16)
    normed, scale_inv = normalize(matmul(node_hidden, w_node_out))
    upstream = node_grads.astype(jnp.float32)
    out_pre_grad, gain_grad = norm_back(normed, scale_inv, gain_node, upstream)
    out_pre_grad = out_pre_grad.astype(jnp.bfloat16)
    pre_grad = (matmul_nt(out_pre_grad, w_node_out) * silu_slope(node_pre)).astype(jnp.bfloat16)
    input_grad = matmul_nt(pre_grad, w_node_in)
    node_part = upstream + input_grad[:, :width]
    agg_grad = input_grad[:, width:].astype(jnp.bfloat16)
    return (node_part, agg_grad, matmul_tn(node_inputs, pre_grad), matmul_tn(node_hidden, out_pre_grad), gain_grad)

def edge_backward(extended, local_nodes, edge_tiles, grad_tiles, sender_tiles, receiver_tiles, live_tiles, agg_grad, w_edge_in, w_edge_out, gain_edge):
    ext_count = extended.shape[0]
    node_count = local_nodes.shape[0]
    width = local_nodes.shape[1]

    def visit(carry, items):
        ext_grad, recv_grad, first_grad, second_grad, gain_grad = carry
        edge_tile, grad_tile, sender_ids, receiver_ids, tile_live = items
        inputs, pre_act, hidden, normed, scale_inv = edge_forward(extended, local_nodes, edge_tile, sender_ids, receiver_ids, w_edge_in, w_edge_out)
        message_grad = tile_live * (grad_tile.astype(jnp.float32) + jnp.take(agg_grad, receiver_ids, axis=0).astype(jnp.float32))
        out_pre_grad, gain_part = norm_back(normed, scale_inv, gain_edge, message_grad)
        out_pre_grad = out_pre_grad.astype(jnp.bfloat16)
        pre_grad = (matmul_nt(out_pre_grad, w_edge_out) * silu_slope(pre_act)).astype(jnp.bfloat16)
        input_grad = matmul_nt(pre_grad, w_edge_in)
        edge_grad = (grad_tile.astype(jnp.float32) + input_grad[:, :width]).astype(jnp.bfloat16)
        sender_grad = input_grad[:, width:2 * width].astype(jnp.bfloat16)
        receiver_grad = input_grad[:, 2 * width:].astype(jnp.bfloat16)
        carry = (ext_grad + matmul_tn(one_hot(sender_ids, ext_count), sender_grad), recv_grad + matmul_tn(one_hot(receiver_ids, node_count), receiver_grad), first_grad + matmul_tn(inputs, pre_grad), second_grad + matmul_tn(hidden, out_pre_grad), gain_grad + gain_part)
        return (carry, edge_grad)
    start = (jnp.zeros((ext_count, width), jnp.float32), jnp.zeros((node_count, width), jnp.float32), jnp.zeros((3 * width, width), jnp.float32), jnp.zeros((width, width), jnp.float32), jnp.zeros((width,), jnp.float32))
    carry, edge_grads_out = lax.scan(visit, start, (edge_tiles, grad_tiles, sender_tiles, receiver_tiles, live_tiles))
    return (edge_grads_out,) + carry

def reference(nodes, edges, edge_grads, node_grads, send_list, senders, receivers, tile_count, w_edge_in, w_edge_out, gain_edge, w_node_in, w_node_out, gain_node):
    patches = N_PX * N_PY
    nodes_p = nodes.reshape(patches, NODES_DEV, D)
    lists = send_list.reshape(patches, 8, SLOT)
    index = jnp.arange(patches, dtype=jnp.int32)
    first_idx = index // N_PY
    second_idx = index % N_PY
    owners = []
    halo_parts = []
    for direction in range(8):
        shift_a, shift_b = OFFSETS[direction]
        source = ((first_idx - shift_a) % N_PX * N_PY + (second_idx - shift_b) % N_PY).astype(jnp.int32)
        owners.append(source)
        halo_parts.append(nodes_p[source[:, None], lists[source, direction]])
    halo = jnp.stack(halo_parts, axis=1).reshape(patches, 8 * SLOT, D)
    extended = jnp.concatenate([nodes_p, halo], axis=1)
    edge_tiles = edges.reshape(patches, TILES, TILE, D)
    grad_tiles = edge_grads.reshape(patches, TILES, TILE, D)
    sender_tiles = senders.reshape(patches, TILES, TILE)
    receiver_tiles = receivers.reshape(patches, TILES, TILE)
    node_grads_p = node_grads.reshape(patches, NODES_DEV, D)

    def patch_step(carry, items):
        ext_rows, local_nodes, e_tiles, g_tiles, s_tiles, r_tiles, count, upstream = items
        live_tiles = (jnp.arange(TILES, dtype=jnp.int32) < count).astype(jnp.float32)
        aggregated = aggregate(ext_rows, local_nodes, e_tiles, s_tiles, r_tiles, live_tiles, w_edge_in, w_edge_out, gain_edge)
        node_part, agg_grad, node_first, node_second, node_gain = node_backward(local_nodes, aggregated, upstream, w_node_in, w_node_out, gain_node)
        edge_out, ext_grad, recv_grad, edge_first, edge_second, edge_gain = edge_backward(ext_rows, local_nodes, e_tiles, g_tiles, s_tiles, r_tiles, live_tiles, agg_grad, w_edge_in, w_edge_out, gain_edge)
        local_grad = node_part + ext_grad[:NODES_DEV] + recv_grad
        halo_grad = ext_grad[NODES_DEV:].astype(jnp.bfloat16)
        terms = (edge_first, edge_second, edge_gain, node_first, node_second, node_gain)
        carry = tuple((total + term for total, term in zip(carry, terms)))
        return (carry, (local_grad, halo_grad, edge_out))
    start = (jnp.zeros((3 * D, D), jnp.float32), jnp.zeros((D, D), jnp.float32), jnp.zeros((D,), jnp.float32), jnp.zeros((2 * D, D), jnp.float32), jnp.zeros((D, D), jnp.float32), jnp.zeros((D,), jnp.float32))
    sums, (local_grad, halo_grad, edge_out) = lax.scan(patch_step, start, (extended, nodes_p, edge_tiles, grad_tiles, sender_tiles, receiver_tiles, tile_count, node_grads_p))
    halo_grad = halo_grad.reshape(patches, 8, SLOT, D).astype(jnp.float32)
    for direction in range(8):
        source = owners[direction]
        local_grad = local_grad.at[source[:, None], lists[source, direction]].add(halo_grad[:, direction])
    return (local_grad.reshape(NODES, D).astype(jnp.bfloat16), edge_out.reshape(EDGES, D), sums[0].astype(jnp.bfloat16), sums[1].astype(jnp.bfloat16), sums[2].astype(jnp.bfloat16), sums[3].astype(jnp.bfloat16), sums[4].astype(jnp.bfloat16), sums[5].astype(jnp.bfloat16))
```

```python
import jax
import jax.numpy as jnp
from jax import lax
from jax.experimental import pallas as pl
from jax.experimental.pallas import tpu as pltpu
from jax.sharding import PartitionSpec as P

EPS = 1e-05
BF16 = jnp.bfloat16
F32 = jnp.float32
VMEM_LIMIT = 24 * 1024 * 1024


def passed_along(array, axis, by):
    size = lax.axis_size(axis)
    return lax.ppermute(array, axis, [(i, (i + by) % size) for i in range(size)])


def dot(left, right):
    return jnp.dot(left, right, preferred_element_type=F32)


def dot_tn(left, right):
    return lax.dot_general(left, right, (((0,), (0,)), ((), ())), preferred_element_type=F32)


def dot_nt(left, right):
    return lax.dot_general(left, right, (((1,), (1,)), ((), ())), preferred_element_type=F32)


def sigmoid(value):
    return 1.0 / (1.0 + jnp.exp(-value))


def normalize(value):
    centered = value - jnp.mean(value, axis=-1, keepdims=True)
    scale_inv = lax.rsqrt(jnp.mean(centered * centered, axis=-1, keepdims=True) + EPS)
    return centered * scale_inv, scale_inv


def norm_back(normed, scale_inv, gain, upstream):
    scaled = upstream * gain
    inner = (
        scaled
        - jnp.mean(scaled, axis=-1, keepdims=True)
        - normed * jnp.mean(scaled * normed, axis=-1, keepdims=True)
    )
    return inner * scale_inv


def columns_of(ids):
    rows, lanes = ids.shape
    padded = -(-rows // 8) * 8
    if padded > rows:
        ids = jnp.concatenate([ids, jnp.zeros((padded - rows, lanes), ids.dtype)], axis=0)
    return ids.T


def hot_rows(columns, tiles, base, count):
    parts = []
    for tile in tiles:
        column = columns[:, tile : tile + 1] - base
        lanes = lax.broadcasted_iota(jnp.int32, (columns.shape[0], count), 1)
        parts.append(jnp.where(lanes == column, 1.0, 0.0).astype(BF16))
    return jnp.concatenate(parts, axis=0) if len(parts) > 1 else parts[0]


def hot_columns(ids, tiles, base, count):
    parts = []
    for tile in tiles:
        row = ids[tile : tile + 1, :] - base
        subs = lax.broadcasted_iota(jnp.int32, (count, ids.shape[1]), 0)
        parts.append(jnp.where(subs == row, 1.0, 0.0).astype(BF16))
    return jnp.concatenate(parts, axis=1) if len(parts) > 1 else parts[0]


def list_hot(ids, count):
    directions, slots = ids.shape
    wide = jnp.concatenate([ids, jnp.zeros((directions, 128 - slots), ids.dtype)], axis=1)
    columns = wide.T
    parts = []
    for k in range(directions):
        lanes = lax.broadcasted_iota(jnp.int32, (slots, count), 1)
        parts.append(jnp.where(lanes == columns[:slots, k : k + 1], 1.0, 0.0).astype(BF16))
    return jnp.concatenate(parts, axis=0)


def live_rows(count_ref, first_tile, tiles, tile_rows):
    rows = lax.broadcasted_iota(jnp.int32, (tiles * tile_rows, 1), 0)
    return jnp.where(rows < (count_ref[0] - first_tile) * tile_rows, 1.0, 0.0)


def chunks_of(tiles):
    step = 3 if tiles % 3 == 0 else 1
    return [list(range(first, first + step)) for first in range(0, tiles, step)]


def send_kernel(nodes, send_list, low, mid, high):
    slots = send_list.shape[1]
    rows = dot(list_hot(send_list[...], nodes.shape[0]), nodes[...]).astype(BF16)
    low[...] = rows[: 3 * slots]
    mid[...] = rows[3 * slots : 5 * slots]
    high[...] = rows[5 * slots :]


def local_kernel(nodes, edges, senders, receivers, w_in, pre):
    count, width = nodes.shape
    tile_rows = senders.shape[1]
    x = nodes[...]
    table = jnp.concatenate(
        [
            dot(x, w_in[width : 2 * width]).astype(BF16),
            dot(x, w_in[2 * width :]).astype(BF16),
        ],
        axis=0,
    )
    by_sender = columns_of(senders[...])
    by_receiver = columns_of(receivers[...])
    w_edge = w_in[:width]
    for tiles in chunks_of(senders.shape[0]):
        rows = pl.ds(tiles[0] * tile_rows, len(tiles) * tile_rows)
        hot = jnp.concatenate(
            [hot_rows(by_sender, tiles, 0, count), hot_rows(by_receiver, tiles, 0, count)], axis=1
        )
        pre[rows, :] = dot(edges[rows, :], w_edge) + dot(hot, table)


def forward_kernel(
    count_ref,
    nodes,
    node_grads,
    senders,
    receivers,
    pre_local,
    from_high,
    from_low,
    upward,
    downward,
    w_in,
    w_out,
    gain_edge,
    w_node_in,
    w_node_out,
    gain_node,
    halo_out,
    pre_out,
    normed_out,
    scale_out,
    agg_grad_out,
    node_part_out,
    node_sums,
):
    count, width = nodes.shape
    tile_rows = senders.shape[1]
    slots = from_high.shape[0] // 3
    halo = jnp.concatenate(
        [
            downward[:slots],
            from_high[slots : 2 * slots],
            upward[:slots],
            downward[slots : 2 * slots],
            upward[slots : 2 * slots],
            downward[2 * slots :],
            from_low[slots : 2 * slots],
            upward[2 * slots :],
        ],
        axis=0,
    )
    halo_out[...] = halo
    table = dot(halo, w_in[width : 2 * width]).astype(BF16)
    by_sender = columns_of(senders[...])
    receiver_ids = receivers[...]
    gain = gain_edge[...].astype(F32)
    total = jnp.zeros((count, width), F32)
    for tiles in chunks_of(senders.shape[0]):
        rows = pl.ds(tiles[0] * tile_rows, len(tiles) * tile_rows)
        value = pre_local[rows, :] + dot(hot_rows(by_sender, tiles, count, halo.shape[0]), table)
        pre_out[rows, :] = value
        hidden = (value * sigmoid(value)).astype(BF16)
        normed, scale_inv = normalize(dot(hidden, w_out[...]))
        normed_out[rows, :] = normed
        scale_out[rows, :] = jnp.broadcast_to(scale_inv, (len(tiles) * tile_rows, 128))
        live = live_rows(count_ref, tiles[0], len(tiles), tile_rows)
        message = (live * gain * normed).astype(BF16)
        total = total + dot(hot_columns(receiver_ids, tiles, 0, count), message)
    aggregated = total.astype(BF16)
    x = nodes[...]
    w_first = w_node_in[:width]
    w_second = w_node_in[width:]
    node_pre = dot(x, w_first) + dot(aggregated, w_second)
    sigma = sigmoid(node_pre)
    node_hidden = (node_pre * sigma).astype(BF16)
    normed, scale_inv = normalize(dot(node_hidden, w_node_out[...]))
    upstream = node_grads[...].astype(F32)
    out_grad = norm_back(normed, scale_inv, gain_node[...].astype(F32), upstream).astype(BF16)
    slope = sigma * (1.0 + node_pre * (1.0 - sigma))
    pre_grad = (dot_nt(out_grad, w_node_out[...]) * slope).astype(BF16)
    agg_grad_out[...] = dot_nt(pre_grad, w_second).astype(BF16)
    node_part_out[...] = upstream + dot_nt(pre_grad, w_first)
    node_sums[:width] = dot_tn(x, pre_grad)
    node_sums[width : 2 * width] = dot_tn(aggregated, pre_grad)
    node_sums[2 * width : 3 * width] = dot_tn(node_hidden, out_grad)
    node_sums[3 * width :] = jnp.broadcast_to(
        jnp.sum(upstream * normed, axis=0, keepdims=True), (8, width)
    )


def backward_kernel(
    count_ref,
    nodes,
    halo,
    edges,
    edge_grads,
    senders,
    receivers,
    pre,
    normed,
    scale,
    agg_grad,
    w_in,
    w_out,
    gain_edge,
    pre_grad_out,
    sender_out,
    receiver_out,
    up_out,
    down_out,
    rest_out,
    edge_sums,
):
    count, width = nodes.shape
    tile_rows = senders.shape[1]
    slots = up_out.shape[0] // 3
    by_receiver = columns_of(receivers[...])
    sender_ids = senders[...]
    receiver_ids = receivers[...]
    gain = gain_edge[...].astype(F32)
    extended = count + halo.shape[0]
    sender_total = jnp.zeros((extended, width), F32)
    receiver_total = jnp.zeros((count, width), F32)
    first = jnp.zeros((width, width), F32)
    second = jnp.zeros((width, width), F32)
    gain_total = jnp.zeros((1, width), F32)
    for tiles in chunks_of(senders.shape[0]):
        rows = pl.ds(tiles[0] * tile_rows, len(tiles) * tile_rows)
        live = live_rows(count_ref, tiles[0], len(tiles), tile_rows)
        upstream = live * (
            edge_grads[rows, :].astype(F32)
            + dot(hot_rows(by_receiver, tiles, 0, count), agg_grad[...])
        )
        chunk_normed = normed[rows, :]
        gain_total = gain_total + jnp.sum(upstream * chunk_normed, axis=0, keepdims=True)
        out_grad = norm_back(chunk_normed, scale[rows, :1], gain, upstream).astype(BF16)
        value = pre[rows, :]
        sigma = sigmoid(value)
        hidden = (value * sigma).astype(BF16)
        slope = sigma * (1.0 + value * (1.0 - sigma))
        pre_grad = (dot_nt(out_grad, w_out[...]) * slope).astype(BF16)
        pre_grad_out[rows, :] = pre_grad
        second = second + dot_tn(hidden, out_grad)
        first = first + dot_tn(edges[rows, :], pre_grad)
        sender_total = sender_total + dot(hot_columns(sender_ids, tiles, 0, extended), pre_grad)
        receiver_total = receiver_total + dot(
            hot_columns(receiver_ids, tiles, 0, count), pre_grad
        )
    own = sender_total[:count].astype(BF16)
    away = sender_total[count:].astype(BF16)
    received = receiver_total.astype(BF16)
    sender_out[...] = own
    receiver_out[...] = received
    halo_grad = dot_nt(away, w_in[width : 2 * width]).astype(BF16)
    parts = [halo_grad[k * slots : (k + 1) * slots] for k in range(8)]
    up_out[...] = jnp.concatenate([parts[0], parts[3], parts[5]], axis=0)
    down_out[...] = jnp.concatenate([parts[2], parts[4], parts[7]], axis=0)
    rest_out[...] = jnp.concatenate([parts[1], parts[6]], axis=0)
    x = nodes[...]
    edge_sums[:width] = first
    edge_sums[width : 2 * width] = dot_tn(x, own) + dot_tn(halo[...], away)
    edge_sums[2 * width : 3 * width] = dot_tn(x, received)
    edge_sums[3 * width : 4 * width] = second
    edge_sums[4 * width :] = jnp.broadcast_to(gain_total, (8, width))


def finish_kernel(
    edge_grads, pre_grad, sender_sum, receiver_sum, node_part, w_in, edges_grad, local_grad
):
    width = w_in.shape[1]
    edges_grad[...] = (
        edge_grads[...].astype(F32) + dot_nt(pre_grad[...], w_in[:width])
    ).astype(BF16)
    local_grad[...] = (
        node_part[...]
        + dot_nt(sender_sum[...], w_in[width : 2 * width])
        + dot_nt(receiver_sum[...], w_in[2 * width :])
    )


def return_kernel(send_list, local_grad, up_back, down_back, to_high, to_low, nodes_grad):
    slots = send_list.shape[1]

    def block(ref, k):
        return ref[k * slots : (k + 1) * slots]

    returned = jnp.concatenate(
        [
            block(to_high, 0),
            block(to_high, 2),
            block(to_high, 1),
            block(up_back, 1),
            block(down_back, 1),
            block(to_low, 0),
            block(to_low, 2),
            block(to_low, 1),
        ],
        axis=0,
    )
    hot = list_hot(send_list[...], local_grad.shape[0])
    nodes_grad[...] = (local_grad[...] + dot_tn(hot, returned)).astype(BF16)


def call(body, outs, flops, *operands, scalars=0):
    moved = sum(x.size * x.dtype.itemsize for x in operands)
    moved += sum(x.size * jnp.dtype(x.dtype).itemsize for x in outs)
    smem = pl.BlockSpec(memory_space=pltpu.SMEM)
    vmem = pl.BlockSpec(memory_space=pltpu.VMEM)
    return pl.pallas_call(
        body,
        out_shape=outs,
        in_specs=[smem] * scalars + [vmem] * (len(operands) - scalars),
        out_specs=[vmem] * len(outs),
        compiler_params=pltpu.CompilerParams(vmem_limit_bytes=VMEM_LIMIT),
        cost_estimate=pl.CostEstimate(flops=flops, bytes_accessed=moved, transcendentals=0),
    )(*operands)


def shaped(rows, columns, dtype):
    return jax.ShapeDtypeStruct((rows, columns), dtype)


def on_device(
    nodes,
    edges,
    edge_grads,
    node_grads,
    send_list,
    senders,
    receivers,
    tile_count,
    w_edge_in,
    w_edge_out,
    gain_edge,
    w_node_in,
    w_node_out,
    gain_node,
):
    count, width = nodes.shape
    slots = send_list.shape[1]
    halo_rows = 8 * slots
    edge_rows = edges.shape[0]
    square = 2 * width * width
    gain_edge = gain_edge.reshape(1, width)
    gain_node = gain_node.reshape(1, width)

    low, mid, high = call(
        send_kernel,
        [
            shaped(3 * slots, width, BF16),
            shaped(2 * slots, width, BF16),
            shaped(3 * slots, width, BF16),
        ],
        2 * halo_rows * count * width,
        nodes,
        send_list,
    )
    from_low = passed_along(high, "px", 1)
    from_high = passed_along(low, "px", -1)
    upward = passed_along(
        jnp.concatenate([from_high[2 * slots :], mid[slots:], from_low[2 * slots :]]), "py", 1
    )
    downward = passed_along(
        jnp.concatenate([from_high[:slots], mid[:slots], from_low[:slots]]), "py", -1
    )
    (pre_local,) = call(
        local_kernel,
        [shaped(edge_rows, width, F32)],
        square * (2 * count + edge_rows) + 4 * edge_rows * count * width,
        nodes,
        edges,
        senders,
        receivers,
        w_edge_in,
    )
    halo, pre, normed, scale, agg_grad, node_part, node_sums = call(
        forward_kernel,
        [
            shaped(halo_rows, width, BF16),
            shaped(edge_rows, width, F32),
            shaped(edge_rows, width, F32),
            shaped(edge_rows, 128, F32),
            shaped(count, width, BF16),
            shaped(count, width, F32),
            shaped(3 * width + 8, width, F32),
        ],
        square * (2 * edge_rows + 9 * count) + 2 * edge_rows * count * width,
        tile_count,
        nodes,
        node_grads,
        senders,
        receivers,
        pre_local,
        from_high,
        from_low,
        upward,
        downward,
        w_edge_in,
        w_edge_out,
        gain_edge,
        w_node_in,
        w_node_out,
        gain_node,
        scalars=1,
    )
    node_sums = lax.psum(node_sums, ("px", "py"))
    pre_grad, sender_sum, receiver_sum, up, down, rest, edge_sums = call(
        backward_kernel,
        [
            shaped(edge_rows, width, BF16),
            shaped(count, width, BF16),
            shaped(count, width, BF16),
            shaped(3 * slots, width, BF16),
            shaped(3 * slots, width, BF16),
            shaped(2 * slots, width, BF16),
            shaped(4 * width + 8, width, F32),
        ],
        square * (4 * edge_rows + 2 * count + 2 * halo_rows)
        + 2 * edge_rows * (3 * count + halo_rows) * width,
        tile_count,
        nodes,
        halo,
        edges,
        edge_grads,
        senders,
        receivers,
        pre,
        normed,
        scale,
        agg_grad,
        w_edge_in,
        w_edge_out,
        gain_edge,
        scalars=1,
    )
    edge_sums = lax.psum(edge_sums, ("px", "py"))
    up_back = passed_along(up, "py", 1)
    down_back = passed_along(down, "py", -1)
    to_high = passed_along(
        jnp.concatenate([up_back[:slots], down_back[:slots], rest[:slots]]), "px", 1
    )
    to_low = passed_along(
        jnp.concatenate([up_back[2 * slots :], down_back[2 * slots :], rest[slots:]]), "px", -1
    )
    edges_grad, local_grad = call(
        finish_kernel,
        [shaped(edge_rows, width, BF16), shaped(count, width, F32)],
        square * (edge_rows + 2 * count),
        edge_grads,
        pre_grad,
        sender_sum,
        receiver_sum,
        node_part,
        w_edge_in,
    )
    (nodes_grad,) = call(
        return_kernel,
        [shaped(count, width, BF16)],
        2 * halo_rows * count * width,
        send_list,
        local_grad,
        up_back,
        down_back,
        to_high,
        to_low,
    )
    return (
        nodes_grad,
        edges_grad,
        edge_sums[: 3 * width].astype(BF16),
        edge_sums[3 * width : 4 * width].astype(BF16),
        edge_sums[4 * width].astype(BF16),
        node_sums[: 2 * width].astype(BF16),
        node_sums[2 * width : 3 * width].astype(BF16),
        node_sums[3 * width].astype(BF16),
    )


def solution(mesh):
    in_specs = (
        P(("groups", "px", "py"), None),
        P(("groups", "px", "py"), None),
        P(("groups", "px", "py"), None),
        P(("groups", "px", "py"), None),
        P(("groups", "px", "py"), None),
        P(("groups", "px", "py"), None),
        P(("groups", "px", "py"), None),
        P(("groups", "px", "py")),
        P(),
        P(),
        P(),
        P(),
        P(),
        P(),
    )
    out_specs = (
        P(("groups", "px", "py"), None),
        P(("groups", "px", "py"), None),
        P("groups", None),
        P("groups", None),
        P("groups"),
        P("groups", None),
        P("groups", None),
        P("groups"),
    )
    return jax.shard_map(
        on_device, mesh=mesh, in_specs=in_specs, out_specs=out_specs, check_vma=False
    )
```

```python
import jax
import jax.numpy as jnp
from jax import lax
from jax.experimental import pallas as pl
from jax.experimental.pallas import tpu as pltpu
from jax.sharding import PartitionSpec as P

EPS = 1e-05
BF16 = jnp.bfloat16
F32 = jnp.float32
VMEM_LIMIT = 24 * 1024 * 1024


def passed_along(array, axis, by):
    size = lax.axis_size(axis)
    return lax.ppermute(array, axis, [(i, (i + by) % size) for i in range(size)])


def dot(left, right):
    return jnp.dot(left, right, preferred_element_type=F32)


def dot_tn(left, right):
    return lax.dot_general(left, right, (((0,), (0,)), ((), ())), preferred_element_type=F32)


def dot_nt(left, right):
    return lax.dot_general(left, right, (((1,), (1,)), ((), ())), preferred_element_type=F32)


def sigmoid(value):
    return 1.0 / (1.0 + jnp.exp(-value))


def normalize(value):
    centered = value - jnp.mean(value, axis=-1, keepdims=True)
    scale_inv = lax.rsqrt(jnp.mean(centered * centered, axis=-1, keepdims=True) + EPS)
    return centered * scale_inv, scale_inv


def norm_back(normed, scale_inv, gain, upstream):
    scaled = upstream * gain
    inner = (
        scaled
        - jnp.mean(scaled, axis=-1, keepdims=True)
        - normed * jnp.mean(scaled * normed, axis=-1, keepdims=True)
    )
    return inner * scale_inv


def columns_of(ids):
    rows, lanes = ids.shape
    padded = -(-rows // 8) * 8
    if padded > rows:
        ids = jnp.concatenate([ids, jnp.zeros((padded - rows, lanes), ids.dtype)], axis=0)
    return ids.T


def hot_rows(columns, tiles, base, count):
    parts = []
    for tile in tiles:
        column = columns[:, tile : tile + 1] - base
        lanes = lax.broadcasted_iota(jnp.int32, (columns.shape[0], count), 1)
        parts.append(jnp.where(lanes == column, 1.0, 0.0).astype(BF16))
    return jnp.concatenate(parts, axis=0) if len(parts) > 1 else parts[0]


def hot_columns(ids, tiles, base, count):
    parts = []
    for tile in tiles:
        row = ids[tile : tile + 1, :] - base
        subs = lax.broadcasted_iota(jnp.int32, (count, ids.shape[1]), 0)
        parts.append(jnp.where(subs == row, 1.0, 0.0).astype(BF16))
    return jnp.concatenate(parts, axis=1) if len(parts) > 1 else parts[0]


def list_hot(ids, count):
    directions, slots = ids.shape
    wide = jnp.concatenate([ids, jnp.zeros((directions, 128 - slots), ids.dtype)], axis=1)
    columns = wide.T
    parts = []
    for k in range(directions):
        lanes = lax.broadcasted_iota(jnp.int32, (slots, count), 1)
        parts.append(jnp.where(lanes == columns[:slots, k : k + 1], 1.0, 0.0).astype(BF16))
    return jnp.concatenate(parts, axis=0)


def live_rows(count_ref, first_tile, tiles, tile_rows):
    rows = lax.broadcasted_iota(jnp.int32, (tiles * tile_rows, 1), 0)
    return jnp.where(rows < (count_ref[0] - first_tile) * tile_rows, 1.0, 0.0)


def chunks_of(tiles):
    step = 3 if tiles % 3 == 0 else 1
    return [list(range(first, first + step)) for first in range(0, tiles, step)]


def send_kernel(nodes, send_list, low, mid, high):
    slots = send_list.shape[1]
    rows = dot(list_hot(send_list[...], nodes.shape[0]), nodes[...]).astype(BF16)
    low[...] = rows[: 3 * slots]
    mid[...] = rows[3 * slots : 5 * slots]
    high[...] = rows[5 * slots :]


def local_kernel(nodes, edges, senders, receivers, w_in, pre):
    count, width = nodes.shape
    tile_rows = senders.shape[1]
    x = nodes[...]
    table = jnp.concatenate(
        [
            dot(x, w_in[width : 2 * width]).astype(BF16),
            dot(x, w_in[2 * width :]).astype(BF16),
        ],
        axis=0,
    )
    by_sender = columns_of(senders[...])
    by_receiver = columns_of(receivers[...])
    w_edge = w_in[:width]
    for tiles in chunks_of(senders.shape[0]):
        rows = pl.ds(tiles[0] * tile_rows, len(tiles) * tile_rows)
        hot = jnp.concatenate(
            [hot_rows(by_sender, tiles, 0, count), hot_rows(by_receiver, tiles, 0, count)], axis=1
        )
        pre[rows, :] = dot(edges[rows, :], w_edge) + dot(hot, table)


def forward_kernel(
    count_ref,
    nodes,
    node_grads,
    senders,
    receivers,
    pre_local,
    from_high,
    from_low,
    upward,
    downward,
    w_in,
    w_out,
    gain_edge,
    w_node_in,
    w_node_out,
    gain_node,
    halo_out,
    pre_out,
    normed_out,
    scale_out,
    agg_grad_out,
    node_part_out,
    node_sums,
):
    count, width = nodes.shape
    tile_rows = senders.shape[1]
    slots = from_high.shape[0] // 3
    halo = jnp.concatenate(
        [
            downward[:slots],
            from_high[slots : 2 * slots],
            upward[:slots],
            downward[slots : 2 * slots],
            upward[slots : 2 * slots],
            downward[2 * slots :],
            from_low[slots : 2 * slots],
            upward[2 * slots :],
        ],
        axis=0,
    )
    halo_out[...] = halo
    table = dot(halo, w_in[width : 2 * width]).astype(BF16)
    by_sender = columns_of(senders[...])
    receiver_ids = receivers[...]
    gain = gain_edge[...].astype(F32)
    total = jnp.zeros((count, width), F32)
    for tiles in chunks_of(senders.shape[0]):
        rows = pl.ds(tiles[0] * tile_rows, len(tiles) * tile_rows)
        value = pre_local[rows, :] + dot(hot_rows(by_sender, tiles, count, halo.shape[0]), table)
        pre_out[rows, :] = value
        hidden = (value * sigmoid(value)).astype(BF16)
        normed, scale_inv = normalize(dot(hidden, w_out[...]))
        normed_out[rows, :] = normed
        scale_out[rows, :] = jnp.broadcast_to(scale_inv, (len(tiles) * tile_rows, 128))
        live = live_rows(count_ref, tiles[0], len(tiles), tile_rows)
        message = (live * gain * normed).astype(BF16)
        total = total + dot(hot_columns(receiver_ids, tiles, 0, count), message)
    aggregated = total.astype(BF16)
    x = nodes[...]
    w_first = w_node_in[:width]
    w_second = w_node_in[width:]
    node_pre = dot(x, w_first) + dot(aggregated, w_second)
    sigma = sigmoid(node_pre)
    node_hidden = (node_pre * sigma).astype(BF16)
    normed, scale_inv = normalize(dot(node_hidden, w_node_out[...]))
    upstream = node_grads[...].astype(F32)
    out_grad = norm_back(normed, scale_inv, gain_node[...].astype(F32), upstream).astype(BF16)
    slope = sigma * (1.0 + node_pre * (1.0 - sigma))
    pre_grad = (dot_nt(out_grad, w_node_out[...]) * slope).astype(BF16)
    agg_grad_out[...] = dot_nt(pre_grad, w_second).astype(BF16)
    node_part_out[...] = upstream + dot_nt(pre_grad, w_first)
    node_sums[:width] = dot_tn(x, pre_grad)
    node_sums[width : 2 * width] = dot_tn(aggregated, pre_grad)
    node_sums[2 * width : 3 * width] = dot_tn(node_hidden, out_grad)
    node_sums[3 * width :] = jnp.broadcast_to(
        jnp.sum(upstream * normed, axis=0, keepdims=True), (8, width)
    )


def backward_kernel(
    count_ref,
    nodes,
    halo,
    edges,
    edge_grads,
    senders,
    receivers,
    pre,
    normed,
    scale,
    agg_grad,
    w_in,
    w_out,
    gain_edge,
    pre_grad_out,
    sender_out,
    receiver_out,
    up_out,
    down_out,
    rest_out,
    edge_sums,
):
    count, width = nodes.shape
    tile_rows = senders.shape[1]
    slots = up_out.shape[0] // 3
    by_receiver = columns_of(receivers[...])
    sender_ids = senders[...]
    receiver_ids = receivers[...]
    gain = gain_edge[...].astype(F32)
    extended = count + halo.shape[0]
    sender_total = jnp.zeros((extended, width), F32)
    receiver_total = jnp.zeros((count, width), F32)
    first = jnp.zeros((width, width), F32)
    second = jnp.zeros((width, width), F32)
    gain_total = jnp.zeros((1, width), F32)
    for tiles in chunks_of(senders.shape[0]):
        rows = pl.ds(tiles[0] * tile_rows, len(tiles) * tile_rows)
        live = live_rows(count_ref, tiles[0], len(tiles), tile_rows)
        upstream = live * (
            edge_grads[rows, :].astype(F32)
            + dot(hot_rows(by_receiver, tiles, 0, count), agg_grad[...])
        )
        chunk_normed = normed[rows, :]
        gain_total = gain_total + jnp.sum(upstream * chunk_normed, axis=0, keepdims=True)
        out_grad = norm_back(chunk_normed, scale[rows, :1], gain, upstream).astype(BF16)
        value = pre[rows, :]
        sigma = sigmoid(value)
        hidden = (value * sigma).astype(BF16)
        slope = sigma * (1.0 + value * (1.0 - sigma))
        pre_grad = (dot_nt(out_grad, w_out[...]) * slope).astype(BF16)
        pre_grad_out[rows, :] = pre_grad
        second = second + dot_tn(hidden, out_grad)
        first = first + dot_tn(edges[rows, :], pre_grad)
        sender_total = sender_total + dot(hot_columns(sender_ids, tiles, 0, extended), pre_grad)
        receiver_total = receiver_total + dot(
            hot_columns(receiver_ids, tiles, 0, count), pre_grad
        )
    own = sender_total[:count].astype(BF16)
    away = sender_total[count:].astype(BF16)
    received = receiver_total.astype(BF16)
    sender_out[...] = own
    receiver_out[...] = received
    halo_grad = dot_nt(away, w_in[width : 2 * width]).astype(BF16)
    parts = [halo_grad[k * slots : (k + 1) * slots] for k in range(8)]
    up_out[...] = jnp.concatenate([parts[0], parts[3], parts[5]], axis=0)
    down_out[...] = jnp.concatenate([parts[2], parts[4], parts[7]], axis=0)
    rest_out[...] = jnp.concatenate([parts[1], parts[6]], axis=0)
    x = nodes[...]
    edge_sums[:width] = first
    edge_sums[width : 2 * width] = dot_tn(x, own) + dot_tn(halo[...], away)
    edge_sums[2 * width : 3 * width] = dot_tn(x, received)
    edge_sums[3 * width : 4 * width] = second
    edge_sums[4 * width :] = jnp.broadcast_to(gain_total, (8, width))


def finish_kernel(
    edge_grads, pre_grad, sender_sum, receiver_sum, node_part, w_in, edges_grad, local_grad
):
    width = w_in.shape[1]
    edges_grad[...] = (
        edge_grads[...].astype(F32) + dot_nt(pre_grad[...], w_in[:width])
    ).astype(BF16)
    local_grad[...] = (
        node_part[...]
        + dot_nt(sender_sum[...], w_in[width : 2 * width])
        + dot_nt(receiver_sum[...], w_in[2 * width :])
    )


def return_kernel(send_list, local_grad, up_back, down_back, to_high, to_low, nodes_grad):
    slots = send_list.shape[1]

    def block(ref, k):
        return ref[k * slots : (k + 1) * slots]

    returned = jnp.concatenate(
        [
            block(to_high, 0),
            block(to_high, 2),
            block(to_high, 1),
            block(up_back, 1),
            block(down_back, 1),
            block(to_low, 0),
            block(to_low, 2),
            block(to_low, 1),
        ],
        axis=0,
    )
    hot = list_hot(send_list[...], local_grad.shape[0])
    nodes_grad[...] = (local_grad[...] + dot_tn(hot, returned)).astype(BF16)


def call(body, outs, flops, *operands, scalars=0):
    moved = sum(x.size * x.dtype.itemsize for x in operands)
    moved += sum(x.size * jnp.dtype(x.dtype).itemsize for x in outs)
    smem = pl.BlockSpec(memory_space=pltpu.SMEM)
    vmem = pl.BlockSpec(memory_space=pltpu.VMEM)
    return pl.pallas_call(
        body,
        out_shape=outs,
        in_specs=[smem] * scalars + [vmem] * (len(operands) - scalars),
        out_specs=[vmem] * len(outs),
        compiler_params=pltpu.CompilerParams(vmem_limit_bytes=VMEM_LIMIT),
        cost_estimate=pl.CostEstimate(flops=flops, bytes_accessed=moved, transcendentals=0),
    )(*operands)


def shaped(rows, columns, dtype):
    return jax.ShapeDtypeStruct((rows, columns), dtype)


def on_device(
    nodes,
    edges,
    edge_grads,
    node_grads,
    send_list,
    senders,
    receivers,
    tile_count,
    w_edge_in,
    w_edge_out,
    gain_edge,
    w_node_in,
    w_node_out,
    gain_node,
):
    count, width = nodes.shape
    slots = send_list.shape[1]
    halo_rows = 8 * slots
    edge_rows = edges.shape[0]
    square = 2 * width * width
    gain_edge = gain_edge.reshape(1, width)
    gain_node = gain_node.reshape(1, width)

    low, mid, high = call(
        send_kernel,
        [
            shaped(3 * slots, width, BF16),
            shaped(2 * slots, width, BF16),
            shaped(3 * slots, width, BF16),
        ],
        2 * halo_rows * count * width,
        nodes,
        send_list,
    )
    from_low = passed_along(high, "px", 1)
    from_high = passed_along(low, "px", -1)
    upward = passed_along(
        jnp.concatenate([from_high[2 * slots :], mid[slots:], from_low[2 * slots :]]), "py", 1
    )
    downward = passed_along(
        jnp.concatenate([from_high[:slots], mid[:slots], from_low[:slots]]), "py", -1
    )
    (pre_local,) = call(
        local_kernel,
        [shaped(edge_rows, width, F32)],
        square * (2 * count + edge_rows) + 4 * edge_rows * count * width,
        nodes,
        edges,
        senders,
        receivers,
        w_edge_in,
    )
    halo, pre, normed, scale, agg_grad, node_part, node_sums = call(
        forward_kernel,
        [
            shaped(halo_rows, width, BF16),
            shaped(edge_rows, width, F32),
            shaped(edge_rows, width, F32),
            shaped(edge_rows, 128, F32),
            shaped(count, width, BF16),
            shaped(count, width, F32),
            shaped(3 * width + 8, width, F32),
        ],
        square * (2 * edge_rows + 9 * count) + 2 * edge_rows * count * width,
        tile_count,
        nodes,
        node_grads,
        senders,
        receivers,
        pre_local,
        from_high,
        from_low,
        upward,
        downward,
        w_edge_in,
        w_edge_out,
        gain_edge,
        w_node_in,
        w_node_out,
        gain_node,
        scalars=1,
    )
    devices = lax.axis_size("px") * lax.axis_size("py")
    node_parts = lax.all_to_all(
        node_sums[: 3 * width].astype(BF16).reshape(devices, -1, width), ("px", "py"), 0, 0
    )
    node_rows = lax.all_gather(
        jnp.sum(node_parts.astype(F32), axis=0).astype(BF16), ("px", "py"), axis=0, tiled=True
    )
    pre_grad, sender_sum, receiver_sum, up, down, rest, edge_sums = call(
        backward_kernel,
        [
            shaped(edge_rows, width, BF16),
            shaped(count, width, BF16),
            shaped(count, width, BF16),
            shaped(3 * slots, width, BF16),
            shaped(3 * slots, width, BF16),
            shaped(2 * slots, width, BF16),
            shaped(4 * width + 8, width, F32),
        ],
        square * (4 * edge_rows + 2 * count + 2 * halo_rows)
        + 2 * edge_rows * (3 * count + halo_rows) * width,
        tile_count,
        nodes,
        halo,
        edges,
        edge_grads,
        senders,
        receivers,
        pre,
        normed,
        scale,
        agg_grad,
        w_edge_in,
        w_edge_out,
        gain_edge,
        scalars=1,
    )
    edge_part = lax.psum_scatter(
        edge_sums[: 4 * width], ("px", "py"), scatter_dimension=0, tiled=True
    )
    edge_rows_all = lax.all_gather(edge_part.astype(BF16), ("px", "py"), axis=0, tiled=True)
    gains = jnp.concatenate([edge_sums[4 * width :][:1], node_sums[3 * width :][:1]])
    gains = lax.psum(gains, ("px", "py")).astype(BF16)
    up_back = passed_along(up, "py", 1)
    down_back = passed_along(down, "py", -1)
    to_high = passed_along(
        jnp.concatenate([up_back[:slots], down_back[:slots], rest[:slots]]), "px", 1
    )
    to_low = passed_along(
        jnp.concatenate([up_back[2 * slots :], down_back[2 * slots :], rest[slots:]]), "px", -1
    )
    edges_grad, local_grad = call(
        finish_kernel,
        [shaped(edge_rows, width, BF16), shaped(count, width, F32)],
        square * (edge_rows + 2 * count),
        edge_grads,
        pre_grad,
        sender_sum,
        receiver_sum,
        node_part,
        w_edge_in,
    )
    (nodes_grad,) = call(
        return_kernel,
        [shaped(count, width, BF16)],
        2 * halo_rows * count * width,
        send_list,
        local_grad,
        up_back,
        down_back,
        to_high,
        to_low,
    )
    return (
        nodes_grad,
        edges_grad,
        edge_rows_all[: 3 * width],
        edge_rows_all[3 * width :],
        gains[0],
        node_rows[: 2 * width],
        node_rows[2 * width :],
        gains[1],
    )


def solution(mesh):
    in_specs = (
        P(("groups", "px", "py"), None),
        P(("groups", "px", "py"), None),
        P(("groups", "px", "py"), None),
        P(("groups", "px", "py"), None),
        P(("groups", "px", "py"), None),
        P(("groups", "px", "py"), None),
        P(("groups", "px", "py"), None),
        P(("groups", "px", "py")),
        P(),
        P(),
        P(),
        P(),
        P(),
        P(),
    )
    out_specs = (
        P(("groups", "px", "py"), None),
        P(("groups", "px", "py"), None),
        P("groups", None),
        P("groups", None),
        P("groups"),
        P("groups", None),
        P("groups", None),
        P("groups"),
    )
    return jax.shard_map(
        on_device, mesh=mesh, in_specs=in_specs, out_specs=out_specs, check_vma=False
    )
```

```python
import jax
import jax.numpy as jnp
from jax import lax
from jax.experimental import pallas as pl
from jax.experimental.pallas import tpu as pltpu
from jax.sharding import PartitionSpec as P

EPS = 1e-05
BF16 = jnp.bfloat16
F32 = jnp.float32
VMEM_LIMIT = 24 * 1024 * 1024


CORE = "core"
PY = ("side", "core")
CHIPS = ("px", "side")


def passed_along(array, axis, by):
    size = lax.axis_size(axis)
    return lax.ppermute(array, axis, [(i, (i + by) % size) for i in range(size)])


def across_cores(array):
    return lax.ppermute(array, CORE, [(0, 1), (1, 0)])


def dot(left, right):
    return jnp.dot(left, right, preferred_element_type=F32)


def dot_tn(left, right):
    return lax.dot_general(left, right, (((0,), (0,)), ((), ())), preferred_element_type=F32)


def dot_nt(left, right):
    return lax.dot_general(left, right, (((1,), (1,)), ((), ())), preferred_element_type=F32)


def sigmoid(value):
    return 1.0 / (1.0 + jnp.exp(-value))


def normalize(value):
    centered = value - jnp.mean(value, axis=-1, keepdims=True)
    scale_inv = lax.rsqrt(jnp.mean(centered * centered, axis=-1, keepdims=True) + EPS)
    return centered * scale_inv, scale_inv


def norm_back(normed, scale_inv, gain, upstream):
    scaled = upstream * gain
    inner = (
        scaled
        - jnp.mean(scaled, axis=-1, keepdims=True)
        - normed * jnp.mean(scaled * normed, axis=-1, keepdims=True)
    )
    return inner * scale_inv


def columns_of(ids):
    rows, lanes = ids.shape
    padded = -(-rows // 8) * 8
    if padded > rows:
        ids = jnp.concatenate([ids, jnp.zeros((padded - rows, lanes), ids.dtype)], axis=0)
    return ids.T


def hot_rows(columns, tiles, base, count):
    parts = []
    for tile in tiles:
        column = columns[:, tile : tile + 1] - base
        lanes = lax.broadcasted_iota(jnp.int32, (columns.shape[0], count), 1)
        parts.append(jnp.where(lanes == column, 1.0, 0.0).astype(BF16))
    return jnp.concatenate(parts, axis=0) if len(parts) > 1 else parts[0]


def hot_columns(ids, tiles, base, count):
    parts = []
    for tile in tiles:
        row = ids[tile : tile + 1, :] - base
        subs = lax.broadcasted_iota(jnp.int32, (count, ids.shape[1]), 0)
        parts.append(jnp.where(subs == row, 1.0, 0.0).astype(BF16))
    return jnp.concatenate(parts, axis=1) if len(parts) > 1 else parts[0]


def list_hot(ids, count):
    directions, slots = ids.shape
    wide = jnp.concatenate([ids, jnp.zeros((directions, 128 - slots), ids.dtype)], axis=1)
    columns = wide.T
    parts = []
    for k in range(directions):
        lanes = lax.broadcasted_iota(jnp.int32, (slots, count), 1)
        parts.append(jnp.where(lanes == columns[:slots, k : k + 1], 1.0, 0.0).astype(BF16))
    return jnp.concatenate(parts, axis=0)


def live_rows(count_ref, first_tile, tiles, tile_rows):
    rows = lax.broadcasted_iota(jnp.int32, (tiles * tile_rows, 1), 0)
    return jnp.where(rows < (count_ref[0] - first_tile) * tile_rows, 1.0, 0.0)


def chunks_of(tiles):
    step = 3 if tiles % 3 == 0 else 1
    return [list(range(first, first + step)) for first in range(0, tiles, step)]


def fetch_all(sources, targets, sems):
    copies = [
        pltpu.make_async_copy(source, target, sems.at[i])
        for i, (source, target) in enumerate(zip(sources, targets))
    ]
    for copy in copies:
        copy.start()
    return copies


def send_kernel(nodes_hbm, list_hbm, low, mid, high, nodes, send_list, sems):
    slots = send_list.shape[1]
    for copy in fetch_all([list_hbm, nodes_hbm], [send_list, nodes], sems):
        copy.wait()
    rows = dot(list_hot(send_list[...], nodes.shape[0]), nodes[...]).astype(BF16)
    low[...] = rows[: 3 * slots]
    mid[...] = rows[3 * slots : 5 * slots]
    high[...] = rows[5 * slots :]


def local_kernel(nodes, *refs):
    fetched = (len(refs) - 2) // 2
    pre, sems = refs[fetched], refs[-1]
    targets = refs[fetched + 1 : -1]
    w_in, senders, receivers, edges = targets[:4]
    copies = fetch_all(refs[:fetched], targets, sems)
    count, width = nodes.shape
    tile_rows = senders.shape[1]
    x = nodes[...]
    for copy in copies[:4]:
        copy.wait()
    table = jnp.concatenate(
        [
            dot(x, w_in[width : 2 * width]).astype(BF16),
            dot(x, w_in[2 * width :]).astype(BF16),
        ],
        axis=0,
    )
    by_sender = columns_of(senders[...])
    by_receiver = columns_of(receivers[...])
    w_edge = w_in[:width]
    for tiles in chunks_of(senders.shape[0]):
        rows = pl.ds(tiles[0] * tile_rows, len(tiles) * tile_rows)
        hot = jnp.concatenate(
            [hot_rows(by_sender, tiles, 0, count), hot_rows(by_receiver, tiles, 0, count)], axis=1
        )
        pre[rows, :] = dot(edges[rows, :], w_edge) + dot(hot, table)
    for copy in copies[4:]:
        copy.wait()


def split_by_core(sums, keep_out, away_out):
    half = keep_out.shape[0]
    core = lax.axis_index(CORE)
    keep_out[...] = sums[pl.ds(pl.multiple_of(core * half, half), half), :]
    away = sums[pl.ds(pl.multiple_of((1 - core) * half, half), half), :]
    away_out[:half] = away.astype(BF16)


def pack_gains(edge_gain, node_gain):
    edge_high = edge_gain.astype(BF16).astype(F32)
    node_high = node_gain.astype(BF16).astype(F32)
    row = lax.broadcasted_iota(jnp.int32, (16, edge_gain.shape[1]), 0)
    packed = jnp.where(row == 0, edge_high, 0.0)
    packed = jnp.where(row == 1, edge_gain - edge_high, packed)
    packed = jnp.where(row == 2, node_high, packed)
    packed = jnp.where(row == 3, node_gain - node_high, packed)
    return packed.astype(BF16)


def forward_kernel(
    count_ref,
    nodes,
    node_grads,
    senders,
    receivers,
    pre_local,
    from_high,
    from_low,
    upward,
    downward,
    w_in,
    w_out,
    gain_edge,
    w_node_in,
    w_node_out,
    gain_node,
    halo_out,
    pre_out,
    normed_out,
    scale_out,
    agg_grad_out,
    node_part_out,
    keep_out,
    away_out,
    node_gain_out,
    node_sums,
):
    count, width = nodes.shape
    tile_rows = senders.shape[1]
    slots = from_high.shape[0] // 3
    halo = jnp.concatenate(
        [
            downward[:slots],
            from_high[slots : 2 * slots],
            upward[:slots],
            downward[slots : 2 * slots],
            upward[slots : 2 * slots],
            downward[2 * slots :],
            from_low[slots : 2 * slots],
            upward[2 * slots :],
        ],
        axis=0,
    )
    halo_out[...] = halo
    table = dot(halo, w_in[width : 2 * width]).astype(BF16)
    by_sender = columns_of(senders[...])
    receiver_ids = receivers[...]
    gain = gain_edge[...].astype(F32)
    total = jnp.zeros((count, width), F32)
    for tiles in chunks_of(senders.shape[0]):
        rows = pl.ds(tiles[0] * tile_rows, len(tiles) * tile_rows)
        value = pre_local[rows, :] + dot(hot_rows(by_sender, tiles, count, halo.shape[0]), table)
        pre_out[rows, :] = value
        hidden = (value * sigmoid(value)).astype(BF16)
        normed, scale_inv = normalize(dot(hidden, w_out[...]))
        normed_out[rows, :] = normed
        scale_out[rows, :] = jnp.broadcast_to(scale_inv, (len(tiles) * tile_rows, 128))
        live = live_rows(count_ref, tiles[0], len(tiles), tile_rows)
        message = (live * gain * normed).astype(BF16)
        total = total + dot(hot_columns(receiver_ids, tiles, 0, count), message)
    aggregated = total.astype(BF16)
    x = nodes[...]
    w_first = w_node_in[:width]
    w_second = w_node_in[width:]
    node_pre = dot(x, w_first) + dot(aggregated, w_second)
    sigma = sigmoid(node_pre)
    node_hidden = (node_pre * sigma).astype(BF16)
    normed, scale_inv = normalize(dot(node_hidden, w_node_out[...]))
    upstream = node_grads[...].astype(F32)
    out_grad = norm_back(normed, scale_inv, gain_node[...].astype(F32), upstream).astype(BF16)
    slope = sigma * (1.0 + node_pre * (1.0 - sigma))
    pre_grad = (dot_nt(out_grad, w_node_out[...]) * slope).astype(BF16)
    agg_grad_out[...] = dot_nt(pre_grad, w_second).astype(BF16)
    node_part_out[...] = upstream + dot_nt(pre_grad, w_first)
    node_sums[:width] = dot_tn(x, pre_grad)
    node_sums[width : 2 * width] = dot_tn(aggregated, pre_grad)
    node_sums[2 * width : 3 * width] = dot_tn(node_hidden, out_grad)
    split_by_core(node_sums, keep_out, away_out)
    node_gain_out[...] = jnp.broadcast_to(
        jnp.sum(upstream * normed, axis=0, keepdims=True), (8, width)
    )


def backward_kernel(
    count_ref,
    nodes,
    halo,
    edges,
    edge_grads,
    senders,
    receivers,
    pre,
    normed,
    scale,
    agg_grad,
    w_in,
    w_out,
    gain_edge,
    node_gain,
    pre_grad_out,
    sender_out,
    receiver_out,
    up_out,
    down_out,
    rest_out,
    keep_out,
    away_out,
    gains_out,
    edge_sums,
):
    count, width = nodes.shape
    tile_rows = senders.shape[1]
    slots = up_out.shape[0] // 3
    by_receiver = columns_of(receivers[...])
    sender_ids = senders[...]
    receiver_ids = receivers[...]
    gain = gain_edge[...].astype(F32)
    extended = count + halo.shape[0]
    sender_total = jnp.zeros((extended, width), F32)
    receiver_total = jnp.zeros((count, width), F32)
    first = jnp.zeros((width, width), F32)
    second = jnp.zeros((width, width), F32)
    gain_total = jnp.zeros((1, width), F32)
    for tiles in chunks_of(senders.shape[0]):
        rows = pl.ds(tiles[0] * tile_rows, len(tiles) * tile_rows)
        live = live_rows(count_ref, tiles[0], len(tiles), tile_rows)
        upstream = live * (
            edge_grads[rows, :].astype(F32)
            + dot(hot_rows(by_receiver, tiles, 0, count), agg_grad[...])
        )
        chunk_normed = normed[rows, :]
        gain_total = gain_total + jnp.sum(upstream * chunk_normed, axis=0, keepdims=True)
        out_grad = norm_back(chunk_normed, scale[rows, :1], gain, upstream).astype(BF16)
        value = pre[rows, :]
        sigma = sigmoid(value)
        hidden = (value * sigma).astype(BF16)
        slope = sigma * (1.0 + value * (1.0 - sigma))
        pre_grad = (dot_nt(out_grad, w_out[...]) * slope).astype(BF16)
        pre_grad_out[rows, :] = pre_grad
        second = second + dot_tn(hidden, out_grad)
        first = first + dot_tn(edges[rows, :], pre_grad)
        sender_total = sender_total + dot(hot_columns(sender_ids, tiles, 0, extended), pre_grad)
        receiver_total = receiver_total + dot(
            hot_columns(receiver_ids, tiles, 0, count), pre_grad
        )
    own = sender_total[:count].astype(BF16)
    away = sender_total[count:].astype(BF16)
    received = receiver_total.astype(BF16)
    sender_out[...] = own
    receiver_out[...] = received
    halo_grad = dot_nt(away, w_in[width : 2 * width]).astype(BF16)
    parts = [halo_grad[k * slots : (k + 1) * slots] for k in range(8)]
    up_out[...] = jnp.concatenate([parts[0], parts[3], parts[5]], axis=0)
    down_out[...] = jnp.concatenate([parts[2], parts[4], parts[7]], axis=0)
    rest_out[...] = jnp.concatenate([parts[1], parts[6]], axis=0)
    x = nodes[...]
    edge_sums[:width] = first
    edge_sums[width : 2 * width] = dot_tn(x, own) + dot_tn(halo[...], away)
    edge_sums[2 * width : 3 * width] = dot_tn(x, received)
    edge_sums[3 * width : 4 * width] = second
    split_by_core(edge_sums, keep_out, away_out)
    gains = pack_gains(gain_total, node_gain[:1])
    away_out[keep_out.shape[0] :] = gains
    gains_out[...] = gains


def edge_pair_kernel(keep, gains, other, rows_out, gains_out):
    half = keep.shape[0]
    rows_out[...] = (keep[...] + other[:half].astype(F32)).astype(BF16)
    both = gains[...].astype(F32) + other[half:].astype(F32)
    gains_out[...] = pack_gains(both[0:1] + both[1:2], both[2:3] + both[3:4])


def node_pair_kernel(keep, other, rows_out):
    rows_out[...] = (keep[...] + other[...].astype(F32)).astype(BF16)


def place_kernel(own, other, first, second, sems):
    half = own.shape[0]
    rest = first.shape[0] - half
    core = lax.axis_index(CORE)

    def place(low, high):
        copies = [
            pltpu.make_async_copy(low, first.at[:half], sems.at[0]),
            pltpu.make_async_copy(high.at[:rest], first.at[half:], sems.at[1]),
            pltpu.make_async_copy(high.at[rest:], second, sems.at[2]),
        ]
        for copy in copies:
            copy.start()
        for copy in copies:
            copy.wait()

    @pl.when(core == 0)
    def _():
        place(own, other)

    @pl.when(core == 1)
    def _():
        place(other, own)


def finish_kernel(
    edge_grads, pre_grad, sender_sum, receiver_sum, node_part, w_in, edges_grad, local_grad
):
    width = w_in.shape[1]
    edges_grad[...] = (
        edge_grads[...].astype(F32) + dot_nt(pre_grad[...], w_in[:width])
    ).astype(BF16)
    local_grad[...] = (
        node_part[...]
        + dot_nt(sender_sum[...], w_in[width : 2 * width])
        + dot_nt(receiver_sum[...], w_in[2 * width :])
    )


def return_kernel(send_list, local_grad, up_back, down_back, to_high, to_low, nodes_grad):
    slots = send_list.shape[1]

    def block(ref, k):
        return ref[k * slots : (k + 1) * slots]

    returned = jnp.concatenate(
        [
            block(to_high, 0),
            block(to_high, 2),
            block(to_high, 1),
            block(up_back, 1),
            block(down_back, 1),
            block(to_low, 0),
            block(to_low, 2),
            block(to_low, 1),
        ],
        axis=0,
    )
    hot = list_hot(send_list[...], local_grad.shape[0])
    nodes_grad[...] = (local_grad[...] + dot_tn(hot, returned)).astype(BF16)


SMEM = pltpu.SMEM
VMEM = pltpu.VMEM
HBM = pltpu.HBM


def call(body, outs, flops, *operands, spaces=(), out_space=VMEM, scratch=()):
    moved = sum(x.size * x.dtype.itemsize for x in operands)
    moved += sum(x.size * jnp.dtype(x.dtype).itemsize for x in outs)
    spaces = list(spaces) + [VMEM] * (len(operands) - len(spaces))
    return pl.pallas_call(
        body,
        out_shape=outs,
        in_specs=[pl.BlockSpec(memory_space=space) for space in spaces],
        out_specs=[pl.BlockSpec(memory_space=out_space) for _ in outs],
        scratch_shapes=list(scratch),
        compiler_params=pltpu.CompilerParams(vmem_limit_bytes=VMEM_LIMIT),
        cost_estimate=pl.CostEstimate(flops=flops, bytes_accessed=moved, transcendentals=0),
    )(*operands)


def like(array):
    return jax.ShapeDtypeStruct(array.shape, array.dtype)


def spread(rows):
    chips = lax.axis_size(CHIPS)
    copies = jnp.broadcast_to(rows[None], (chips,) + rows.shape)
    return lax.all_to_all(copies, CHIPS, 0, 0).reshape(chips * rows.shape[0], rows.shape[1])


def shaped(rows, columns, dtype):
    return jax.ShapeDtypeStruct((rows, columns), dtype)


def placed(own, first_rows, second_rows):
    width = own.shape[1]
    return call(
        place_kernel,
        [shaped(first_rows, width, BF16), shaped(second_rows, width, BF16)],
        0,
        own,
        across_cores(own),
        out_space=HBM,
        scratch=[pltpu.SemaphoreType.DMA((3,))],
    )


def on_device(
    nodes,
    edges,
    edge_grads,
    node_grads,
    send_list,
    senders,
    receivers,
    tile_count,
    w_edge_in,
    w_edge_out,
    gain_edge,
    w_node_in,
    w_node_out,
    gain_node,
):
    count, width = nodes.shape
    slots = send_list.shape[1]
    halo_rows = 8 * slots
    edge_rows = edges.shape[0]
    square = 2 * width * width
    gain_edge = gain_edge.reshape(1, width)
    gain_node = gain_node.reshape(1, width)

    low, mid, high, nodes, send_list = call(
        send_kernel,
        [
            shaped(3 * slots, width, BF16),
            shaped(2 * slots, width, BF16),
            shaped(3 * slots, width, BF16),
            like(nodes),
            like(send_list),
        ],
        2 * halo_rows * count * width,
        nodes,
        send_list,
        spaces=[HBM, HBM],
        scratch=[pltpu.SemaphoreType.DMA((2,))],
    )
    from_low = passed_along(high, "px", 1)
    from_high = passed_along(low, "px", -1)
    upward = passed_along(
        jnp.concatenate([from_high[2 * slots :], mid[slots:], from_low[2 * slots :]]), PY, 1
    )
    downward = passed_along(
        jnp.concatenate([from_high[:slots], mid[:slots], from_low[:slots]]), PY, -1
    )
    fetched = [
        w_edge_in,
        senders,
        receivers,
        edges,
        w_edge_out,
        w_node_in,
        w_node_out,
        node_grads,
        edge_grads,
    ]
    pre_local, *fetched = call(
        local_kernel,
        [shaped(edge_rows, width, F32)] + [like(x) for x in fetched],
        square * (2 * count + edge_rows) + 4 * edge_rows * count * width,
        nodes,
        *fetched,
        spaces=[VMEM] + [HBM] * len(fetched),
        scratch=[pltpu.SemaphoreType.DMA((len(fetched),))],
    )
    (
        w_edge_in,
        senders,
        receivers,
        edges,
        w_edge_out,
        w_node_in,
        w_node_out,
        node_grads,
        edge_grads,
    ) = fetched
    halo, pre, normed, scale, agg_grad, node_part, node_keep, node_away, node_gain = call(
        forward_kernel,
        [
            shaped(halo_rows, width, BF16),
            shaped(edge_rows, width, F32),
            shaped(edge_rows, width, F32),
            shaped(edge_rows, 128, F32),
            shaped(count, width, BF16),
            shaped(count, width, F32),
            shaped(3 * width // 2, width, F32),
            shaped(3 * width // 2, width, BF16),
            shaped(8, width, F32),
        ],
        square * (2 * edge_rows + 9 * count) + 2 * edge_rows * count * width,
        tile_count,
        nodes,
        node_grads,
        senders,
        receivers,
        pre_local,
        from_high,
        from_low,
        upward,
        downward,
        w_edge_in,
        w_edge_out,
        gain_edge,
        w_node_in,
        w_node_out,
        gain_node,
        spaces=[SMEM],
        scratch=[pltpu.VMEM((3 * width, width), F32)],
    )
    node_other = across_cores(node_away)
    pre_grad, sender_sum, receiver_sum, up, down, rest, edge_keep, edge_away, gains = call(
        backward_kernel,
        [
            shaped(edge_rows, width, BF16),
            shaped(count, width, BF16),
            shaped(count, width, BF16),
            shaped(3 * slots, width, BF16),
            shaped(3 * slots, width, BF16),
            shaped(2 * slots, width, BF16),
            shaped(2 * width, width, F32),
            shaped(2 * width + 16, width, BF16),
            shaped(16, width, BF16),
        ],
        square * (4 * edge_rows + 2 * count + 2 * halo_rows)
        + 2 * edge_rows * (3 * count + halo_rows) * width,
        tile_count,
        nodes,
        halo,
        edges,
        edge_grads,
        senders,
        receivers,
        pre,
        normed,
        scale,
        agg_grad,
        w_edge_in,
        w_edge_out,
        gain_edge,
        node_gain,
        spaces=[SMEM],
        scratch=[pltpu.VMEM((4 * width, width), F32)],
    )
    edge_other = across_cores(edge_away)
    (node_pair,) = call(
        node_pair_kernel, [shaped(3 * width // 2, width, BF16)], 0, node_keep, node_other
    )
    edge_pair, gains = call(
        edge_pair_kernel,
        [shaped(2 * width, width, BF16), like(gains)],
        0,
        edge_keep,
        gains,
        edge_other,
    )
    chips = lax.axis_size(CHIPS)
    blocks = jnp.concatenate(
        [
            edge_pair.reshape(chips, -1, width),
            jnp.broadcast_to(gains[None], (chips,) + gains.shape),
        ],
        axis=1,
    )
    edge_part = jnp.sum(lax.all_to_all(blocks, CHIPS, 0, 0).astype(F32), axis=0)
    node_part_sum = jnp.sum(
        lax.all_to_all(node_pair.reshape(chips, -1, width), CHIPS, 0, 0).astype(F32), axis=0
    )
    gains = edge_part[2 * width // chips :]
    edge_half = spread(edge_part[: 2 * width // chips].astype(BF16))
    node_half = spread(node_part_sum.astype(BF16))
    up_back = passed_along(up, PY, 1)
    down_back = passed_along(down, PY, -1)
    to_high = passed_along(
        jnp.concatenate([up_back[:slots], down_back[:slots], rest[:slots]]), "px", 1
    )
    to_low = passed_along(
        jnp.concatenate([up_back[2 * slots :], down_back[2 * slots :], rest[slots:]]), "px", -1
    )
    edges_grad, local_grad = call(
        finish_kernel,
        [shaped(edge_rows, width, BF16), shaped(count, width, F32)],
        square * (edge_rows + 2 * count),
        edge_grads,
        pre_grad,
        sender_sum,
        receiver_sum,
        node_part,
        w_edge_in,
    )
    (nodes_grad,) = call(
        return_kernel,
        [shaped(count, width, BF16)],
        2 * halo_rows * count * width,
        send_list,
        local_grad,
        up_back,
        down_back,
        to_high,
        to_low,
    )
    w_edge_in_grad, w_edge_out_grad = placed(edge_half, 3 * width, width)
    w_node_in_grad, w_node_out_grad = placed(node_half, 2 * width, width)
    return (
        nodes_grad,
        edges_grad,
        w_edge_in_grad,
        w_edge_out_grad,
        (gains[0] + gains[1]).astype(BF16),
        w_node_in_grad,
        w_node_out_grad,
        (gains[2] + gains[3]).astype(BF16),
    )


def solution(mesh):
    in_specs = (
        P(("groups", "px") + PY, None),
        P(("groups", "px") + PY, None),
        P(("groups", "px") + PY, None),
        P(("groups", "px") + PY, None),
        P(("groups", "px") + PY, None),
        P(("groups", "px") + PY, None),
        P(("groups", "px") + PY, None),
        P(("groups", "px") + PY),
        P(),
        P(),
        P(),
        P(),
        P(),
        P(),
    )
    out_specs = (
        P(("groups", "px") + PY, None),
        P(("groups", "px") + PY, None),
        P("groups", None),
        P("groups", None),
        P("groups"),
        P("groups", None),
        P("groups", None),
        P("groups"),
    )
    groups, px, py = mesh.devices.shape
    by_core = jax.sharding.Mesh(
        mesh.devices.reshape(groups, px, py // 2, 2), ("groups", "px") + PY
    )
    return jax.shard_map(
        on_device, mesh=by_core, in_specs=in_specs, out_specs=out_specs, check_vma=False
    )
```

```python
import functools

import jax
import jax.numpy as jnp
from jax import lax
from jax.experimental import pallas as pl
from jax.experimental.pallas import tpu as pltpu
from jax.sharding import PartitionSpec as P

EPS = 1e-05
BF16 = jnp.bfloat16
F32 = jnp.float32
VMEM_LIMIT = 24 * 1024 * 1024


CORE = "core"
PY = ("side", "core")
CHIPS = ("px", "side")


def passed_along(array, axis, by):
    size = lax.axis_size(axis)
    return lax.ppermute(array, axis, [(i, (i + by) % size) for i in range(size)])


def across_cores(array):
    return lax.ppermute(array, CORE, [(0, 1), (1, 0)])


def dot(left, right):
    return jnp.dot(left, right, preferred_element_type=F32)


def dot_tn(left, right):
    return lax.dot_general(left, right, (((0,), (0,)), ((), ())), preferred_element_type=F32)


def dot_nt(left, right):
    return lax.dot_general(left, right, (((1,), (1,)), ((), ())), preferred_element_type=F32)


def sigmoid(value):
    return 1.0 / (1.0 + jnp.exp(-value))


def normalize(value):
    centered = value - jnp.mean(value, axis=-1, keepdims=True)
    scale_inv = lax.rsqrt(jnp.mean(centered * centered, axis=-1, keepdims=True) + EPS)
    return centered * scale_inv, scale_inv


def norm_back(normed, scale_inv, gain, upstream):
    scaled = upstream * gain
    inner = (
        scaled
        - jnp.mean(scaled, axis=-1, keepdims=True)
        - normed * jnp.mean(scaled * normed, axis=-1, keepdims=True)
    )
    return inner * scale_inv


def columns_of(ids):
    rows, lanes = ids.shape
    padded = -(-rows // 8) * 8
    if padded > rows:
        ids = jnp.concatenate([ids, jnp.zeros((padded - rows, lanes), ids.dtype)], axis=0)
    return ids.T


def hot_rows(columns, tiles, base, count):
    parts = []
    for tile in tiles:
        column = columns[:, tile : tile + 1] - base
        lanes = lax.broadcasted_iota(jnp.int32, (columns.shape[0], count), 1)
        parts.append(jnp.where(lanes == column, 1.0, 0.0).astype(BF16))
    return jnp.concatenate(parts, axis=0) if len(parts) > 1 else parts[0]


def hot_columns(ids, tiles, base, count):
    parts = []
    for tile in tiles:
        row = ids[tile : tile + 1, :] - base
        subs = lax.broadcasted_iota(jnp.int32, (count, ids.shape[1]), 0)
        parts.append(jnp.where(subs == row, 1.0, 0.0).astype(BF16))
    return jnp.concatenate(parts, axis=1) if len(parts) > 1 else parts[0]


def list_hot(ids, count):
    directions, slots = ids.shape
    wide = jnp.concatenate([ids, jnp.zeros((directions, 128 - slots), ids.dtype)], axis=1)
    columns = wide.T
    parts = []
    for k in range(directions):
        lanes = lax.broadcasted_iota(jnp.int32, (slots, count), 1)
        parts.append(jnp.where(lanes == columns[:slots, k : k + 1], 1.0, 0.0).astype(BF16))
    return jnp.concatenate(parts, axis=0)


def live_rows(count_ref, first_tile, tiles, tile_rows):
    rows = lax.broadcasted_iota(jnp.int32, (tiles * tile_rows, 1), 0)
    return jnp.where(rows < (count_ref[0] - first_tile) * tile_rows, 1.0, 0.0)


def chunks_of(tiles):
    step = 3 if tiles % 3 == 0 else 1
    return [list(range(first, first + step)) for first in range(0, tiles, step)]


def fetch_all(sources, targets, sems):
    copies = [
        pltpu.make_async_copy(source, target, sems.at[i])
        for i, (source, target) in enumerate(zip(sources, targets))
    ]
    for copy in copies:
        copy.start()
    return copies


def send_kernel(nodes_hbm, list_hbm, low, mid, high, nodes, send_list, sems):
    slots = send_list.shape[1]
    for copy in fetch_all([list_hbm, nodes_hbm], [send_list, nodes], sems):
        copy.wait()
    rows = dot(list_hot(send_list[...], nodes.shape[0]), nodes[...]).astype(BF16)
    low[...] = rows[: 3 * slots]
    mid[...] = rows[3 * slots : 5 * slots]
    high[...] = rows[5 * slots :]


def local_kernel(nodes, *refs):
    fetched = (len(refs) - 2) // 2
    pre, sems = refs[fetched], refs[-1]
    targets = refs[fetched + 1 : -1]
    w_in, senders, receivers, edges = targets[:4]
    copies = fetch_all(refs[:fetched], targets, sems)
    count, width = nodes.shape
    tile_rows = senders.shape[1]
    x = nodes[...]
    for copy in copies[:4]:
        copy.wait()
    table = jnp.concatenate(
        [
            dot(x, w_in[width : 2 * width]).astype(BF16),
            dot(x, w_in[2 * width :]).astype(BF16),
        ],
        axis=0,
    )
    by_sender = columns_of(senders[...])
    by_receiver = columns_of(receivers[...])
    w_edge = w_in[:width]
    for tiles in chunks_of(senders.shape[0]):
        rows = pl.ds(tiles[0] * tile_rows, len(tiles) * tile_rows)
        hot = jnp.concatenate(
            [hot_rows(by_sender, tiles, 0, count), hot_rows(by_receiver, tiles, 0, count)], axis=1
        )
        pre[rows, :] = dot(edges[rows, :], w_edge) + dot(hot, table)
    for copy in copies[4:]:
        copy.wait()


def split_by_core(sums, first, keep_out, away_out):
    half = sums.shape[0] // 2
    core = lax.axis_index(CORE)
    keep_out[first : first + half] = sums[pl.ds(pl.multiple_of(core * half, half), half), :]
    away = sums[pl.ds(pl.multiple_of((1 - core) * half, half), half), :]
    away_out[first : first + half] = away.astype(BF16)


def pack_gains(edge_gain, node_gain):
    edge_high = edge_gain.astype(BF16).astype(F32)
    node_high = node_gain.astype(BF16).astype(F32)
    row = lax.broadcasted_iota(jnp.int32, (16, edge_gain.shape[1]), 0)
    packed = jnp.where(row == 0, edge_high, 0.0)
    packed = jnp.where(row == 1, edge_gain - edge_high, packed)
    packed = jnp.where(row == 2, node_high, packed)
    packed = jnp.where(row == 3, node_gain - node_high, packed)
    return packed.astype(BF16)


def layer_kernel(
    count_ref,
    nodes,
    node_grads,
    edges,
    edge_grads,
    senders,
    receivers,
    pre_local,
    from_high,
    from_low,
    upward,
    downward,
    w_in,
    w_out,
    gain_edge,
    w_node_in,
    w_node_out,
    gain_node,
    pre_grad_out,
    sender_out,
    receiver_out,
    node_part_out,
    up_out,
    down_out,
    rest_out,
    keep_out,
    away_out,
    gains_out,
    pre_kept,
    normed_kept,
    scale_kept,
    node_sums,
    edge_sums,
):
    count, width = nodes.shape
    tile_rows = senders.shape[1]
    slots = from_high.shape[0] // 3
    halo = jnp.concatenate(
        [
            downward[:slots],
            from_high[slots : 2 * slots],
            upward[:slots],
            downward[slots : 2 * slots],
            upward[slots : 2 * slots],
            downward[2 * slots :],
            from_low[slots : 2 * slots],
            upward[2 * slots :],
        ],
        axis=0,
    )
    table = dot(halo, w_in[width : 2 * width]).astype(BF16)
    by_sender = columns_of(senders[...])
    receiver_ids = receivers[...]
    gain = gain_edge[...].astype(F32)
    total = jnp.zeros((count, width), F32)
    for tiles in chunks_of(senders.shape[0]):
        rows = pl.ds(tiles[0] * tile_rows, len(tiles) * tile_rows)
        value = pre_local[rows, :] + dot(hot_rows(by_sender, tiles, count, halo.shape[0]), table)
        pre_kept[rows, :] = value
        hidden = (value * sigmoid(value)).astype(BF16)
        normed, scale_inv = normalize(dot(hidden, w_out[...]))
        normed_kept[rows, :] = normed
        scale_kept[rows, :] = jnp.broadcast_to(scale_inv, (len(tiles) * tile_rows, 128))
        live = live_rows(count_ref, tiles[0], len(tiles), tile_rows)
        message = (live * gain * normed).astype(BF16)
        total = total + dot(hot_columns(receiver_ids, tiles, 0, count), message)
    aggregated = total.astype(BF16)
    x = nodes[...]
    w_first = w_node_in[:width]
    w_second = w_node_in[width:]
    node_pre = dot(x, w_first) + dot(aggregated, w_second)
    sigma = sigmoid(node_pre)
    node_hidden = (node_pre * sigma).astype(BF16)
    normed, scale_inv = normalize(dot(node_hidden, w_node_out[...]))
    upstream = node_grads[...].astype(F32)
    out_grad = norm_back(normed, scale_inv, gain_node[...].astype(F32), upstream).astype(BF16)
    slope = sigma * (1.0 + node_pre * (1.0 - sigma))
    pre_grad = (dot_nt(out_grad, w_node_out[...]) * slope).astype(BF16)
    agg_grad = dot_nt(pre_grad, w_second).astype(BF16)
    node_part_out[...] = upstream + dot_nt(pre_grad, w_first)
    node_sums[:width] = dot_tn(x, pre_grad)
    node_sums[width : 2 * width] = dot_tn(aggregated, pre_grad)
    node_sums[2 * width : 3 * width] = dot_tn(node_hidden, out_grad)
    node_gain = jnp.sum(upstream * normed, axis=0, keepdims=True)
    by_receiver = columns_of(receivers[...])
    sender_ids = senders[...]
    extended = count + halo.shape[0]
    sender_total = jnp.zeros((extended, width), F32)
    receiver_total = jnp.zeros((count, width), F32)
    first = jnp.zeros((width, width), F32)
    second = jnp.zeros((width, width), F32)
    gain_total = jnp.zeros((1, width), F32)
    for tiles in chunks_of(senders.shape[0]):
        rows = pl.ds(tiles[0] * tile_rows, len(tiles) * tile_rows)
        live = live_rows(count_ref, tiles[0], len(tiles), tile_rows)
        upstream = live * (
            edge_grads[rows, :].astype(F32)
            + dot(hot_rows(by_receiver, tiles, 0, count), agg_grad)
        )
        chunk_normed = normed_kept[rows, :]
        gain_total = gain_total + jnp.sum(upstream * chunk_normed, axis=0, keepdims=True)
        out_grad = norm_back(chunk_normed, scale_kept[rows, :1], gain, upstream).astype(BF16)
        value = pre_kept[rows, :]
        sigma = sigmoid(value)
        hidden = (value * sigma).astype(BF16)
        slope = sigma * (1.0 + value * (1.0 - sigma))
        pre_grad = (dot_nt(out_grad, w_out[...]) * slope).astype(BF16)
        pre_grad_out[rows, :] = pre_grad
        second = second + dot_tn(hidden, out_grad)
        first = first + dot_tn(edges[rows, :], pre_grad)
        sender_total = sender_total + dot(hot_columns(sender_ids, tiles, 0, extended), pre_grad)
        receiver_total = receiver_total + dot(
            hot_columns(receiver_ids, tiles, 0, count), pre_grad
        )
    own = sender_total[:count].astype(BF16)
    away = sender_total[count:].astype(BF16)
    received = receiver_total.astype(BF16)
    sender_out[...] = own
    receiver_out[...] = received
    halo_grad = dot_nt(away, w_in[width : 2 * width]).astype(BF16)
    parts = [halo_grad[k * slots : (k + 1) * slots] for k in range(8)]
    up_out[...] = jnp.concatenate([parts[0], parts[3], parts[5]], axis=0)
    down_out[...] = jnp.concatenate([parts[2], parts[4], parts[7]], axis=0)
    rest_out[...] = jnp.concatenate([parts[1], parts[6]], axis=0)
    edge_sums[:width] = first
    edge_sums[width : 2 * width] = dot_tn(x, own) + dot_tn(halo, away)
    edge_sums[2 * width : 3 * width] = dot_tn(x, received)
    edge_sums[3 * width : 4 * width] = second
    split_by_core(edge_sums, 0, keep_out, away_out)
    split_by_core(node_sums, edge_sums.shape[0] // 2, keep_out, away_out)
    gains = pack_gains(gain_total, node_gain)
    away_out[keep_out.shape[0] :] = gains
    gains_out[...] = gains


def pair_kernel(parts, keep, gains, other, blocks_out, total, staged, sems):
    rows = keep.shape[0]
    chips = blocks_out.shape[0]
    packed = gains.shape[0]
    both = gains[...].astype(F32) + other[rows:].astype(F32)
    summed = pack_gains(both[0:1] + both[1:2], both[2:3] + both[3:4])
    total[...] = (keep[...] + other[:rows].astype(F32)).astype(BF16)
    copies = []
    for chip in range(chips):
        staged[chip, :packed, :] = summed
        first, at = 0, packed
        for part in parts:
            step = part // chips
            staged[chip, at : at + step, :] = total[first + chip * step : first + (chip + 1) * step]
            first, at = first + part, at + step
        copies.append(
            pltpu.make_async_copy(staged.at[chip], blocks_out.at[chip], sems.at[chip])
        )
        copies[-1].start()
    for copy in copies:
        copy.wait()


def place_kernel(parts, own, other, *refs):
    outs, sems = refs[:-1], refs[-1]
    chips = own.shape[0]
    core = lax.axis_index(CORE)

    def place(halves):
        copies = []

        def put(source, target):
            copies.append(pltpu.make_async_copy(source, target, sems.at[len(copies)]))
            copies[-1].start()

        for half, blocks in enumerate(halves):
            for chip in range(chips):
                at = 0
                for i, part in enumerate(parts):
                    step = part // chips
                    row = half * part + chip * step
                    cut = outs[2 * i].shape[0]
                    split = min(max(cut - row, 0), step)
                    if split > 0:
                        put(blocks.at[chip, at : at + split], outs[2 * i].at[row : row + split])
                    if split < step:
                        rest = row + split - cut
                        put(
                            blocks.at[chip, at + split : at + step],
                            outs[2 * i + 1].at[rest : rest + step - split],
                        )
                    at += step
        for copy in copies:
            copy.wait()

    @pl.when(core == 0)
    def _():
        place([own, other])

    @pl.when(core == 1)
    def _():
        place([other, own])


def finish_kernel(
    edge_grads, pre_grad, sender_sum, receiver_sum, node_part, w_in, edges_grad, local_grad
):
    width = w_in.shape[1]
    edges_grad[...] = (
        edge_grads[...].astype(F32) + dot_nt(pre_grad[...], w_in[:width])
    ).astype(BF16)
    local_grad[...] = (
        node_part[...]
        + dot_nt(sender_sum[...], w_in[width : 2 * width])
        + dot_nt(receiver_sum[...], w_in[2 * width :])
    )


def return_kernel(send_list, local_grad, up_back, down_back, to_high, to_low, nodes_grad):
    slots = send_list.shape[1]

    def block(ref, k):
        return ref[k * slots : (k + 1) * slots]

    returned = jnp.concatenate(
        [
            block(to_high, 0),
            block(to_high, 2),
            block(to_high, 1),
            block(up_back, 1),
            block(down_back, 1),
            block(to_low, 0),
            block(to_low, 2),
            block(to_low, 1),
        ],
        axis=0,
    )
    hot = list_hot(send_list[...], local_grad.shape[0])
    nodes_grad[...] = (local_grad[...] + dot_tn(hot, returned)).astype(BF16)


SMEM = pltpu.SMEM
VMEM = pltpu.VMEM
HBM = pltpu.HBM


def call(body, outs, flops, *operands, spaces=(), out_space=VMEM, scratch=()):
    moved = sum(x.size * x.dtype.itemsize for x in operands)
    moved += sum(x.size * jnp.dtype(x.dtype).itemsize for x in outs)
    spaces = list(spaces) + [VMEM] * (len(operands) - len(spaces))
    operands = [
        pltpu.with_memory_space_constraint(x, HBM) if space is HBM else x
        for x, space in zip(operands, spaces)
    ]
    return pl.pallas_call(
        body,
        out_shape=outs,
        in_specs=[pl.BlockSpec(memory_space=space) for space in spaces],
        out_specs=[pl.BlockSpec(memory_space=out_space) for _ in outs],
        scratch_shapes=list(scratch),
        compiler_params=pltpu.CompilerParams(vmem_limit_bytes=VMEM_LIMIT),
        cost_estimate=pl.CostEstimate(flops=flops, bytes_accessed=moved, transcendentals=0),
    )(*operands)


def like(array):
    return jax.ShapeDtypeStruct(array.shape, array.dtype)


def shaped(rows, columns, dtype):
    return jax.ShapeDtypeStruct((rows, columns), dtype)


def placed(parts, own, other, width):
    chips = own.shape[0]
    outs = [
        shaped(3 * width, width, BF16),
        shaped(width, width, BF16),
        shaped(2 * width, width, BF16),
        shaped(width, width, BF16),
    ]
    steps = [part // chips for part in parts]
    cuts = [x.shape[0] for x in outs[::2]]
    if all(x % 16 == 0 for x in steps + cuts):
        return call(
            functools.partial(place_kernel, parts),
            outs,
            0,
            own,
            other,
            out_space=HBM,
            scratch=[pltpu.SemaphoreType.DMA((2 * len(parts) * chips + len(parts),))],
        )
    core = lax.axis_index(CORE)
    low = jnp.where(core == 0, own, other)
    high = jnp.where(core == 0, other, own)
    results = []
    at = 0
    for step, cut in zip(steps, cuts):
        whole = jnp.concatenate(
            [x[:, at : at + step].reshape(chips * step, width) for x in (low, high)]
        )
        results += [whole[:cut], whole[cut:]]
        at += step
    return results


def blocks_of(parts, keep, gains, other):
    chips = lax.axis_size(CHIPS)
    rows, width = keep.shape
    packed = gains.shape[0]
    steps = [part // chips for part in parts]
    shape = (chips, packed + sum(steps), width)
    body = functools.partial(pair_kernel, parts)
    if all(x % 16 == 0 for x in steps):
        (blocks,) = call(
            body,
            [jax.ShapeDtypeStruct(shape, BF16)],
            0,
            keep,
            gains,
            other,
            out_space=HBM,
            scratch=[
                pltpu.VMEM((rows, width), BF16),
                pltpu.VMEM(shape, BF16),
                pltpu.SemaphoreType.DMA((chips,)),
            ],
        )
        return blocks
    both = gains.astype(F32) + other[rows:].astype(F32)
    summed = jnp.where(
        jnp.arange(packed)[:, None] % 2 == 0,
        both + jnp.roll(both, -1, axis=0),
        0.0,
    )
    high = summed.astype(BF16).astype(F32)
    summed = (high + jnp.roll(summed - high, 1, axis=0)).astype(BF16)
    total = (keep + other[:rows].astype(F32)).astype(BF16)
    pieces = [jnp.broadcast_to(summed[None], (chips, packed, width))]
    first = 0
    for part, step in zip(parts, steps):
        pieces.append(total[first : first + part].reshape(chips, step, width))
        first += part
    return jnp.concatenate(pieces, axis=1)


def on_device(
    nodes,
    edges,
    edge_grads,
    node_grads,
    send_list,
    senders,
    receivers,
    tile_count,
    w_edge_in,
    w_edge_out,
    gain_edge,
    w_node_in,
    w_node_out,
    gain_node,
):
    count, width = nodes.shape
    slots = send_list.shape[1]
    halo_rows = 8 * slots
    edge_rows = edges.shape[0]
    square = 2 * width * width
    gain_edge = gain_edge.reshape(1, width)
    gain_node = gain_node.reshape(1, width)

    low, mid, high, nodes, send_list = call(
        send_kernel,
        [
            shaped(3 * slots, width, BF16),
            shaped(2 * slots, width, BF16),
            shaped(3 * slots, width, BF16),
            like(nodes),
            like(send_list),
        ],
        2 * halo_rows * count * width,
        nodes,
        send_list,
        spaces=[HBM, HBM],
        scratch=[pltpu.SemaphoreType.DMA((2,))],
    )
    from_low = passed_along(high, "px", 1)
    from_high = passed_along(low, "px", -1)
    upward = passed_along(
        jnp.concatenate([from_high[2 * slots :], mid[slots:], from_low[2 * slots :]]), PY, 1
    )
    downward = passed_along(
        jnp.concatenate([from_high[:slots], mid[:slots], from_low[:slots]]), PY, -1
    )
    fetched = [
        w_edge_in,
        senders,
        receivers,
        edges,
        w_edge_out,
        w_node_in,
        w_node_out,
        node_grads,
        edge_grads,
    ]
    pre_local, *fetched = call(
        local_kernel,
        [shaped(edge_rows, width, F32)] + [like(x) for x in fetched],
        square * (2 * count + edge_rows) + 4 * edge_rows * count * width,
        nodes,
        *fetched,
        spaces=[VMEM] + [HBM] * len(fetched),
        scratch=[pltpu.SemaphoreType.DMA((len(fetched),))],
    )
    (
        w_edge_in,
        senders,
        receivers,
        edges,
        w_edge_out,
        w_node_in,
        w_node_out,
        node_grads,
        edge_grads,
    ) = fetched
    parts = (2 * width, 3 * width // 2)
    halves = sum(parts)
    pre_grad, sender_sum, receiver_sum, node_part, up, down, rest, keep, away, gains = call(
        layer_kernel,
        [
            shaped(edge_rows, width, BF16),
            shaped(count, width, BF16),
            shaped(count, width, BF16),
            shaped(count, width, F32),
            shaped(3 * slots, width, BF16),
            shaped(3 * slots, width, BF16),
            shaped(2 * slots, width, BF16),
            shaped(halves, width, F32),
            shaped(halves + 16, width, BF16),
            shaped(16, width, BF16),
        ],
        square * (6 * edge_rows + 11 * count + 2 * halo_rows)
        + 2 * edge_rows * (4 * count + halo_rows) * width,
        tile_count,
        nodes,
        node_grads,
        edges,
        edge_grads,
        senders,
        receivers,
        pre_local,
        from_high,
        from_low,
        upward,
        downward,
        w_edge_in,
        w_edge_out,
        gain_edge,
        w_node_in,
        w_node_out,
        gain_node,
        spaces=[SMEM],
        scratch=[
            pltpu.VMEM((edge_rows, width), F32),
            pltpu.VMEM((edge_rows, width), F32),
            pltpu.VMEM((edge_rows, 128), F32),
            pltpu.VMEM((3 * width, width), F32),
            pltpu.VMEM((4 * width, width), F32),
        ],
    )
    blocks = blocks_of(parts, keep, gains, across_cores(away))
    received = lax.all_to_all(blocks, CHIPS, 0, 0)
    sums = jnp.sum(received.astype(F32), axis=0)
    gains = sums[:16]
    mine = sums[16:].astype(BF16)
    spread = jnp.broadcast_to(mine[None], (blocks.shape[0],) + mine.shape)
    own = lax.all_to_all(spread, CHIPS, 0, 0)
    up_back = passed_along(up, PY, 1)
    down_back = passed_along(down, PY, -1)
    to_high = passed_along(
        jnp.concatenate([up_back[:slots], down_back[:slots], rest[:slots]]), "px", 1
    )
    to_low = passed_along(
        jnp.concatenate([up_back[2 * slots :], down_back[2 * slots :], rest[slots:]]), "px", -1
    )
    edges_grad, local_grad = call(
        finish_kernel,
        [shaped(edge_rows, width, BF16), shaped(count, width, F32)],
        square * (edge_rows + 2 * count),
        edge_grads,
        pre_grad,
        sender_sum,
        receiver_sum,
        node_part,
        w_edge_in,
    )
    (nodes_grad,) = call(
        return_kernel,
        [shaped(count, width, BF16)],
        2 * halo_rows * count * width,
        send_list,
        local_grad,
        up_back,
        down_back,
        to_high,
        to_low,
    )
    own, nodes_grad, edges_grad = lax.optimization_barrier((own, nodes_grad, edges_grad))
    w_edge_in_grad, w_edge_out_grad, w_node_in_grad, w_node_out_grad = placed(
        parts, own, across_cores(own), width
    )
    return (
        nodes_grad,
        edges_grad,
        w_edge_in_grad,
        w_edge_out_grad,
        (gains[0] + gains[1]).astype(BF16),
        w_node_in_grad,
        w_node_out_grad,
        (gains[2] + gains[3]).astype(BF16),
    )


def solution(mesh):
    in_specs = (
        P(("groups", "px") + PY, None),
        P(("groups", "px") + PY, None),
        P(("groups", "px") + PY, None),
        P(("groups", "px") + PY, None),
        P(("groups", "px") + PY, None),
        P(("groups", "px") + PY, None),
        P(("groups", "px") + PY, None),
        P(("groups", "px") + PY),
        P(),
        P(),
        P(),
        P(),
        P(),
        P(),
    )
    out_specs = (
        P(("groups", "px") + PY, None),
        P(("groups", "px") + PY, None),
        P("groups", None),
        P("groups", None),
        P("groups"),
        P("groups", None),
        P("groups", None),
        P("groups"),
    )
    groups, px, py = mesh.devices.shape
    by_core = jax.sharding.Mesh(
        mesh.devices.reshape(groups, px, py // 2, 2), ("groups", "px") + PY
    )
    return jax.shard_map(
        on_device, mesh=by_core, in_specs=in_specs, out_specs=out_specs, check_vma=False
    )
```

```python
import functools

import jax
import jax.numpy as jnp
from jax import lax
from jax.experimental import pallas as pl
from jax.experimental.pallas import tpu as pltpu
from jax.sharding import PartitionSpec as P

EPS = 1e-05
BF16 = jnp.bfloat16
F32 = jnp.float32
VMEM_LIMIT = 24 * 1024 * 1024


CORE = "core"
PY = ("side", "core")
CHIPS = ("px", "side")


def passed_along(array, axis, by):
    size = lax.axis_size(axis)
    return lax.ppermute(array, axis, [(i, (i + by) % size) for i in range(size)])


def across_cores(array):
    return lax.ppermute(array, CORE, [(0, 1), (1, 0)])


def dot(left, right):
    return jnp.dot(left, right, preferred_element_type=F32)


def dot_tn(left, right):
    return lax.dot_general(left, right, (((0,), (0,)), ((), ())), preferred_element_type=F32)


def dot_nt(left, right):
    return lax.dot_general(left, right, (((1,), (1,)), ((), ())), preferred_element_type=F32)


def sigmoid(value):
    return 0.5 + 0.5 * jnp.tanh(0.5 * value)


def normalize(value):
    centered = value - jnp.mean(value, axis=-1, keepdims=True)
    scale_inv = lax.rsqrt(jnp.mean(centered * centered, axis=-1, keepdims=True) + EPS)
    return centered * scale_inv, scale_inv


def norm_back(normed, scale_inv, gain, upstream):
    scaled = upstream * gain
    inner = (
        scaled
        - jnp.mean(scaled, axis=-1, keepdims=True)
        - normed * jnp.mean(scaled * normed, axis=-1, keepdims=True)
    )
    return inner * scale_inv


def columns_of(ids):
    rows, lanes = ids.shape
    padded = -(-rows // 8) * 8
    if padded > rows:
        ids = jnp.concatenate([ids, jnp.zeros((padded - rows, lanes), ids.dtype)], axis=0)
    return ids.T


def hot_rows(columns, tiles, base, count):
    parts = []
    for tile in tiles:
        column = columns[:, tile : tile + 1] - base
        lanes = lax.broadcasted_iota(jnp.int32, (columns.shape[0], count), 1)
        parts.append(jnp.where(lanes == column, 1.0, 0.0).astype(BF16))
    return jnp.concatenate(parts, axis=0) if len(parts) > 1 else parts[0]


def hot_columns(ids, tiles, base, count):
    parts = []
    for tile in tiles:
        row = ids[tile : tile + 1, :] - base
        subs = lax.broadcasted_iota(jnp.int32, (count, ids.shape[1]), 0)
        parts.append(jnp.where(subs == row, 1.0, 0.0).astype(BF16))
    return jnp.concatenate(parts, axis=1) if len(parts) > 1 else parts[0]


def list_hot(ids, count):
    directions, slots = ids.shape
    wide = jnp.concatenate([ids, jnp.zeros((directions, 128 - slots), ids.dtype)], axis=1)
    columns = wide.T
    parts = []
    for k in range(directions):
        lanes = lax.broadcasted_iota(jnp.int32, (slots, count), 1)
        parts.append(jnp.where(lanes == columns[:slots, k : k + 1], 1.0, 0.0).astype(BF16))
    return jnp.concatenate(parts, axis=0)


def live_rows(count_ref, tile_rows, rows):
    index = lax.broadcasted_iota(jnp.int32, (rows.stop - rows.start, 1), 0)
    return jnp.where(index < count_ref[0] * tile_rows - rows.start, 1.0, 0.0)


def chunks_of(tiles):
    step = 3 if tiles % 3 == 0 else 1
    return [list(range(first, first + step)) for first in range(0, tiles, step)]


def fetch_all(sources, targets, sems):
    copies = [
        pltpu.make_async_copy(source, target, sems.at[i])
        for i, (source, target) in enumerate(zip(sources, targets))
    ]
    for copy in copies:
        copy.start()
    return copies


def send_kernel(nodes_hbm, list_hbm, low, mid, high, nodes, send_list, sems):
    slots = send_list.shape[1]
    for copy in fetch_all([list_hbm, nodes_hbm], [send_list, nodes], sems):
        copy.wait()
    rows = dot(list_hot(send_list[...], nodes.shape[0]), nodes[...]).astype(BF16)
    low[...] = rows[: 3 * slots]
    mid[...] = rows[3 * slots : 5 * slots]
    high[...] = rows[5 * slots :]


def local_kernel(nodes, *refs):
    fetched = (len(refs) - 3) // 2
    pre, receiver_rows, sems = refs[fetched], refs[fetched + 1], refs[-1]
    targets = refs[fetched + 2 : -1]
    w_in, senders, receivers, edges = targets[:4]
    copies = fetch_all(refs[:fetched], targets, sems)
    count, width = nodes.shape
    tile_rows = senders.shape[1]
    x = nodes[...]
    for copy in copies[:4]:
        copy.wait()
    table = jnp.concatenate(
        [
            dot(x, w_in[width : 2 * width]).astype(BF16),
            dot(x, w_in[2 * width :]).astype(BF16),
        ],
        axis=0,
    )
    by_sender = columns_of(senders[...])
    by_receiver = columns_of(receivers[...])
    w_edge = w_in[:width]
    for tiles in chunks_of(senders.shape[0]):
        rows = pl.ds(tiles[0] * tile_rows, len(tiles) * tile_rows)
        by_receiver_hot = hot_rows(by_receiver, tiles, 0, count)
        receiver_rows[rows, :] = by_receiver_hot
        hot = jnp.concatenate([hot_rows(by_sender, tiles, 0, count), by_receiver_hot], axis=1)
        pre[rows, :] = dot(edges[rows, :], w_edge) + dot(hot, table)
    for copy in copies[4:]:
        copy.wait()


def index_kernel(senders, receivers, halo_rows, sender_columns, receiver_columns):
    tile_rows = senders.shape[1]
    extended = sender_columns.shape[0]
    count = receiver_columns.shape[0]
    sender_ids = senders[...]
    receiver_ids = receivers[...]
    by_sender = columns_of(sender_ids)
    for tile in range(senders.shape[0]):
        rows = slice(tile * tile_rows, (tile + 1) * tile_rows)
        halo_rows[rows, :] = hot_rows(by_sender, [tile], count, halo_rows.shape[1])
        sender_columns[:, rows] = hot_columns(sender_ids, [tile], 0, extended)
        receiver_columns[:, rows] = hot_columns(receiver_ids, [tile], 0, count)


def split_by_core(sums, first, keep_out, away_out):
    half = sums.shape[0] // 2
    core = lax.axis_index(CORE)
    keep_out[first : first + half] = sums[pl.ds(pl.multiple_of(core * half, half), half), :]
    away = sums[pl.ds(pl.multiple_of((1 - core) * half, half), half), :]
    away_out[first : first + half] = away.astype(BF16)


def pack_gains(edge_gain, node_gain):
    edge_high = edge_gain.astype(BF16).astype(F32)
    node_high = node_gain.astype(BF16).astype(F32)
    row = lax.broadcasted_iota(jnp.int32, (16, edge_gain.shape[1]), 0)
    packed = jnp.where(row == 0, edge_high, 0.0)
    packed = jnp.where(row == 1, edge_gain - edge_high, packed)
    packed = jnp.where(row == 2, node_high, packed)
    packed = jnp.where(row == 3, node_gain - node_high, packed)
    return packed.astype(BF16)


def layer_kernel(
    tile_rows,
    count_ref,
    nodes,
    node_grads,
    edges,
    edge_grads,
    pre_local,
    halo_rows,
    receiver_rows,
    sender_columns,
    receiver_columns,
    from_high,
    from_low,
    upward,
    downward,
    w_in,
    w_out,
    gain_edge,
    w_node_in,
    w_node_out,
    gain_node,
    pre_grad_out,
    sender_out,
    receiver_out,
    node_part_out,
    up_out,
    down_out,
    rest_out,
    keep_out,
    away_out,
    gains_out,
    slope_kept,
    hidden_kept,
    normed_kept,
    scale_kept,
    node_sums,
    edge_sums,
):
    count, width = nodes.shape
    edge_rows = edges.shape[0]
    step = edge_rows // 3 if edge_rows % 48 == 0 else edge_rows
    chunks = [slice(first, first + step) for first in range(0, edge_rows, step)]
    slots = from_high.shape[0] // 3
    halo = jnp.concatenate(
        [
            downward[:slots],
            from_high[slots : 2 * slots],
            upward[:slots],
            downward[slots : 2 * slots],
            upward[slots : 2 * slots],
            downward[2 * slots :],
            from_low[slots : 2 * slots],
            upward[2 * slots :],
        ],
        axis=0,
    )
    table = dot(halo, w_in[width : 2 * width]).astype(BF16)
    gain = gain_edge[...].astype(F32)
    total = jnp.zeros((count, width), F32)
    for rows in chunks:
        value = pre_local[rows, :] + dot(halo_rows[rows, :], table)
        sigma = sigmoid(value)
        hidden = (value * sigma).astype(BF16)
        hidden_kept[rows, :] = hidden
        slope_kept[rows, :] = sigma * (1.0 + value * (1.0 - sigma))
        normed, scale_inv = normalize(dot(hidden, w_out[...]))
        normed_kept[rows, :] = normed
        scale_kept[rows, :] = jnp.broadcast_to(scale_inv, (step, 128))
        message = (live_rows(count_ref, tile_rows, rows) * gain * normed).astype(BF16)
        total = total + dot(receiver_columns[:, rows], message)
    aggregated = total.astype(BF16)
    x = nodes[...]
    w_first = w_node_in[:width]
    w_second = w_node_in[width:]
    node_pre = dot(x, w_first) + dot(aggregated, w_second)
    sigma = sigmoid(node_pre)
    node_hidden = (node_pre * sigma).astype(BF16)
    normed, scale_inv = normalize(dot(node_hidden, w_node_out[...]))
    upstream = node_grads[...].astype(F32)
    out_grad = norm_back(normed, scale_inv, gain_node[...].astype(F32), upstream).astype(BF16)
    slope = sigma * (1.0 + node_pre * (1.0 - sigma))
    pre_grad = (dot_nt(out_grad, w_node_out[...]) * slope).astype(BF16)
    agg_grad = dot_nt(pre_grad, w_second).astype(BF16)
    node_part_out[...] = upstream + dot_nt(pre_grad, w_first)
    node_sums[:width] = dot_tn(x, pre_grad)
    node_sums[width : 2 * width] = dot_tn(aggregated, pre_grad)
    node_sums[2 * width : 3 * width] = dot_tn(node_hidden, out_grad)
    node_gain = jnp.sum(upstream * normed, axis=0, keepdims=True)
    extended = count + halo.shape[0]
    sender_total = jnp.zeros((extended, width), F32)
    receiver_total = jnp.zeros((count, width), F32)
    first = jnp.zeros((width, width), F32)
    second = jnp.zeros((width, width), F32)
    gain_total = jnp.zeros((1, width), F32)
    for rows in chunks:
        upstream = live_rows(count_ref, tile_rows, rows) * (
            edge_grads[rows, :].astype(F32) + dot(receiver_rows[rows, :], agg_grad)
        )
        chunk_normed = normed_kept[rows, :]
        gain_total = gain_total + jnp.sum(upstream * chunk_normed, axis=0, keepdims=True)
        out_grad = norm_back(chunk_normed, scale_kept[rows, :1], gain, upstream).astype(BF16)
        pre_grad = (dot_nt(out_grad, w_out[...]) * slope_kept[rows, :]).astype(BF16)
        pre_grad_out[rows, :] = pre_grad
        second = second + dot_tn(hidden_kept[rows, :], out_grad)
        first = first + dot_tn(edges[rows, :], pre_grad)
        sender_total = sender_total + dot(sender_columns[:, rows], pre_grad)
        receiver_total = receiver_total + dot(receiver_columns[:, rows], pre_grad)
    own = sender_total[:count].astype(BF16)
    away = sender_total[count:].astype(BF16)
    received = receiver_total.astype(BF16)
    sender_out[...] = own
    receiver_out[...] = received
    halo_grad = dot_nt(away, w_in[width : 2 * width]).astype(BF16)
    parts = [halo_grad[k * slots : (k + 1) * slots] for k in range(8)]
    up_out[...] = jnp.concatenate([parts[0], parts[3], parts[5]], axis=0)
    down_out[...] = jnp.concatenate([parts[2], parts[4], parts[7]], axis=0)
    rest_out[...] = jnp.concatenate([parts[1], parts[6]], axis=0)
    edge_sums[:width] = first
    edge_sums[width : 2 * width] = dot_tn(x, own) + dot_tn(halo, away)
    edge_sums[2 * width : 3 * width] = dot_tn(x, received)
    edge_sums[3 * width : 4 * width] = second
    split_by_core(edge_sums, 0, keep_out, away_out)
    split_by_core(node_sums, edge_sums.shape[0] // 2, keep_out, away_out)
    gains = pack_gains(gain_total, node_gain)
    away_out[keep_out.shape[0] :] = gains
    gains_out[...] = gains


def pair_kernel(parts, keep, gains, other, blocks_out, total, staged, sems):
    rows = keep.shape[0]
    chips = blocks_out.shape[0]
    packed = gains.shape[0]
    both = gains[...].astype(F32) + other[rows:].astype(F32)
    summed = pack_gains(both[0:1] + both[1:2], both[2:3] + both[3:4])
    total[...] = (keep[...] + other[:rows].astype(F32)).astype(BF16)
    copies = []
    for chip in range(chips):
        staged[chip, :packed, :] = summed
        first, at = 0, packed
        for part in parts:
            step = part // chips
            staged[chip, at : at + step, :] = total[first + chip * step : first + (chip + 1) * step]
            first, at = first + part, at + step
        copies.append(
            pltpu.make_async_copy(staged.at[chip], blocks_out.at[chip], sems.at[chip])
        )
        copies[-1].start()
    for copy in copies:
        copy.wait()


def spread_kernel(packed, received, gains_out, spread_out, mine, sems):
    sums = received[0].astype(F32)
    for chip in range(1, received.shape[0]):
        sums = sums + received[chip].astype(F32)
    gains_out[...] = sums[:packed]
    mine[...] = sums[packed:].astype(BF16)
    copies = [
        pltpu.make_async_copy(mine, spread_out.at[chip], sems.at[chip])
        for chip in range(received.shape[0])
    ]
    for copy in copies:
        copy.start()
    for copy in copies:
        copy.wait()


def place_kernel(parts, own, other, *refs):
    outs, sems = refs[:-1], refs[-1]
    chips = own.shape[0]
    core = lax.axis_index(CORE)

    def place(halves):
        copies = []

        def put(source, target):
            copies.append(pltpu.make_async_copy(source, target, sems.at[len(copies)]))
            copies[-1].start()

        for half, blocks in enumerate(halves):
            for chip in range(chips):
                at = 0
                for i, part in enumerate(parts):
                    step = part // chips
                    row = half * part + chip * step
                    cut = outs[2 * i].shape[0]
                    split = min(max(cut - row, 0), step)
                    if split > 0:
                        put(blocks.at[chip, at : at + split], outs[2 * i].at[row : row + split])
                    if split < step:
                        rest = row + split - cut
                        put(
                            blocks.at[chip, at + split : at + step],
                            outs[2 * i + 1].at[rest : rest + step - split],
                        )
                    at += step
        for copy in copies:
            copy.wait()

    @pl.when(core == 0)
    def _():
        place([own, other])

    @pl.when(core == 1)
    def _():
        place([other, own])


def finish_kernel(
    edge_grads, pre_grad, sender_sum, receiver_sum, node_part, w_in, edges_grad, local_grad
):
    width = w_in.shape[1]
    edges_grad[...] = (
        edge_grads[...].astype(F32) + dot_nt(pre_grad[...], w_in[:width])
    ).astype(BF16)
    local_grad[...] = (
        node_part[...]
        + dot_nt(sender_sum[...], w_in[width : 2 * width])
        + dot_nt(receiver_sum[...], w_in[2 * width :])
    )


def return_kernel(send_list, local_grad, up_back, down_back, to_high, to_low, nodes_grad):
    slots = send_list.shape[1]

    def block(ref, k):
        return ref[k * slots : (k + 1) * slots]

    returned = jnp.concatenate(
        [
            block(to_high, 0),
            block(to_high, 2),
            block(to_high, 1),
            block(up_back, 1),
            block(down_back, 1),
            block(to_low, 0),
            block(to_low, 2),
            block(to_low, 1),
        ],
        axis=0,
    )
    hot = list_hot(send_list[...], local_grad.shape[0])
    nodes_grad[...] = (local_grad[...] + dot_tn(hot, returned)).astype(BF16)


SMEM = pltpu.SMEM
VMEM = pltpu.VMEM
HBM = pltpu.HBM


def call(body, outs, flops, *operands, spaces=(), out_space=VMEM, scratch=()):
    moved = sum(x.size * x.dtype.itemsize for x in operands)
    moved += sum(x.size * jnp.dtype(x.dtype).itemsize for x in outs)
    spaces = list(spaces) + [VMEM] * (len(operands) - len(spaces))
    out_spaces = out_space if isinstance(out_space, list) else [out_space] * len(outs)
    operands = [
        pltpu.with_memory_space_constraint(x, HBM) if space is HBM else x
        for x, space in zip(operands, spaces)
    ]
    return pl.pallas_call(
        body,
        out_shape=outs,
        in_specs=[pl.BlockSpec(memory_space=space) for space in spaces],
        out_specs=[pl.BlockSpec(memory_space=space) for space in out_spaces],
        scratch_shapes=list(scratch),
        compiler_params=pltpu.CompilerParams(vmem_limit_bytes=VMEM_LIMIT),
        cost_estimate=pl.CostEstimate(flops=flops, bytes_accessed=moved, transcendentals=0),
    )(*operands)


def like(array):
    return jax.ShapeDtypeStruct(array.shape, array.dtype)


def shaped(rows, columns, dtype):
    return jax.ShapeDtypeStruct((rows, columns), dtype)


def placed(parts, own, other, width):
    chips = own.shape[0]
    outs = [
        shaped(3 * width, width, BF16),
        shaped(width, width, BF16),
        shaped(2 * width, width, BF16),
        shaped(width, width, BF16),
    ]
    steps = [part // chips for part in parts]
    cuts = [x.shape[0] for x in outs[::2]]
    if all(x % 16 == 0 for x in steps + cuts):
        return call(
            functools.partial(place_kernel, parts),
            outs,
            0,
            own,
            other,
            out_space=HBM,
            scratch=[pltpu.SemaphoreType.DMA((2 * len(parts) * chips + len(parts),))],
        )
    core = lax.axis_index(CORE)
    low = jnp.where(core == 0, own, other)
    high = jnp.where(core == 0, other, own)
    results = []
    at = 0
    for step, cut in zip(steps, cuts):
        whole = jnp.concatenate(
            [x[:, at : at + step].reshape(chips * step, width) for x in (low, high)]
        )
        results += [whole[:cut], whole[cut:]]
        at += step
    return results


def spread_of(received, packed):
    chips, rows, width = received.shape
    mine = rows - packed
    if mine % 16 == 0:
        return call(
            functools.partial(spread_kernel, packed),
            [shaped(packed, width, F32), jax.ShapeDtypeStruct((chips, mine, width), BF16)],
            0,
            received,
            out_space=[VMEM, HBM],
            scratch=[pltpu.VMEM((mine, width), BF16), pltpu.SemaphoreType.DMA((chips,))],
        )
    sums = jnp.sum(received.astype(F32), axis=0)
    return sums[:packed], jnp.broadcast_to(sums[packed:].astype(BF16)[None], (chips, mine, width))


def blocks_of(parts, keep, gains, other):
    chips = lax.axis_size(CHIPS)
    rows, width = keep.shape
    packed = gains.shape[0]
    steps = [part // chips for part in parts]
    shape = (chips, packed + sum(steps), width)
    body = functools.partial(pair_kernel, parts)
    if all(x % 16 == 0 for x in steps):
        (blocks,) = call(
            body,
            [jax.ShapeDtypeStruct(shape, BF16)],
            0,
            keep,
            gains,
            other,
            out_space=HBM,
            scratch=[
                pltpu.VMEM((rows, width), BF16),
                pltpu.VMEM(shape, BF16),
                pltpu.SemaphoreType.DMA((chips,)),
            ],
        )
        return blocks
    both = gains.astype(F32) + other[rows:].astype(F32)
    summed = jnp.where(
        jnp.arange(packed)[:, None] % 2 == 0,
        both + jnp.roll(both, -1, axis=0),
        0.0,
    )
    high = summed.astype(BF16).astype(F32)
    summed = (high + jnp.roll(summed - high, 1, axis=0)).astype(BF16)
    total = (keep + other[:rows].astype(F32)).astype(BF16)
    pieces = [jnp.broadcast_to(summed[None], (chips, packed, width))]
    first = 0
    for part, step in zip(parts, steps):
        pieces.append(total[first : first + part].reshape(chips, step, width))
        first += part
    return jnp.concatenate(pieces, axis=1)


def on_device(
    nodes,
    edges,
    edge_grads,
    node_grads,
    send_list,
    senders,
    receivers,
    tile_count,
    w_edge_in,
    w_edge_out,
    gain_edge,
    w_node_in,
    w_node_out,
    gain_node,
):
    count, width = nodes.shape
    slots = send_list.shape[1]
    halo_rows = 8 * slots
    edge_rows = edges.shape[0]
    tile_rows = senders.shape[1]
    square = 2 * width * width
    gain_edge = gain_edge.reshape(1, width)
    gain_node = gain_node.reshape(1, width)

    low, mid, high, nodes, send_list = call(
        send_kernel,
        [
            shaped(3 * slots, width, BF16),
            shaped(2 * slots, width, BF16),
            shaped(3 * slots, width, BF16),
            like(nodes),
            like(send_list),
        ],
        2 * halo_rows * count * width,
        nodes,
        send_list,
        spaces=[HBM, HBM],
        scratch=[pltpu.SemaphoreType.DMA((2,))],
    )
    from_low = passed_along(high, "px", 1)
    from_high = passed_along(low, "px", -1)
    fetched = [
        w_edge_in,
        senders,
        receivers,
        edges,
        w_edge_out,
        w_node_in,
        w_node_out,
        node_grads,
        edge_grads,
    ]
    pre_local, receiver_rows, *fetched = call(
        local_kernel,
        [shaped(edge_rows, width, F32), shaped(edge_rows, count, BF16)]
        + [like(x) for x in fetched],
        square * (2 * count + edge_rows) + 4 * edge_rows * count * width,
        nodes,
        *fetched,
        spaces=[VMEM] + [HBM] * len(fetched),
        scratch=[pltpu.SemaphoreType.DMA((len(fetched),))],
    )
    (
        w_edge_in,
        senders,
        receivers,
        edges,
        w_edge_out,
        w_node_in,
        w_node_out,
        node_grads,
        edge_grads,
    ) = fetched
    from_low, from_high, pre_local = lax.optimization_barrier((from_low, from_high, pre_local))
    upward = passed_along(
        jnp.concatenate([from_high[2 * slots :], mid[slots:], from_low[2 * slots :]]), PY, 1
    )
    downward = passed_along(
        jnp.concatenate([from_high[:slots], mid[:slots], from_low[:slots]]), PY, -1
    )
    halo_hot, sender_columns, receiver_columns = call(
        index_kernel,
        [
            shaped(edge_rows, halo_rows, BF16),
            shaped(count + halo_rows, edge_rows, BF16),
            shaped(count, edge_rows, BF16),
        ],
        0,
        senders,
        receivers,
    )
    parts = (2 * width, 3 * width // 2)
    halves = sum(parts)
    pre_grad, sender_sum, receiver_sum, node_part, up, down, rest, keep, away, gains = call(
        functools.partial(layer_kernel, tile_rows),
        [
            shaped(edge_rows, width, BF16),
            shaped(count, width, BF16),
            shaped(count, width, BF16),
            shaped(count, width, F32),
            shaped(3 * slots, width, BF16),
            shaped(3 * slots, width, BF16),
            shaped(2 * slots, width, BF16),
            shaped(halves, width, F32),
            shaped(halves + 16, width, BF16),
            shaped(16, width, BF16),
        ],
        square * (6 * edge_rows + 11 * count + 2 * halo_rows)
        + 2 * edge_rows * (4 * count + halo_rows) * width,
        tile_count,
        nodes,
        node_grads,
        edges,
        edge_grads,
        pre_local,
        halo_hot,
        receiver_rows,
        sender_columns,
        receiver_columns,
        from_high,
        from_low,
        upward,
        downward,
        w_edge_in,
        w_edge_out,
        gain_edge,
        w_node_in,
        w_node_out,
        gain_node,
        spaces=[SMEM],
        scratch=[
            pltpu.VMEM((edge_rows, width), F32),
            pltpu.VMEM((edge_rows, width), BF16),
            pltpu.VMEM((edge_rows, width), F32),
            pltpu.VMEM((edge_rows, 128), F32),
            pltpu.VMEM((3 * width, width), F32),
            pltpu.VMEM((4 * width, width), F32),
        ],
    )
    blocks = blocks_of(parts, keep, gains, across_cores(away))
    received = lax.all_to_all(blocks, CHIPS, 0, 0)
    gains, spread = spread_of(received, gains.shape[0])
    own = lax.all_to_all(spread, CHIPS, 0, 0)
    up_back = passed_along(up, PY, 1)
    down_back = passed_along(down, PY, -1)
    to_high = passed_along(
        jnp.concatenate([up_back[:slots], down_back[:slots], rest[:slots]]), "px", 1
    )
    to_low = passed_along(
        jnp.concatenate([up_back[2 * slots :], down_back[2 * slots :], rest[slots:]]), "px", -1
    )
    edges_grad, local_grad = call(
        finish_kernel,
        [shaped(edge_rows, width, BF16), shaped(count, width, F32)],
        square * (edge_rows + 2 * count),
        edge_grads,
        pre_grad,
        sender_sum,
        receiver_sum,
        node_part,
        w_edge_in,
    )
    (nodes_grad,) = call(
        return_kernel,
        [shaped(count, width, BF16)],
        2 * halo_rows * count * width,
        send_list,
        local_grad,
        up_back,
        down_back,
        to_high,
        to_low,
    )
    own, nodes_grad, edges_grad = lax.optimization_barrier((own, nodes_grad, edges_grad))
    w_edge_in_grad, w_edge_out_grad, w_node_in_grad, w_node_out_grad = placed(
        parts, own, across_cores(own), width
    )
    return (
        nodes_grad,
        edges_grad,
        w_edge_in_grad,
        w_edge_out_grad,
        (gains[0] + gains[1]).astype(BF16),
        w_node_in_grad,
        w_node_out_grad,
        (gains[2] + gains[3]).astype(BF16),
    )


def solution(mesh):
    in_specs = (
        P(("groups", "px") + PY, None),
        P(("groups", "px") + PY, None),
        P(("groups", "px") + PY, None),
        P(("groups", "px") + PY, None),
        P(("groups", "px") + PY, None),
        P(("groups", "px") + PY, None),
        P(("groups", "px") + PY, None),
        P(("groups", "px") + PY),
        P(),
        P(),
        P(),
        P(),
        P(),
        P(),
    )
    out_specs = (
        P(("groups", "px") + PY, None),
        P(("groups", "px") + PY, None),
        P("groups", None),
        P("groups", None),
        P("groups"),
        P("groups", None),
        P("groups", None),
        P("groups"),
    )
    groups, px, py = mesh.devices.shape
    by_core = jax.sharding.Mesh(
        mesh.devices.reshape(groups, px, py // 2, 2), ("groups", "px") + PY
    )
    return jax.shard_map(
        on_device, mesh=by_core, in_specs=in_specs, out_specs=out_specs, check_vma=False
    )
```

```python
import functools

import jax
import jax.numpy as jnp
from jax import lax
from jax.experimental import pallas as pl
from jax.experimental.pallas import tpu as pltpu
from jax.sharding import PartitionSpec as P

EPS = 1e-05
BF16 = jnp.bfloat16
F32 = jnp.float32
VMEM_LIMIT = 24 * 1024 * 1024


CORE = "core"
PY = ("side", "core")
CHIPS = ("px", "side")


def passed_along(array, axis, by):
    size = lax.axis_size(axis)
    return lax.ppermute(array, axis, [(i, (i + by) % size) for i in range(size)])


def across_cores(array):
    return lax.ppermute(array, CORE, [(0, 1), (1, 0)])


def dot(left, right):
    return jnp.dot(left, right, preferred_element_type=F32)


def dot_tn(left, right):
    return lax.dot_general(left, right, (((0,), (0,)), ((), ())), preferred_element_type=F32)


def dot_nt(left, right):
    return lax.dot_general(left, right, (((1,), (1,)), ((), ())), preferred_element_type=F32)


def sigmoid(value):
    return 0.5 + 0.5 * jnp.tanh(0.5 * value)


def normalize(value):
    centered = value - jnp.mean(value, axis=-1, keepdims=True)
    scale_inv = lax.rsqrt(jnp.mean(centered * centered, axis=-1, keepdims=True) + EPS)
    return centered * scale_inv, scale_inv


def norm_back(normed, scale_inv, gain, upstream):
    scaled = upstream * gain
    inner = (
        scaled
        - jnp.mean(scaled, axis=-1, keepdims=True)
        - normed * jnp.mean(scaled * normed, axis=-1, keepdims=True)
    )
    return inner * scale_inv


def columns_of(ids):
    rows, lanes = ids.shape
    padded = -(-rows // 8) * 8
    if padded > rows:
        ids = jnp.concatenate([ids, jnp.zeros((padded - rows, lanes), ids.dtype)], axis=0)
    return ids.T


def hot_rows(columns, tiles, base, count):
    parts = []
    for tile in tiles:
        column = columns[:, tile : tile + 1] - base
        lanes = lax.broadcasted_iota(jnp.int32, (columns.shape[0], count), 1)
        parts.append(jnp.where(lanes == column, 1.0, 0.0).astype(BF16))
    return jnp.concatenate(parts, axis=0) if len(parts) > 1 else parts[0]


def hot_columns(ids, tiles, base, count):
    parts = []
    for tile in tiles:
        row = ids[tile : tile + 1, :] - base
        subs = lax.broadcasted_iota(jnp.int32, (count, ids.shape[1]), 0)
        parts.append(jnp.where(subs == row, 1.0, 0.0).astype(BF16))
    return jnp.concatenate(parts, axis=1) if len(parts) > 1 else parts[0]


def list_hot(ids, count):
    directions, slots = ids.shape
    wide = jnp.concatenate([ids, jnp.zeros((directions, 128 - slots), ids.dtype)], axis=1)
    columns = wide.T
    parts = []
    for k in range(directions):
        lanes = lax.broadcasted_iota(jnp.int32, (slots, count), 1)
        parts.append(jnp.where(lanes == columns[:slots, k : k + 1], 1.0, 0.0).astype(BF16))
    return jnp.concatenate(parts, axis=0)


def live_rows(count_ref, tile_rows, rows):
    index = lax.broadcasted_iota(jnp.int32, (rows, 1), 0)
    return jnp.where(index < count_ref[0] * tile_rows, 1.0, 0.0)


def fetch_all(sources, targets, sems):
    copies = [
        pltpu.make_async_copy(source, target, sems.at[i])
        for i, (source, target) in enumerate(zip(sources, targets))
    ]
    for copy in copies:
        copy.start()
    return copies


def send_kernel(nodes_hbm, list_hbm, low, mid, high, nodes, send_list, sems):
    slots = send_list.shape[1]
    for copy in fetch_all([list_hbm, nodes_hbm], [send_list, nodes], sems):
        copy.wait()
    rows = dot(list_hot(send_list[...], nodes.shape[0]), nodes[...]).astype(BF16)
    low[...] = rows[: 3 * slots]
    mid[...] = rows[3 * slots : 5 * slots]
    high[...] = rows[5 * slots :]


def index_kernel(sources, *refs):
    fetched, refs = refs[:sources], refs[sources:]
    near_rows, halo_rows, sender_columns, receiver_columns = refs[:4]
    targets, sems = refs[4:-1], refs[-1]
    senders, receivers = targets[:2]
    copies = fetch_all(fetched, targets, sems)
    for copy in copies[:2]:
        copy.wait()
    tile_rows = senders.shape[1]
    extended = sender_columns.shape[0]
    count = receiver_columns.shape[0]
    sender_ids = senders[...]
    receiver_ids = receivers[...]
    by_sender = columns_of(sender_ids)
    by_receiver = columns_of(receiver_ids)
    for tile in range(senders.shape[0]):
        rows = slice(tile * tile_rows, (tile + 1) * tile_rows)
        near_rows[rows, :count] = hot_rows(by_sender, [tile], 0, count)
        near_rows[rows, count:] = hot_rows(by_receiver, [tile], 0, count)
        halo_rows[rows, :] = hot_rows(by_sender, [tile], count, halo_rows.shape[1])
        sender_columns[:, rows] = hot_columns(sender_ids, [tile], 0, extended)
        receiver_columns[:, rows] = hot_columns(receiver_ids, [tile], 0, count)
    for copy in copies[2:]:
        copy.wait()


def local_kernel(nodes, edges, near_rows, w_in, pre):
    width = nodes.shape[1]
    x = nodes[...]
    table = jnp.concatenate(
        [
            dot(x, w_in[width : 2 * width]).astype(BF16),
            dot(x, w_in[2 * width :]).astype(BF16),
        ],
        axis=0,
    )
    pre[...] = dot(edges[...], w_in[:width]) + dot(near_rows[...], table)


def split_by_core(sums, first, keep_out, away_out):
    half = sums.shape[0] // 2
    core = lax.axis_index(CORE)
    keep_out[first : first + half] = sums[pl.ds(pl.multiple_of(core * half, half), half), :]
    away = sums[pl.ds(pl.multiple_of((1 - core) * half, half), half), :]
    away_out[first : first + half] = away.astype(BF16)


def pack_gains(edge_gain, node_gain):
    edge_high = edge_gain.astype(BF16).astype(F32)
    node_high = node_gain.astype(BF16).astype(F32)
    row = lax.broadcasted_iota(jnp.int32, (16, edge_gain.shape[1]), 0)
    packed = jnp.where(row == 0, edge_high, 0.0)
    packed = jnp.where(row == 1, edge_gain - edge_high, packed)
    packed = jnp.where(row == 2, node_high, packed)
    packed = jnp.where(row == 3, node_gain - node_high, packed)
    return packed.astype(BF16)


def layer_kernel(
    tile_rows,
    count_ref,
    nodes,
    node_grads,
    edges,
    edge_grads,
    pre_local,
    halo_rows,
    near_rows,
    sender_columns,
    receiver_columns,
    from_high,
    from_low,
    upward,
    downward,
    w_in,
    w_out,
    gain_edge,
    w_node_in,
    w_node_out,
    gain_node,
    pre_grad_out,
    sender_out,
    receiver_out,
    node_part_out,
    up_out,
    down_out,
    rest_out,
    keep_out,
    away_out,
    gains_out,
    slope_kept,
    hidden_kept,
    normed_kept,
    scale_kept,
    node_sums,
    edge_sums,
):
    count, width = nodes.shape
    edge_rows = edges.shape[0]
    live = live_rows(count_ref, tile_rows, edge_rows)
    slots = from_high.shape[0] // 3
    halo = jnp.concatenate(
        [
            downward[:slots],
            from_high[slots : 2 * slots],
            upward[:slots],
            downward[slots : 2 * slots],
            upward[slots : 2 * slots],
            downward[2 * slots :],
            from_low[slots : 2 * slots],
            upward[2 * slots :],
        ],
        axis=0,
    )
    table = dot(halo, w_in[width : 2 * width]).astype(BF16)
    gain = gain_edge[...].astype(F32)[None, :]
    value = pre_local[...] + dot(halo_rows[...], table)
    sigma = sigmoid(value)
    hidden = (value * sigma).astype(BF16)
    hidden_kept[...] = hidden
    slope_kept[...] = sigma * (1.0 + value * (1.0 - sigma))
    edge_normed, edge_scale = normalize(dot(hidden, w_out[...]))
    normed_kept[...] = edge_normed
    scale_kept[...] = jnp.broadcast_to(edge_scale, (edge_rows, 128))
    message = (live * gain * edge_normed).astype(BF16)
    total = dot(receiver_columns[...], message)
    aggregated = total.astype(BF16)
    x = nodes[...]
    w_first = w_node_in[:width]
    w_second = w_node_in[width:]
    node_pre = dot(x, w_first) + dot(aggregated, w_second)
    sigma = sigmoid(node_pre)
    node_hidden = (node_pre * sigma).astype(BF16)
    normed, scale_inv = normalize(dot(node_hidden, w_node_out[...]))
    upstream = node_grads[...].astype(F32)
    out_grad = norm_back(normed, scale_inv, gain_node[...].astype(F32)[None, :], upstream).astype(BF16)
    slope = sigma * (1.0 + node_pre * (1.0 - sigma))
    pre_grad = (dot_nt(out_grad, w_node_out[...]) * slope).astype(BF16)
    agg_grad = dot_nt(pre_grad, w_second).astype(BF16)
    node_part_out[...] = upstream + dot_nt(pre_grad, w_first)
    node_sums[:width] = dot_tn(x, pre_grad)
    node_sums[width : 2 * width] = dot_tn(aggregated, pre_grad)
    node_sums[2 * width : 3 * width] = dot_tn(node_hidden, out_grad)
    node_gain = jnp.sum(upstream * normed, axis=0, keepdims=True)
    upstream = live * (
        edge_grads[...].astype(F32) + dot(near_rows[:, count:], agg_grad)
    )
    edge_normed = normed_kept[...]
    edge_gain = jnp.sum(upstream * edge_normed, axis=0, keepdims=True)
    out_grad = norm_back(edge_normed, scale_kept[:, :1], gain, upstream).astype(BF16)
    pre_grad = (dot_nt(out_grad, w_out[...]) * slope_kept[...]).astype(BF16)
    pre_grad_out[...] = pre_grad
    sender_total = dot(sender_columns[...], pre_grad)
    receiver_total = dot(receiver_columns[...], pre_grad)
    own = sender_total[:count].astype(BF16)
    away = sender_total[count:].astype(BF16)
    received = receiver_total.astype(BF16)
    sender_out[...] = own
    receiver_out[...] = received
    halo_grad = dot_nt(away, w_in[width : 2 * width]).astype(BF16)
    parts = [halo_grad[k * slots : (k + 1) * slots] for k in range(8)]
    up_out[...] = jnp.concatenate([parts[0], parts[3], parts[5]], axis=0)
    down_out[...] = jnp.concatenate([parts[2], parts[4], parts[7]], axis=0)
    rest_out[...] = jnp.concatenate([parts[1], parts[6]], axis=0)
    edge_sums[:width] = dot_tn(edges[...], pre_grad)
    edge_sums[width : 2 * width] = dot_tn(x, own) + dot_tn(halo, away)
    edge_sums[2 * width : 3 * width] = dot_tn(x, received)
    edge_sums[3 * width : 4 * width] = dot_tn(hidden_kept[...], out_grad)
    split_by_core(edge_sums, 0, keep_out, away_out)
    split_by_core(node_sums, edge_sums.shape[0] // 2, keep_out, away_out)
    gains = pack_gains(edge_gain, node_gain)
    away_out[keep_out.shape[0] :] = gains
    gains_out[...] = gains


def add_gains(own, other):
    both = own.astype(F32) + other.astype(F32)
    return pack_gains(both[0:1] + both[1:2], both[2:3] + both[3:4])


def gains_kernel(own, other, gains_out):
    gains_out[...] = add_gains(own[...], other[...])


def pair_kernel(parts, keep, gains, other, blocks_out, gains_out, total, staged, sems):
    rows = keep.shape[0]
    chips = blocks_out.shape[0]
    total[...] = (keep[...] + other[:rows].astype(F32)).astype(BF16)
    copies = []
    for chip in range(chips):
        first, at = 0, 0
        for part in parts:
            step = part // chips
            staged[chip, at : at + step, :] = total[first + chip * step : first + (chip + 1) * step]
            first, at = first + part, at + step
        copies.append(
            pltpu.make_async_copy(staged.at[chip], blocks_out.at[chip], sems.at[chip])
        )
        copies[-1].start()
    gains_out[...] = add_gains(gains[...], other[rows:])
    for copy in copies:
        copy.wait()


def spread_kernel(received, spread_out, mine, sems):
    sums = received[0].astype(F32)
    for chip in range(1, received.shape[0]):
        sums = sums + received[chip].astype(F32)
    mine[...] = sums.astype(BF16)
    copies = [
        pltpu.make_async_copy(mine, spread_out.at[chip], sems.at[chip])
        for chip in range(received.shape[0])
    ]
    for copy in copies:
        copy.start()
    for copy in copies:
        copy.wait()


def place_kernel(parts, own, other, *refs):
    outs, sems = refs[:-1], refs[-1]
    chips = own.shape[0]
    core = lax.axis_index(CORE)

    def place(halves):
        copies = []

        def put(source, target):
            copies.append(pltpu.make_async_copy(source, target, sems.at[len(copies)]))
            copies[-1].start()

        for half, blocks in enumerate(halves):
            for chip in range(chips):
                at = 0
                for i, part in enumerate(parts):
                    step = part // chips
                    row = half * part + chip * step
                    cut = outs[2 * i].shape[0]
                    split = min(max(cut - row, 0), step)
                    if split > 0:
                        put(blocks.at[chip, at : at + split], outs[2 * i].at[row : row + split])
                    if split < step:
                        rest = row + split - cut
                        put(
                            blocks.at[chip, at + split : at + step],
                            outs[2 * i + 1].at[rest : rest + step - split],
                        )
                    at += step
        for copy in copies:
            copy.wait()

    @pl.when(core == 0)
    def _():
        place([own, other])

    @pl.when(core == 1)
    def _():
        place([other, own])


def finish_kernel(
    edge_grads, pre_grad, sender_sum, receiver_sum, node_part, w_in, edges_grad, local_grad
):
    width = w_in.shape[1]
    edges_grad[...] = (
        edge_grads[...].astype(F32) + dot_nt(pre_grad[...], w_in[:width])
    ).astype(BF16)
    local_grad[...] = (
        node_part[...]
        + dot_nt(sender_sum[...], w_in[width : 2 * width])
        + dot_nt(receiver_sum[...], w_in[2 * width :])
    )


def return_kernel(send_list, local_grad, up_back, down_back, to_high, to_low, nodes_grad):
    slots = send_list.shape[1]

    def block(ref, k):
        return ref[k * slots : (k + 1) * slots]

    returned = jnp.concatenate(
        [
            block(to_high, 0),
            block(to_high, 2),
            block(to_high, 1),
            block(up_back, 1),
            block(down_back, 1),
            block(to_low, 0),
            block(to_low, 2),
            block(to_low, 1),
        ],
        axis=0,
    )
    hot = list_hot(send_list[...], local_grad.shape[0])
    nodes_grad[...] = (local_grad[...] + dot_tn(hot, returned)).astype(BF16)


SMEM = pltpu.SMEM
VMEM = pltpu.VMEM
HBM = pltpu.HBM


def call(body, outs, flops, *operands, spaces=(), out_space=VMEM, scratch=()):
    moved = sum(x.size * x.dtype.itemsize for x in operands)
    moved += sum(x.size * jnp.dtype(x.dtype).itemsize for x in outs)
    spaces = list(spaces) + [VMEM] * (len(operands) - len(spaces))
    out_spaces = out_space if isinstance(out_space, list) else [out_space] * len(outs)
    operands = [
        pltpu.with_memory_space_constraint(x, HBM) if space is HBM else x
        for x, space in zip(operands, spaces)
    ]
    return pl.pallas_call(
        body,
        out_shape=outs,
        in_specs=[pl.BlockSpec(memory_space=space) for space in spaces],
        out_specs=[pl.BlockSpec(memory_space=space) for space in out_spaces],
        scratch_shapes=list(scratch),
        compiler_params=pltpu.CompilerParams(vmem_limit_bytes=VMEM_LIMIT),
        cost_estimate=pl.CostEstimate(flops=flops, bytes_accessed=moved, transcendentals=0),
    )(*operands)


def like(array):
    return jax.ShapeDtypeStruct(array.shape, array.dtype)


def shaped(rows, columns, dtype):
    return jax.ShapeDtypeStruct((rows, columns), dtype)


def placed(parts, own, other, width):
    chips = own.shape[0]
    outs = [
        shaped(3 * width, width, BF16),
        shaped(width, width, BF16),
        shaped(2 * width, width, BF16),
        shaped(width, width, BF16),
    ]
    steps = [part // chips for part in parts]
    cuts = [x.shape[0] for x in outs[::2]]
    if all(x % 16 == 0 for x in steps + cuts):
        return call(
            functools.partial(place_kernel, parts),
            outs,
            0,
            own,
            other,
            out_space=HBM,
            scratch=[pltpu.SemaphoreType.DMA((2 * len(parts) * chips + len(parts),))],
        )
    core = lax.axis_index(CORE)
    low = jnp.where(core == 0, own, other)
    high = jnp.where(core == 0, other, own)
    results = []
    at = 0
    for step, cut in zip(steps, cuts):
        whole = jnp.concatenate(
            [x[:, at : at + step].reshape(chips * step, width) for x in (low, high)]
        )
        results += [whole[:cut], whole[cut:]]
        at += step
    return results


def spread_of(received):
    chips, rows, width = received.shape
    if rows % 16 == 0:
        return call(
            spread_kernel,
            [like(received)],
            0,
            received,
            out_space=HBM,
            scratch=[pltpu.VMEM((rows, width), BF16), pltpu.SemaphoreType.DMA((chips,))],
        )[0]
    sums = jnp.sum(received.astype(F32), axis=0)
    return jnp.broadcast_to(sums.astype(BF16)[None], received.shape)


def summed_gains(gains):
    for axis in ("side", "px"):
        size = lax.axis_size(axis)
        distance = 1
        while distance < size:
            other = lax.ppermute(gains, axis, [(i, i ^ distance) for i in range(size)])
            (gains,) = call(gains_kernel, [like(gains)], 0, gains, other)
            distance *= 2
    return gains


def blocks_of(parts, keep, gains, other):
    chips = lax.axis_size(CHIPS)
    rows, width = keep.shape
    steps = [part // chips for part in parts]
    shape = (chips, sum(steps), width)
    if all(x % 16 == 0 for x in steps):
        return call(
            functools.partial(pair_kernel, parts),
            [jax.ShapeDtypeStruct(shape, BF16), like(gains)],
            0,
            keep,
            gains,
            other,
            out_space=[HBM, VMEM],
            scratch=[
                pltpu.VMEM((rows, width), BF16),
                pltpu.VMEM(shape, BF16),
                pltpu.SemaphoreType.DMA((chips,)),
            ],
        )
    total = (keep + other[:rows].astype(F32)).astype(BF16)
    pieces = []
    first = 0
    for part, step in zip(parts, steps):
        pieces.append(total[first : first + part].reshape(chips, step, width))
        first += part
    (gains,) = call(gains_kernel, [like(gains)], 0, gains, other[rows:])
    return jnp.concatenate(pieces, axis=1), gains


def on_device(
    nodes,
    edges,
    edge_grads,
    node_grads,
    send_list,
    senders,
    receivers,
    tile_count,
    w_edge_in,
    w_edge_out,
    gain_edge,
    w_node_in,
    w_node_out,
    gain_node,
):
    count, width = nodes.shape
    slots = send_list.shape[1]
    halo_rows = 8 * slots
    edge_rows = edges.shape[0]
    tile_rows = senders.shape[1]
    square = 2 * width * width
    low, mid, high, nodes, send_list = call(
        send_kernel,
        [
            shaped(3 * slots, width, BF16),
            shaped(2 * slots, width, BF16),
            shaped(3 * slots, width, BF16),
            like(nodes),
            like(send_list),
        ],
        2 * halo_rows * count * width,
        nodes,
        send_list,
        spaces=[HBM, HBM],
        scratch=[pltpu.SemaphoreType.DMA((2,))],
    )
    from_low = passed_along(high, "px", 1)
    from_high = passed_along(low, "px", -1)
    fetched = [
        senders,
        receivers,
        edges,
        w_edge_in,
        w_edge_out,
        gain_edge,
        w_node_in,
        w_node_out,
        gain_node,
        node_grads,
        edge_grads,
    ]
    near_hot, halo_hot, sender_columns, receiver_columns, *fetched = call(
        functools.partial(index_kernel, len(fetched)),
        [
            shaped(edge_rows, 2 * count, BF16),
            shaped(edge_rows, halo_rows, BF16),
            shaped(count + halo_rows, edge_rows, BF16),
            shaped(count, edge_rows, BF16),
        ]
        + [like(x) for x in fetched],
        0,
        *fetched,
        spaces=[HBM] * len(fetched),
        scratch=[pltpu.SemaphoreType.DMA((len(fetched),))],
    )
    (
        senders,
        receivers,
        edges,
        w_edge_in,
        w_edge_out,
        gain_edge,
        w_node_in,
        w_node_out,
        gain_node,
        node_grads,
        edge_grads,
    ) = fetched
    from_low, from_high, near_hot = lax.optimization_barrier((from_low, from_high, near_hot))
    upward = passed_along(
        jnp.concatenate([from_high[2 * slots :], mid[slots:], from_low[2 * slots :]]), PY, 1
    )
    downward = passed_along(
        jnp.concatenate([from_high[:slots], mid[:slots], from_low[:slots]]), PY, -1
    )
    (pre_local,) = call(
        local_kernel,
        [shaped(edge_rows, width, F32)],
        square * (2 * count + edge_rows) + 4 * edge_rows * count * width,
        nodes,
        edges,
        near_hot,
        w_edge_in,
    )
    parts = (2 * width, 3 * width // 2)
    halves = sum(parts)
    pre_grad, sender_sum, receiver_sum, node_part, up, down, rest, keep, away, gains = call(
        functools.partial(layer_kernel, tile_rows),
        [
            shaped(edge_rows, width, BF16),
            shaped(count, width, BF16),
            shaped(count, width, BF16),
            shaped(count, width, F32),
            shaped(3 * slots, width, BF16),
            shaped(3 * slots, width, BF16),
            shaped(2 * slots, width, BF16),
            shaped(halves, width, F32),
            shaped(halves + 16, width, BF16),
            shaped(16, width, BF16),
        ],
        square * (6 * edge_rows + 11 * count + 2 * halo_rows)
        + 2 * edge_rows * (4 * count + halo_rows) * width,
        tile_count,
        nodes,
        node_grads,
        edges,
        edge_grads,
        pre_local,
        halo_hot,
        near_hot,
        sender_columns,
        receiver_columns,
        from_high,
        from_low,
        upward,
        downward,
        w_edge_in,
        w_edge_out,
        gain_edge,
        w_node_in,
        w_node_out,
        gain_node,
        spaces=[SMEM],
        scratch=[
            pltpu.VMEM((edge_rows, width), F32),
            pltpu.VMEM((edge_rows, width), BF16),
            pltpu.VMEM((edge_rows, width), F32),
            pltpu.VMEM((edge_rows, 128), F32),
            pltpu.VMEM((3 * width, width), F32),
            pltpu.VMEM((4 * width, width), F32),
        ],
    )
    blocks, gains = blocks_of(parts, keep, gains, across_cores(away))
    received = lax.all_to_all(blocks, CHIPS, 0, 0)
    gains = summed_gains(gains)
    up_back = passed_along(up, PY, 1)
    down_back = passed_along(down, PY, -1)
    received, gains, up_back, down_back = lax.optimization_barrier(
        (received, gains, up_back, down_back)
    )
    own = lax.all_to_all(spread_of(received), CHIPS, 0, 0)
    to_high = passed_along(
        jnp.concatenate([up_back[:slots], down_back[:slots], rest[:slots]]), "px", 1
    )
    to_low = passed_along(
        jnp.concatenate([up_back[2 * slots :], down_back[2 * slots :], rest[slots:]]), "px", -1
    )
    edges_grad, local_grad = call(
        finish_kernel,
        [shaped(edge_rows, width, BF16), shaped(count, width, F32)],
        square * (edge_rows + 2 * count),
        edge_grads,
        pre_grad,
        sender_sum,
        receiver_sum,
        node_part,
        w_edge_in,
    )
    (nodes_grad,) = call(
        return_kernel,
        [shaped(count, width, BF16)],
        2 * halo_rows * count * width,
        send_list,
        local_grad,
        up_back,
        down_back,
        to_high,
        to_low,
    )
    own, nodes_grad, edges_grad = lax.optimization_barrier((own, nodes_grad, edges_grad))
    w_edge_in_grad, w_edge_out_grad, w_node_in_grad, w_node_out_grad = placed(
        parts, own, across_cores(own), width
    )
    return (
        nodes_grad,
        edges_grad,
        w_edge_in_grad,
        w_edge_out_grad,
        (gains[0].astype(F32) + gains[1].astype(F32)).astype(BF16),
        w_node_in_grad,
        w_node_out_grad,
        (gains[2].astype(F32) + gains[3].astype(F32)).astype(BF16),
    )


def solution(mesh):
    in_specs = (
        P(("groups", "px") + PY, None),
        P(("groups", "px") + PY, None),
        P(("groups", "px") + PY, None),
        P(("groups", "px") + PY, None),
        P(("groups", "px") + PY, None),
        P(("groups", "px") + PY, None),
        P(("groups", "px") + PY, None),
        P(("groups", "px") + PY),
        P(),
        P(),
        P(),
        P(),
        P(),
        P(),
    )
    out_specs = (
        P(("groups", "px") + PY, None),
        P(("groups", "px") + PY, None),
        P("groups", None),
        P("groups", None),
        P("groups"),
        P("groups", None),
        P("groups", None),
        P("groups"),
    )
    groups, px, py = mesh.devices.shape
    by_core = jax.sharding.Mesh(
        mesh.devices.reshape(groups, px, py // 2, 2), ("groups", "px") + PY
    )
    return jax.shard_map(
        on_device, mesh=by_core, in_specs=in_specs, out_specs=out_specs, check_vma=False
    )
```

```python
import functools

import jax
import jax.numpy as jnp
from jax import lax
from jax.experimental import pallas as pl
from jax.experimental.pallas import tpu as pltpu
from jax.sharding import PartitionSpec as P

EPS = 1e-05
BF16 = jnp.bfloat16
F32 = jnp.float32
VMEM_LIMIT = 24 * 1024 * 1024


CORE = "core"
PY = ("side", "core")
CHIPS = ("px", "side")


def passed_along(array, axis, by):
    size = lax.axis_size(axis)
    return lax.ppermute(array, axis, [(i, (i + by) % size) for i in range(size)])


def across_cores(array):
    return lax.ppermute(array, CORE, [(0, 1), (1, 0)])


def dot(left, right):
    return jnp.dot(left, right, preferred_element_type=F32)


def dot_tn(left, right):
    return lax.dot_general(left, right, (((0,), (0,)), ((), ())), preferred_element_type=F32)


def dot_nt(left, right):
    return lax.dot_general(left, right, (((1,), (1,)), ((), ())), preferred_element_type=F32)


def sigmoid(value):
    return 0.5 + 0.5 * jnp.tanh(0.5 * value)


def normalize(value):
    centered = value - jnp.mean(value, axis=-1, keepdims=True)
    scale_inv = lax.rsqrt(jnp.mean(centered * centered, axis=-1, keepdims=True) + EPS)
    return centered * scale_inv, scale_inv


def row_mean(value, split):
    width = value.shape[1]
    high = value.astype(BF16)
    if split:
        high = jnp.concatenate([high, (value - high.astype(F32)).astype(BF16)], axis=1)
    return dot(high, jnp.full((high.shape[1], width), 1.0 / width, BF16))


def normalize_wide(value):
    centered = value - row_mean(value, True)
    scale_inv = lax.rsqrt(row_mean(centered * centered, False) + EPS)
    return centered * scale_inv, scale_inv


def norm_back_wide(normed, scale_inv, gain, upstream):
    scaled = upstream * gain
    inner = scaled - row_mean(scaled, True) - normed * row_mean(scaled * normed, False)
    return inner * scale_inv


def norm_back(normed, scale_inv, gain, upstream):
    scaled = upstream * gain
    inner = (
        scaled
        - jnp.mean(scaled, axis=-1, keepdims=True)
        - normed * jnp.mean(scaled * normed, axis=-1, keepdims=True)
    )
    return inner * scale_inv


def columns_of(ids):
    rows, lanes = ids.shape
    padded = -(-rows // 8) * 8
    if padded > rows:
        ids = jnp.concatenate([ids, jnp.zeros((padded - rows, lanes), ids.dtype)], axis=0)
    return ids.T


def hot_rows(columns, tiles, base, count):
    parts = []
    for tile in tiles:
        column = columns[:, tile : tile + 1] - base
        lanes = lax.broadcasted_iota(jnp.int32, (columns.shape[0], count), 1)
        parts.append(jnp.where(lanes == column, 1.0, 0.0).astype(BF16))
    return jnp.concatenate(parts, axis=0) if len(parts) > 1 else parts[0]


def hot_columns(ids, tiles, base, count):
    parts = []
    for tile in tiles:
        row = ids[tile : tile + 1, :] - base
        subs = lax.broadcasted_iota(jnp.int32, (count, ids.shape[1]), 0)
        parts.append(jnp.where(subs == row, 1.0, 0.0).astype(BF16))
    return jnp.concatenate(parts, axis=1) if len(parts) > 1 else parts[0]


def list_hot(ids, count):
    directions, slots = ids.shape
    wide = jnp.concatenate([ids, jnp.zeros((directions, 128 - slots), ids.dtype)], axis=1)
    columns = wide.T
    parts = []
    for k in range(directions):
        lanes = lax.broadcasted_iota(jnp.int32, (slots, count), 1)
        parts.append(jnp.where(lanes == columns[:slots, k : k + 1], 1.0, 0.0).astype(BF16))
    return jnp.concatenate(parts, axis=0)


def live_rows(count_ref, tile_rows, rows):
    index = lax.broadcasted_iota(jnp.int32, (rows, 1), 0)
    return jnp.where(index < count_ref[0] * tile_rows, 1.0, 0.0)


def fetch_all(sources, targets, sems):
    copies = [
        pltpu.make_async_copy(source, target, sems.at[i])
        for i, (source, target) in enumerate(zip(sources, targets))
    ]
    for copy in copies:
        copy.start()
    return copies


def send_kernel(nodes_hbm, list_hbm, low, mid, high, nodes, send_list, sems):
    slots = send_list.shape[1]
    for copy in fetch_all([list_hbm, nodes_hbm], [send_list, nodes], sems):
        copy.wait()
    rows = dot(list_hot(send_list[...], nodes.shape[0]), nodes[...]).astype(BF16)
    low[...] = rows[: 3 * slots]
    mid[...] = rows[3 * slots : 5 * slots]
    high[...] = rows[5 * slots :]


def index_kernel(sources, *refs):
    fetched, refs = refs[:sources], refs[sources:]
    near_rows, halo_rows, sender_columns, receiver_columns = refs[:4]
    targets, sems = refs[4:-1], refs[-1]
    senders, receivers = targets[:2]
    copies = fetch_all(fetched, targets, sems)
    for copy in copies[:2]:
        copy.wait()
    tile_rows = senders.shape[1]
    extended = sender_columns.shape[0]
    count = receiver_columns.shape[0]
    sender_ids = senders[...]
    receiver_ids = receivers[...]
    by_sender = columns_of(sender_ids)
    by_receiver = columns_of(receiver_ids)
    for tile in range(senders.shape[0]):
        rows = slice(tile * tile_rows, (tile + 1) * tile_rows)
        near_rows[rows, :count] = hot_rows(by_sender, [tile], 0, count)
        near_rows[rows, count:] = hot_rows(by_receiver, [tile], 0, count)
        halo_rows[rows, :] = hot_rows(by_sender, [tile], count, halo_rows.shape[1])
        sender_columns[:, rows] = hot_columns(sender_ids, [tile], 0, extended)
        receiver_columns[:, rows] = hot_columns(receiver_ids, [tile], 0, count)
    for copy in copies[2:]:
        copy.wait()


def local_kernel(nodes, edges, near_rows, w_in, pre):
    width = nodes.shape[1]
    x = nodes[...]
    table = jnp.concatenate(
        [
            dot(x, w_in[width : 2 * width]).astype(BF16),
            dot(x, w_in[2 * width :]).astype(BF16),
        ],
        axis=0,
    )
    pre[...] = dot(edges[...], w_in[:width]) + dot(near_rows[...], table)


def split_by_core(sums, first, keep_out, away_out):
    half = sums.shape[0] // 2
    core = lax.axis_index(CORE)
    keep_out[first : first + half] = sums[pl.ds(pl.multiple_of(core * half, half), half), :]
    away = sums[pl.ds(pl.multiple_of((1 - core) * half, half), half), :]
    away_out[first : first + half] = away.astype(BF16)


def pack_gains(edge_gain, node_gain):
    edge_high = edge_gain.astype(BF16).astype(F32)
    node_high = node_gain.astype(BF16).astype(F32)
    row = lax.broadcasted_iota(jnp.int32, (16, edge_gain.shape[1]), 0)
    packed = jnp.where(row == 0, edge_high, 0.0)
    packed = jnp.where(row == 1, edge_gain - edge_high, packed)
    packed = jnp.where(row == 2, node_high, packed)
    packed = jnp.where(row == 3, node_gain - node_high, packed)
    return packed.astype(BF16)


def layer_kernel(
    tile_rows,
    count_ref,
    nodes,
    node_grads,
    edges,
    edge_grads,
    pre_local,
    halo_rows,
    near_rows,
    sender_columns,
    receiver_columns,
    from_high,
    from_low,
    upward,
    downward,
    w_in,
    w_out,
    gain_edge,
    w_node_in,
    w_node_out,
    gain_node,
    pre_grad_out,
    sender_out,
    receiver_out,
    node_part_out,
    up_out,
    down_out,
    rest_out,
    keep_out,
    away_out,
    gains_out,
    slope_kept,
    hidden_kept,
    normed_kept,
    scale_kept,
    node_sums,
    edge_sums,
):
    count, width = nodes.shape
    edge_rows = edges.shape[0]
    live = live_rows(count_ref, tile_rows, edge_rows)
    slots = from_high.shape[0] // 3
    halo = jnp.concatenate(
        [
            downward[:slots],
            from_high[slots : 2 * slots],
            upward[:slots],
            downward[slots : 2 * slots],
            upward[slots : 2 * slots],
            downward[2 * slots :],
            from_low[slots : 2 * slots],
            upward[2 * slots :],
        ],
        axis=0,
    )
    table = dot(halo, w_in[width : 2 * width]).astype(BF16)
    gain = gain_edge[...].astype(F32)[None, :]
    value = pre_local[...] + dot(halo_rows[...], table)
    sigma = sigmoid(value)
    hidden = (value * sigma).astype(BF16)
    hidden_kept[...] = hidden
    slope_kept[...] = sigma * (1.0 + value * (1.0 - sigma))
    edge_normed, edge_scale = normalize_wide(dot(hidden, w_out[...]))
    normed_kept[...] = edge_normed
    scale_kept[...] = edge_scale
    message = (live * gain * edge_normed).astype(BF16)
    total = dot(receiver_columns[...], message)
    aggregated = total.astype(BF16)
    x = nodes[...]
    w_first = w_node_in[:width]
    w_second = w_node_in[width:]
    node_pre = dot(x, w_first) + dot(aggregated, w_second)
    sigma = sigmoid(node_pre)
    node_hidden = (node_pre * sigma).astype(BF16)
    normed, scale_inv = normalize(dot(node_hidden, w_node_out[...]))
    upstream = node_grads[...].astype(F32)
    out_grad = norm_back(normed, scale_inv, gain_node[...].astype(F32)[None, :], upstream).astype(BF16)
    slope = sigma * (1.0 + node_pre * (1.0 - sigma))
    pre_grad = (dot_nt(out_grad, w_node_out[...]) * slope).astype(BF16)
    agg_grad = dot_nt(pre_grad, w_second).astype(BF16)
    node_part_out[...] = upstream + dot_nt(pre_grad, w_first)
    node_sums[:width] = dot_tn(x, pre_grad)
    node_sums[width : 2 * width] = dot_tn(aggregated, pre_grad)
    node_sums[2 * width : 3 * width] = dot_tn(node_hidden, out_grad)
    node_gain = jnp.sum(upstream * normed, axis=0, keepdims=True)
    upstream = live * (
        edge_grads[...].astype(F32) + dot(near_rows[:, count:], agg_grad)
    )
    edge_normed = normed_kept[...]
    edge_gain = jnp.sum(upstream * edge_normed, axis=0, keepdims=True)
    out_grad = norm_back_wide(edge_normed, scale_kept[...], gain, upstream).astype(BF16)
    pre_grad = (dot_nt(out_grad, w_out[...]) * slope_kept[...]).astype(BF16)
    pre_grad_out[...] = pre_grad
    sender_total = dot(sender_columns[...], pre_grad)
    receiver_total = dot(receiver_columns[...], pre_grad)
    own = sender_total[:count].astype(BF16)
    away = sender_total[count:].astype(BF16)
    received = receiver_total.astype(BF16)
    sender_out[...] = own
    receiver_out[...] = received
    halo_grad = dot_nt(away, w_in[width : 2 * width]).astype(BF16)
    parts = [halo_grad[k * slots : (k + 1) * slots] for k in range(8)]
    up_out[...] = jnp.concatenate([parts[0], parts[3], parts[5]], axis=0)
    down_out[...] = jnp.concatenate([parts[2], parts[4], parts[7]], axis=0)
    rest_out[...] = jnp.concatenate([parts[1], parts[6]], axis=0)
    edge_sums[:width] = dot_tn(edges[...], pre_grad)
    edge_sums[width : 2 * width] = dot_tn(x, own) + dot_tn(halo, away)
    edge_sums[2 * width : 3 * width] = dot_tn(x, received)
    edge_sums[3 * width : 4 * width] = dot_tn(hidden_kept[...], out_grad)
    split_by_core(edge_sums, 0, keep_out, away_out)
    split_by_core(node_sums, edge_sums.shape[0] // 2, keep_out, away_out)
    gains = pack_gains(edge_gain, node_gain)
    away_out[keep_out.shape[0] :] = gains
    gains_out[...] = gains


def pair_kernel(parts, keep, gains, other, blocks_out, total, staged, sems):
    rows = keep.shape[0]
    chips = blocks_out.shape[0]
    packed = gains.shape[0]
    both = gains[...].astype(F32) + other[rows:].astype(F32)
    summed = pack_gains(both[0:1] + both[1:2], both[2:3] + both[3:4])
    total[...] = (keep[...] + other[:rows].astype(F32)).astype(BF16)
    copies = []
    for chip in range(chips):
        staged[chip, :packed, :] = summed
        first, at = 0, packed
        for part in parts:
            step = part // chips
            staged[chip, at : at + step, :] = total[first + chip * step : first + (chip + 1) * step]
            first, at = first + part, at + step
        copies.append(
            pltpu.make_async_copy(staged.at[chip], blocks_out.at[chip], sems.at[chip])
        )
        copies[-1].start()
    for copy in copies:
        copy.wait()


def spread_kernel(packed, received, gains_out, spread_out, mine, sems):
    sums = received[0].astype(F32)
    for chip in range(1, received.shape[0]):
        sums = sums + received[chip].astype(F32)
    gains_out[...] = sums[:packed]
    mine[...] = sums[packed:].astype(BF16)
    copies = [
        pltpu.make_async_copy(mine, spread_out.at[chip], sems.at[chip])
        for chip in range(received.shape[0])
    ]
    for copy in copies:
        copy.start()
    for copy in copies:
        copy.wait()


def place_kernel(parts, own, other, *refs):
    outs, sems = refs[:-1], refs[-1]
    chips = own.shape[0]
    core = lax.axis_index(CORE)

    def place(halves):
        copies = []

        def put(source, target):
            copies.append(pltpu.make_async_copy(source, target, sems.at[len(copies)]))
            copies[-1].start()

        for half, blocks in enumerate(halves):
            for chip in range(chips):
                at = 0
                for i, part in enumerate(parts):
                    step = part // chips
                    row = half * part + chip * step
                    cut = outs[2 * i].shape[0]
                    split = min(max(cut - row, 0), step)
                    if split > 0:
                        put(blocks.at[chip, at : at + split], outs[2 * i].at[row : row + split])
                    if split < step:
                        rest = row + split - cut
                        put(
                            blocks.at[chip, at + split : at + step],
                            outs[2 * i + 1].at[rest : rest + step - split],
                        )
                    at += step
        for copy in copies:
            copy.wait()

    @pl.when(core == 0)
    def _():
        place([own, other])

    @pl.when(core == 1)
    def _():
        place([other, own])


def finish_kernel(
    edge_grads, pre_grad, sender_sum, receiver_sum, node_part, w_in, edges_grad, local_grad
):
    width = w_in.shape[1]
    edges_grad[...] = (
        edge_grads[...].astype(F32) + dot_nt(pre_grad[...], w_in[:width])
    ).astype(BF16)
    local_grad[...] = (
        node_part[...]
        + dot_nt(sender_sum[...], w_in[width : 2 * width])
        + dot_nt(receiver_sum[...], w_in[2 * width :])
    )


def return_kernel(send_list, local_grad, up_back, down_back, to_high, to_low, nodes_grad):
    slots = send_list.shape[1]

    def block(ref, k):
        return ref[k * slots : (k + 1) * slots]

    returned = jnp.concatenate(
        [
            block(to_high, 0),
            block(to_high, 2),
            block(to_high, 1),
            block(up_back, 1),
            block(down_back, 1),
            block(to_low, 0),
            block(to_low, 2),
            block(to_low, 1),
        ],
        axis=0,
    )
    hot = list_hot(send_list[...], local_grad.shape[0])
    nodes_grad[...] = (local_grad[...] + dot_tn(hot, returned)).astype(BF16)


SMEM = pltpu.SMEM
VMEM = pltpu.VMEM
HBM = pltpu.HBM


def call(body, outs, flops, *operands, spaces=(), out_space=VMEM, scratch=()):
    moved = sum(x.size * x.dtype.itemsize for x in operands)
    moved += sum(x.size * jnp.dtype(x.dtype).itemsize for x in outs)
    spaces = list(spaces) + [VMEM] * (len(operands) - len(spaces))
    out_spaces = out_space if isinstance(out_space, list) else [out_space] * len(outs)
    operands = [
        pltpu.with_memory_space_constraint(x, HBM) if space is HBM else x
        for x, space in zip(operands, spaces)
    ]
    return pl.pallas_call(
        body,
        out_shape=outs,
        in_specs=[pl.BlockSpec(memory_space=space) for space in spaces],
        out_specs=[pl.BlockSpec(memory_space=space) for space in out_spaces],
        scratch_shapes=list(scratch),
        compiler_params=pltpu.CompilerParams(vmem_limit_bytes=VMEM_LIMIT),
        cost_estimate=pl.CostEstimate(flops=flops, bytes_accessed=moved, transcendentals=0),
    )(*operands)


def like(array):
    return jax.ShapeDtypeStruct(array.shape, array.dtype)


def shaped(rows, columns, dtype):
    return jax.ShapeDtypeStruct((rows, columns), dtype)


def placed(parts, own, other, width):
    chips = own.shape[0]
    outs = [
        shaped(3 * width, width, BF16),
        shaped(width, width, BF16),
        shaped(2 * width, width, BF16),
        shaped(width, width, BF16),
    ]
    steps = [part // chips for part in parts]
    cuts = [x.shape[0] for x in outs[::2]]
    if all(x % 16 == 0 for x in steps + cuts):
        return call(
            functools.partial(place_kernel, parts),
            outs,
            0,
            own,
            other,
            out_space=HBM,
            scratch=[pltpu.SemaphoreType.DMA((2 * len(parts) * chips + len(parts),))],
        )
    core = lax.axis_index(CORE)
    low = jnp.where(core == 0, own, other)
    high = jnp.where(core == 0, other, own)
    results = []
    at = 0
    for step, cut in zip(steps, cuts):
        whole = jnp.concatenate(
            [x[:, at : at + step].reshape(chips * step, width) for x in (low, high)]
        )
        results += [whole[:cut], whole[cut:]]
        at += step
    return results


def spread_of(received, packed):
    chips, rows, width = received.shape
    mine = rows - packed
    if mine % 16 == 0:
        return call(
            functools.partial(spread_kernel, packed),
            [shaped(packed, width, F32), jax.ShapeDtypeStruct((chips, mine, width), BF16)],
            0,
            received,
            out_space=[VMEM, HBM],
            scratch=[pltpu.VMEM((mine, width), BF16), pltpu.SemaphoreType.DMA((chips,))],
        )
    sums = jnp.sum(received.astype(F32), axis=0)
    return sums[:packed], jnp.broadcast_to(sums[packed:].astype(BF16)[None], (chips, mine, width))


def blocks_of(parts, keep, gains, other):
    chips = lax.axis_size(CHIPS)
    rows, width = keep.shape
    packed = gains.shape[0]
    steps = [part // chips for part in parts]
    shape = (chips, packed + sum(steps), width)
    body = functools.partial(pair_kernel, parts)
    if all(x % 16 == 0 for x in steps):
        (blocks,) = call(
            body,
            [jax.ShapeDtypeStruct(shape, BF16)],
            0,
            keep,
            gains,
            other,
            out_space=HBM,
            scratch=[
                pltpu.VMEM((rows, width), BF16),
                pltpu.VMEM(shape, BF16),
                pltpu.SemaphoreType.DMA((chips,)),
            ],
        )
        return blocks
    both = gains.astype(F32) + other[rows:].astype(F32)
    summed = jnp.where(
        jnp.arange(packed)[:, None] % 2 == 0,
        both + jnp.roll(both, -1, axis=0),
        0.0,
    )
    high = summed.astype(BF16).astype(F32)
    summed = (high + jnp.roll(summed - high, 1, axis=0)).astype(BF16)
    total = (keep + other[:rows].astype(F32)).astype(BF16)
    pieces = [jnp.broadcast_to(summed[None], (chips, packed, width))]
    first = 0
    for part, step in zip(parts, steps):
        pieces.append(total[first : first + part].reshape(chips, step, width))
        first += part
    return jnp.concatenate(pieces, axis=1)


def on_device(
    nodes,
    edges,
    edge_grads,
    node_grads,
    send_list,
    senders,
    receivers,
    tile_count,
    w_edge_in,
    w_edge_out,
    gain_edge,
    w_node_in,
    w_node_out,
    gain_node,
):
    count, width = nodes.shape
    slots = send_list.shape[1]
    halo_rows = 8 * slots
    edge_rows = edges.shape[0]
    tile_rows = senders.shape[1]
    square = 2 * width * width
    low, mid, high, nodes, send_list = call(
        send_kernel,
        [
            shaped(3 * slots, width, BF16),
            shaped(2 * slots, width, BF16),
            shaped(3 * slots, width, BF16),
            like(nodes),
            like(send_list),
        ],
        2 * halo_rows * count * width,
        nodes,
        send_list,
        spaces=[HBM, HBM],
        scratch=[pltpu.SemaphoreType.DMA((2,))],
    )
    from_low = passed_along(high, "px", 1)
    from_high = passed_along(low, "px", -1)
    fetched = [
        senders,
        receivers,
        edges,
        w_edge_in,
        w_edge_out,
        gain_edge,
        w_node_in,
        w_node_out,
        gain_node,
        node_grads,
        edge_grads,
    ]
    near_hot, halo_hot, sender_columns, receiver_columns, *fetched = call(
        functools.partial(index_kernel, len(fetched)),
        [
            shaped(edge_rows, 2 * count, BF16),
            shaped(edge_rows, halo_rows, BF16),
            shaped(count + halo_rows, edge_rows, BF16),
            shaped(count, edge_rows, BF16),
        ]
        + [like(x) for x in fetched],
        0,
        *fetched,
        spaces=[HBM] * len(fetched),
        scratch=[pltpu.SemaphoreType.DMA((len(fetched),))],
    )
    (
        senders,
        receivers,
        edges,
        w_edge_in,
        w_edge_out,
        gain_edge,
        w_node_in,
        w_node_out,
        gain_node,
        node_grads,
        edge_grads,
    ) = fetched
    from_low, from_high, near_hot = lax.optimization_barrier((from_low, from_high, near_hot))
    upward = passed_along(
        jnp.concatenate([from_high[2 * slots :], mid[slots:], from_low[2 * slots :]]), PY, 1
    )
    downward = passed_along(
        jnp.concatenate([from_high[:slots], mid[:slots], from_low[:slots]]), PY, -1
    )
    (pre_local,) = call(
        local_kernel,
        [shaped(edge_rows, width, F32)],
        square * (2 * count + edge_rows) + 4 * edge_rows * count * width,
        nodes,
        edges,
        near_hot,
        w_edge_in,
    )
    parts = (2 * width, 3 * width // 2)
    halves = sum(parts)
    pre_grad, sender_sum, receiver_sum, node_part, up, down, rest, keep, away, gains = call(
        functools.partial(layer_kernel, tile_rows),
        [
            shaped(edge_rows, width, BF16),
            shaped(count, width, BF16),
            shaped(count, width, BF16),
            shaped(count, width, F32),
            shaped(3 * slots, width, BF16),
            shaped(3 * slots, width, BF16),
            shaped(2 * slots, width, BF16),
            shaped(halves, width, F32),
            shaped(halves + 16, width, BF16),
            shaped(16, width, BF16),
        ],
        square * (6 * edge_rows + 11 * count + 2 * halo_rows)
        + 2 * edge_rows * (4 * count + halo_rows) * width,
        tile_count,
        nodes,
        node_grads,
        edges,
        edge_grads,
        pre_local,
        halo_hot,
        near_hot,
        sender_columns,
        receiver_columns,
        from_high,
        from_low,
        upward,
        downward,
        w_edge_in,
        w_edge_out,
        gain_edge,
        w_node_in,
        w_node_out,
        gain_node,
        spaces=[SMEM],
        scratch=[
            pltpu.VMEM((edge_rows, width), F32),
            pltpu.VMEM((edge_rows, width), BF16),
            pltpu.VMEM((edge_rows, width), F32),
            pltpu.VMEM((edge_rows, width), F32),
            pltpu.VMEM((3 * width, width), F32),
            pltpu.VMEM((4 * width, width), F32),
        ],
    )
    blocks = blocks_of(parts, keep, gains, across_cores(away))
    received = lax.all_to_all(blocks, CHIPS, 0, 0)
    up_back = passed_along(up, PY, 1)
    down_back = passed_along(down, PY, -1)
    to_high = passed_along(
        jnp.concatenate([up_back[:slots], down_back[:slots], rest[:slots]]), "px", 1
    )
    to_low = passed_along(
        jnp.concatenate([up_back[2 * slots :], down_back[2 * slots :], rest[slots:]]), "px", -1
    )
    received, to_high, to_low = lax.optimization_barrier((received, to_high, to_low))
    gains, spread = spread_of(received, gains.shape[0])
    own = lax.all_to_all(spread, CHIPS, 0, 0)
    edges_grad, local_grad = call(
        finish_kernel,
        [shaped(edge_rows, width, BF16), shaped(count, width, F32)],
        square * (edge_rows + 2 * count),
        edge_grads,
        pre_grad,
        sender_sum,
        receiver_sum,
        node_part,
        w_edge_in,
    )
    (nodes_grad,) = call(
        return_kernel,
        [shaped(count, width, BF16)],
        2 * halo_rows * count * width,
        send_list,
        local_grad,
        up_back,
        down_back,
        to_high,
        to_low,
    )
    own, nodes_grad, edges_grad = lax.optimization_barrier((own, nodes_grad, edges_grad))
    w_edge_in_grad, w_edge_out_grad, w_node_in_grad, w_node_out_grad = placed(
        parts, own, across_cores(own), width
    )
    return (
        nodes_grad,
        edges_grad,
        w_edge_in_grad,
        w_edge_out_grad,
        (gains[0] + gains[1]).astype(BF16),
        w_node_in_grad,
        w_node_out_grad,
        (gains[2] + gains[3]).astype(BF16),
    )


def solution(mesh):
    in_specs = (
        P(("groups", "px") + PY, None),
        P(("groups", "px") + PY, None),
        P(("groups", "px") + PY, None),
        P(("groups", "px") + PY, None),
        P(("groups", "px") + PY, None),
        P(("groups", "px") + PY, None),
        P(("groups", "px") + PY, None),
        P(("groups", "px") + PY),
        P(),
        P(),
        P(),
        P(),
        P(),
        P(),
    )
    out_specs = (
        P(("groups", "px") + PY, None),
        P(("groups", "px") + PY, None),
        P("groups", None),
        P("groups", None),
        P("groups"),
        P("groups", None),
        P("groups", None),
        P("groups"),
    )
    groups, px, py = mesh.devices.shape
    by_core = jax.sharding.Mesh(
        mesh.devices.reshape(groups, px, py // 2, 2), ("groups", "px") + PY
    )
    return jax.shard_map(
        on_device, mesh=by_core, in_specs=in_specs, out_specs=out_specs, check_vma=False
    )
```

```python
import functools

import jax
import jax.numpy as jnp
from jax import lax
from jax.experimental import pallas as pl
from jax.experimental.pallas import tpu as pltpu
from jax.sharding import PartitionSpec as P

EPS = 1e-05
BF16 = jnp.bfloat16
F32 = jnp.float32
VMEM_LIMIT = 24 * 1024 * 1024


CORE = "core"
PY = ("side", "core")
CHIPS = ("px", "side")


def passed_along(array, axis, by):
    size = lax.axis_size(axis)
    return lax.ppermute(array, axis, [(i, (i + by) % size) for i in range(size)])


def across_cores(array):
    return lax.ppermute(array, CORE, [(0, 1), (1, 0)])


def dot(left, right):
    return jnp.dot(left, right, preferred_element_type=F32)


def dot_tn(left, right):
    return lax.dot_general(left, right, (((0,), (0,)), ((), ())), preferred_element_type=F32)


def dot_nt(left, right):
    return lax.dot_general(left, right, (((1,), (1,)), ((), ())), preferred_element_type=F32)


def sigmoid(value):
    return 0.5 + 0.5 * jnp.tanh(0.5 * value)


def normalize(value):
    centered = value - jnp.mean(value, axis=-1, keepdims=True)
    scale_inv = lax.rsqrt(jnp.mean(centered * centered, axis=-1, keepdims=True) + EPS)
    return centered * scale_inv, scale_inv


def norm_back(normed, scale_inv, gain, upstream):
    scaled = upstream * gain
    inner = (
        scaled
        - jnp.mean(scaled, axis=-1, keepdims=True)
        - normed * jnp.mean(scaled * normed, axis=-1, keepdims=True)
    )
    return inner * scale_inv


def columns_of(ids):
    rows, lanes = ids.shape
    padded = -(-rows // 8) * 8
    if padded > rows:
        ids = jnp.concatenate([ids, jnp.zeros((padded - rows, lanes), ids.dtype)], axis=0)
    return ids.T


def hot_rows(columns, tiles, base, count):
    parts = []
    for tile in tiles:
        column = columns[:, tile : tile + 1] - base
        lanes = lax.broadcasted_iota(jnp.int32, (columns.shape[0], count), 1)
        parts.append(jnp.where(lanes == column, 1.0, 0.0).astype(BF16))
    return jnp.concatenate(parts, axis=0) if len(parts) > 1 else parts[0]


def hot_columns(ids, tiles, base, count):
    parts = []
    for tile in tiles:
        row = ids[tile : tile + 1, :] - base
        subs = lax.broadcasted_iota(jnp.int32, (count, ids.shape[1]), 0)
        parts.append(jnp.where(subs == row, 1.0, 0.0).astype(BF16))
    return jnp.concatenate(parts, axis=1) if len(parts) > 1 else parts[0]


def list_hot(ids, count):
    directions, slots = ids.shape
    wide = jnp.concatenate([ids, jnp.zeros((directions, 128 - slots), ids.dtype)], axis=1)
    columns = wide.T
    parts = []
    for k in range(directions):
        lanes = lax.broadcasted_iota(jnp.int32, (slots, count), 1)
        parts.append(jnp.where(lanes == columns[:slots, k : k + 1], 1.0, 0.0).astype(BF16))
    return jnp.concatenate(parts, axis=0)


def live_rows(count_ref, tile_rows, rows):
    index = lax.broadcasted_iota(jnp.int32, (rows, 1), 0)
    return jnp.where(index < count_ref[0] * tile_rows, 1.0, 0.0)


def fetch_all(sources, targets, sems):
    copies = [
        pltpu.make_async_copy(source, target, sems.at[i])
        for i, (source, target) in enumerate(zip(sources, targets))
    ]
    for copy in copies:
        copy.start()
    return copies


def send_kernel(nodes_hbm, list_hbm, low, mid, high, nodes, send_list, sems):
    slots = send_list.shape[1]
    for copy in fetch_all([list_hbm, nodes_hbm], [send_list, nodes], sems):
        copy.wait()
    rows = dot(list_hot(send_list[...], nodes.shape[0]), nodes[...]).astype(BF16)
    low[...] = rows[: 3 * slots]
    mid[...] = rows[3 * slots : 5 * slots]
    high[...] = rows[5 * slots :]


def index_kernel(sources, *refs):
    fetched, refs = refs[:sources], refs[sources:]
    near_rows, halo_rows = refs[:2]
    targets, sems = refs[2:-1], refs[-1]
    senders, receivers = targets[:2]
    copies = fetch_all(fetched, targets, sems)
    for copy in copies[:2]:
        copy.wait()
    tile_rows = senders.shape[1]
    count = near_rows.shape[1] // 2
    by_sender = columns_of(senders[...])
    by_receiver = columns_of(receivers[...])
    for tile in range(senders.shape[0]):
        rows = slice(tile * tile_rows, (tile + 1) * tile_rows)
        near_rows[rows, :count] = hot_rows(by_sender, [tile], 0, count)
        near_rows[rows, count:] = hot_rows(by_receiver, [tile], 0, count)
        halo_rows[rows, :] = hot_rows(by_sender, [tile], count, halo_rows.shape[1])
    for copy in copies[2:]:
        copy.wait()


def local_kernel(
    nodes, edges, senders, receivers, near_rows, w_in, pre, sender_columns, receiver_columns
):
    width = nodes.shape[1]
    tile_rows = senders.shape[1]
    extended = sender_columns.shape[0]
    count = receiver_columns.shape[0]
    sender_ids = senders[...]
    receiver_ids = receivers[...]
    for tile in range(senders.shape[0]):
        rows = slice(tile * tile_rows, (tile + 1) * tile_rows)
        sender_columns[:, rows] = hot_columns(sender_ids, [tile], 0, extended)
        receiver_columns[:, rows] = hot_columns(receiver_ids, [tile], 0, count)
    x = nodes[...]
    table = jnp.concatenate(
        [
            dot(x, w_in[width : 2 * width]).astype(BF16),
            dot(x, w_in[2 * width :]).astype(BF16),
        ],
        axis=0,
    )
    pre[...] = dot(edges[...], w_in[:width]) + dot(near_rows[...], table)


def split_by_core(sums, first, keep_out, away_out):
    half = sums.shape[0] // 2
    core = lax.axis_index(CORE)
    keep_out[first : first + half] = sums[pl.ds(pl.multiple_of(core * half, half), half), :]
    away = sums[pl.ds(pl.multiple_of((1 - core) * half, half), half), :]
    away_out[first : first + half] = away.astype(BF16)


def pack_gains(edge_gain, node_gain):
    edge_high = edge_gain.astype(BF16).astype(F32)
    node_high = node_gain.astype(BF16).astype(F32)
    row = lax.broadcasted_iota(jnp.int32, (16, edge_gain.shape[1]), 0)
    packed = jnp.where(row == 0, edge_high, 0.0)
    packed = jnp.where(row == 1, edge_gain - edge_high, packed)
    packed = jnp.where(row == 2, node_high, packed)
    packed = jnp.where(row == 3, node_gain - node_high, packed)
    return packed.astype(BF16)


def layer_kernel(
    tile_rows,
    count_ref,
    nodes,
    node_grads,
    edges,
    edge_grads,
    pre_local,
    halo_rows,
    near_rows,
    sender_columns,
    receiver_columns,
    from_high,
    from_low,
    upward,
    downward,
    w_in,
    w_out,
    gain_edge,
    w_node_in,
    w_node_out,
    gain_node,
    pre_grad_out,
    sender_out,
    receiver_out,
    node_part_out,
    up_out,
    down_out,
    rest_out,
    keep_out,
    away_out,
    gains_out,
    slope_kept,
    hidden_kept,
    normed_kept,
    scale_kept,
    node_sums,
    edge_sums,
):
    count, width = nodes.shape
    edge_rows = edges.shape[0]
    live = live_rows(count_ref, tile_rows, edge_rows)
    slots = from_high.shape[0] // 3
    halo = jnp.concatenate(
        [
            downward[:slots],
            from_high[slots : 2 * slots],
            upward[:slots],
            downward[slots : 2 * slots],
            upward[slots : 2 * slots],
            downward[2 * slots :],
            from_low[slots : 2 * slots],
            upward[2 * slots :],
        ],
        axis=0,
    )
    table = dot(halo, w_in[width : 2 * width]).astype(BF16)
    gain = gain_edge[...].astype(F32)[None, :]
    value = pre_local[...] + dot(halo_rows[...], table)
    sigma = sigmoid(value)
    hidden = (value * sigma).astype(BF16)
    hidden_kept[...] = hidden
    slope_kept[...] = sigma * (1.0 + value * (1.0 - sigma))
    edge_normed, edge_scale = normalize(dot(hidden, w_out[...]))
    normed_kept[...] = edge_normed
    scale_kept[...] = jnp.broadcast_to(edge_scale, (edge_rows, 128))
    message = (live * gain * edge_normed).astype(BF16)
    total = dot(receiver_columns[...], message)
    aggregated = total.astype(BF16)
    x = nodes[...]
    w_first = w_node_in[:width]
    w_second = w_node_in[width:]
    node_pre = dot(x, w_first) + dot(aggregated, w_second)
    sigma = sigmoid(node_pre)
    node_hidden = (node_pre * sigma).astype(BF16)
    normed, scale_inv = normalize(dot(node_hidden, w_node_out[...]))
    upstream = node_grads[...].astype(F32)
    out_grad = norm_back(normed, scale_inv, gain_node[...].astype(F32)[None, :], upstream).astype(BF16)
    slope = sigma * (1.0 + node_pre * (1.0 - sigma))
    pre_grad = (dot_nt(out_grad, w_node_out[...]) * slope).astype(BF16)
    agg_grad = dot_nt(pre_grad, w_second).astype(BF16)
    node_part_out[...] = upstream + dot_nt(pre_grad, w_first)
    node_sums[:width] = dot_tn(x, pre_grad)
    node_sums[width : 2 * width] = dot_tn(aggregated, pre_grad)
    node_sums[2 * width : 3 * width] = dot_tn(node_hidden, out_grad)
    node_gain = jnp.sum(upstream * normed, axis=0, keepdims=True)
    upstream = live * (
        edge_grads[...].astype(F32) + dot(near_rows[:, count:], agg_grad)
    )
    edge_normed = normed_kept[...]
    edge_gain = jnp.sum(upstream * edge_normed, axis=0, keepdims=True)
    out_grad = norm_back(edge_normed, scale_kept[:, :1], gain, upstream).astype(BF16)
    pre_grad = (dot_nt(out_grad, w_out[...]) * slope_kept[...]).astype(BF16)
    pre_grad_out[...] = pre_grad
    sender_total = dot(sender_columns[...], pre_grad)
    receiver_total = dot(receiver_columns[...], pre_grad)
    own = sender_total[:count].astype(BF16)
    away = sender_total[count:].astype(BF16)
    received = receiver_total.astype(BF16)
    sender_out[...] = own
    receiver_out[...] = received
    halo_grad = dot_nt(away, w_in[width : 2 * width]).astype(BF16)
    parts = [halo_grad[k * slots : (k + 1) * slots] for k in range(8)]
    up_out[...] = jnp.concatenate([parts[0], parts[3], parts[5]], axis=0)
    down_out[...] = jnp.concatenate([parts[2], parts[4], parts[7]], axis=0)
    rest_out[...] = jnp.concatenate([parts[1], parts[6]], axis=0)
    edge_sums[:width] = dot_tn(edges[...], pre_grad)
    edge_sums[width : 2 * width] = dot_tn(x, own) + dot_tn(halo, away)
    edge_sums[2 * width : 3 * width] = dot_tn(x, received)
    edge_sums[3 * width : 4 * width] = dot_tn(hidden_kept[...], out_grad)
    split_by_core(edge_sums, 0, keep_out, away_out)
    split_by_core(node_sums, edge_sums.shape[0] // 2, keep_out, away_out)
    gains = pack_gains(edge_gain, node_gain)
    away_out[keep_out.shape[0] :] = gains
    gains_out[...] = gains


def pair_kernel(keep, gains, other, sums_out):
    rows = keep.shape[0]
    sums_out[:rows] = (keep[...] + other[:rows].astype(F32)).astype(BF16)
    both = gains[...].astype(F32) + other[rows:].astype(F32)
    sums_out[rows:] = pack_gains(both[0:1] + both[1:2], both[2:3] + both[3:4])


def place_kernel(parts, own, other, *refs):
    outs, sems = refs[:-1], refs[-1]
    chips = own.shape[0]
    core = lax.axis_index(CORE)

    def place(halves):
        copies = []

        def put(source, target):
            copies.append(pltpu.make_async_copy(source, target, sems.at[len(copies)]))
            copies[-1].start()

        for half, blocks in enumerate(halves):
            for chip in range(chips):
                at = 0
                for i, part in enumerate(parts):
                    step = part // chips
                    row = half * part + chip * step
                    cut = outs[2 * i].shape[0]
                    split = min(max(cut - row, 0), step)
                    if split > 0:
                        put(blocks.at[chip, at : at + split], outs[2 * i].at[row : row + split])
                    if split < step:
                        rest = row + split - cut
                        put(
                            blocks.at[chip, at + split : at + step],
                            outs[2 * i + 1].at[rest : rest + step - split],
                        )
                    at += step
        for copy in copies:
            copy.wait()

    @pl.when(core == 0)
    def _():
        place([own, other])

    @pl.when(core == 1)
    def _():
        place([other, own])


def finish_kernel(
    edge_grads, pre_grad, sender_sum, receiver_sum, node_part, w_in, edges_grad, local_grad
):
    width = w_in.shape[1]
    edges_grad[...] = (
        edge_grads[...].astype(F32) + dot_nt(pre_grad[...], w_in[:width])
    ).astype(BF16)
    local_grad[...] = (
        node_part[...]
        + dot_nt(sender_sum[...], w_in[width : 2 * width])
        + dot_nt(receiver_sum[...], w_in[2 * width :])
    )


def return_kernel(send_list, local_grad, up_back, down_back, to_high, to_low, nodes_grad):
    slots = send_list.shape[1]

    def block(ref, k):
        return ref[k * slots : (k + 1) * slots]

    returned = jnp.concatenate(
        [
            block(to_high, 0),
            block(to_high, 2),
            block(to_high, 1),
            block(up_back, 1),
            block(down_back, 1),
            block(to_low, 0),
            block(to_low, 2),
            block(to_low, 1),
        ],
        axis=0,
    )
    hot = list_hot(send_list[...], local_grad.shape[0])
    nodes_grad[...] = (local_grad[...] + dot_tn(hot, returned)).astype(BF16)


SMEM = pltpu.SMEM
VMEM = pltpu.VMEM
HBM = pltpu.HBM


def call(body, outs, flops, *operands, spaces=(), out_space=VMEM, scratch=()):
    moved = sum(x.size * x.dtype.itemsize for x in operands)
    moved += sum(x.size * jnp.dtype(x.dtype).itemsize for x in outs)
    spaces = list(spaces) + [VMEM] * (len(operands) - len(spaces))
    out_spaces = out_space if isinstance(out_space, list) else [out_space] * len(outs)
    operands = [
        pltpu.with_memory_space_constraint(x, HBM) if space is HBM else x
        for x, space in zip(operands, spaces)
    ]
    return pl.pallas_call(
        body,
        out_shape=outs,
        in_specs=[pl.BlockSpec(memory_space=space) for space in spaces],
        out_specs=[pl.BlockSpec(memory_space=space) for space in out_spaces],
        scratch_shapes=list(scratch),
        compiler_params=pltpu.CompilerParams(vmem_limit_bytes=VMEM_LIMIT),
        cost_estimate=pl.CostEstimate(flops=flops, bytes_accessed=moved, transcendentals=0),
    )(*operands)


def like(array):
    return jax.ShapeDtypeStruct(array.shape, array.dtype)


def shaped(rows, columns, dtype):
    return jax.ShapeDtypeStruct((rows, columns), dtype)


def placed(parts, own, other, width):
    chips = own.shape[0]
    outs = [
        shaped(3 * width, width, BF16),
        shaped(width, width, BF16),
        shaped(2 * width, width, BF16),
        shaped(width, width, BF16),
    ]
    steps = [part // chips for part in parts]
    cuts = [x.shape[0] for x in outs[::2]]
    if all(x % 16 == 0 for x in steps + cuts):
        return call(
            functools.partial(place_kernel, parts),
            outs,
            0,
            own,
            other,
            out_space=HBM,
            scratch=[pltpu.SemaphoreType.DMA((2 * len(parts) * chips + len(parts),))],
        )
    core = lax.axis_index(CORE)
    low = jnp.where(core == 0, own, other)
    high = jnp.where(core == 0, other, own)
    results = []
    at = 0
    for step, cut in zip(steps, cuts):
        whole = jnp.concatenate(
            [x[:, at : at + step].reshape(chips * step, width) for x in (low, high)]
        )
        results += [whole[:cut], whole[cut:]]
        at += step
    return results


def on_device(
    nodes,
    edges,
    edge_grads,
    node_grads,
    send_list,
    senders,
    receivers,
    tile_count,
    w_edge_in,
    w_edge_out,
    gain_edge,
    w_node_in,
    w_node_out,
    gain_node,
):
    count, width = nodes.shape
    slots = send_list.shape[1]
    halo_rows = 8 * slots
    edge_rows = edges.shape[0]
    tile_rows = senders.shape[1]
    square = 2 * width * width
    low, mid, high, nodes, send_list = call(
        send_kernel,
        [
            shaped(3 * slots, width, BF16),
            shaped(2 * slots, width, BF16),
            shaped(3 * slots, width, BF16),
            like(nodes),
            like(send_list),
        ],
        2 * halo_rows * count * width,
        nodes,
        send_list,
        spaces=[HBM, HBM],
        scratch=[pltpu.SemaphoreType.DMA((2,))],
    )
    from_low = passed_along(high, "px", 1)
    from_high = passed_along(low, "px", -1)
    fetched = [
        senders,
        receivers,
        edges,
        w_edge_in,
        w_edge_out,
        gain_edge,
        w_node_in,
        w_node_out,
        gain_node,
        node_grads,
        edge_grads,
    ]
    near_hot, halo_hot, *fetched = call(
        functools.partial(index_kernel, len(fetched)),
        [
            shaped(edge_rows, 2 * count, BF16),
            shaped(edge_rows, halo_rows, BF16),
        ]
        + [like(x) for x in fetched],
        0,
        *fetched,
        spaces=[HBM] * len(fetched),
        scratch=[pltpu.SemaphoreType.DMA((len(fetched),))],
    )
    (
        senders,
        receivers,
        edges,
        w_edge_in,
        w_edge_out,
        gain_edge,
        w_node_in,
        w_node_out,
        gain_node,
        node_grads,
        edge_grads,
    ) = fetched
    from_low, from_high, near_hot = lax.optimization_barrier((from_low, from_high, near_hot))
    upward = passed_along(
        jnp.concatenate([from_high[2 * slots :], mid[slots:], from_low[2 * slots :]]), PY, 1
    )
    downward = passed_along(
        jnp.concatenate([from_high[:slots], mid[:slots], from_low[:slots]]), PY, -1
    )
    pre_local, sender_columns, receiver_columns = call(
        local_kernel,
        [
            shaped(edge_rows, width, F32),
            shaped(count + halo_rows, edge_rows, BF16),
            shaped(count, edge_rows, BF16),
        ],
        square * (2 * count + edge_rows) + 4 * edge_rows * count * width,
        nodes,
        edges,
        senders,
        receivers,
        near_hot,
        w_edge_in,
    )
    parts = (2 * width, 3 * width // 2)
    halves = sum(parts)
    pre_grad, sender_sum, receiver_sum, node_part, up, down, rest, keep, away, gains = call(
        functools.partial(layer_kernel, tile_rows),
        [
            shaped(edge_rows, width, BF16),
            shaped(count, width, BF16),
            shaped(count, width, BF16),
            shaped(count, width, F32),
            shaped(3 * slots, width, BF16),
            shaped(3 * slots, width, BF16),
            shaped(2 * slots, width, BF16),
            shaped(halves, width, F32),
            shaped(halves + 16, width, BF16),
            shaped(16, width, BF16),
        ],
        square * (6 * edge_rows + 11 * count + 2 * halo_rows)
        + 2 * edge_rows * (4 * count + halo_rows) * width,
        tile_count,
        nodes,
        node_grads,
        edges,
        edge_grads,
        pre_local,
        halo_hot,
        near_hot,
        sender_columns,
        receiver_columns,
        from_high,
        from_low,
        upward,
        downward,
        w_edge_in,
        w_edge_out,
        gain_edge,
        w_node_in,
        w_node_out,
        gain_node,
        spaces=[SMEM],
        scratch=[
            pltpu.VMEM((edge_rows, width), F32),
            pltpu.VMEM((edge_rows, width), BF16),
            pltpu.VMEM((edge_rows, width), F32),
            pltpu.VMEM((edge_rows, 128), F32),
            pltpu.VMEM((3 * width, width), F32),
            pltpu.VMEM((4 * width, width), F32),
        ],
    )
    (sums,) = call(pair_kernel, [like(away)], 0, keep, gains, across_cores(away))
    sums = lax.psum(sums, CHIPS)
    gains = sums[halves:].astype(F32)
    own = sums[None, :halves]
    up_back = passed_along(up, PY, 1)
    down_back = passed_along(down, PY, -1)
    to_high = passed_along(
        jnp.concatenate([up_back[:slots], down_back[:slots], rest[:slots]]), "px", 1
    )
    to_low = passed_along(
        jnp.concatenate([up_back[2 * slots :], down_back[2 * slots :], rest[slots:]]), "px", -1
    )
    edges_grad, local_grad = call(
        finish_kernel,
        [shaped(edge_rows, width, BF16), shaped(count, width, F32)],
        square * (edge_rows + 2 * count),
        edge_grads,
        pre_grad,
        sender_sum,
        receiver_sum,
        node_part,
        w_edge_in,
    )
    (nodes_grad,) = call(
        return_kernel,
        [shaped(count, width, BF16)],
        2 * halo_rows * count * width,
        send_list,
        local_grad,
        up_back,
        down_back,
        to_high,
        to_low,
    )
    own, nodes_grad, edges_grad = lax.optimization_barrier((own, nodes_grad, edges_grad))
    w_edge_in_grad, w_edge_out_grad, w_node_in_grad, w_node_out_grad = placed(
        parts, own, across_cores(own), width
    )
    return (
        nodes_grad,
        edges_grad,
        w_edge_in_grad,
        w_edge_out_grad,
        (gains[0] + gains[1]).astype(BF16),
        w_node_in_grad,
        w_node_out_grad,
        (gains[2] + gains[3]).astype(BF16),
    )


def solution(mesh):
    in_specs = (
        P(("groups", "px") + PY, None),
        P(("groups", "px") + PY, None),
        P(("groups", "px") + PY, None),
        P(("groups", "px") + PY, None),
        P(("groups", "px") + PY, None),
        P(("groups", "px") + PY, None),
        P(("groups", "px") + PY, None),
        P(("groups", "px") + PY),
        P(),
        P(),
        P(),
        P(),
        P(),
        P(),
    )
    out_specs = (
        P(("groups", "px") + PY, None),
        P(("groups", "px") + PY, None),
        P("groups", None),
        P("groups", None),
        P("groups"),
        P("groups", None),
        P("groups", None),
        P("groups"),
    )
    groups, px, py = mesh.devices.shape
    by_core = jax.sharding.Mesh(
        mesh.devices.reshape(groups, px, py // 2, 2), ("groups", "px") + PY
    )
    return jax.shard_map(
        on_device, mesh=by_core, in_specs=in_specs, out_specs=out_specs, check_vma=False
    )
```

```python
import functools

import jax
import jax.numpy as jnp
from jax import lax
from jax.experimental import pallas as pl
from jax.experimental.pallas import tpu as pltpu
from jax.sharding import PartitionSpec as P

EPS = 1e-05
BF16 = jnp.bfloat16
F32 = jnp.float32
VMEM_LIMIT = 24 * 1024 * 1024


CORE = "core"
FAR = "far"
PX = (FAR, "near")
PY = ("side", CORE)
SQUARE = ("near", "side")


def passed_along(array, axis, by):
    size = lax.axis_size(axis)
    return lax.ppermute(array, axis, [(i, (i + by) % size) for i in range(size)])


def across_cores(array):
    return lax.ppermute(array, CORE, [(0, 1), (1, 0)])


def dot(left, right):
    return jnp.dot(left, right, preferred_element_type=F32)


def dot_tn(left, right):
    return lax.dot_general(left, right, (((0,), (0,)), ((), ())), preferred_element_type=F32)


def dot_nt(left, right):
    return lax.dot_general(left, right, (((1,), (1,)), ((), ())), preferred_element_type=F32)


def sigmoid(value):
    return 0.5 + 0.5 * jnp.tanh(0.5 * value)


def normalize(value):
    centered = value - jnp.mean(value, axis=-1, keepdims=True)
    scale_inv = lax.rsqrt(jnp.mean(centered * centered, axis=-1, keepdims=True) + EPS)
    return centered * scale_inv, scale_inv


def norm_back(normed, scale_inv, gain, upstream):
    scaled = upstream * gain
    inner = (
        scaled
        - jnp.mean(scaled, axis=-1, keepdims=True)
        - normed * jnp.mean(scaled * normed, axis=-1, keepdims=True)
    )
    return inner * scale_inv


def columns_of(ids):
    rows, lanes = ids.shape
    padded = -(-rows // 8) * 8
    if padded > rows:
        ids = jnp.concatenate([ids, jnp.zeros((padded - rows, lanes), ids.dtype)], axis=0)
    return ids.T


def hot_rows(columns, tiles, base, count):
    parts = []
    for tile in tiles:
        column = columns[:, tile : tile + 1] - base
        lanes = lax.broadcasted_iota(jnp.int32, (columns.shape[0], count), 1)
        parts.append(jnp.where(lanes == column, 1.0, 0.0).astype(BF16))
    return jnp.concatenate(parts, axis=0) if len(parts) > 1 else parts[0]


def hot_columns(ids, tiles, base, count):
    parts = []
    for tile in tiles:
        row = ids[tile : tile + 1, :] - base
        subs = lax.broadcasted_iota(jnp.int32, (count, ids.shape[1]), 0)
        parts.append(jnp.where(subs == row, 1.0, 0.0).astype(BF16))
    return jnp.concatenate(parts, axis=1) if len(parts) > 1 else parts[0]


def list_hot(ids, count):
    directions, slots = ids.shape
    wide = jnp.concatenate([ids, jnp.zeros((directions, 128 - slots), ids.dtype)], axis=1)
    columns = wide.T
    parts = []
    for k in range(directions):
        lanes = lax.broadcasted_iota(jnp.int32, (slots, count), 1)
        parts.append(jnp.where(lanes == columns[:slots, k : k + 1], 1.0, 0.0).astype(BF16))
    return jnp.concatenate(parts, axis=0)


def live_rows(count_ref, tile_rows, rows):
    index = lax.broadcasted_iota(jnp.int32, (rows, 1), 0)
    return jnp.where(index < count_ref[0] * tile_rows, 1.0, 0.0)


def fetch_all(sources, targets, sems):
    copies = [
        pltpu.make_async_copy(source, target, sems.at[i])
        for i, (source, target) in enumerate(zip(sources, targets))
    ]
    for copy in copies:
        copy.start()
    return copies


def send_kernel(nodes_hbm, list_hbm, low, mid, high, nodes, send_list, sems):
    slots = send_list.shape[1]
    for copy in fetch_all([list_hbm, nodes_hbm], [send_list, nodes], sems):
        copy.wait()
    rows = dot(list_hot(send_list[...], nodes.shape[0]), nodes[...]).astype(BF16)
    low[...] = rows[: 3 * slots]
    mid[...] = rows[3 * slots : 5 * slots]
    high[...] = rows[5 * slots :]


def index_kernel(sources, *refs):
    fetched, refs = refs[:sources], refs[sources:]
    near_rows, halo_rows = refs[:2]
    targets, sems = refs[2:-1], refs[-1]
    senders, receivers = targets[:2]
    copies = fetch_all(fetched, targets, sems)
    for copy in copies[:2]:
        copy.wait()
    tile_rows = senders.shape[1]
    count = near_rows.shape[1] // 2
    by_sender = columns_of(senders[...])
    by_receiver = columns_of(receivers[...])
    for tile in range(senders.shape[0]):
        rows = slice(tile * tile_rows, (tile + 1) * tile_rows)
        near_rows[rows, :count] = hot_rows(by_sender, [tile], 0, count)
        near_rows[rows, count:] = hot_rows(by_receiver, [tile], 0, count)
        halo_rows[rows, :] = hot_rows(by_sender, [tile], count, halo_rows.shape[1])
    for copy in copies[2:]:
        copy.wait()


def local_kernel(
    nodes, edges, senders, receivers, near_rows, w_in, pre, sender_columns, receiver_columns
):
    width = nodes.shape[1]
    tile_rows = senders.shape[1]
    extended = sender_columns.shape[0]
    count = receiver_columns.shape[0]
    sender_ids = senders[...]
    receiver_ids = receivers[...]
    for tile in range(senders.shape[0]):
        rows = slice(tile * tile_rows, (tile + 1) * tile_rows)
        sender_columns[:, rows] = hot_columns(sender_ids, [tile], 0, extended)
        receiver_columns[:, rows] = hot_columns(receiver_ids, [tile], 0, count)
    x = nodes[...]
    table = jnp.concatenate(
        [
            dot(x, w_in[width : 2 * width]).astype(BF16),
            dot(x, w_in[2 * width :]).astype(BF16),
        ],
        axis=0,
    )
    pre[...] = dot(edges[...], w_in[:width]) + dot(near_rows[...], table)


def split_by_core(sums, first, keep_out, away_out):
    half = sums.shape[0] // 2
    core = lax.axis_index(CORE)
    keep_out[first : first + half] = sums[pl.ds(pl.multiple_of(core * half, half), half), :]
    away = sums[pl.ds(pl.multiple_of((1 - core) * half, half), half), :]
    away_out[first : first + half] = away.astype(BF16)


def pack_gains(edge_gain, node_gain):
    edge_high = edge_gain.astype(BF16).astype(F32)
    node_high = node_gain.astype(BF16).astype(F32)
    row = lax.broadcasted_iota(jnp.int32, (16, edge_gain.shape[1]), 0)
    packed = jnp.where(row == 0, edge_high, 0.0)
    packed = jnp.where(row == 1, edge_gain - edge_high, packed)
    packed = jnp.where(row == 2, node_high, packed)
    packed = jnp.where(row == 3, node_gain - node_high, packed)
    return packed.astype(BF16)


def layer_kernel(
    tile_rows,
    count_ref,
    nodes,
    node_grads,
    edges,
    edge_grads,
    pre_local,
    halo_rows,
    near_rows,
    sender_columns,
    receiver_columns,
    from_high,
    from_low,
    upward,
    downward,
    w_in,
    w_out,
    gain_edge,
    w_node_in,
    w_node_out,
    gain_node,
    pre_grad_out,
    sender_out,
    receiver_out,
    node_part_out,
    up_out,
    down_out,
    rest_out,
    keep_out,
    away_out,
    gains_out,
    slope_kept,
    hidden_kept,
    normed_kept,
    scale_kept,
    node_sums,
    edge_sums,
):
    count, width = nodes.shape
    edge_rows = edges.shape[0]
    live = live_rows(count_ref, tile_rows, edge_rows)
    slots = from_high.shape[0] // 3
    halo = jnp.concatenate(
        [
            downward[:slots],
            from_high[slots : 2 * slots],
            upward[:slots],
            downward[slots : 2 * slots],
            upward[slots : 2 * slots],
            downward[2 * slots :],
            from_low[slots : 2 * slots],
            upward[2 * slots :],
        ],
        axis=0,
    )
    table = dot(halo, w_in[width : 2 * width]).astype(BF16)
    gain = gain_edge[...].astype(F32)[None, :]
    value = pre_local[...] + dot(halo_rows[...], table)
    sigma = sigmoid(value)
    hidden = (value * sigma).astype(BF16)
    hidden_kept[...] = hidden
    slope_kept[...] = sigma * (1.0 + value * (1.0 - sigma))
    edge_normed, edge_scale = normalize(dot(hidden, w_out[...]))
    normed_kept[...] = edge_normed
    scale_kept[...] = jnp.broadcast_to(edge_scale, (edge_rows, 128))
    message = (live * gain * edge_normed).astype(BF16)
    total = dot(receiver_columns[...], message)
    aggregated = total.astype(BF16)
    x = nodes[...]
    w_first = w_node_in[:width]
    w_second = w_node_in[width:]
    node_pre = dot(x, w_first) + dot(aggregated, w_second)
    sigma = sigmoid(node_pre)
    node_hidden = (node_pre * sigma).astype(BF16)
    normed, scale_inv = normalize(dot(node_hidden, w_node_out[...]))
    upstream = node_grads[...].astype(F32)
    out_grad = norm_back(normed, scale_inv, gain_node[...].astype(F32)[None, :], upstream).astype(BF16)
    slope = sigma * (1.0 + node_pre * (1.0 - sigma))
    pre_grad = (dot_nt(out_grad, w_node_out[...]) * slope).astype(BF16)
    agg_grad = dot_nt(pre_grad, w_second).astype(BF16)
    node_part_out[...] = upstream + dot_nt(pre_grad, w_first)
    node_sums[:width] = dot_tn(x, pre_grad)
    node_sums[width : 2 * width] = dot_tn(aggregated, pre_grad)
    node_sums[2 * width : 3 * width] = dot_tn(node_hidden, out_grad)
    node_gain = jnp.sum(upstream * normed, axis=0, keepdims=True)
    upstream = live * (
        edge_grads[...].astype(F32) + dot(near_rows[:, count:], agg_grad)
    )
    edge_normed = normed_kept[...]
    edge_gain = jnp.sum(upstream * edge_normed, axis=0, keepdims=True)
    out_grad = norm_back(edge_normed, scale_kept[:, :1], gain, upstream).astype(BF16)
    pre_grad = (dot_nt(out_grad, w_out[...]) * slope_kept[...]).astype(BF16)
    pre_grad_out[...] = pre_grad
    sender_total = dot(sender_columns[...], pre_grad)
    receiver_total = dot(receiver_columns[...], pre_grad)
    own = sender_total[:count].astype(BF16)
    away = sender_total[count:].astype(BF16)
    received = receiver_total.astype(BF16)
    sender_out[...] = own
    receiver_out[...] = received
    halo_grad = dot_nt(away, w_in[width : 2 * width]).astype(BF16)
    parts = [halo_grad[k * slots : (k + 1) * slots] for k in range(8)]
    up_out[...] = jnp.concatenate([parts[0], parts[3], parts[5]], axis=0)
    down_out[...] = jnp.concatenate([parts[2], parts[4], parts[7]], axis=0)
    rest_out[...] = jnp.concatenate([parts[1], parts[6]], axis=0)
    edge_sums[:width] = dot_tn(edges[...], pre_grad)
    edge_sums[width : 2 * width] = dot_tn(x, own) + dot_tn(halo, away)
    edge_sums[2 * width : 3 * width] = dot_tn(x, received)
    edge_sums[3 * width : 4 * width] = dot_tn(hidden_kept[...], out_grad)
    split_by_core(edge_sums, 0, keep_out, away_out)
    split_by_core(node_sums, edge_sums.shape[0] // 2, keep_out, away_out)
    gains = pack_gains(edge_gain, node_gain)
    away_out[keep_out.shape[0] :] = gains
    gains_out[...] = gains


def pair_kernel(parts, keep, gains, other, blocks_out, total, staged, sems):
    rows = keep.shape[0]
    chips = blocks_out.shape[0]
    packed = gains.shape[0]
    both = gains[...].astype(F32) + other[rows:].astype(F32)
    summed = pack_gains(both[0:1] + both[1:2], both[2:3] + both[3:4])
    total[...] = (keep[...] + other[:rows].astype(F32)).astype(BF16)
    copies = []
    for chip in range(chips):
        staged[chip, :packed, :] = summed
        first, at = 0, packed
        for part in parts:
            step = part // chips
            staged[chip, at : at + step, :] = total[first + chip * step : first + (chip + 1) * step]
            first, at = first + part, at + step
        copies.append(
            pltpu.make_async_copy(staged.at[chip], blocks_out.at[chip], sems.at[chip])
        )
        copies[-1].start()
    for copy in copies:
        copy.wait()


def add_packed(values):
    packed = 16
    gains = values[:packed]
    return pack_gains(gains[0:1] + gains[1:2], gains[2:3] + gains[3:4])


def sum_kernel(received, sums_out):
    sums = received[0].astype(F32)
    for chip in range(1, received.shape[0]):
        sums = sums + received[chip].astype(F32)
    sums_out[...] = sums.astype(BF16)
    sums_out[:16] = add_packed(sums)


def join_kernel(own, other, sums_out):
    sums = own[...].astype(F32) + other[...].astype(F32)
    sums_out[...] = sums.astype(BF16)
    sums_out[:16] = add_packed(sums)


def spread_kernel(own, other, gains_out, spread_out, mine, sems):
    packed = gains_out.shape[0]
    sums = own[...].astype(F32) + other[...].astype(F32)
    mine[...] = sums[packed:].astype(BF16)
    copies = [
        pltpu.make_async_copy(mine, spread_out.at[chip], sems.at[chip])
        for chip in range(spread_out.shape[0])
    ]
    for copy in copies:
        copy.start()
    gains_out[...] = sums[:packed]
    for copy in copies:
        copy.wait()


def place_kernel(parts, own, other, *refs):
    outs, sems = refs[:-1], refs[-1]
    chips = own.shape[0]
    core = lax.axis_index(CORE)

    def place(halves):
        copies = []

        def put(source, target):
            copies.append(pltpu.make_async_copy(source, target, sems.at[len(copies)]))
            copies[-1].start()

        for half, blocks in enumerate(halves):
            for chip in range(chips):
                at = 0
                for i, part in enumerate(parts):
                    step = part // chips
                    row = half * part + chip * step
                    cut = outs[2 * i].shape[0]
                    split = min(max(cut - row, 0), step)
                    if split > 0:
                        put(blocks.at[chip, at : at + split], outs[2 * i].at[row : row + split])
                    if split < step:
                        rest = row + split - cut
                        put(
                            blocks.at[chip, at + split : at + step],
                            outs[2 * i + 1].at[rest : rest + step - split],
                        )
                    at += step
        for copy in copies:
            copy.wait()

    @pl.when(core == 0)
    def _():
        place([own, other])

    @pl.when(core == 1)
    def _():
        place([other, own])


def finish_kernel(
    edge_grads, pre_grad, sender_sum, receiver_sum, node_part, w_in, edges_grad, local_grad
):
    width = w_in.shape[1]
    edges_grad[...] = (
        edge_grads[...].astype(F32) + dot_nt(pre_grad[...], w_in[:width])
    ).astype(BF16)
    local_grad[...] = (
        node_part[...]
        + dot_nt(sender_sum[...], w_in[width : 2 * width])
        + dot_nt(receiver_sum[...], w_in[2 * width :])
    )


def return_kernel(send_list, local_grad, up_back, down_back, to_high, to_low, nodes_grad):
    slots = send_list.shape[1]

    def block(ref, k):
        return ref[k * slots : (k + 1) * slots]

    returned = jnp.concatenate(
        [
            block(to_high, 0),
            block(to_high, 2),
            block(to_high, 1),
            block(up_back, 1),
            block(down_back, 1),
            block(to_low, 0),
            block(to_low, 2),
            block(to_low, 1),
        ],
        axis=0,
    )
    hot = list_hot(send_list[...], local_grad.shape[0])
    nodes_grad[...] = (local_grad[...] + dot_tn(hot, returned)).astype(BF16)


SMEM = pltpu.SMEM
VMEM = pltpu.VMEM
HBM = pltpu.HBM


def call(body, outs, flops, *operands, spaces=(), out_space=VMEM, scratch=()):
    moved = sum(x.size * x.dtype.itemsize for x in operands)
    moved += sum(x.size * jnp.dtype(x.dtype).itemsize for x in outs)
    spaces = list(spaces) + [VMEM] * (len(operands) - len(spaces))
    out_spaces = out_space if isinstance(out_space, list) else [out_space] * len(outs)
    operands = [
        pltpu.with_memory_space_constraint(x, HBM) if space is HBM else x
        for x, space in zip(operands, spaces)
    ]
    return pl.pallas_call(
        body,
        out_shape=outs,
        in_specs=[pl.BlockSpec(memory_space=space) for space in spaces],
        out_specs=[pl.BlockSpec(memory_space=space) for space in out_spaces],
        scratch_shapes=list(scratch),
        compiler_params=pltpu.CompilerParams(vmem_limit_bytes=VMEM_LIMIT),
        cost_estimate=pl.CostEstimate(flops=flops, bytes_accessed=moved, transcendentals=0),
    )(*operands)


def like(array):
    return jax.ShapeDtypeStruct(array.shape, array.dtype)


def shaped(rows, columns, dtype):
    return jax.ShapeDtypeStruct((rows, columns), dtype)


def placed(parts, own, other, width):
    chips = own.shape[0]
    outs = [
        shaped(3 * width, width, BF16),
        shaped(width, width, BF16),
        shaped(2 * width, width, BF16),
        shaped(width, width, BF16),
    ]
    return call(
        functools.partial(place_kernel, parts),
        outs,
        0,
        own,
        other,
        out_space=HBM,
        scratch=[pltpu.SemaphoreType.DMA((2 * len(parts) * chips + len(parts),))],
    )


def spread_of(received, packed):
    chips, rows, width = received.shape
    (sums,) = call(sum_kernel, [shaped(rows, width, BF16)], 0, received)
    size = lax.axis_size(FAR)
    distance = 1
    while True:
        other = lax.ppermute(sums, FAR, [(i, i ^ distance) for i in range(size)])
        distance *= 2
        if distance == size:
            break
        (sums,) = call(join_kernel, [like(sums)], 0, sums, other)
    mine = rows - packed
    return call(
        spread_kernel,
        [shaped(packed, width, F32), jax.ShapeDtypeStruct((chips, mine, width), BF16)],
        0,
        sums,
        other,
        out_space=[VMEM, HBM],
        scratch=[pltpu.VMEM((mine, width), BF16), pltpu.SemaphoreType.DMA((chips,))],
    )


def blocks_of(parts, keep, gains, other):
    chips = lax.axis_size(SQUARE)
    rows, width = keep.shape
    shape = (chips, gains.shape[0] + rows // chips, width)
    (blocks,) = call(
        functools.partial(pair_kernel, parts),
        [jax.ShapeDtypeStruct(shape, BF16)],
        0,
        keep,
        gains,
        other,
        out_space=HBM,
        scratch=[
            pltpu.VMEM((rows, width), BF16),
            pltpu.VMEM(shape, BF16),
            pltpu.SemaphoreType.DMA((chips,)),
        ],
    )
    return blocks


def on_device(
    nodes,
    edges,
    edge_grads,
    node_grads,
    send_list,
    senders,
    receivers,
    tile_count,
    w_edge_in,
    w_edge_out,
    gain_edge,
    w_node_in,
    w_node_out,
    gain_node,
):
    count, width = nodes.shape
    slots = send_list.shape[1]
    halo_rows = 8 * slots
    edge_rows = edges.shape[0]
    tile_rows = senders.shape[1]
    square = 2 * width * width
    low, mid, high, nodes, send_list = call(
        send_kernel,
        [
            shaped(3 * slots, width, BF16),
            shaped(2 * slots, width, BF16),
            shaped(3 * slots, width, BF16),
            like(nodes),
            like(send_list),
        ],
        2 * halo_rows * count * width,
        nodes,
        send_list,
        spaces=[HBM, HBM],
        scratch=[pltpu.SemaphoreType.DMA((2,))],
    )
    from_low = passed_along(high, PX, 1)
    from_high = passed_along(low, PX, -1)
    fetched = [
        senders,
        receivers,
        edges,
        w_edge_in,
        w_edge_out,
        gain_edge,
        w_node_in,
        w_node_out,
        gain_node,
        node_grads,
        edge_grads,
    ]
    near_hot, halo_hot, *fetched = call(
        functools.partial(index_kernel, len(fetched)),
        [
            shaped(edge_rows, 2 * count, BF16),
            shaped(edge_rows, halo_rows, BF16),
        ]
        + [like(x) for x in fetched],
        0,
        *fetched,
        spaces=[HBM] * len(fetched),
        scratch=[pltpu.SemaphoreType.DMA((len(fetched),))],
    )
    (
        senders,
        receivers,
        edges,
        w_edge_in,
        w_edge_out,
        gain_edge,
        w_node_in,
        w_node_out,
        gain_node,
        node_grads,
        edge_grads,
    ) = fetched
    from_low, from_high, near_hot = lax.optimization_barrier((from_low, from_high, near_hot))
    upward = passed_along(
        jnp.concatenate([from_high[2 * slots :], mid[slots:], from_low[2 * slots :]]), PY, 1
    )
    downward = passed_along(
        jnp.concatenate([from_high[:slots], mid[:slots], from_low[:slots]]), PY, -1
    )
    pre_local, sender_columns, receiver_columns = call(
        local_kernel,
        [
            shaped(edge_rows, width, F32),
            shaped(count + halo_rows, edge_rows, BF16),
            shaped(count, edge_rows, BF16),
        ],
        square * (2 * count + edge_rows) + 4 * edge_rows * count * width,
        nodes,
        edges,
        senders,
        receivers,
        near_hot,
        w_edge_in,
    )
    parts = (2 * width, 3 * width // 2)
    halves = sum(parts)
    pre_grad, sender_sum, receiver_sum, node_part, up, down, rest, keep, away, gains = call(
        functools.partial(layer_kernel, tile_rows),
        [
            shaped(edge_rows, width, BF16),
            shaped(count, width, BF16),
            shaped(count, width, BF16),
            shaped(count, width, F32),
            shaped(3 * slots, width, BF16),
            shaped(3 * slots, width, BF16),
            shaped(2 * slots, width, BF16),
            shaped(halves, width, F32),
            shaped(halves + 16, width, BF16),
            shaped(16, width, BF16),
        ],
        square * (6 * edge_rows + 11 * count + 2 * halo_rows)
        + 2 * edge_rows * (4 * count + halo_rows) * width,
        tile_count,
        nodes,
        node_grads,
        edges,
        edge_grads,
        pre_local,
        halo_hot,
        near_hot,
        sender_columns,
        receiver_columns,
        from_high,
        from_low,
        upward,
        downward,
        w_edge_in,
        w_edge_out,
        gain_edge,
        w_node_in,
        w_node_out,
        gain_node,
        spaces=[SMEM],
        scratch=[
            pltpu.VMEM((edge_rows, width), F32),
            pltpu.VMEM((edge_rows, width), BF16),
            pltpu.VMEM((edge_rows, width), F32),
            pltpu.VMEM((edge_rows, 128), F32),
            pltpu.VMEM((3 * width, width), F32),
            pltpu.VMEM((4 * width, width), F32),
        ],
    )
    blocks = blocks_of(parts, keep, gains, across_cores(away))
    received = lax.all_to_all(blocks, SQUARE, 0, 0)
    up_back = passed_along(up, PY, 1)
    down_back = passed_along(down, PY, -1)
    received, up_back, down_back = lax.optimization_barrier((received, up_back, down_back))
    to_high = passed_along(
        jnp.concatenate([up_back[:slots], down_back[:slots], rest[:slots]]), PX, 1
    )
    to_low = passed_along(
        jnp.concatenate([up_back[2 * slots :], down_back[2 * slots :], rest[slots:]]), PX, -1
    )
    gains, spread = spread_of(received, gains.shape[0])
    own = lax.all_to_all(spread, SQUARE, 0, 0)
    edges_grad, local_grad = call(
        finish_kernel,
        [shaped(edge_rows, width, BF16), shaped(count, width, F32)],
        square * (edge_rows + 2 * count),
        edge_grads,
        pre_grad,
        sender_sum,
        receiver_sum,
        node_part,
        w_edge_in,
    )
    (nodes_grad,) = call(
        return_kernel,
        [shaped(count, width, BF16)],
        2 * halo_rows * count * width,
        send_list,
        local_grad,
        up_back,
        down_back,
        to_high,
        to_low,
    )
    own, nodes_grad, edges_grad = lax.optimization_barrier((own, nodes_grad, edges_grad))
    w_edge_in_grad, w_edge_out_grad, w_node_in_grad, w_node_out_grad = placed(
        parts, own, across_cores(own), width
    )
    return (
        nodes_grad,
        edges_grad,
        w_edge_in_grad,
        w_edge_out_grad,
        (gains[0] + gains[1]).astype(BF16),
        w_node_in_grad,
        w_node_out_grad,
        (gains[2] + gains[3]).astype(BF16),
    )


def solution(mesh):
    in_specs = (
        P(("groups",) + PX + PY, None),
        P(("groups",) + PX + PY, None),
        P(("groups",) + PX + PY, None),
        P(("groups",) + PX + PY, None),
        P(("groups",) + PX + PY, None),
        P(("groups",) + PX + PY, None),
        P(("groups",) + PX + PY, None),
        P(("groups",) + PX + PY),
        P(),
        P(),
        P(),
        P(),
        P(),
        P(),
    )
    out_specs = (
        P(("groups",) + PX + PY, None),
        P(("groups",) + PX + PY, None),
        P("groups", None),
        P("groups", None),
        P("groups"),
        P("groups", None),
        P("groups", None),
        P("groups"),
    )
    groups, px, py = mesh.devices.shape
    by_core = jax.sharding.Mesh(
        mesh.devices.reshape(groups, px // 2, 2, py // 2, 2), ("groups",) + PX + PY
    )
    return jax.shard_map(
        on_device, mesh=by_core, in_specs=in_specs, out_specs=out_specs, check_vma=False
    )
```

```python
import functools

import jax
import jax.numpy as jnp
from jax import lax
from jax.experimental import pallas as pl
from jax.experimental.pallas import tpu as pltpu
from jax.sharding import PartitionSpec as P

EPS = 1e-05
BF16 = jnp.bfloat16
F32 = jnp.float32
VMEM_LIMIT = 24 * 1024 * 1024


CORE = "core"
FAR = "far"
PX = (FAR, "near")
PY = ("side", CORE)
SQUARE = ("near", "side")


def passed_along(array, axis, by):
    size = lax.axis_size(axis)
    return lax.ppermute(array, axis, [(i, (i + by) % size) for i in range(size)])


def across_chips(array):
    size = lax.axis_size(PY)
    pairs = [(i, (i + 1 if i % 2 else i - 1) % size) for i in range(size)]
    return lax.ppermute(array, PY, pairs)


def across_cores(array):
    return lax.ppermute(array, CORE, [(0, 1), (1, 0)])


def dot(left, right):
    return jnp.dot(left, right, preferred_element_type=F32)


def dot_tn(left, right):
    return lax.dot_general(left, right, (((0,), (0,)), ((), ())), preferred_element_type=F32)


def dot_nt(left, right):
    return lax.dot_general(left, right, (((1,), (1,)), ((), ())), preferred_element_type=F32)


def sigmoid(value):
    return 0.5 + 0.5 * jnp.tanh(0.5 * value)


def normalize(value):
    centered = value - jnp.mean(value, axis=-1, keepdims=True)
    scale_inv = lax.rsqrt(jnp.mean(centered * centered, axis=-1, keepdims=True) + EPS)
    return centered * scale_inv, scale_inv


def norm_back(normed, scale_inv, gain, upstream):
    scaled = upstream * gain
    inner = (
        scaled
        - jnp.mean(scaled, axis=-1, keepdims=True)
        - normed * jnp.mean(scaled * normed, axis=-1, keepdims=True)
    )
    return inner * scale_inv


def columns_of(ids):
    rows, lanes = ids.shape
    padded = -(-rows // 8) * 8
    if padded > rows:
        ids = jnp.concatenate([ids, jnp.zeros((padded - rows, lanes), ids.dtype)], axis=0)
    return ids.T


def hot_rows(columns, tiles, base, count):
    parts = []
    for tile in tiles:
        column = columns[:, tile : tile + 1] - base
        lanes = lax.broadcasted_iota(jnp.int32, (columns.shape[0], count), 1)
        parts.append(jnp.where(lanes == column, 1.0, 0.0).astype(BF16))
    return jnp.concatenate(parts, axis=0) if len(parts) > 1 else parts[0]


def hot_columns(ids, tiles, base, count):
    parts = []
    for tile in tiles:
        row = ids[tile : tile + 1, :] - base
        subs = lax.broadcasted_iota(jnp.int32, (count, ids.shape[1]), 0)
        parts.append(jnp.where(subs == row, 1.0, 0.0).astype(BF16))
    return jnp.concatenate(parts, axis=1) if len(parts) > 1 else parts[0]


def list_hot(ids, count):
    directions, slots = ids.shape
    wide = jnp.concatenate([ids, jnp.zeros((directions, 128 - slots), ids.dtype)], axis=1)
    columns = wide.T
    parts = []
    for k in range(directions):
        lanes = lax.broadcasted_iota(jnp.int32, (slots, count), 1)
        parts.append(jnp.where(lanes == columns[:slots, k : k + 1], 1.0, 0.0).astype(BF16))
    return jnp.concatenate(parts, axis=0)


def live_rows(count_ref, tile_rows, rows):
    index = lax.broadcasted_iota(jnp.int32, (rows, 1), 0)
    return jnp.where(index < count_ref[0] * tile_rows, 1.0, 0.0)


def fetch_all(sources, targets, sems):
    copies = [
        pltpu.make_async_copy(source, target, sems.at[i])
        for i, (source, target) in enumerate(zip(sources, targets))
    ]
    for copy in copies:
        copy.start()
    return copies


def send_kernel(nodes_hbm, list_hbm, low, mid, high, nodes, send_list, sems):
    slots = send_list.shape[1]
    for copy in fetch_all([list_hbm, nodes_hbm], [send_list, nodes], sems):
        copy.wait()
    rows = dot(list_hot(send_list[...], nodes.shape[0]), nodes[...]).astype(BF16)
    low[...] = rows[: 3 * slots]
    mid[...] = rows[3 * slots : 5 * slots]
    high[...] = rows[5 * slots :]


def index_kernel(sources, *refs):
    fetched, refs = refs[:sources], refs[sources:]
    near_rows, halo_rows = refs[:2]
    targets, sems = refs[2:-1], refs[-1]
    senders, receivers = targets[:2]
    copies = fetch_all(fetched, targets, sems)
    for copy in copies[:2]:
        copy.wait()
    tile_rows = senders.shape[1]
    count = near_rows.shape[1] // 2
    by_sender = columns_of(senders[...])
    by_receiver = columns_of(receivers[...])
    for tile in range(senders.shape[0]):
        rows = slice(tile * tile_rows, (tile + 1) * tile_rows)
        near_rows[rows, :count] = hot_rows(by_sender, [tile], 0, count)
        near_rows[rows, count:] = hot_rows(by_receiver, [tile], 0, count)
        halo_rows[rows, :] = hot_rows(by_sender, [tile], count, halo_rows.shape[1])
    for copy in copies[2:]:
        copy.wait()


def local_kernel(
    nodes, edges, senders, receivers, near_rows, w_in, pre, sender_columns, receiver_columns
):
    width = nodes.shape[1]
    tile_rows = senders.shape[1]
    extended = sender_columns.shape[0]
    count = receiver_columns.shape[0]
    sender_ids = senders[...]
    receiver_ids = receivers[...]
    for tile in range(senders.shape[0]):
        rows = slice(tile * tile_rows, (tile + 1) * tile_rows)
        sender_columns[:, rows] = hot_columns(sender_ids, [tile], 0, extended)
        receiver_columns[:, rows] = hot_columns(receiver_ids, [tile], 0, count)
    x = nodes[...]
    table = jnp.concatenate(
        [
            dot(x, w_in[width : 2 * width]).astype(BF16),
            dot(x, w_in[2 * width :]).astype(BF16),
        ],
        axis=0,
    )
    pre[...] = dot(edges[...], w_in[:width]) + dot(near_rows[...], table)


def split_by_core(sums, first, keep_out, away_out):
    half = sums.shape[0] // 2
    core = lax.axis_index(CORE)
    keep_out[first : first + half] = sums[pl.ds(pl.multiple_of(core * half, half), half), :]
    away = sums[pl.ds(pl.multiple_of((1 - core) * half, half), half), :]
    away_out[first : first + half] = away.astype(BF16)


def pack_gains(edge_gain, node_gain):
    edge_high = edge_gain.astype(BF16).astype(F32)
    node_high = node_gain.astype(BF16).astype(F32)
    row = lax.broadcasted_iota(jnp.int32, (16, edge_gain.shape[1]), 0)
    packed = jnp.where(row == 0, edge_high, 0.0)
    packed = jnp.where(row == 1, edge_gain - edge_high, packed)
    packed = jnp.where(row == 2, node_high, packed)
    packed = jnp.where(row == 3, node_gain - node_high, packed)
    return packed.astype(BF16)


def layer_kernel(
    tile_rows,
    count_ref,
    nodes,
    node_grads,
    edges,
    edge_grads,
    pre_local,
    halo_rows,
    near_rows,
    sender_columns,
    receiver_columns,
    from_high,
    from_low,
    upward,
    downward,
    w_in,
    w_out,
    gain_edge,
    w_node_in,
    w_node_out,
    gain_node,
    pre_grad_out,
    sender_out,
    receiver_out,
    node_part_out,
    across_out,
    rest_out,
    keep_out,
    away_out,
    gains_out,
    slope_kept,
    hidden_kept,
    normed_kept,
    scale_kept,
    node_sums,
    edge_sums,
):
    count, width = nodes.shape
    edge_rows = edges.shape[0]
    live = live_rows(count_ref, tile_rows, edge_rows)
    slots = from_high.shape[0] // 3
    halo = jnp.concatenate(
        [
            downward[:slots],
            from_high[slots : 2 * slots],
            upward[:slots],
            downward[slots : 2 * slots],
            upward[slots : 2 * slots],
            downward[2 * slots :],
            from_low[slots : 2 * slots],
            upward[2 * slots :],
        ],
        axis=0,
    )
    table = dot(halo, w_in[width : 2 * width]).astype(BF16)
    gain = gain_edge[...].astype(F32)[None, :]
    value = pre_local[...] + dot(halo_rows[...], table)
    sigma = sigmoid(value)
    hidden = (value * sigma).astype(BF16)
    hidden_kept[...] = hidden
    slope_kept[...] = sigma * (1.0 + value * (1.0 - sigma))
    edge_normed, edge_scale = normalize(dot(hidden, w_out[...]))
    normed_kept[...] = edge_normed
    scale_kept[...] = jnp.broadcast_to(edge_scale, (edge_rows, 128))
    message = (live * gain * edge_normed).astype(BF16)
    total = dot(receiver_columns[...], message)
    aggregated = total.astype(BF16)
    x = nodes[...]
    w_first = w_node_in[:width]
    w_second = w_node_in[width:]
    node_pre = dot(x, w_first) + dot(aggregated, w_second)
    sigma = sigmoid(node_pre)
    node_hidden = (node_pre * sigma).astype(BF16)
    normed, scale_inv = normalize(dot(node_hidden, w_node_out[...]))
    upstream = node_grads[...].astype(F32)
    out_grad = norm_back(normed, scale_inv, gain_node[...].astype(F32)[None, :], upstream).astype(BF16)
    slope = sigma * (1.0 + node_pre * (1.0 - sigma))
    pre_grad = (dot_nt(out_grad, w_node_out[...]) * slope).astype(BF16)
    agg_grad = dot_nt(pre_grad, w_second).astype(BF16)
    node_part_out[...] = upstream + dot_nt(pre_grad, w_first)
    node_sums[:width] = dot_tn(x, pre_grad)
    node_sums[width : 2 * width] = dot_tn(aggregated, pre_grad)
    node_sums[2 * width : 3 * width] = dot_tn(node_hidden, out_grad)
    node_gain = jnp.sum(upstream * normed, axis=0, keepdims=True)
    upstream = live * (
        edge_grads[...].astype(F32) + dot(near_rows[:, count:], agg_grad)
    )
    edge_normed = normed_kept[...]
    edge_gain = jnp.sum(upstream * edge_normed, axis=0, keepdims=True)
    out_grad = norm_back(edge_normed, scale_kept[:, :1], gain, upstream).astype(BF16)
    pre_grad = (dot_nt(out_grad, w_out[...]) * slope_kept[...]).astype(BF16)
    pre_grad_out[...] = pre_grad
    sender_total = dot(sender_columns[...], pre_grad)
    receiver_total = dot(receiver_columns[...], pre_grad)
    own = sender_total[:count].astype(BF16)
    away = sender_total[count:].astype(BF16)
    received = receiver_total.astype(BF16)
    sender_out[...] = own
    receiver_out[...] = received
    halo_grad = dot_nt(away, w_in[width : 2 * width]).astype(BF16)
    parts = [halo_grad[k * slots : (k + 1) * slots] for k in range(8)]
    up = jnp.concatenate([parts[0], parts[3], parts[5]], axis=0)
    down = jnp.concatenate([parts[2], parts[4], parts[7]], axis=0)
    core = lax.axis_index(CORE)
    sums_rows = gains_out.shape[0] + keep_out.shape[0]

    @pl.when(core == 0)
    def _():
        away_out[sums_rows:] = up
        across_out[...] = down

    @pl.when(core == 1)
    def _():
        away_out[sums_rows:] = down
        across_out[...] = up

    rest_out[...] = jnp.concatenate([parts[1], parts[6]], axis=0)
    edge_sums[:width] = dot_tn(edges[...], pre_grad)
    edge_sums[width : 2 * width] = dot_tn(x, own) + dot_tn(halo, away)
    edge_sums[2 * width : 3 * width] = dot_tn(x, received)
    edge_sums[3 * width : 4 * width] = dot_tn(hidden_kept[...], out_grad)
    split_by_core(edge_sums, 0, keep_out, away_out)
    split_by_core(node_sums, edge_sums.shape[0] // 2, keep_out, away_out)
    gains = pack_gains(edge_gain, node_gain)
    away_out[keep_out.shape[0] : sums_rows] = gains
    gains_out[...] = gains


def pair_kernel(parts, keep, gains, other, blocks_out, total, staged, sems):
    rows = keep.shape[0]
    chips = blocks_out.shape[0]
    packed = gains.shape[0]
    both = gains[...].astype(F32) + other[rows : rows + packed].astype(F32)
    summed = pack_gains(both[0:1] + both[1:2], both[2:3] + both[3:4])
    total[...] = (keep[...] + other[:rows].astype(F32)).astype(BF16)
    copies = []
    for chip in range(chips):
        staged[chip, :packed, :] = summed
        first, at = 0, packed
        for part in parts:
            step = part // chips
            staged[chip, at : at + step, :] = total[first + chip * step : first + (chip + 1) * step]
            first, at = first + part, at + step
        copies.append(
            pltpu.make_async_copy(staged.at[chip], blocks_out.at[chip], sems.at[chip])
        )
        copies[-1].start()
    for copy in copies:
        copy.wait()


def add_packed(values):
    packed = 16
    gains = values[:packed]
    return pack_gains(gains[0:1] + gains[1:2], gains[2:3] + gains[3:4])


def sum_kernel(received, sums_out):
    sums = received[0].astype(F32)
    for chip in range(1, received.shape[0]):
        sums = sums + received[chip].astype(F32)
    sums_out[...] = sums.astype(BF16)
    sums_out[:16] = add_packed(sums)


def join_kernel(own, other, sums_out):
    sums = own[...].astype(F32) + other[...].astype(F32)
    sums_out[...] = sums.astype(BF16)
    sums_out[:16] = add_packed(sums)


def spread_kernel(own, other, gains_out, spread_out, mine, sems):
    packed = gains_out.shape[0]
    sums = own[...].astype(F32) + other[...].astype(F32)
    mine[...] = sums[packed:].astype(BF16)
    copies = [
        pltpu.make_async_copy(mine, spread_out.at[chip], sems.at[chip])
        for chip in range(spread_out.shape[0])
    ]
    for copy in copies:
        copy.start()
    gains_out[...] = sums[:packed]
    for copy in copies:
        copy.wait()


def place_kernel(parts, own, other, *refs):
    outs, sems = refs[:-1], refs[-1]
    chips = own.shape[0]
    core = lax.axis_index(CORE)

    def place(halves):
        copies = []

        def put(source, target):
            copies.append(pltpu.make_async_copy(source, target, sems.at[len(copies)]))
            copies[-1].start()

        for half, blocks in enumerate(halves):
            for chip in range(chips):
                at = 0
                for i, part in enumerate(parts):
                    step = part // chips
                    row = half * part + chip * step
                    cut = outs[2 * i].shape[0]
                    split = min(max(cut - row, 0), step)
                    if split > 0:
                        put(blocks.at[chip, at : at + split], outs[2 * i].at[row : row + split])
                    if split < step:
                        rest = row + split - cut
                        put(
                            blocks.at[chip, at + split : at + step],
                            outs[2 * i + 1].at[rest : rest + step - split],
                        )
                    at += step
        for copy in copies:
            copy.wait()

    @pl.when(core == 0)
    def _():
        place([own, other])

    @pl.when(core == 1)
    def _():
        place([other, own])


def finish_kernel(
    edge_grads, pre_grad, sender_sum, receiver_sum, node_part, w_in, edges_grad, local_grad
):
    width = w_in.shape[1]
    edges_grad[...] = (
        edge_grads[...].astype(F32) + dot_nt(pre_grad[...], w_in[:width])
    ).astype(BF16)
    local_grad[...] = (
        node_part[...]
        + dot_nt(sender_sum[...], w_in[width : 2 * width])
        + dot_nt(receiver_sum[...], w_in[2 * width :])
    )


def turn_kernel(other, across, rest, high, low, middle):
    slots = rest.shape[0] // 2
    first = other.shape[0] - 3 * slots

    def turn(up_back, down_back):
        high[:slots] = up_back[:slots]
        high[slots : 2 * slots] = down_back[:slots]
        high[2 * slots :] = rest[:slots]
        low[:slots] = up_back[2 * slots :]
        low[slots : 2 * slots] = down_back[2 * slots :]
        low[2 * slots :] = rest[slots:]
        middle[:slots] = up_back[slots : 2 * slots]
        middle[slots:] = down_back[slots : 2 * slots]

    core = lax.axis_index(CORE)

    @pl.when(core == 0)
    def _():
        turn(across, other.at[first:])

    @pl.when(core == 1)
    def _():
        turn(other.at[first:], across)


def return_kernel(send_list, local_grad, middle, to_high, to_low, nodes_grad):
    slots = send_list.shape[1]

    def block(ref, k):
        return ref[k * slots : (k + 1) * slots]

    returned = jnp.concatenate(
        [
            block(to_high, 0),
            block(to_high, 2),
            block(to_high, 1),
            block(middle, 0),
            block(middle, 1),
            block(to_low, 0),
            block(to_low, 2),
            block(to_low, 1),
        ],
        axis=0,
    )
    hot = list_hot(send_list[...], local_grad.shape[0])
    nodes_grad[...] = (local_grad[...] + dot_tn(hot, returned)).astype(BF16)


SMEM = pltpu.SMEM
VMEM = pltpu.VMEM
HBM = pltpu.HBM


def call(body, outs, flops, *operands, spaces=(), out_space=VMEM, scratch=()):
    moved = sum(x.size * x.dtype.itemsize for x in operands)
    moved += sum(x.size * jnp.dtype(x.dtype).itemsize for x in outs)
    spaces = list(spaces) + [VMEM] * (len(operands) - len(spaces))
    out_spaces = out_space if isinstance(out_space, list) else [out_space] * len(outs)
    operands = [
        pltpu.with_memory_space_constraint(x, HBM) if space is HBM else x
        for x, space in zip(operands, spaces)
    ]
    return pl.pallas_call(
        body,
        out_shape=outs,
        in_specs=[pl.BlockSpec(memory_space=space) for space in spaces],
        out_specs=[pl.BlockSpec(memory_space=space) for space in out_spaces],
        scratch_shapes=list(scratch),
        compiler_params=pltpu.CompilerParams(vmem_limit_bytes=VMEM_LIMIT),
        cost_estimate=pl.CostEstimate(flops=flops, bytes_accessed=moved, transcendentals=0),
    )(*operands)


def like(array):
    return jax.ShapeDtypeStruct(array.shape, array.dtype)


def shaped(rows, columns, dtype):
    return jax.ShapeDtypeStruct((rows, columns), dtype)


def placed(parts, own, other, width):
    chips = own.shape[0]
    outs = [
        shaped(3 * width, width, BF16),
        shaped(width, width, BF16),
        shaped(2 * width, width, BF16),
        shaped(width, width, BF16),
    ]
    return call(
        functools.partial(place_kernel, parts),
        outs,
        0,
        own,
        other,
        out_space=HBM,
        scratch=[pltpu.SemaphoreType.DMA((2 * len(parts) * chips + len(parts),))],
    )


def spread_of(received, packed, *beside):
    chips, rows, width = received.shape
    (sums,) = call(sum_kernel, [shaped(rows, width, BF16)], 0, received)
    size = lax.axis_size(FAR)
    distance = 1
    while True:
        other = lax.ppermute(sums, FAR, [(i, i ^ distance) for i in range(size)])
        distance *= 2
        if distance == size:
            break
        (sums,) = call(join_kernel, [like(sums)], 0, sums, other)
    mine = rows - packed
    other, *beside = lax.optimization_barrier((other, *beside))
    gains, spread = call(
        spread_kernel,
        [shaped(packed, width, F32), jax.ShapeDtypeStruct((chips, mine, width), BF16)],
        0,
        sums,
        other,
        out_space=[VMEM, HBM],
        scratch=[pltpu.VMEM((mine, width), BF16), pltpu.SemaphoreType.DMA((chips,))],
    )
    return gains, spread, *beside


def blocks_of(parts, keep, gains, other):
    chips = lax.axis_size(SQUARE)
    rows, width = keep.shape
    shape = (chips, gains.shape[0] + rows // chips, width)
    (blocks,) = call(
        functools.partial(pair_kernel, parts),
        [jax.ShapeDtypeStruct(shape, BF16)],
        0,
        keep,
        gains,
        other,
        out_space=HBM,
        scratch=[
            pltpu.VMEM((rows, width), BF16),
            pltpu.VMEM(shape, BF16),
            pltpu.SemaphoreType.DMA((chips,)),
        ],
    )
    return blocks


def on_device(
    nodes,
    edges,
    edge_grads,
    node_grads,
    send_list,
    senders,
    receivers,
    tile_count,
    w_edge_in,
    w_edge_out,
    gain_edge,
    w_node_in,
    w_node_out,
    gain_node,
):
    count, width = nodes.shape
    slots = send_list.shape[1]
    halo_rows = 8 * slots
    edge_rows = edges.shape[0]
    tile_rows = senders.shape[1]
    square = 2 * width * width
    low, mid, high, nodes, send_list = call(
        send_kernel,
        [
            shaped(3 * slots, width, BF16),
            shaped(2 * slots, width, BF16),
            shaped(3 * slots, width, BF16),
            like(nodes),
            like(send_list),
        ],
        2 * halo_rows * count * width,
        nodes,
        send_list,
        spaces=[HBM, HBM],
        scratch=[pltpu.SemaphoreType.DMA((2,))],
    )
    from_low = passed_along(high, PX, 1)
    from_high = passed_along(low, PX, -1)
    fetched = [
        senders,
        receivers,
        edges,
        w_edge_in,
        w_edge_out,
        gain_edge,
        w_node_in,
        w_node_out,
        gain_node,
        node_grads,
        edge_grads,
    ]
    near_hot, halo_hot, *fetched = call(
        functools.partial(index_kernel, len(fetched)),
        [
            shaped(edge_rows, 2 * count, BF16),
            shaped(edge_rows, halo_rows, BF16),
        ]
        + [like(x) for x in fetched],
        0,
        *fetched,
        spaces=[HBM] * len(fetched),
        scratch=[pltpu.SemaphoreType.DMA((len(fetched),))],
    )
    (
        senders,
        receivers,
        edges,
        w_edge_in,
        w_edge_out,
        gain_edge,
        w_node_in,
        w_node_out,
        gain_node,
        node_grads,
        edge_grads,
    ) = fetched
    from_low, from_high, near_hot = lax.optimization_barrier((from_low, from_high, near_hot))
    upward = passed_along(
        jnp.concatenate([from_high[2 * slots :], mid[slots:], from_low[2 * slots :]]), PY, 1
    )
    downward = passed_along(
        jnp.concatenate([from_high[:slots], mid[:slots], from_low[:slots]]), PY, -1
    )
    pre_local, sender_columns, receiver_columns = call(
        local_kernel,
        [
            shaped(edge_rows, width, F32),
            shaped(count + halo_rows, edge_rows, BF16),
            shaped(count, edge_rows, BF16),
        ],
        square * (2 * count + edge_rows) + 4 * edge_rows * count * width,
        nodes,
        edges,
        senders,
        receivers,
        near_hot,
        w_edge_in,
    )
    parts = (2 * width, 3 * width // 2)
    halves = sum(parts)
    pre_grad, sender_sum, receiver_sum, node_part, across, rest, keep, away, gains = call(
        functools.partial(layer_kernel, tile_rows),
        [
            shaped(edge_rows, width, BF16),
            shaped(count, width, BF16),
            shaped(count, width, BF16),
            shaped(count, width, F32),
            shaped(3 * slots, width, BF16),
            shaped(2 * slots, width, BF16),
            shaped(halves, width, F32),
            shaped(halves + 16 + 3 * slots, width, BF16),
            shaped(16, width, BF16),
        ],
        square * (6 * edge_rows + 11 * count + 2 * halo_rows)
        + 2 * edge_rows * (4 * count + halo_rows) * width,
        tile_count,
        nodes,
        node_grads,
        edges,
        edge_grads,
        pre_local,
        halo_hot,
        near_hot,
        sender_columns,
        receiver_columns,
        from_high,
        from_low,
        upward,
        downward,
        w_edge_in,
        w_edge_out,
        gain_edge,
        w_node_in,
        w_node_out,
        gain_node,
        spaces=[SMEM],
        scratch=[
            pltpu.VMEM((edge_rows, width), F32),
            pltpu.VMEM((edge_rows, width), BF16),
            pltpu.VMEM((edge_rows, width), F32),
            pltpu.VMEM((edge_rows, 128), F32),
            pltpu.VMEM((3 * width, width), F32),
            pltpu.VMEM((4 * width, width), F32),
        ],
    )
    other = across_cores(away)
    blocks = blocks_of(parts, keep, gains, other)
    received = lax.all_to_all(blocks, SQUARE, 0, 0)
    high, low, middle = call(
        turn_kernel,
        [
            shaped(3 * slots, width, BF16),
            shaped(3 * slots, width, BF16),
            shaped(2 * slots, width, BF16),
        ],
        0,
        other,
        across_chips(across),
        rest,
    )
    received, high, low = lax.optimization_barrier((received, high, low))
    gains, spread, to_high, to_low = spread_of(
        received, gains.shape[0], passed_along(high, PX, 1), passed_along(low, PX, -1)
    )
    own = lax.all_to_all(spread, SQUARE, 0, 0)
    edges_grad, local_grad = call(
        finish_kernel,
        [shaped(edge_rows, width, BF16), shaped(count, width, F32)],
        square * (edge_rows + 2 * count),
        edge_grads,
        pre_grad,
        sender_sum,
        receiver_sum,
        node_part,
        w_edge_in,
    )
    (nodes_grad,) = call(
        return_kernel,
        [shaped(count, width, BF16)],
        2 * halo_rows * count * width,
        send_list,
        local_grad,
        middle,
        to_high,
        to_low,
    )
    own, nodes_grad, edges_grad = lax.optimization_barrier((own, nodes_grad, edges_grad))
    w_edge_in_grad, w_edge_out_grad, w_node_in_grad, w_node_out_grad = placed(
        parts, own, across_cores(own), width
    )
    return (
        nodes_grad,
        edges_grad,
        w_edge_in_grad,
        w_edge_out_grad,
        (gains[0] + gains[1]).astype(BF16),
        w_node_in_grad,
        w_node_out_grad,
        (gains[2] + gains[3]).astype(BF16),
    )


def solution(mesh):
    in_specs = (
        P(("groups",) + PX + PY, None),
        P(("groups",) + PX + PY, None),
        P(("groups",) + PX + PY, None),
        P(("groups",) + PX + PY, None),
        P(("groups",) + PX + PY, None),
        P(("groups",) + PX + PY, None),
        P(("groups",) + PX + PY, None),
        P(("groups",) + PX + PY),
        P(),
        P(),
        P(),
        P(),
        P(),
        P(),
    )
    out_specs = (
        P(("groups",) + PX + PY, None),
        P(("groups",) + PX + PY, None),
        P("groups", None),
        P("groups", None),
        P("groups"),
        P("groups", None),
        P("groups", None),
        P("groups"),
    )
    groups, px, py = mesh.devices.shape
    by_core = jax.sharding.Mesh(
        mesh.devices.reshape(groups, px // 2, 2, py // 2, 2), ("groups",) + PX + PY
    )
    return jax.shard_map(
        on_device, mesh=by_core, in_specs=in_specs, out_specs=out_specs, check_vma=False
    )
```

```python
import functools

import jax
import jax.numpy as jnp
from jax import lax
from jax.experimental import pallas as pl
from jax.experimental.pallas import tpu as pltpu
from jax.sharding import PartitionSpec as P

EPS = 1e-05
BF16 = jnp.bfloat16
F32 = jnp.float32
VMEM_LIMIT = 24 * 1024 * 1024


CORE = "core"
FAR = "far"
PX = (FAR, "near")
PY = ("side", CORE)
SQUARE = ("near", "side")


def passed_along(array, axis, by):
    size = lax.axis_size(axis)
    return lax.ppermute(array, axis, [(i, (i + by) % size) for i in range(size)])


def across_chips(array):
    size = lax.axis_size(PY)
    pairs = [(i, (i + 1 if i % 2 else i - 1) % size) for i in range(size)]
    return lax.ppermute(array, PY, pairs)


def across_cores(array):
    return lax.ppermute(array, CORE, [(0, 1), (1, 0)])


def dot(left, right):
    return jnp.dot(left, right, preferred_element_type=F32)


def dot_tn(left, right):
    return lax.dot_general(left, right, (((0,), (0,)), ((), ())), preferred_element_type=F32)


def dot_nt(left, right):
    return lax.dot_general(left, right, (((1,), (1,)), ((), ())), preferred_element_type=F32)


def sigmoid(value):
    return 0.5 + 0.5 * jnp.tanh(0.5 * value)


def normalize(value):
    centered = value - jnp.mean(value, axis=-1, keepdims=True)
    scale_inv = lax.rsqrt(jnp.mean(centered * centered, axis=-1, keepdims=True) + EPS)
    return centered * scale_inv, scale_inv


def norm_back(normed, scale_inv, gain, upstream):
    scaled = upstream * gain
    inner = (
        scaled
        - jnp.mean(scaled, axis=-1, keepdims=True)
        - normed * jnp.mean(scaled * normed, axis=-1, keepdims=True)
    )
    return inner * scale_inv


def columns_of(ids):
    rows, lanes = ids.shape
    padded = -(-rows // 8) * 8
    if padded > rows:
        ids = jnp.concatenate([ids, jnp.zeros((padded - rows, lanes), ids.dtype)], axis=0)
    return ids.T


def hot_rows(columns, tiles, base, count):
    parts = []
    for tile in tiles:
        column = columns[:, tile : tile + 1] - base
        lanes = lax.broadcasted_iota(jnp.int32, (columns.shape[0], count), 1)
        parts.append(jnp.where(lanes == column, 1.0, 0.0).astype(BF16))
    return jnp.concatenate(parts, axis=0) if len(parts) > 1 else parts[0]


def hot_columns(ids, tiles, base, count):
    parts = []
    for tile in tiles:
        row = ids[tile : tile + 1, :] - base
        subs = lax.broadcasted_iota(jnp.int32, (count, ids.shape[1]), 0)
        parts.append(jnp.where(subs == row, 1.0, 0.0).astype(BF16))
    return jnp.concatenate(parts, axis=1) if len(parts) > 1 else parts[0]


def list_hot(ids, count):
    directions, slots = ids.shape
    wide = jnp.concatenate([ids, jnp.zeros((directions, 128 - slots), ids.dtype)], axis=1)
    columns = wide.T
    parts = []
    for k in range(directions):
        lanes = lax.broadcasted_iota(jnp.int32, (slots, count), 1)
        parts.append(jnp.where(lanes == columns[:slots, k : k + 1], 1.0, 0.0).astype(BF16))
    return jnp.concatenate(parts, axis=0)


def live_rows(count_ref, tile_rows, rows):
    index = lax.broadcasted_iota(jnp.int32, (rows, 1), 0)
    return jnp.where(index < count_ref[0] * tile_rows, 1.0, 0.0)


def fetch_all(sources, targets, sems):
    copies = [
        pltpu.make_async_copy(source, target, sems.at[i])
        for i, (source, target) in enumerate(zip(sources, targets))
    ]
    for copy in copies:
        copy.start()
    return copies


def send_kernel(nodes_hbm, list_hbm, low, mid, high, nodes, send_list, sems):
    slots = send_list.shape[1]
    for copy in fetch_all([list_hbm, nodes_hbm], [send_list, nodes], sems):
        copy.wait()
    rows = dot(list_hot(send_list[...], nodes.shape[0]), nodes[...]).astype(BF16)
    low[...] = rows[: 3 * slots]
    mid[...] = rows[3 * slots : 5 * slots]
    high[...] = rows[5 * slots :]


def index_kernel(sources, *refs):
    fetched, refs = refs[:sources], refs[sources:]
    near_rows, halo_rows = refs[:2]
    targets, sems = refs[2:-1], refs[-1]
    senders, receivers = targets[:2]
    copies = fetch_all(fetched, targets, sems)
    for copy in copies[:2]:
        copy.wait()
    tile_rows = senders.shape[1]
    count = near_rows.shape[1] // 2
    by_sender = columns_of(senders[...])
    by_receiver = columns_of(receivers[...])
    for tile in range(senders.shape[0]):
        rows = slice(tile * tile_rows, (tile + 1) * tile_rows)
        near_rows[rows, :count] = hot_rows(by_sender, [tile], 0, count)
        near_rows[rows, count:] = hot_rows(by_receiver, [tile], 0, count)
        halo_rows[rows, :] = hot_rows(by_sender, [tile], count, halo_rows.shape[1])
    for copy in copies[2:]:
        copy.wait()


def local_kernel(
    nodes,
    edges,
    senders,
    receivers,
    near_rows,
    w_in,
    pre,
    sender_columns,
    receiver_columns,
    nodes_turned,
    edges_turned,
):
    width = nodes.shape[1]
    tile_rows = senders.shape[1]
    extended = sender_columns.shape[0]
    count = receiver_columns.shape[0]
    sender_ids = senders[...]
    receiver_ids = receivers[...]
    for tile in range(senders.shape[0]):
        rows = slice(tile * tile_rows, (tile + 1) * tile_rows)
        sender_columns[:, rows] = hot_columns(sender_ids, [tile], 0, extended)
        receiver_columns[:, rows] = hot_columns(receiver_ids, [tile], 0, count)
    x = nodes[...]
    table = jnp.concatenate(
        [
            dot(x, w_in[width : 2 * width]).astype(BF16),
            dot(x, w_in[2 * width :]).astype(BF16),
        ],
        axis=0,
    )
    pre[...] = dot(edges[...], w_in[:width]) + dot(near_rows[...], table)
    nodes_turned[...] = x.T
    edges_turned[...] = edges[...].T


def split_by_core(sums, first, keep_out, away_out):
    half = sums.shape[0] // 2
    core = lax.axis_index(CORE)
    keep_out[first : first + half] = sums[pl.ds(pl.multiple_of(core * half, half), half), :]
    away = sums[pl.ds(pl.multiple_of((1 - core) * half, half), half), :]
    away_out[first : first + half] = away.astype(BF16)


def pack_gains(edge_gain, node_gain):
    edge_high = edge_gain.astype(BF16).astype(F32)
    node_high = node_gain.astype(BF16).astype(F32)
    row = lax.broadcasted_iota(jnp.int32, (16, edge_gain.shape[1]), 0)
    packed = jnp.where(row == 0, edge_high, 0.0)
    packed = jnp.where(row == 1, edge_gain - edge_high, packed)
    packed = jnp.where(row == 2, node_high, packed)
    packed = jnp.where(row == 3, node_gain - node_high, packed)
    return packed.astype(BF16)


def layer_kernel(
    tile_rows,
    count_ref,
    nodes,
    node_grads,
    nodes_turned,
    edges_turned,
    edge_grads,
    pre_local,
    halo_rows,
    near_rows,
    sender_columns,
    receiver_columns,
    from_high,
    from_low,
    upward,
    downward,
    w_in,
    w_out,
    gain_edge,
    w_node_in,
    w_node_out,
    gain_node,
    pre_grad_out,
    sender_out,
    receiver_out,
    node_grad_out,
    across_out,
    rest_out,
    keep_out,
    away_out,
    gains_out,
    slope_kept,
    hidden_kept,
    normed_kept,
    scale_kept,
    node_sums,
    edge_sums,
):
    count, width = nodes.shape
    edge_rows = edge_grads.shape[0]
    live = live_rows(count_ref, tile_rows, edge_rows)
    slots = from_high.shape[0] // 3
    halo = jnp.concatenate(
        [
            downward[:slots],
            from_high[slots : 2 * slots],
            upward[:slots],
            downward[slots : 2 * slots],
            upward[slots : 2 * slots],
            downward[2 * slots :],
            from_low[slots : 2 * slots],
            upward[2 * slots :],
        ],
        axis=0,
    )
    table = dot(halo, w_in[width : 2 * width]).astype(BF16)
    gain = gain_edge[...].astype(F32)[None, :]
    value = pre_local[...] + dot(halo_rows[...], table)
    sigma = sigmoid(value)
    hidden = (value * sigma).astype(BF16)
    hidden_kept[...] = hidden
    slope_kept[...] = sigma * (1.0 + value * (1.0 - sigma))
    edge_normed, edge_scale = normalize(dot(hidden, w_out[...]))
    normed_kept[...] = edge_normed
    scale_kept[...] = jnp.broadcast_to(edge_scale, (edge_rows, 128))
    message = (live * gain * edge_normed).astype(BF16)
    total = dot(receiver_columns[...], message)
    aggregated = total.astype(BF16)
    x = nodes[...]
    w_first = w_node_in[:width]
    w_second = w_node_in[width:]
    node_pre = dot(x, w_first) + dot(aggregated, w_second)
    sigma = sigmoid(node_pre)
    node_hidden = (node_pre * sigma).astype(BF16)
    normed, scale_inv = normalize(dot(node_hidden, w_node_out[...]))
    upstream = node_grads[...].astype(F32)
    out_grad = norm_back(normed, scale_inv, gain_node[...].astype(F32)[None, :], upstream).astype(BF16)
    slope = sigma * (1.0 + node_pre * (1.0 - sigma))
    pre_grad = (dot_nt(out_grad, w_node_out[...]) * slope).astype(BF16)
    agg_grad = dot_nt(pre_grad, w_second).astype(BF16)
    node_grad_out[...] = pre_grad
    node_sums[:width] = dot(nodes_turned[...], pre_grad)
    node_sums[width : 2 * width] = dot_tn(aggregated, pre_grad)
    node_sums[2 * width : 3 * width] = dot_tn(node_hidden, out_grad)
    node_gain = jnp.sum(upstream * normed, axis=0, keepdims=True)
    upstream = live * (
        edge_grads[...].astype(F32) + dot(near_rows[:, count:], agg_grad)
    )
    edge_normed = normed_kept[...]
    edge_gain = jnp.sum(upstream * edge_normed, axis=0, keepdims=True)
    out_grad = norm_back(edge_normed, scale_kept[:, :1], gain, upstream).astype(BF16)
    pre_grad = (dot_nt(out_grad, w_out[...]) * slope_kept[...]).astype(BF16)
    pre_grad_out[...] = pre_grad
    sender_total = dot(sender_columns[...], pre_grad)
    receiver_total = dot(receiver_columns[...], pre_grad)
    own = sender_total[:count].astype(BF16)
    away = sender_total[count:].astype(BF16)
    received = receiver_total.astype(BF16)
    sender_out[...] = own
    receiver_out[...] = received
    halo_grad = dot_nt(away, w_in[width : 2 * width]).astype(BF16)
    parts = [halo_grad[k * slots : (k + 1) * slots] for k in range(8)]
    up = jnp.concatenate([parts[0], parts[3], parts[5]], axis=0)
    down = jnp.concatenate([parts[2], parts[4], parts[7]], axis=0)
    core = lax.axis_index(CORE)
    sums_rows = gains_out.shape[0] + keep_out.shape[0]

    @pl.when(core == 0)
    def _():
        away_out[sums_rows:] = up
        across_out[...] = down

    @pl.when(core == 1)
    def _():
        away_out[sums_rows:] = down
        across_out[...] = up

    rest_out[...] = jnp.concatenate([parts[1], parts[6]], axis=0)
    edge_sums[:width] = dot(edges_turned[...], pre_grad)
    edge_sums[width : 2 * width] = dot(nodes_turned[...], own) + dot_tn(halo, away)
    edge_sums[2 * width : 3 * width] = dot(nodes_turned[...], received)
    edge_sums[3 * width : 4 * width] = dot_tn(hidden_kept[...], out_grad)
    split_by_core(edge_sums, 0, keep_out, away_out)
    split_by_core(node_sums, edge_sums.shape[0] // 2, keep_out, away_out)
    gains = pack_gains(edge_gain, node_gain)
    away_out[keep_out.shape[0] : sums_rows] = gains
    gains_out[...] = gains


def pair_kernel(parts, keep, gains, other, blocks_out):
    rows = keep.shape[0]
    chips = blocks_out.shape[0]
    packed = gains.shape[0]
    both = gains[...].astype(F32) + other[rows : rows + packed].astype(F32)
    summed = pack_gains(both[0:1] + both[1:2], both[2:3] + both[3:4])
    for chip in range(chips):
        blocks_out[chip, :packed, :] = summed
        first, at = 0, packed
        for part in parts:
            step = part // chips
            rows_in = slice(first + chip * step, first + (chip + 1) * step)
            blocks_out[chip, at : at + step, :] = (
                keep[rows_in] + other[rows_in].astype(F32)
            ).astype(BF16)
            first, at = first + part, at + step


def add_packed(values):
    packed = 16
    gains = values[:packed]
    return pack_gains(gains[0:1] + gains[1:2], gains[2:3] + gains[3:4])


def sum_kernel(received, sums_out):
    sums = received[0].astype(F32)
    for chip in range(1, received.shape[0]):
        sums = sums + received[chip].astype(F32)
    sums_out[...] = sums.astype(BF16)
    sums_out[:16] = add_packed(sums)


def join_kernel(own, other, sums_out):
    sums = own[...].astype(F32) + other[...].astype(F32)
    sums_out[...] = sums.astype(BF16)
    sums_out[:16] = add_packed(sums)


def spread_kernel(own, other, gains_out, spread_out):
    packed = gains_out.shape[0]
    sums = own[...].astype(F32) + other[...].astype(F32)
    gains_out[...] = sums[:packed]
    mine = sums[packed:].astype(BF16)
    for chip in range(spread_out.shape[0]):
        spread_out[chip] = mine


def place_kernel(parts, own, other, *refs):
    outs, sems = refs[:-1], refs[-1]
    chips = own.shape[0]
    core = lax.axis_index(CORE)

    def place(halves):
        copies = []

        def put(source, target):
            copies.append(pltpu.make_async_copy(source, target, sems.at[len(copies)]))
            copies[-1].start()

        for half, blocks in enumerate(halves):
            for chip in range(chips):
                at = 0
                for i, part in enumerate(parts):
                    step = part // chips
                    row = half * part + chip * step
                    cut = outs[2 * i].shape[0]
                    split = min(max(cut - row, 0), step)
                    if split > 0:
                        put(blocks.at[chip, at : at + split], outs[2 * i].at[row : row + split])
                    if split < step:
                        rest = row + split - cut
                        put(
                            blocks.at[chip, at + split : at + step],
                            outs[2 * i + 1].at[rest : rest + step - split],
                        )
                    at += step
        for copy in copies:
            copy.wait()

    @pl.when(core == 0)
    def _():
        place([own, other])

    @pl.when(core == 1)
    def _():
        place([other, own])


def finish_kernel(
    edge_grads,
    node_grads,
    pre_grad,
    sender_sum,
    receiver_sum,
    node_pre_grad,
    w_in,
    w_node_in,
    edges_grad,
    local_grad,
):
    width = w_in.shape[1]
    edges_grad[...] = (
        edge_grads[...].astype(F32) + dot_nt(pre_grad[...], w_in[:width])
    ).astype(BF16)
    local_grad[...] = (
        node_grads[...].astype(F32)
        + dot_nt(node_pre_grad[...], w_node_in[:width])
        + dot_nt(sender_sum[...], w_in[width : 2 * width])
        + dot_nt(receiver_sum[...], w_in[2 * width :])
    )


def turn_kernel(other, across, rest, high, low, middle):
    slots = rest.shape[0] // 2
    first = other.shape[0] - 3 * slots

    def turn(up_back, down_back):
        high[:slots] = up_back[:slots]
        high[slots : 2 * slots] = down_back[:slots]
        high[2 * slots :] = rest[:slots]
        low[:slots] = up_back[2 * slots :]
        low[slots : 2 * slots] = down_back[2 * slots :]
        low[2 * slots :] = rest[slots:]
        middle[:slots] = up_back[slots : 2 * slots]
        middle[slots:] = down_back[slots : 2 * slots]

    core = lax.axis_index(CORE)

    @pl.when(core == 0)
    def _():
        turn(across, other.at[first:])

    @pl.when(core == 1)
    def _():
        turn(other.at[first:], across)


def return_kernel(send_list, local_grad, middle, to_high, to_low, nodes_grad):
    slots = send_list.shape[1]

    def block(ref, k):
        return ref[k * slots : (k + 1) * slots]

    returned = jnp.concatenate(
        [
            block(to_high, 0),
            block(to_high, 2),
            block(to_high, 1),
            block(middle, 0),
            block(middle, 1),
            block(to_low, 0),
            block(to_low, 2),
            block(to_low, 1),
        ],
        axis=0,
    )
    hot = list_hot(send_list[...], local_grad.shape[0])
    nodes_grad[...] = (local_grad[...] + dot_tn(hot, returned)).astype(BF16)


SMEM = pltpu.SMEM
VMEM = pltpu.VMEM
HBM = pltpu.HBM


def call(body, outs, flops, *operands, spaces=(), out_space=VMEM, scratch=()):
    moved = sum(x.size * x.dtype.itemsize for x in operands)
    moved += sum(x.size * jnp.dtype(x.dtype).itemsize for x in outs)
    spaces = list(spaces) + [VMEM] * (len(operands) - len(spaces))
    out_spaces = out_space if isinstance(out_space, list) else [out_space] * len(outs)
    operands = [
        pltpu.with_memory_space_constraint(x, HBM) if space is HBM else x
        for x, space in zip(operands, spaces)
    ]
    return pl.pallas_call(
        body,
        out_shape=outs,
        in_specs=[pl.BlockSpec(memory_space=space) for space in spaces],
        out_specs=[pl.BlockSpec(memory_space=space) for space in out_spaces],
        scratch_shapes=list(scratch),
        compiler_params=pltpu.CompilerParams(vmem_limit_bytes=VMEM_LIMIT),
        cost_estimate=pl.CostEstimate(flops=flops, bytes_accessed=moved, transcendentals=0),
    )(*operands)


def like(array):
    return jax.ShapeDtypeStruct(array.shape, array.dtype)


def shaped(rows, columns, dtype):
    return jax.ShapeDtypeStruct((rows, columns), dtype)


def placed(parts, own, other, width):
    chips = own.shape[0]
    outs = [
        shaped(3 * width, width, BF16),
        shaped(width, width, BF16),
        shaped(2 * width, width, BF16),
        shaped(width, width, BF16),
    ]
    return call(
        functools.partial(place_kernel, parts),
        outs,
        0,
        own,
        other,
        out_space=HBM,
        scratch=[pltpu.SemaphoreType.DMA((2 * len(parts) * chips + len(parts),))],
    )


def spread_of(received, packed, *beside):
    chips, rows, width = received.shape
    (sums,) = call(sum_kernel, [shaped(rows, width, BF16)], 0, received)
    size = lax.axis_size(FAR)
    distance = 1
    while True:
        other = lax.ppermute(sums, FAR, [(i, i ^ distance) for i in range(size)])
        distance *= 2
        if distance == size:
            break
        (sums,) = call(join_kernel, [like(sums)], 0, sums, other)
    mine = rows - packed
    other, *beside = lax.optimization_barrier((other, *beside))
    gains, spread = call(
        spread_kernel,
        [shaped(packed, width, F32), jax.ShapeDtypeStruct((chips, mine, width), BF16)],
        0,
        sums,
        other,
    )
    return gains, spread, *beside


def blocks_of(parts, keep, gains, other):
    chips = lax.axis_size(SQUARE)
    rows, width = keep.shape
    shape = (chips, gains.shape[0] + rows // chips, width)
    (blocks,) = call(
        functools.partial(pair_kernel, parts),
        [jax.ShapeDtypeStruct(shape, BF16)],
        0,
        keep,
        gains,
        other,
    )
    return blocks


def on_device(
    nodes,
    edges,
    edge_grads,
    node_grads,
    send_list,
    senders,
    receivers,
    tile_count,
    w_edge_in,
    w_edge_out,
    gain_edge,
    w_node_in,
    w_node_out,
    gain_node,
):
    count, width = nodes.shape
    slots = send_list.shape[1]
    halo_rows = 8 * slots
    edge_rows = edges.shape[0]
    tile_rows = senders.shape[1]
    square = 2 * width * width
    low, mid, high, nodes, send_list = call(
        send_kernel,
        [
            shaped(3 * slots, width, BF16),
            shaped(2 * slots, width, BF16),
            shaped(3 * slots, width, BF16),
            like(nodes),
            like(send_list),
        ],
        2 * halo_rows * count * width,
        nodes,
        send_list,
        spaces=[HBM, HBM],
        scratch=[pltpu.SemaphoreType.DMA((2,))],
    )
    from_low = passed_along(high, PX, 1)
    from_high = passed_along(low, PX, -1)
    fetched = [
        senders,
        receivers,
        edges,
        w_edge_in,
        w_edge_out,
        gain_edge,
        w_node_in,
        w_node_out,
        gain_node,
        node_grads,
        edge_grads,
    ]
    near_hot, halo_hot, *fetched = call(
        functools.partial(index_kernel, len(fetched)),
        [
            shaped(edge_rows, 2 * count, BF16),
            shaped(edge_rows, halo_rows, BF16),
        ]
        + [like(x) for x in fetched],
        0,
        *fetched,
        spaces=[HBM] * len(fetched),
        scratch=[pltpu.SemaphoreType.DMA((len(fetched),))],
    )
    (
        senders,
        receivers,
        edges,
        w_edge_in,
        w_edge_out,
        gain_edge,
        w_node_in,
        w_node_out,
        gain_node,
        node_grads,
        edge_grads,
    ) = fetched
    from_low, from_high, near_hot = lax.optimization_barrier((from_low, from_high, near_hot))
    upward = passed_along(
        jnp.concatenate([from_high[2 * slots :], mid[slots:], from_low[2 * slots :]]), PY, 1
    )
    downward = passed_along(
        jnp.concatenate([from_high[:slots], mid[:slots], from_low[:slots]]), PY, -1
    )
    pre_local, sender_columns, receiver_columns, nodes_turned, edges_turned = call(
        local_kernel,
        [
            shaped(edge_rows, width, F32),
            shaped(count + halo_rows, edge_rows, BF16),
            shaped(count, edge_rows, BF16),
            shaped(width, count, BF16),
            shaped(width, edge_rows, BF16),
        ],
        square * (2 * count + edge_rows) + 4 * edge_rows * count * width,
        nodes,
        edges,
        senders,
        receivers,
        near_hot,
        w_edge_in,
    )
    parts = (2 * width, 3 * width // 2)
    halves = sum(parts)
    pre_grad, sender_sum, receiver_sum, node_pre_grad, across, rest, keep, away, gains = call(
        functools.partial(layer_kernel, tile_rows),
        [
            shaped(edge_rows, width, BF16),
            shaped(count, width, BF16),
            shaped(count, width, BF16),
            shaped(count, width, BF16),
            shaped(3 * slots, width, BF16),
            shaped(2 * slots, width, BF16),
            shaped(halves, width, F32),
            shaped(halves + 16 + 3 * slots, width, BF16),
            shaped(16, width, BF16),
        ],
        square * (6 * edge_rows + 11 * count + 2 * halo_rows)
        + 2 * edge_rows * (4 * count + halo_rows) * width,
        tile_count,
        nodes,
        node_grads,
        nodes_turned,
        edges_turned,
        edge_grads,
        pre_local,
        halo_hot,
        near_hot,
        sender_columns,
        receiver_columns,
        from_high,
        from_low,
        upward,
        downward,
        w_edge_in,
        w_edge_out,
        gain_edge,
        w_node_in,
        w_node_out,
        gain_node,
        spaces=[SMEM],
        scratch=[
            pltpu.VMEM((edge_rows, width), F32),
            pltpu.VMEM((edge_rows, width), BF16),
            pltpu.VMEM((edge_rows, width), F32),
            pltpu.VMEM((edge_rows, 128), F32),
            pltpu.VMEM((3 * width, width), F32),
            pltpu.VMEM((4 * width, width), F32),
        ],
    )
    other = across_cores(away)
    blocks = blocks_of(parts, keep, gains, other)
    received = lax.all_to_all(blocks, SQUARE, 0, 0)
    high, low, middle = call(
        turn_kernel,
        [
            shaped(3 * slots, width, BF16),
            shaped(3 * slots, width, BF16),
            shaped(2 * slots, width, BF16),
        ],
        10**10,
        other,
        across_chips(across),
        rest,
    )
    received, high, low = lax.optimization_barrier((received, high, low))
    gains, spread, to_high, to_low = spread_of(
        received, gains.shape[0], passed_along(high, PX, 1), passed_along(low, PX, -1)
    )
    own = lax.all_to_all(spread, SQUARE, 0, 0)
    edges_grad, local_grad = call(
        finish_kernel,
        [shaped(edge_rows, width, BF16), shaped(count, width, F32)],
        square * (edge_rows + 3 * count),
        edge_grads,
        node_grads,
        pre_grad,
        sender_sum,
        receiver_sum,
        node_pre_grad,
        w_edge_in,
        w_node_in,
    )
    (nodes_grad,) = call(
        return_kernel,
        [shaped(count, width, BF16)],
        2 * halo_rows * count * width,
        send_list,
        local_grad,
        middle,
        to_high,
        to_low,
    )
    own, nodes_grad, edges_grad = lax.optimization_barrier((own, nodes_grad, edges_grad))
    w_edge_in_grad, w_edge_out_grad, w_node_in_grad, w_node_out_grad = placed(
        parts, own, across_cores(own), width
    )
    return (
        nodes_grad,
        edges_grad,
        w_edge_in_grad,
        w_edge_out_grad,
        (gains[0] + gains[1]).astype(BF16),
        w_node_in_grad,
        w_node_out_grad,
        (gains[2] + gains[3]).astype(BF16),
    )


def solution(mesh):
    in_specs = (
        P(("groups",) + PX + PY, None),
        P(("groups",) + PX + PY, None),
        P(("groups",) + PX + PY, None),
        P(("groups",) + PX + PY, None),
        P(("groups",) + PX + PY, None),
        P(("groups",) + PX + PY, None),
        P(("groups",) + PX + PY, None),
        P(("groups",) + PX + PY),
        P(),
        P(),
        P(),
        P(),
        P(),
        P(),
    )
    out_specs = (
        P(("groups",) + PX + PY, None),
        P(("groups",) + PX + PY, None),
        P("groups", None),
        P("groups", None),
        P("groups"),
        P("groups", None),
        P("groups", None),
        P("groups"),
    )
    groups, px, py = mesh.devices.shape
    by_core = jax.sharding.Mesh(
        mesh.devices.reshape(groups, px // 2, 2, py // 2, 2), ("groups",) + PX + PY
    )
    return jax.shard_map(
        on_device, mesh=by_core, in_specs=in_specs, out_specs=out_specs, check_vma=False
    )
```

```python
import functools

import jax
import jax.numpy as jnp
from jax import lax
from jax.experimental import pallas as pl
from jax.experimental.pallas import tpu as pltpu
from jax.sharding import PartitionSpec as P

EPS = 1e-05
BF16 = jnp.bfloat16
F32 = jnp.float32
VMEM_LIMIT = 24 * 1024 * 1024


CORE = "core"
FAR = "far"
PX = (FAR, "near")
PY = ("side", CORE)
SQUARE = ("near", "side")


def passed_along(array, axis, by):
    size = lax.axis_size(axis)
    return lax.ppermute(array, axis, [(i, (i + by) % size) for i in range(size)])


def across_chips(array):
    size = lax.axis_size(PY)
    pairs = [(i, (i + 1 if i % 2 else i - 1) % size) for i in range(size)]
    return lax.ppermute(array, PY, pairs)


def square_members():
    return lax.axis_size(SQUARE)


def place_in_square():
    near, side = SQUARE
    return lax.axis_index(near) * lax.axis_size(side) + lax.axis_index(side)


def in_square(array, offset):
    return lax.ppermute(array, SQUARE, [(i, i ^ offset) for i in range(square_members())])


def tree_sum(terms):
    while len(terms) > 1:
        terms = [terms[i] + terms[i + 1] for i in range(0, len(terms), 2)]
    return terms[0]


def across_cores(array):
    return lax.ppermute(array, CORE, [(0, 1), (1, 0)])


def dot(left, right):
    return jnp.dot(left, right, preferred_element_type=F32)


def dot_tn(left, right):
    return lax.dot_general(left, right, (((0,), (0,)), ((), ())), preferred_element_type=F32)


def dot_nt(left, right):
    return lax.dot_general(left, right, (((1,), (1,)), ((), ())), preferred_element_type=F32)


def sigmoid(value):
    return 0.5 + 0.5 * jnp.tanh(0.5 * value)


def normalize(value):
    centered = value - jnp.mean(value, axis=-1, keepdims=True)
    scale_inv = lax.rsqrt(jnp.mean(centered * centered, axis=-1, keepdims=True) + EPS)
    return centered * scale_inv, scale_inv


def norm_back(normed, scale_inv, gain, upstream):
    scaled = upstream * gain
    inner = (
        scaled
        - jnp.mean(scaled, axis=-1, keepdims=True)
        - normed * jnp.mean(scaled * normed, axis=-1, keepdims=True)
    )
    return inner * scale_inv


def columns_of(ids):
    rows, lanes = ids.shape
    padded = -(-rows // 8) * 8
    if padded > rows:
        ids = jnp.concatenate([ids, jnp.zeros((padded - rows, lanes), ids.dtype)], axis=0)
    return ids.T


def hot_rows(columns, tiles, base, count):
    parts = []
    for tile in tiles:
        column = columns[:, tile : tile + 1] - base
        lanes = lax.broadcasted_iota(jnp.int32, (columns.shape[0], count), 1)
        parts.append(jnp.where(lanes == column, 1.0, 0.0).astype(BF16))
    return jnp.concatenate(parts, axis=0) if len(parts) > 1 else parts[0]


def hot_columns(ids, tiles, base, count):
    parts = []
    for tile in tiles:
        row = ids[tile : tile + 1, :] - base
        subs = lax.broadcasted_iota(jnp.int32, (count, ids.shape[1]), 0)
        parts.append(jnp.where(subs == row, 1.0, 0.0).astype(BF16))
    return jnp.concatenate(parts, axis=1) if len(parts) > 1 else parts[0]


def list_hot(ids, count):
    directions, slots = ids.shape
    wide = jnp.concatenate([ids, jnp.zeros((directions, 128 - slots), ids.dtype)], axis=1)
    columns = wide.T
    parts = []
    for k in range(directions):
        lanes = lax.broadcasted_iota(jnp.int32, (slots, count), 1)
        parts.append(jnp.where(lanes == columns[:slots, k : k + 1], 1.0, 0.0).astype(BF16))
    return jnp.concatenate(parts, axis=0)


def live_rows(count_ref, tile_rows, rows):
    index = lax.broadcasted_iota(jnp.int32, (rows, 1), 0)
    return jnp.where(index < count_ref[0] * tile_rows, 1.0, 0.0)


def fetch_all(sources, targets, sems):
    copies = [
        pltpu.make_async_copy(source, target, sems.at[i])
        for i, (source, target) in enumerate(zip(sources, targets))
    ]
    for copy in copies:
        copy.start()
    return copies


def send_kernel(nodes_hbm, list_hbm, low, mid, high, nodes, send_list, sems):
    slots = send_list.shape[1]
    for copy in fetch_all([list_hbm, nodes_hbm], [send_list, nodes], sems):
        copy.wait()
    rows = dot(list_hot(send_list[...], nodes.shape[0]), nodes[...]).astype(BF16)
    low[...] = rows[: 3 * slots]
    mid[...] = rows[3 * slots : 5 * slots]
    high[...] = rows[5 * slots :]


def index_kernel(sources, *refs):
    fetched, refs = refs[:sources], refs[sources:]
    near_rows, halo_rows = refs[:2]
    targets, sems = refs[2:-1], refs[-1]
    senders, receivers = targets[:2]
    copies = fetch_all(fetched, targets, sems)
    for copy in copies[:2]:
        copy.wait()
    tile_rows = senders.shape[1]
    count = near_rows.shape[1] // 2
    by_sender = columns_of(senders[...])
    by_receiver = columns_of(receivers[...])
    for tile in range(senders.shape[0]):
        rows = slice(tile * tile_rows, (tile + 1) * tile_rows)
        near_rows[rows, :count] = hot_rows(by_sender, [tile], 0, count)
        near_rows[rows, count:] = hot_rows(by_receiver, [tile], 0, count)
        halo_rows[rows, :] = hot_rows(by_sender, [tile], count, halo_rows.shape[1])
    for copy in copies[2:]:
        copy.wait()


def local_kernel(
    nodes, edges, senders, receivers, near_rows, w_in, pre, sender_columns, receiver_columns
):
    width = nodes.shape[1]
    tile_rows = senders.shape[1]
    extended = sender_columns.shape[0]
    count = receiver_columns.shape[0]
    sender_ids = senders[...]
    receiver_ids = receivers[...]
    for tile in range(senders.shape[0]):
        rows = slice(tile * tile_rows, (tile + 1) * tile_rows)
        sender_columns[:, rows] = hot_columns(sender_ids, [tile], 0, extended)
        receiver_columns[:, rows] = hot_columns(receiver_ids, [tile], 0, count)
    x = nodes[...]
    table = jnp.concatenate(
        [
            dot(x, w_in[width : 2 * width]).astype(BF16),
            dot(x, w_in[2 * width :]).astype(BF16),
        ],
        axis=0,
    )
    pre[...] = dot(edges[...], w_in[:width]) + dot(near_rows[...], table)


def split_by_core(sums, first, keep_out, away_out):
    half = sums.shape[0] // 2
    core = lax.axis_index(CORE)
    keep_out[first : first + half] = sums[pl.ds(pl.multiple_of(core * half, half), half), :]
    away = sums[pl.ds(pl.multiple_of((1 - core) * half, half), half), :]
    away_out[first : first + half] = away.astype(BF16)


def pack_gains(edge_gain, node_gain):
    edge_high = edge_gain.astype(BF16).astype(F32)
    node_high = node_gain.astype(BF16).astype(F32)
    row = lax.broadcasted_iota(jnp.int32, (16, edge_gain.shape[1]), 0)
    packed = jnp.where(row == 0, edge_high, 0.0)
    packed = jnp.where(row == 1, edge_gain - edge_high, packed)
    packed = jnp.where(row == 2, node_high, packed)
    packed = jnp.where(row == 3, node_gain - node_high, packed)
    return packed.astype(BF16)


def layer_kernel(
    tile_rows,
    count_ref,
    nodes,
    node_grads,
    edges,
    edge_grads,
    pre_local,
    halo_rows,
    near_rows,
    sender_columns,
    receiver_columns,
    from_high,
    from_low,
    upward,
    downward,
    w_in,
    w_out,
    gain_edge,
    w_node_in,
    w_node_out,
    gain_node,
    pre_grad_out,
    sender_out,
    receiver_out,
    node_part_out,
    across_out,
    rest_out,
    keep_out,
    away_out,
    gains_out,
    slope_kept,
    hidden_kept,
    normed_kept,
    scale_kept,
    node_sums,
    edge_sums,
):
    count, width = nodes.shape
    edge_rows = edges.shape[0]
    live = live_rows(count_ref, tile_rows, edge_rows)
    slots = from_high.shape[0] // 3
    halo = jnp.concatenate(
        [
            downward[:slots],
            from_high[slots : 2 * slots],
            upward[:slots],
            downward[slots : 2 * slots],
            upward[slots : 2 * slots],
            downward[2 * slots :],
            from_low[slots : 2 * slots],
            upward[2 * slots :],
        ],
        axis=0,
    )
    table = dot(halo, w_in[width : 2 * width]).astype(BF16)
    gain = gain_edge[...].astype(F32)[None, :]
    value = pre_local[...] + dot(halo_rows[...], table)
    sigma = sigmoid(value)
    hidden = (value * sigma).astype(BF16)
    hidden_kept[...] = hidden
    slope_kept[...] = sigma * (1.0 + value * (1.0 - sigma))
    edge_normed, edge_scale = normalize(dot(hidden, w_out[...]))
    normed_kept[...] = edge_normed
    scale_kept[...] = jnp.broadcast_to(edge_scale, (edge_rows, 128))
    message = (live * gain * edge_normed).astype(BF16)
    total = dot(receiver_columns[...], message)
    aggregated = total.astype(BF16)
    x = nodes[...]
    w_first = w_node_in[:width]
    w_second = w_node_in[width:]
    node_pre = dot(x, w_first) + dot(aggregated, w_second)
    sigma = sigmoid(node_pre)
    node_hidden = (node_pre * sigma).astype(BF16)
    normed, scale_inv = normalize(dot(node_hidden, w_node_out[...]))
    upstream = node_grads[...].astype(F32)
    out_grad = norm_back(normed, scale_inv, gain_node[...].astype(F32)[None, :], upstream).astype(BF16)
    slope = sigma * (1.0 + node_pre * (1.0 - sigma))
    pre_grad = (dot_nt(out_grad, w_node_out[...]) * slope).astype(BF16)
    agg_grad = dot_nt(pre_grad, w_second).astype(BF16)
    node_part_out[...] = upstream + dot_nt(pre_grad, w_first)
    node_sums[:width] = dot_tn(x, pre_grad)
    node_sums[width : 2 * width] = dot_tn(aggregated, pre_grad)
    node_sums[2 * width : 3 * width] = dot_tn(node_hidden, out_grad)
    node_gain = jnp.sum(upstream * normed, axis=0, keepdims=True)
    upstream = live * (
        edge_grads[...].astype(F32) + dot(near_rows[:, count:], agg_grad)
    )
    edge_normed = normed_kept[...]
    edge_gain = jnp.sum(upstream * edge_normed, axis=0, keepdims=True)
    out_grad = norm_back(edge_normed, scale_kept[:, :1], gain, upstream).astype(BF16)
    pre_grad = (dot_nt(out_grad, w_out[...]) * slope_kept[...]).astype(BF16)
    pre_grad_out[...] = pre_grad
    sender_total = dot(sender_columns[...], pre_grad)
    receiver_total = dot(receiver_columns[...], pre_grad)
    own = sender_total[:count].astype(BF16)
    away = sender_total[count:].astype(BF16)
    received = receiver_total.astype(BF16)
    sender_out[...] = own
    receiver_out[...] = received
    halo_grad = dot_nt(away, w_in[width : 2 * width]).astype(BF16)
    parts = [halo_grad[k * slots : (k + 1) * slots] for k in range(8)]
    up = jnp.concatenate([parts[0], parts[3], parts[5]], axis=0)
    down = jnp.concatenate([parts[2], parts[4], parts[7]], axis=0)
    core = lax.axis_index(CORE)
    sums_rows = gains_out.shape[0] + keep_out.shape[0]

    @pl.when(core == 0)
    def _():
        away_out[sums_rows:] = up
        across_out[...] = down

    @pl.when(core == 1)
    def _():
        away_out[sums_rows:] = down
        across_out[...] = up

    rest_out[...] = jnp.concatenate([parts[1], parts[6]], axis=0)
    edge_sums[:width] = dot_tn(edges[...], pre_grad)
    edge_sums[width : 2 * width] = dot_tn(x, own) + dot_tn(halo, away)
    edge_sums[2 * width : 3 * width] = dot_tn(x, received)
    edge_sums[3 * width : 4 * width] = dot_tn(hidden_kept[...], out_grad)
    split_by_core(edge_sums, 0, keep_out, away_out)
    split_by_core(node_sums, edge_sums.shape[0] // 2, keep_out, away_out)
    gains = pack_gains(edge_gain, node_gain)
    away_out[keep_out.shape[0] : sums_rows] = gains
    gains_out[...] = gains


def pair_kernel(parts, keep, gains, other, *outs):
    rows = keep.shape[0]
    packed = gains.shape[0]
    members = len(outs)
    both = gains[...].astype(F32) + other[rows : rows + packed].astype(F32)
    summed = pack_gains(both[0:1] + both[1:2], both[2:3] + both[3:4])
    me = place_in_square()
    for offset, out in enumerate(outs):
        owner = me ^ offset
        out[:packed] = summed
        first, at = 0, packed
        for part in parts:
            step = part // members
            source = pl.ds(pl.multiple_of(first + owner * step, 16), step)
            out[at : at + step] = (keep[source, :] + other[source, :].astype(F32)).astype(BF16)
            first, at = first + part, at + step


def add_packed(values):
    packed = 16
    gains = values[:packed]
    return pack_gains(gains[0:1] + gains[1:2], gains[2:3] + gains[3:4])


def sum_kernel(*refs):
    sums_out = refs[-1]
    sums = tree_sum([block[...].astype(F32) for block in refs[:-1]])
    sums_out[...] = sums.astype(BF16)
    sums_out[:16] = add_packed(sums)


def join_kernel(own, other, sums_out):
    sums = own[...].astype(F32) + other[...].astype(F32)
    sums_out[...] = sums.astype(BF16)
    sums_out[:16] = add_packed(sums)


def whole_kernel(own, other, gains_out, mine):
    packed = gains_out.shape[0]
    sums = own[...].astype(F32) + other[...].astype(F32)
    gains_out[...] = sums[:packed]
    mine[...] = sums[packed:].astype(BF16)


def place_kernel(parts, *refs):
    count = 2 * len(parts)
    sems, wholes = refs[-1], refs[-1 - len(parts) : -1]
    outs = refs[-1 - len(parts) - count : -1 - len(parts)]
    blocks = refs[: -1 - len(parts) - count]
    members = len(blocks) // 2
    core = lax.axis_index(CORE)
    me = place_in_square()
    for position, block in enumerate(blocks):
        half = core if position < members else 1 - core
        owner = me ^ (position % members)
        at = 0
        for part, whole in zip(parts, wholes):
            step = part // members
            row = pl.multiple_of(half * part + owner * step, 16)
            whole[pl.ds(row, step), :] = block[at : at + step]
            at += step
    copies = []
    for i, whole in enumerate(wholes):
        cut = outs[2 * i].shape[0]
        copies.append(pltpu.make_async_copy(whole.at[:cut], outs[2 * i], sems.at[2 * i]))
        copies.append(pltpu.make_async_copy(whole.at[cut:], outs[2 * i + 1], sems.at[2 * i + 1]))
    for copy in copies:
        copy.start()
    for copy in copies:
        copy.wait()


def finish_kernel(
    edge_grads, pre_grad, sender_sum, receiver_sum, node_part, w_in, edges_grad, local_grad
):
    width = w_in.shape[1]
    edges_grad[...] = (
        edge_grads[...].astype(F32) + dot_nt(pre_grad[...], w_in[:width])
    ).astype(BF16)
    local_grad[...] = (
        node_part[...]
        + dot_nt(sender_sum[...], w_in[width : 2 * width])
        + dot_nt(receiver_sum[...], w_in[2 * width :])
    )


def turn_kernel(other, across, rest, high, low, middle):
    slots = rest.shape[0] // 2
    first = other.shape[0] - 3 * slots

    def turn(up_back, down_back):
        high[:slots] = up_back[:slots]
        high[slots : 2 * slots] = down_back[:slots]
        high[2 * slots :] = rest[:slots]
        low[:slots] = up_back[2 * slots :]
        low[slots : 2 * slots] = down_back[2 * slots :]
        low[2 * slots :] = rest[slots:]
        middle[:slots] = up_back[slots : 2 * slots]
        middle[slots:] = down_back[slots : 2 * slots]

    core = lax.axis_index(CORE)

    @pl.when(core == 0)
    def _():
        turn(across, other.at[first:])

    @pl.when(core == 1)
    def _():
        turn(other.at[first:], across)


def return_kernel(send_list, local_grad, middle, to_high, to_low, nodes_grad):
    slots = send_list.shape[1]

    def block(ref, k):
        return ref[k * slots : (k + 1) * slots]

    returned = jnp.concatenate(
        [
            block(to_high, 0),
            block(to_high, 2),
            block(to_high, 1),
            block(middle, 0),
            block(middle, 1),
            block(to_low, 0),
            block(to_low, 2),
            block(to_low, 1),
        ],
        axis=0,
    )
    hot = list_hot(send_list[...], local_grad.shape[0])
    nodes_grad[...] = (local_grad[...] + dot_tn(hot, returned)).astype(BF16)


SMEM = pltpu.SMEM
VMEM = pltpu.VMEM
HBM = pltpu.HBM


def call(body, outs, flops, *operands, spaces=(), out_space=VMEM, scratch=()):
    moved = sum(x.size * x.dtype.itemsize for x in operands)
    moved += sum(x.size * jnp.dtype(x.dtype).itemsize for x in outs)
    spaces = list(spaces) + [VMEM] * (len(operands) - len(spaces))
    out_spaces = out_space if isinstance(out_space, list) else [out_space] * len(outs)
    operands = [
        pltpu.with_memory_space_constraint(x, HBM) if space is HBM else x
        for x, space in zip(operands, spaces)
    ]
    return pl.pallas_call(
        body,
        out_shape=outs,
        in_specs=[pl.BlockSpec(memory_space=space) for space in spaces],
        out_specs=[pl.BlockSpec(memory_space=space) for space in out_spaces],
        scratch_shapes=list(scratch),
        compiler_params=pltpu.CompilerParams(vmem_limit_bytes=VMEM_LIMIT),
        cost_estimate=pl.CostEstimate(flops=flops, bytes_accessed=moved, transcendentals=0),
    )(*operands)


def like(array):
    return jax.ShapeDtypeStruct(array.shape, array.dtype)


def shaped(rows, columns, dtype):
    return jax.ShapeDtypeStruct((rows, columns), dtype)


def placed(parts, blocks, width):
    return call(
        functools.partial(place_kernel, parts),
        [
            shaped(3 * width, width, BF16),
            shaped(width, width, BF16),
            shaped(2 * width, width, BF16),
            shaped(width, width, BF16),
        ],
        0,
        *blocks,
        out_space=HBM,
        scratch=[pltpu.VMEM((2 * part, width), BF16) for part in parts]
        + [pltpu.SemaphoreType.DMA((2 * len(parts),))],
    )


def joined(sums, packed, *beside):
    rows, width = sums.shape
    size = lax.axis_size(FAR)
    distance = 1
    while True:
        other = lax.ppermute(sums, FAR, [(i, i ^ distance) for i in range(size)])
        distance *= 2
        if distance == size:
            break
        (sums,) = call(join_kernel, [like(sums)], 0, sums, other)
    other, *beside = lax.optimization_barrier((other, *beside))
    gains, mine = call(
        whole_kernel,
        [shaped(packed, width, F32), shaped(rows - packed, width, BF16)],
        0,
        sums,
        other,
    )
    return gains, mine, *beside


def on_device(
    nodes,
    edges,
    edge_grads,
    node_grads,
    send_list,
    senders,
    receivers,
    tile_count,
    w_edge_in,
    w_edge_out,
    gain_edge,
    w_node_in,
    w_node_out,
    gain_node,
):
    count, width = nodes.shape
    slots = send_list.shape[1]
    halo_rows = 8 * slots
    edge_rows = edges.shape[0]
    tile_rows = senders.shape[1]
    square = 2 * width * width
    low, mid, high, nodes, send_list = call(
        send_kernel,
        [
            shaped(3 * slots, width, BF16),
            shaped(2 * slots, width, BF16),
            shaped(3 * slots, width, BF16),
            like(nodes),
            like(send_list),
        ],
        2 * halo_rows * count * width,
        nodes,
        send_list,
        spaces=[HBM, HBM],
        scratch=[pltpu.SemaphoreType.DMA((2,))],
    )
    from_low = passed_along(high, PX, 1)
    from_high = passed_along(low, PX, -1)
    fetched = [
        senders,
        receivers,
        edges,
        w_edge_in,
        w_edge_out,
        gain_edge,
        w_node_in,
        w_node_out,
        gain_node,
        node_grads,
        edge_grads,
    ]
    near_hot, halo_hot, *fetched = call(
        functools.partial(index_kernel, len(fetched)),
        [
            shaped(edge_rows, 2 * count, BF16),
            shaped(edge_rows, halo_rows, BF16),
        ]
        + [like(x) for x in fetched],
        0,
        *fetched,
        spaces=[HBM] * len(fetched),
        scratch=[pltpu.SemaphoreType.DMA((len(fetched),))],
    )
    (
        senders,
        receivers,
        edges,
        w_edge_in,
        w_edge_out,
        gain_edge,
        w_node_in,
        w_node_out,
        gain_node,
        node_grads,
        edge_grads,
    ) = fetched
    from_low, from_high, near_hot = lax.optimization_barrier((from_low, from_high, near_hot))
    upward = passed_along(
        jnp.concatenate([from_high[2 * slots :], mid[slots:], from_low[2 * slots :]]), PY, 1
    )
    downward = passed_along(
        jnp.concatenate([from_high[:slots], mid[:slots], from_low[:slots]]), PY, -1
    )
    pre_local, sender_columns, receiver_columns = call(
        local_kernel,
        [
            shaped(edge_rows, width, F32),
            shaped(count + halo_rows, edge_rows, BF16),
            shaped(count, edge_rows, BF16),
        ],
        square * (2 * count + edge_rows) + 4 * edge_rows * count * width,
        nodes,
        edges,
        senders,
        receivers,
        near_hot,
        w_edge_in,
    )
    parts = (2 * width, 3 * width // 2)
    halves = sum(parts)
    pre_grad, sender_sum, receiver_sum, node_part, across, rest, keep, away, gains = call(
        functools.partial(layer_kernel, tile_rows),
        [
            shaped(edge_rows, width, BF16),
            shaped(count, width, BF16),
            shaped(count, width, BF16),
            shaped(count, width, F32),
            shaped(3 * slots, width, BF16),
            shaped(2 * slots, width, BF16),
            shaped(halves, width, F32),
            shaped(halves + 16 + 3 * slots, width, BF16),
            shaped(16, width, BF16),
        ],
        square * (6 * edge_rows + 11 * count + 2 * halo_rows)
        + 2 * edge_rows * (4 * count + halo_rows) * width,
        tile_count,
        nodes,
        node_grads,
        edges,
        edge_grads,
        pre_local,
        halo_hot,
        near_hot,
        sender_columns,
        receiver_columns,
        from_high,
        from_low,
        upward,
        downward,
        w_edge_in,
        w_edge_out,
        gain_edge,
        w_node_in,
        w_node_out,
        gain_node,
        spaces=[SMEM],
        scratch=[
            pltpu.VMEM((edge_rows, width), F32),
            pltpu.VMEM((edge_rows, width), BF16),
            pltpu.VMEM((edge_rows, width), F32),
            pltpu.VMEM((edge_rows, 128), F32),
            pltpu.VMEM((3 * width, width), F32),
            pltpu.VMEM((4 * width, width), F32),
        ],
    )
    other = across_cores(away)
    members = square_members()
    own, *blocks = call(
        functools.partial(pair_kernel, parts),
        [shaped(16 + halves // members, width, BF16)] * members,
        0,
        keep,
        gains,
        other,
    )
    received = [in_square(block, offset) for offset, block in enumerate(blocks, 1)]
    high, low, middle = call(
        turn_kernel,
        [
            shaped(3 * slots, width, BF16),
            shaped(3 * slots, width, BF16),
            shaped(2 * slots, width, BF16),
        ],
        10**10,
        other,
        across_chips(across),
        rest,
    )
    *received, high, low = lax.optimization_barrier((*received, high, low))
    (sums,) = call(sum_kernel, [like(own)], 0, own, *received)
    gains, mine, to_high, to_low = joined(
        sums, gains.shape[0], passed_along(high, PX, 1), passed_along(low, PX, -1)
    )
    blocks = [mine] + [in_square(mine, offset) for offset in range(1, members)]
    blocks += [across_cores(block) for block in blocks]
    edges_grad, local_grad = call(
        finish_kernel,
        [shaped(edge_rows, width, BF16), shaped(count, width, F32)],
        square * (edge_rows + 2 * count),
        edge_grads,
        pre_grad,
        sender_sum,
        receiver_sum,
        node_part,
        w_edge_in,
    )
    (nodes_grad,) = call(
        return_kernel,
        [shaped(count, width, BF16)],
        2 * halo_rows * count * width,
        send_list,
        local_grad,
        middle,
        to_high,
        to_low,
    )
    *blocks, nodes_grad, edges_grad = lax.optimization_barrier((*blocks, nodes_grad, edges_grad))
    w_edge_in_grad, w_edge_out_grad, w_node_in_grad, w_node_out_grad = placed(
        parts, blocks, width
    )
    return (
        nodes_grad,
        edges_grad,
        w_edge_in_grad,
        w_edge_out_grad,
        (gains[0] + gains[1]).astype(BF16),
        w_node_in_grad,
        w_node_out_grad,
        (gains[2] + gains[3]).astype(BF16),
    )


def solution(mesh):
    in_specs = (
        P(("groups",) + PX + PY, None),
        P(("groups",) + PX + PY, None),
        P(("groups",) + PX + PY, None),
        P(("groups",) + PX + PY, None),
        P(("groups",) + PX + PY, None),
        P(("groups",) + PX + PY, None),
        P(("groups",) + PX + PY, None),
        P(("groups",) + PX + PY),
        P(),
        P(),
        P(),
        P(),
        P(),
        P(),
    )
    out_specs = (
        P(("groups",) + PX + PY, None),
        P(("groups",) + PX + PY, None),
        P("groups", None),
        P("groups", None),
        P("groups"),
        P("groups", None),
        P("groups", None),
        P("groups"),
    )
    groups, px, py = mesh.devices.shape
    by_core = jax.sharding.Mesh(
        mesh.devices.reshape(groups, px // 2, 2, py // 2, 2), ("groups",) + PX + PY
    )
    return jax.shard_map(
        on_device, mesh=by_core, in_specs=in_specs, out_specs=out_specs, check_vma=False
    )
```

```python
import functools

import jax
import jax.numpy as jnp
from jax import lax
from jax.experimental import pallas as pl
from jax.experimental.pallas import tpu as pltpu
from jax.sharding import PartitionSpec as P

EPS = 1e-05
BF16 = jnp.bfloat16
F32 = jnp.float32
VMEM_LIMIT = 24 * 1024 * 1024


CORE = "core"
FAR = "far"
PX = (FAR, "near")
PY = ("side", CORE)
SQUARE = ("near", "side")


def passed_along(array, axis, by):
    size = lax.axis_size(axis)
    return lax.ppermute(array, axis, [(i, (i + by) % size) for i in range(size)])


def across_chips(array):
    size = lax.axis_size(PY)
    pairs = [(i, (i + 1 if i % 2 else i - 1) % size) for i in range(size)]
    return lax.ppermute(array, PY, pairs)


def square_members():
    return lax.axis_size(SQUARE)


def place_in_square():
    near, side = SQUARE
    return lax.axis_index(near) * lax.axis_size(side) + lax.axis_index(side)


def in_square(array, offset):
    return lax.ppermute(array, SQUARE, [(i, i ^ offset) for i in range(square_members())])


def tree_sum(terms):
    while len(terms) > 1:
        terms = [terms[i] + terms[i + 1] for i in range(0, len(terms), 2)]
    return terms[0]


def across_cores(array):
    return lax.ppermute(array, CORE, [(0, 1), (1, 0)])


def dot(left, right):
    return jnp.dot(left, right, preferred_element_type=F32)


def dot_tn(left, right):
    return lax.dot_general(left, right, (((0,), (0,)), ((), ())), preferred_element_type=F32)


def dot_nt(left, right):
    return lax.dot_general(left, right, (((1,), (1,)), ((), ())), preferred_element_type=F32)


def sigmoid(value):
    return 0.5 + 0.5 * jnp.tanh(0.5 * value)


def normalize(value):
    centered = value - jnp.mean(value, axis=-1, keepdims=True)
    scale_inv = lax.rsqrt(jnp.mean(centered * centered, axis=-1, keepdims=True) + EPS)
    return centered * scale_inv, scale_inv


def norm_back(normed, scale_inv, gain, upstream):
    scaled = upstream * gain
    inner = (
        scaled
        - jnp.mean(scaled, axis=-1, keepdims=True)
        - normed * jnp.mean(scaled * normed, axis=-1, keepdims=True)
    )
    return inner * scale_inv


def columns_of(ids):
    rows, lanes = ids.shape
    padded = -(-rows // 8) * 8
    if padded > rows:
        ids = jnp.concatenate([ids, jnp.zeros((padded - rows, lanes), ids.dtype)], axis=0)
    return ids.T


def hot_rows(columns, tiles, base, count):
    parts = []
    for tile in tiles:
        column = columns[:, tile : tile + 1] - base
        lanes = lax.broadcasted_iota(jnp.int32, (columns.shape[0], count), 1)
        parts.append(jnp.where(lanes == column, 1.0, 0.0).astype(BF16))
    return jnp.concatenate(parts, axis=0) if len(parts) > 1 else parts[0]


def hot_columns(ids, tiles, base, count):
    parts = []
    for tile in tiles:
        row = ids[tile : tile + 1, :] - base
        subs = lax.broadcasted_iota(jnp.int32, (count, ids.shape[1]), 0)
        parts.append(jnp.where(subs == row, 1.0, 0.0).astype(BF16))
    return jnp.concatenate(parts, axis=1) if len(parts) > 1 else parts[0]


def list_hot(ids, count):
    directions, slots = ids.shape
    wide = jnp.concatenate([ids, jnp.zeros((directions, 128 - slots), ids.dtype)], axis=1)
    columns = wide.T
    parts = []
    for k in range(directions):
        lanes = lax.broadcasted_iota(jnp.int32, (slots, count), 1)
        parts.append(jnp.where(lanes == columns[:slots, k : k + 1], 1.0, 0.0).astype(BF16))
    return jnp.concatenate(parts, axis=0)


def live_rows(count_ref, tile_rows, rows):
    index = lax.broadcasted_iota(jnp.int32, (rows, 1), 0)
    return jnp.where(index < count_ref[0] * tile_rows, 1.0, 0.0)


def fetch_all(sources, targets, sems):
    copies = [
        pltpu.make_async_copy(source, target, sems.at[i])
        for i, (source, target) in enumerate(zip(sources, targets))
    ]
    for copy in copies:
        copy.start()
    return copies


def send_kernel(nodes_hbm, list_hbm, low, mid, high, nodes, send_list, sems):
    slots = send_list.shape[1]
    for copy in fetch_all([list_hbm, nodes_hbm], [send_list, nodes], sems):
        copy.wait()
    rows = dot(list_hot(send_list[...], nodes.shape[0]), nodes[...]).astype(BF16)
    low[...] = rows[: 3 * slots]
    mid[...] = rows[3 * slots : 5 * slots]
    high[...] = rows[5 * slots :]


def index_kernel(sources, *refs):
    fetched, refs = refs[:sources], refs[sources:]
    near_rows, halo_rows = refs[:2]
    targets, sems = refs[2:-1], refs[-1]
    senders, receivers = targets[:2]
    copies = fetch_all(fetched, targets, sems)
    for copy in copies[:2]:
        copy.wait()
    tile_rows = senders.shape[1]
    count = near_rows.shape[1] // 2
    by_sender = columns_of(senders[...])
    by_receiver = columns_of(receivers[...])
    for tile in range(senders.shape[0]):
        rows = slice(tile * tile_rows, (tile + 1) * tile_rows)
        near_rows[rows, :count] = hot_rows(by_sender, [tile], 0, count)
        near_rows[rows, count:] = hot_rows(by_receiver, [tile], 0, count)
        halo_rows[rows, :] = hot_rows(by_sender, [tile], count, halo_rows.shape[1])
    for copy in copies[2:]:
        copy.wait()


def local_kernel(
    nodes, edges, senders, receivers, near_rows, w_in, pre, sender_columns, receiver_columns
):
    width = nodes.shape[1]
    tile_rows = senders.shape[1]
    extended = sender_columns.shape[0]
    count = receiver_columns.shape[0]
    sender_ids = senders[...]
    receiver_ids = receivers[...]
    for tile in range(senders.shape[0]):
        rows = slice(tile * tile_rows, (tile + 1) * tile_rows)
        sender_columns[:, rows] = hot_columns(sender_ids, [tile], 0, extended)
        receiver_columns[:, rows] = hot_columns(receiver_ids, [tile], 0, count)
    x = nodes[...]
    table = jnp.concatenate(
        [
            dot(x, w_in[width : 2 * width]).astype(BF16),
            dot(x, w_in[2 * width :]).astype(BF16),
        ],
        axis=0,
    )
    pre[...] = dot(edges[...], w_in[:width]) + dot(near_rows[...], table)


def split_by_core(sums, keep_out, away_out):
    half = sums.shape[0] // 2
    core = lax.axis_index(CORE)
    keep_out[...] = sums[pl.ds(pl.multiple_of(core * half, half), half), :]
    away = sums[pl.ds(pl.multiple_of((1 - core) * half, half), half), :]
    away_out[:half] = away.astype(BF16)


def pack_gains(edge_gain, node_gain):
    edge_high = edge_gain.astype(BF16).astype(F32)
    node_high = node_gain.astype(BF16).astype(F32)
    row = lax.broadcasted_iota(jnp.int32, (16, edge_gain.shape[1]), 0)
    packed = jnp.where(row == 0, edge_high, 0.0)
    packed = jnp.where(row == 1, edge_gain - edge_high, packed)
    packed = jnp.where(row == 2, node_high, packed)
    packed = jnp.where(row == 3, node_gain - node_high, packed)
    return packed.astype(BF16)


def layer_kernel(
    tile_rows,
    count_ref,
    nodes,
    node_grads,
    edges,
    edge_grads,
    pre_local,
    halo_rows,
    near_rows,
    sender_columns,
    receiver_columns,
    from_high,
    from_low,
    upward,
    downward,
    w_in,
    w_out,
    gain_edge,
    w_node_in,
    w_node_out,
    gain_node,
    pre_grad_out,
    sender_out,
    receiver_out,
    node_part_out,
    top_out,
    middle_out,
    bottom_out,
    edge_keep,
    edge_away,
    node_keep,
    node_away,
    gains_out,
    slope_kept,
    hidden_kept,
    normed_kept,
    scale_kept,
    node_sums,
    edge_sums,
):
    count, width = nodes.shape
    edge_rows = edges.shape[0]
    live = live_rows(count_ref, tile_rows, edge_rows)
    slots = from_high.shape[0] // 3
    halo = jnp.concatenate(
        [
            downward[:slots],
            from_high[slots : 2 * slots],
            upward[:slots],
            downward[slots : 2 * slots],
            upward[slots : 2 * slots],
            downward[2 * slots :],
            from_low[slots : 2 * slots],
            upward[2 * slots :],
        ],
        axis=0,
    )
    table = dot(halo, w_in[width : 2 * width]).astype(BF16)
    gain = gain_edge[...].astype(F32)[None, :]
    value = pre_local[...] + dot(halo_rows[...], table)
    sigma = sigmoid(value)
    hidden = (value * sigma).astype(BF16)
    hidden_kept[...] = hidden
    slope_kept[...] = sigma * (1.0 + value * (1.0 - sigma))
    edge_normed, edge_scale = normalize(dot(hidden, w_out[...]))
    normed_kept[...] = edge_normed
    scale_kept[...] = jnp.broadcast_to(edge_scale, (edge_rows, 128))
    message = (live * gain * edge_normed).astype(BF16)
    total = dot(receiver_columns[...], message)
    aggregated = total.astype(BF16)
    x = nodes[...]
    w_first = w_node_in[:width]
    w_second = w_node_in[width:]
    node_pre = dot(x, w_first) + dot(aggregated, w_second)
    sigma = sigmoid(node_pre)
    node_hidden = (node_pre * sigma).astype(BF16)
    normed, scale_inv = normalize(dot(node_hidden, w_node_out[...]))
    upstream = node_grads[...].astype(F32)
    out_grad = norm_back(normed, scale_inv, gain_node[...].astype(F32)[None, :], upstream).astype(BF16)
    slope = sigma * (1.0 + node_pre * (1.0 - sigma))
    pre_grad = (dot_nt(out_grad, w_node_out[...]) * slope).astype(BF16)
    agg_grad = dot_nt(pre_grad, w_second).astype(BF16)
    node_part_out[...] = upstream + dot_nt(pre_grad, w_first)
    node_sums[:width] = dot_tn(x, pre_grad)
    node_sums[width : 2 * width] = dot_tn(aggregated, pre_grad)
    node_sums[2 * width : 3 * width] = dot_tn(node_hidden, out_grad)
    node_gain = jnp.sum(upstream * normed, axis=0, keepdims=True)
    upstream = live * (
        edge_grads[...].astype(F32) + dot(near_rows[:, count:], agg_grad)
    )
    edge_normed = normed_kept[...]
    edge_gain = jnp.sum(upstream * edge_normed, axis=0, keepdims=True)
    out_grad = norm_back(edge_normed, scale_kept[:, :1], gain, upstream).astype(BF16)
    pre_grad = (dot_nt(out_grad, w_out[...]) * slope_kept[...]).astype(BF16)
    pre_grad_out[...] = pre_grad
    sender_total = dot(sender_columns[...], pre_grad)
    receiver_total = dot(receiver_columns[...], pre_grad)
    own = sender_total[:count].astype(BF16)
    away = sender_total[count:].astype(BF16)
    received = receiver_total.astype(BF16)
    sender_out[...] = own
    receiver_out[...] = received
    halo_grad = dot_nt(away, w_in[width : 2 * width]).astype(BF16)
    top_out[...] = halo_grad[: 3 * slots]
    middle_out[...] = halo_grad[3 * slots : 5 * slots]
    bottom_out[...] = halo_grad[5 * slots :]
    edge_sums[:width] = dot_tn(edges[...], pre_grad)
    edge_sums[width : 2 * width] = dot_tn(x, own) + dot_tn(halo, away)
    edge_sums[2 * width : 3 * width] = dot_tn(x, received)
    edge_sums[3 * width : 4 * width] = dot_tn(hidden_kept[...], out_grad)
    split_by_core(edge_sums, edge_keep, edge_away)
    split_by_core(node_sums, node_keep, node_away)
    gains = pack_gains(edge_gain, node_gain)
    edge_away[edge_keep.shape[0] :] = gains
    gains_out[...] = gains


def pair_kernel(packed, keep, *refs):
    gains, other, outs = (refs[0], refs[1], refs[2:]) if packed else (None, refs[0], refs[1:])
    rows = keep.shape[0]
    step = rows // len(outs)
    me = place_in_square()
    for offset, out in enumerate(outs):
        source = pl.ds(pl.multiple_of((me ^ offset) * step, 16), step)
        out[packed:] = (keep[source, :] + other[source, :].astype(F32)).astype(BF16)
    if packed:
        both = gains[...].astype(F32) + other[rows:].astype(F32)
        summed = pack_gains(both[0:1] + both[1:2], both[2:3] + both[3:4])
        for out in outs:
            out[:packed] = summed


def store_sums(packed, sums, sums_out):
    sums_out[...] = sums.astype(BF16)
    if packed:
        sums_out[:packed] = pack_gains(sums[0:1] + sums[1:2], sums[2:3] + sums[3:4])


def sum_kernel(packed, *refs):
    store_sums(packed, tree_sum([block[...].astype(F32) for block in refs[:-1]]), refs[-1])


def whole_kernel(packed, own, other, mine, *gains_out):
    sums = own[...].astype(F32) + other[...].astype(F32)
    mine[...] = sums[packed:].astype(BF16)
    for out in gains_out:
        out[...] = sums[:packed]


def place_kernel(*refs):
    blocks, first, second, whole, sems = refs[:-4], *refs[-4:]
    members = len(blocks) // 2
    core = lax.axis_index(CORE)
    me = place_in_square()
    for position, block in enumerate(blocks):
        half = core if position < members else 1 - core
        owner = me ^ (position % members)
        step = block.shape[0]
        row = pl.multiple_of((half * members + owner) * step, 16)
        whole[pl.ds(row, step), :] = block[...]
    cut = first.shape[0]
    copies = [
        pltpu.make_async_copy(whole.at[:cut], first, sems.at[0]),
        pltpu.make_async_copy(whole.at[cut:], second, sems.at[1]),
    ]
    for copy in copies:
        copy.start()
    for copy in copies:
        copy.wait()


def finish_kernel(
    edge_grads, pre_grad, sender_sum, receiver_sum, node_part, w_in, edges_grad, local_grad
):
    width = w_in.shape[1]
    edges_grad[...] = (
        edge_grads[...].astype(F32) + dot_nt(pre_grad[...], w_in[:width])
    ).astype(BF16)
    local_grad[...] = (
        node_part[...]
        + dot_nt(sender_sum[...], w_in[width : 2 * width])
        + dot_nt(receiver_sum[...], w_in[2 * width :])
    )


def turn_kernel(top, middle, bottom, along_core, along_chip, center):
    slots = middle.shape[0] // 2

    def turn(up, down):
        up[:slots] = top[:slots]
        up[slots : 2 * slots] = middle[:slots]
        up[2 * slots :] = bottom[:slots]
        down[:slots] = top[2 * slots :]
        down[slots : 2 * slots] = middle[slots:]
        down[2 * slots :] = bottom[2 * slots :]

    core = lax.axis_index(CORE)

    @pl.when(core == 0)
    def _():
        turn(along_core, along_chip)

    @pl.when(core == 1)
    def _():
        turn(along_chip, along_core)

    center[:slots] = top[slots : 2 * slots]
    center[slots:] = bottom[slots : 2 * slots]


def return_kernel(send_list, local_grad, center, along_core, along_chip, nodes_grad, returned):
    slots = send_list.shape[1]

    def fill(up, down):
        for k, (source, i) in enumerate(
            [
                (up, 0),
                (center, 0),
                (down, 0),
                (up, 1),
                (down, 1),
                (up, 2),
                (center, 1),
                (down, 2),
            ]
        ):
            returned[k * slots : (k + 1) * slots] = source[i * slots : (i + 1) * slots]

    core = lax.axis_index(CORE)

    @pl.when(core == 0)
    def _():
        fill(along_chip, along_core)

    @pl.when(core == 1)
    def _():
        fill(along_core, along_chip)

    hot = list_hot(send_list[...], local_grad.shape[0])
    nodes_grad[...] = (local_grad[...] + dot_tn(hot, returned[...])).astype(BF16)


SMEM = pltpu.SMEM
VMEM = pltpu.VMEM
HBM = pltpu.HBM


def call(body, outs, flops, *operands, spaces=(), out_space=VMEM, scratch=(), after=()):
    if after:
        first, rest = len(operands), len(operands) + len(after)
        inner = body

        def body(*refs):
            inner(*refs[:first], *refs[rest:])

        operands = operands + tuple(after)
    moved = sum(x.size * x.dtype.itemsize for x in operands)
    moved += sum(x.size * jnp.dtype(x.dtype).itemsize for x in outs)
    spaces = list(spaces) + [VMEM] * (len(operands) - len(spaces))
    out_spaces = out_space if isinstance(out_space, list) else [out_space] * len(outs)
    operands = [
        pltpu.with_memory_space_constraint(x, HBM) if space is HBM else x
        for x, space in zip(operands, spaces)
    ]
    return pl.pallas_call(
        body,
        out_shape=outs,
        in_specs=[pl.BlockSpec(memory_space=space) for space in spaces],
        out_specs=[pl.BlockSpec(memory_space=space) for space in out_spaces],
        scratch_shapes=list(scratch),
        compiler_params=pltpu.CompilerParams(vmem_limit_bytes=VMEM_LIMIT),
        cost_estimate=pl.CostEstimate(flops=flops, bytes_accessed=moved, transcendentals=0),
    )(*operands)


def like(array):
    return jax.ShapeDtypeStruct(array.shape, array.dtype)


def shaped(rows, columns, dtype):
    return jax.ShapeDtypeStruct((rows, columns), dtype)


def cut_in_blocks(keep, gains, other, after=()):
    packed = 0 if gains is None else gains.shape[0]
    members = square_members()
    block = shaped(packed + keep.shape[0] // members, keep.shape[1], BF16)
    operands = [keep, other] if gains is None else [keep, gains, other]
    return call(functools.partial(pair_kernel, packed), [block] * members, 0, *operands, after=after)


def exchanged(blocks):
    return [blocks[0]] + [in_square(x, offset) for offset, x in enumerate(blocks[1:], 1)]


def summed(packed, blocks, after=()):
    body = functools.partial(sum_kernel, packed)
    return call(body, [like(blocks[0])], 0, *blocks, after=after)[0]


def over_squares(packed, sums):
    size = lax.axis_size(FAR)
    distance = 1
    while True:
        other = lax.ppermute(sums, FAR, [(i, i ^ distance) for i in range(size)])
        distance *= 2
        if distance == size:
            return sums, other
        sums = summed(packed, [sums, other])


def whole_sum(packed, sums, other, after=()):
    rows, width = sums.shape
    outs = [shaped(rows - packed, width, BF16)]
    if packed:
        outs.append(shaped(packed, width, F32))
    return call(functools.partial(whole_kernel, packed), outs, 0, sums, other, after=after)


def gathered(mine):
    blocks = [mine] + [in_square(mine, offset) for offset in range(1, square_members())]
    return blocks + [across_cores(block) for block in blocks]


def placed(blocks, first_rows, second_rows):
    width = blocks[0].shape[1]
    return call(
        place_kernel,
        [shaped(first_rows, width, BF16), shaped(second_rows, width, BF16)],
        0,
        *blocks,
        out_space=HBM,
        scratch=[
            pltpu.VMEM((first_rows + second_rows, width), BF16),
            pltpu.SemaphoreType.DMA((2,)),
        ],
    )


def on_device(
    nodes,
    edges,
    edge_grads,
    node_grads,
    send_list,
    senders,
    receivers,
    tile_count,
    w_edge_in,
    w_edge_out,
    gain_edge,
    w_node_in,
    w_node_out,
    gain_node,
):
    count, width = nodes.shape
    slots = send_list.shape[1]
    halo_rows = 8 * slots
    edge_rows = edges.shape[0]
    tile_rows = senders.shape[1]
    square = 2 * width * width
    low, mid, high, nodes, send_list = call(
        send_kernel,
        [
            shaped(3 * slots, width, BF16),
            shaped(2 * slots, width, BF16),
            shaped(3 * slots, width, BF16),
            like(nodes),
            like(send_list),
        ],
        2 * halo_rows * count * width,
        nodes,
        send_list,
        spaces=[HBM, HBM],
        scratch=[pltpu.SemaphoreType.DMA((2,))],
    )
    from_low = passed_along(high, PX, 1)
    from_high = passed_along(low, PX, -1)
    fetched = [
        senders,
        receivers,
        edges,
        w_edge_in,
        w_edge_out,
        gain_edge,
        w_node_in,
        w_node_out,
        gain_node,
        node_grads,
        edge_grads,
    ]
    near_hot, halo_hot, *fetched = call(
        functools.partial(index_kernel, len(fetched)),
        [
            shaped(edge_rows, 2 * count, BF16),
            shaped(edge_rows, halo_rows, BF16),
        ]
        + [like(x) for x in fetched],
        0,
        *fetched,
        spaces=[HBM] * len(fetched),
        scratch=[pltpu.SemaphoreType.DMA((len(fetched),))],
    )
    (
        senders,
        receivers,
        edges,
        w_edge_in,
        w_edge_out,
        gain_edge,
        w_node_in,
        w_node_out,
        gain_node,
        node_grads,
        edge_grads,
    ) = fetched
    from_low, from_high, near_hot = lax.optimization_barrier((from_low, from_high, near_hot))
    upward = passed_along(
        jnp.concatenate([from_high[2 * slots :], mid[slots:], from_low[2 * slots :]]), PY, 1
    )
    downward = passed_along(
        jnp.concatenate([from_high[:slots], mid[:slots], from_low[:slots]]), PY, -1
    )
    pre_local, sender_columns, receiver_columns = call(
        local_kernel,
        [
            shaped(edge_rows, width, F32),
            shaped(count + halo_rows, edge_rows, BF16),
            shaped(count, edge_rows, BF16),
        ],
        square * (2 * count + edge_rows) + 4 * edge_rows * count * width,
        nodes,
        edges,
        senders,
        receivers,
        near_hot,
        w_edge_in,
    )
    (
        pre_grad,
        sender_sum,
        receiver_sum,
        node_part,
        top,
        middle,
        bottom,
        edge_keep,
        edge_away,
        node_keep,
        node_away,
        gains,
    ) = call(
        functools.partial(layer_kernel, tile_rows),
        [
            shaped(edge_rows, width, BF16),
            shaped(count, width, BF16),
            shaped(count, width, BF16),
            shaped(count, width, F32),
            shaped(3 * slots, width, BF16),
            shaped(2 * slots, width, BF16),
            shaped(3 * slots, width, BF16),
            shaped(2 * width, width, F32),
            shaped(2 * width + 16, width, BF16),
            shaped(3 * width // 2, width, F32),
            shaped(3 * width // 2, width, BF16),
            shaped(16, width, BF16),
        ],
        square * (6 * edge_rows + 11 * count + 2 * halo_rows)
        + 2 * edge_rows * (4 * count + halo_rows) * width,
        tile_count,
        nodes,
        node_grads,
        edges,
        edge_grads,
        pre_local,
        halo_hot,
        near_hot,
        sender_columns,
        receiver_columns,
        from_high,
        from_low,
        upward,
        downward,
        w_edge_in,
        w_edge_out,
        gain_edge,
        w_node_in,
        w_node_out,
        gain_node,
        spaces=[SMEM],
        scratch=[
            pltpu.VMEM((edge_rows, width), F32),
            pltpu.VMEM((edge_rows, width), BF16),
            pltpu.VMEM((edge_rows, width), F32),
            pltpu.VMEM((edge_rows, 128), F32),
            pltpu.VMEM((3 * width, width), F32),
            pltpu.VMEM((4 * width, width), F32),
        ],
    )
    packed = gains.shape[0]
    edge_other = across_cores(edge_away)
    node_other = across_cores(node_away)
    top = passed_along(top, PX, 1)
    bottom = passed_along(bottom, PX, -1)
    edge_cut = cut_in_blocks(edge_keep, gains, edge_other)
    node_cut = cut_in_blocks(node_keep, None, node_other, after=edge_cut[:1])
    edge_blocks = exchanged(edge_cut)
    node_blocks = exchanged(node_cut)
    along_core, along_chip, center = call(
        turn_kernel,
        [
            shaped(3 * slots, width, BF16),
            shaped(3 * slots, width, BF16),
            shaped(2 * slots, width, BF16),
        ],
        10**10,
        top,
        middle,
        bottom,
    )
    edge_sum = summed(packed, edge_blocks, after=node_cut[:1])
    *node_blocks, along_core, along_chip = lax.optimization_barrier(
        (*node_blocks, along_core, along_chip)
    )
    node_sum = summed(0, node_blocks, after=[edge_sum])
    edge_pair = over_squares(packed, edge_sum)
    node_pair = over_squares(0, node_sum)
    along_core = across_cores(along_core)
    along_chip = across_chips(along_chip)
    edge_mine, gains = whole_sum(packed, *edge_pair, after=[node_sum])
    *node_pair, along_core, along_chip = lax.optimization_barrier(
        (*node_pair, along_core, along_chip)
    )
    (node_mine,) = whole_sum(0, *node_pair, after=[edge_mine])
    edge_blocks = gathered(edge_mine)
    node_blocks = gathered(node_mine)
    edges_grad, local_grad = call(
        finish_kernel,
        [shaped(edge_rows, width, BF16), shaped(count, width, F32)],
        square * (edge_rows + 2 * count),
        edge_grads,
        pre_grad,
        sender_sum,
        receiver_sum,
        node_part,
        w_edge_in,
    )
    (nodes_grad,) = call(
        return_kernel,
        [shaped(count, width, BF16)],
        2 * halo_rows * count * width,
        send_list,
        local_grad,
        center,
        along_core,
        along_chip,
        scratch=[pltpu.VMEM((halo_rows, width), BF16)],
    )
    *node_blocks, nodes_grad, edges_grad = lax.optimization_barrier(
        (*node_blocks, nodes_grad, edges_grad)
    )
    w_edge_in_grad, w_edge_out_grad = placed(edge_blocks, 3 * width, width)
    w_node_in_grad, w_node_out_grad = placed(node_blocks, 2 * width, width)
    return (
        nodes_grad,
        edges_grad,
        w_edge_in_grad,
        w_edge_out_grad,
        (gains[0] + gains[1]).astype(BF16),
        w_node_in_grad,
        w_node_out_grad,
        (gains[2] + gains[3]).astype(BF16),
    )


def solution(mesh):
    in_specs = (
        P(("groups",) + PX + PY, None),
        P(("groups",) + PX + PY, None),
        P(("groups",) + PX + PY, None),
        P(("groups",) + PX + PY, None),
        P(("groups",) + PX + PY, None),
        P(("groups",) + PX + PY, None),
        P(("groups",) + PX + PY, None),
        P(("groups",) + PX + PY),
        P(),
        P(),
        P(),
        P(),
        P(),
        P(),
    )
    out_specs = (
        P(("groups",) + PX + PY, None),
        P(("groups",) + PX + PY, None),
        P("groups", None),
        P("groups", None),
        P("groups"),
        P("groups", None),
        P("groups", None),
        P("groups"),
    )
    groups, px, py = mesh.devices.shape
    by_core = jax.sharding.Mesh(
        mesh.devices.reshape(groups, px // 2, 2, py // 2, 2), ("groups",) + PX + PY
    )
    return jax.shard_map(
        on_device, mesh=by_core, in_specs=in_specs, out_specs=out_specs, check_vma=False
    )
```

```python
import functools

import jax
import jax.numpy as jnp
from jax import lax
from jax.experimental import pallas as pl
from jax.experimental.pallas import tpu as pltpu
from jax.sharding import PartitionSpec as P

EPS = 1e-05
BF16 = jnp.bfloat16
F32 = jnp.float32
VMEM_LIMIT = 24 * 1024 * 1024


CORE = "core"
FAR = "far"
PX = (FAR, "near")
PY = ("side", CORE)
SQUARE = ("near", "side")


def passed_along(array, axis, by):
    size = lax.axis_size(axis)
    return lax.ppermute(array, axis, [(i, (i + by) % size) for i in range(size)])


def across_chips(array):
    size = lax.axis_size(PY)
    pairs = [(i, (i + 1 if i % 2 else i - 1) % size) for i in range(size)]
    return lax.ppermute(array, PY, pairs)


def square_members():
    return lax.axis_size(SQUARE)


def place_in_square():
    near, side = SQUARE
    return lax.axis_index(near) * lax.axis_size(side) + lax.axis_index(side)


def in_square(array, offset):
    return lax.ppermute(array, SQUARE, [(i, i ^ offset) for i in range(square_members())])


def tree_sum(terms):
    while len(terms) > 1:
        terms = [terms[i] + terms[i + 1] for i in range(0, len(terms), 2)]
    return terms[0]


def across_cores(array):
    return lax.ppermute(array, CORE, [(0, 1), (1, 0)])


def dot(left, right):
    return jnp.dot(left, right, preferred_element_type=F32)


def dot_tn(left, right):
    return lax.dot_general(left, right, (((0,), (0,)), ((), ())), preferred_element_type=F32)


def dot_nt(left, right):
    return lax.dot_general(left, right, (((1,), (1,)), ((), ())), preferred_element_type=F32)


def sigmoid(value):
    return 0.5 + 0.5 * jnp.tanh(0.5 * value)


def normalize(value):
    centered = value - jnp.mean(value, axis=-1, keepdims=True)
    scale_inv = lax.rsqrt(jnp.mean(centered * centered, axis=-1, keepdims=True) + EPS)
    return centered * scale_inv, scale_inv


def norm_back(normed, scale_inv, gain, upstream):
    scaled = upstream * gain
    inner = (
        scaled
        - jnp.mean(scaled, axis=-1, keepdims=True)
        - normed * jnp.mean(scaled * normed, axis=-1, keepdims=True)
    )
    return inner * scale_inv


def columns_of(ids):
    rows, lanes = ids.shape
    padded = -(-rows // 8) * 8
    if padded > rows:
        ids = jnp.concatenate([ids, jnp.zeros((padded - rows, lanes), ids.dtype)], axis=0)
    return ids.T


def hot_rows(columns, tiles, base, count):
    parts = []
    for tile in tiles:
        column = columns[:, tile : tile + 1] - base
        lanes = lax.broadcasted_iota(jnp.int32, (columns.shape[0], count), 1)
        parts.append(jnp.where(lanes == column, 1.0, 0.0).astype(BF16))
    return jnp.concatenate(parts, axis=0) if len(parts) > 1 else parts[0]


def hot_columns(ids, tiles, base, count):
    parts = []
    for tile in tiles:
        row = ids[tile : tile + 1, :] - base
        subs = lax.broadcasted_iota(jnp.int32, (count, ids.shape[1]), 0)
        parts.append(jnp.where(subs == row, 1.0, 0.0).astype(BF16))
    return jnp.concatenate(parts, axis=1) if len(parts) > 1 else parts[0]


def list_hot(ids, count):
    directions, slots = ids.shape
    wide = jnp.concatenate([ids, jnp.zeros((directions, 128 - slots), ids.dtype)], axis=1)
    columns = wide.T
    parts = []
    for k in range(directions):
        lanes = lax.broadcasted_iota(jnp.int32, (slots, count), 1)
        parts.append(jnp.where(lanes == columns[:slots, k : k + 1], 1.0, 0.0).astype(BF16))
    return jnp.concatenate(parts, axis=0)


def live_rows(count_ref, tile_rows, rows):
    index = lax.broadcasted_iota(jnp.int32, (rows, 1), 0)
    return jnp.where(index < count_ref[0] * tile_rows, 1.0, 0.0)


def fetch_all(sources, targets, sems):
    copies = [
        pltpu.make_async_copy(source, target, sems.at[i])
        for i, (source, target) in enumerate(zip(sources, targets))
    ]
    for copy in copies:
        copy.start()
    return copies


def send_kernel(nodes_hbm, list_hbm, low, mid, high, nodes, send_list, sems):
    slots = send_list.shape[1]
    for copy in fetch_all([list_hbm, nodes_hbm], [send_list, nodes], sems):
        copy.wait()
    rows = dot(list_hot(send_list[...], nodes.shape[0]), nodes[...]).astype(BF16)
    low[...] = rows[: 3 * slots]
    mid[...] = rows[3 * slots : 5 * slots]
    high[...] = rows[5 * slots :]


def index_kernel(sources, *refs):
    fetched, refs = refs[:sources], refs[sources:]
    near_rows, halo_rows = refs[:2]
    targets, sems = refs[2:-1], refs[-1]
    senders, receivers = targets[:2]
    copies = fetch_all(fetched, targets, sems)
    for copy in copies[:2]:
        copy.wait()
    tile_rows = senders.shape[1]
    count = near_rows.shape[1] // 2
    by_sender = columns_of(senders[...])
    by_receiver = columns_of(receivers[...])
    for tile in range(senders.shape[0]):
        rows = slice(tile * tile_rows, (tile + 1) * tile_rows)
        near_rows[rows, :count] = hot_rows(by_sender, [tile], 0, count)
        near_rows[rows, count:] = hot_rows(by_receiver, [tile], 0, count)
        halo_rows[rows, :] = hot_rows(by_sender, [tile], count, halo_rows.shape[1])
    for copy in copies[2:]:
        copy.wait()


def local_kernel(
    nodes, edges, senders, receivers, near_rows, w_in, pre, sender_columns, receiver_columns
):
    width = nodes.shape[1]
    tile_rows = senders.shape[1]
    extended = sender_columns.shape[0]
    count = receiver_columns.shape[0]
    sender_ids = senders[...]
    receiver_ids = receivers[...]
    for tile in range(senders.shape[0]):
        rows = slice(tile * tile_rows, (tile + 1) * tile_rows)
        sender_columns[:, rows] = hot_columns(sender_ids, [tile], 0, extended)
        receiver_columns[:, rows] = hot_columns(receiver_ids, [tile], 0, count)
    x = nodes[...]
    table = jnp.concatenate(
        [
            dot(x, w_in[width : 2 * width]).astype(BF16),
            dot(x, w_in[2 * width :]).astype(BF16),
        ],
        axis=0,
    )
    pre[...] = dot(edges[...], w_in[:width]) + dot(near_rows[...], table)


def split_by_core(sums, first, keep_out, away_out):
    half = sums.shape[0] // 2
    core = lax.axis_index(CORE)
    keep_out[first : first + half] = sums[pl.ds(pl.multiple_of(core * half, half), half), :]
    away = sums[pl.ds(pl.multiple_of((1 - core) * half, half), half), :]
    away_out[first : first + half] = away.astype(BF16)


def pack_gains(edge_gain, node_gain):
    edge_high = edge_gain.astype(BF16).astype(F32)
    node_high = node_gain.astype(BF16).astype(F32)
    row = lax.broadcasted_iota(jnp.int32, (16, edge_gain.shape[1]), 0)
    packed = jnp.where(row == 0, edge_high, 0.0)
    packed = jnp.where(row == 1, edge_gain - edge_high, packed)
    packed = jnp.where(row == 2, node_high, packed)
    packed = jnp.where(row == 3, node_gain - node_high, packed)
    return packed.astype(BF16)


def layer_kernel(
    tile_rows,
    count_ref,
    nodes,
    node_grads,
    edges,
    edge_grads,
    pre_local,
    halo_rows,
    near_rows,
    sender_columns,
    receiver_columns,
    from_high,
    from_low,
    upward,
    downward,
    w_in,
    w_out,
    gain_edge,
    w_node_in,
    w_node_out,
    gain_node,
    pre_grad_out,
    sender_out,
    receiver_out,
    node_part_out,
    top_out,
    middle_out,
    bottom_out,
    keep_out,
    away_out,
    gains_out,
    slope_kept,
    hidden_kept,
    normed_kept,
    scale_kept,
    node_sums,
    edge_sums,
):
    count, width = nodes.shape
    edge_rows = edges.shape[0]
    live = live_rows(count_ref, tile_rows, edge_rows)
    slots = from_high.shape[0] // 3
    halo = jnp.concatenate(
        [
            downward[:slots],
            from_high[slots : 2 * slots],
            upward[:slots],
            downward[slots : 2 * slots],
            upward[slots : 2 * slots],
            downward[2 * slots :],
            from_low[slots : 2 * slots],
            upward[2 * slots :],
        ],
        axis=0,
    )
    table = dot(halo, w_in[width : 2 * width]).astype(BF16)
    gain = gain_edge[...].astype(F32)[None, :]
    value = pre_local[...] + dot(halo_rows[...], table)
    sigma = sigmoid(value)
    hidden = (value * sigma).astype(BF16)
    hidden_kept[...] = hidden
    slope_kept[...] = sigma * (1.0 + value * (1.0 - sigma))
    edge_normed, edge_scale = normalize(dot(hidden, w_out[...]))
    normed_kept[...] = edge_normed
    scale_kept[...] = jnp.broadcast_to(edge_scale, (edge_rows, 128))
    message = (live * gain * edge_normed).astype(BF16)
    total = dot(receiver_columns[...], message)
    aggregated = total.astype(BF16)
    x = nodes[...]
    w_first = w_node_in[:width]
    w_second = w_node_in[width:]
    node_pre = dot(x, w_first) + dot(aggregated, w_second)
    sigma = sigmoid(node_pre)
    node_hidden = (node_pre * sigma).astype(BF16)
    normed, scale_inv = normalize(dot(node_hidden, w_node_out[...]))
    upstream = node_grads[...].astype(F32)
    out_grad = norm_back(normed, scale_inv, gain_node[...].astype(F32)[None, :], upstream).astype(BF16)
    slope = sigma * (1.0 + node_pre * (1.0 - sigma))
    pre_grad = (dot_nt(out_grad, w_node_out[...]) * slope).astype(BF16)
    agg_grad = dot_nt(pre_grad, w_second).astype(BF16)
    node_part_out[...] = upstream + dot_nt(pre_grad, w_first)
    node_sums[:width] = dot_tn(x, pre_grad)
    node_sums[width : 2 * width] = dot_tn(aggregated, pre_grad)
    node_sums[2 * width : 3 * width] = dot_tn(node_hidden, out_grad)
    node_gain = jnp.sum(upstream * normed, axis=0, keepdims=True)
    upstream = live * (
        edge_grads[...].astype(F32) + dot(near_rows[:, count:], agg_grad)
    )
    edge_normed = normed_kept[...]
    edge_gain = jnp.sum(upstream * edge_normed, axis=0, keepdims=True)
    out_grad = norm_back(edge_normed, scale_kept[:, :1], gain, upstream).astype(BF16)
    pre_grad = (dot_nt(out_grad, w_out[...]) * slope_kept[...]).astype(BF16)
    pre_grad_out[...] = pre_grad
    sender_total = dot(sender_columns[...], pre_grad)
    receiver_total = dot(receiver_columns[...], pre_grad)
    own = sender_total[:count].astype(BF16)
    away = sender_total[count:].astype(BF16)
    received = receiver_total.astype(BF16)
    sender_out[...] = own
    receiver_out[...] = received
    halo_grad = dot_nt(away, w_in[width : 2 * width]).astype(BF16)
    top_out[...] = halo_grad[: 3 * slots]
    middle_out[...] = halo_grad[3 * slots : 5 * slots]
    bottom_out[...] = halo_grad[5 * slots :]
    edge_sums[:width] = dot_tn(edges[...], pre_grad)
    edge_sums[width : 2 * width] = dot_tn(x, own) + dot_tn(halo, away)
    edge_sums[2 * width : 3 * width] = dot_tn(x, received)
    edge_sums[3 * width : 4 * width] = dot_tn(hidden_kept[...], out_grad)
    split_by_core(edge_sums, 0, keep_out, away_out)
    split_by_core(node_sums, edge_sums.shape[0] // 2, keep_out, away_out)
    gains = pack_gains(edge_gain, node_gain)
    away_out[keep_out.shape[0] :] = gains
    gains_out[...] = gains


def pair_kernel(parts, keep, gains, other, *outs):
    rows = keep.shape[0]
    packed = gains.shape[0]
    members = len(outs)
    both = gains[...].astype(F32) + other[rows : rows + packed].astype(F32)
    summed = pack_gains(both[0:1] + both[1:2], both[2:3] + both[3:4])
    me = place_in_square()
    for offset, out in enumerate(outs):
        owner = me ^ offset
        out[:packed] = summed
        first, at = 0, packed
        for part in parts:
            step = part // members
            source = pl.ds(pl.multiple_of(first + owner * step, 16), step)
            out[at : at + step] = (keep[source, :] + other[source, :].astype(F32)).astype(BF16)
            first, at = first + part, at + step


def add_packed(values):
    packed = 16
    gains = values[:packed]
    return pack_gains(gains[0:1] + gains[1:2], gains[2:3] + gains[3:4])


def sum_kernel(*refs):
    sums_out = refs[-1]
    sums = tree_sum([block[...].astype(F32) for block in refs[:-1]])
    sums_out[...] = sums.astype(BF16)
    sums_out[:16] = add_packed(sums)


def join_kernel(own, other, sums_out):
    sums = own[...].astype(F32) + other[...].astype(F32)
    sums_out[...] = sums.astype(BF16)
    sums_out[:16] = add_packed(sums)


def whole_kernel(own, other, gains_out, mine):
    packed = gains_out.shape[0]
    sums = own[...].astype(F32) + other[...].astype(F32)
    gains_out[...] = sums[:packed]
    mine[...] = sums[packed:].astype(BF16)


def place_kernel(parts, *refs):
    count = 2 * len(parts)
    sems, wholes = refs[-1], refs[-1 - len(parts) : -1]
    outs = refs[-1 - len(parts) - count : -1 - len(parts)]
    blocks = refs[: -1 - len(parts) - count]
    members = len(blocks) // 2
    core = lax.axis_index(CORE)
    me = place_in_square()
    for position, block in enumerate(blocks):
        half = core if position < members else 1 - core
        owner = me ^ (position % members)
        at = 0
        for part, whole in zip(parts, wholes):
            step = part // members
            row = pl.multiple_of(half * part + owner * step, 16)
            whole[pl.ds(row, step), :] = block[at : at + step]
            at += step
    copies = []
    for i, whole in enumerate(wholes):
        cut = outs[2 * i].shape[0]
        copies.append(pltpu.make_async_copy(whole.at[:cut], outs[2 * i], sems.at[2 * i]))
        copies.append(pltpu.make_async_copy(whole.at[cut:], outs[2 * i + 1], sems.at[2 * i + 1]))
    for copy in copies:
        copy.start()
    for copy in copies:
        copy.wait()


def finish_kernel(
    edge_grads, pre_grad, sender_sum, receiver_sum, node_part, w_in, edges_grad, local_grad
):
    width = w_in.shape[1]
    edges_grad[...] = (
        edge_grads[...].astype(F32) + dot_nt(pre_grad[...], w_in[:width])
    ).astype(BF16)
    local_grad[...] = (
        node_part[...]
        + dot_nt(sender_sum[...], w_in[width : 2 * width])
        + dot_nt(receiver_sum[...], w_in[2 * width :])
    )


def turn_kernel(top, middle, bottom, along_core, along_chip, center):
    slots = middle.shape[0] // 2

    def turn(up, down):
        up[:slots] = top[:slots]
        up[slots : 2 * slots] = middle[:slots]
        up[2 * slots :] = bottom[:slots]
        down[:slots] = top[2 * slots :]
        down[slots : 2 * slots] = middle[slots:]
        down[2 * slots :] = bottom[2 * slots :]

    core = lax.axis_index(CORE)

    @pl.when(core == 0)
    def _():
        turn(along_core, along_chip)

    @pl.when(core == 1)
    def _():
        turn(along_chip, along_core)

    center[:slots] = top[slots : 2 * slots]
    center[slots:] = bottom[slots : 2 * slots]


def return_kernel(send_list, local_grad, center, along_core, along_chip, nodes_grad, returned):
    slots = send_list.shape[1]

    def fill(up, down):
        for k, (source, i) in enumerate(
            [
                (up, 0),
                (center, 0),
                (down, 0),
                (up, 1),
                (down, 1),
                (up, 2),
                (center, 1),
                (down, 2),
            ]
        ):
            returned[k * slots : (k + 1) * slots] = source[i * slots : (i + 1) * slots]

    core = lax.axis_index(CORE)

    @pl.when(core == 0)
    def _():
        fill(along_chip, along_core)

    @pl.when(core == 1)
    def _():
        fill(along_core, along_chip)

    hot = list_hot(send_list[...], local_grad.shape[0])
    nodes_grad[...] = (local_grad[...] + dot_tn(hot, returned[...])).astype(BF16)


SMEM = pltpu.SMEM
VMEM = pltpu.VMEM
HBM = pltpu.HBM


def call(body, outs, flops, *operands, spaces=(), out_space=VMEM, scratch=()):
    moved = sum(x.size * x.dtype.itemsize for x in operands)
    moved += sum(x.size * jnp.dtype(x.dtype).itemsize for x in outs)
    spaces = list(spaces) + [VMEM] * (len(operands) - len(spaces))
    out_spaces = out_space if isinstance(out_space, list) else [out_space] * len(outs)
    operands = [
        pltpu.with_memory_space_constraint(x, HBM) if space is HBM else x
        for x, space in zip(operands, spaces)
    ]
    return pl.pallas_call(
        body,
        out_shape=outs,
        in_specs=[pl.BlockSpec(memory_space=space) for space in spaces],
        out_specs=[pl.BlockSpec(memory_space=space) for space in out_spaces],
        scratch_shapes=list(scratch),
        compiler_params=pltpu.CompilerParams(vmem_limit_bytes=VMEM_LIMIT),
        cost_estimate=pl.CostEstimate(flops=flops, bytes_accessed=moved, transcendentals=0),
    )(*operands)


def like(array):
    return jax.ShapeDtypeStruct(array.shape, array.dtype)


def shaped(rows, columns, dtype):
    return jax.ShapeDtypeStruct((rows, columns), dtype)


def placed(parts, blocks, width):
    return call(
        functools.partial(place_kernel, parts),
        [
            shaped(3 * width, width, BF16),
            shaped(width, width, BF16),
            shaped(2 * width, width, BF16),
            shaped(width, width, BF16),
        ],
        0,
        *blocks,
        out_space=HBM,
        scratch=[pltpu.VMEM((2 * part, width), BF16) for part in parts]
        + [pltpu.SemaphoreType.DMA((2 * len(parts),))],
    )


def joined(sums, packed, *beside):
    rows, width = sums.shape
    size = lax.axis_size(FAR)
    distance = 1
    while True:
        other = lax.ppermute(sums, FAR, [(i, i ^ distance) for i in range(size)])
        distance *= 2
        if distance == size:
            break
        (sums,) = call(join_kernel, [like(sums)], 0, sums, other)
    other, *beside = lax.optimization_barrier((other, *beside))
    gains, mine = call(
        whole_kernel,
        [shaped(packed, width, F32), shaped(rows - packed, width, BF16)],
        0,
        sums,
        other,
    )
    return gains, mine, *beside


def on_device(
    nodes,
    edges,
    edge_grads,
    node_grads,
    send_list,
    senders,
    receivers,
    tile_count,
    w_edge_in,
    w_edge_out,
    gain_edge,
    w_node_in,
    w_node_out,
    gain_node,
):
    count, width = nodes.shape
    slots = send_list.shape[1]
    halo_rows = 8 * slots
    edge_rows = edges.shape[0]
    tile_rows = senders.shape[1]
    square = 2 * width * width
    low, mid, high, nodes, send_list = call(
        send_kernel,
        [
            shaped(3 * slots, width, BF16),
            shaped(2 * slots, width, BF16),
            shaped(3 * slots, width, BF16),
            like(nodes),
            like(send_list),
        ],
        2 * halo_rows * count * width,
        nodes,
        send_list,
        spaces=[HBM, HBM],
        scratch=[pltpu.SemaphoreType.DMA((2,))],
    )
    from_low = passed_along(high, PX, 1)
    from_high = passed_along(low, PX, -1)
    fetched = [
        senders,
        receivers,
        edges,
        w_edge_in,
        w_edge_out,
        gain_edge,
        w_node_in,
        w_node_out,
        gain_node,
        node_grads,
        edge_grads,
    ]
    near_hot, halo_hot, *fetched = call(
        functools.partial(index_kernel, len(fetched)),
        [
            shaped(edge_rows, 2 * count, BF16),
            shaped(edge_rows, halo_rows, BF16),
        ]
        + [like(x) for x in fetched],
        0,
        *fetched,
        spaces=[HBM] * len(fetched),
        scratch=[pltpu.SemaphoreType.DMA((len(fetched),))],
    )
    (
        senders,
        receivers,
        edges,
        w_edge_in,
        w_edge_out,
        gain_edge,
        w_node_in,
        w_node_out,
        gain_node,
        node_grads,
        edge_grads,
    ) = fetched
    from_low, from_high, near_hot = lax.optimization_barrier((from_low, from_high, near_hot))
    upward = passed_along(
        jnp.concatenate([from_high[2 * slots :], mid[slots:], from_low[2 * slots :]]), PY, 1
    )
    downward = passed_along(
        jnp.concatenate([from_high[:slots], mid[:slots], from_low[:slots]]), PY, -1
    )
    pre_local, sender_columns, receiver_columns = call(
        local_kernel,
        [
            shaped(edge_rows, width, F32),
            shaped(count + halo_rows, edge_rows, BF16),
            shaped(count, edge_rows, BF16),
        ],
        square * (2 * count + edge_rows) + 4 * edge_rows * count * width,
        nodes,
        edges,
        senders,
        receivers,
        near_hot,
        w_edge_in,
    )
    parts = (2 * width, 3 * width // 2)
    halves = sum(parts)
    pre_grad, sender_sum, receiver_sum, node_part, top, middle, bottom, keep, away, gains = call(
        functools.partial(layer_kernel, tile_rows),
        [
            shaped(edge_rows, width, BF16),
            shaped(count, width, BF16),
            shaped(count, width, BF16),
            shaped(count, width, F32),
            shaped(3 * slots, width, BF16),
            shaped(2 * slots, width, BF16),
            shaped(3 * slots, width, BF16),
            shaped(halves, width, F32),
            shaped(halves + 16, width, BF16),
            shaped(16, width, BF16),
        ],
        square * (6 * edge_rows + 11 * count + 2 * halo_rows)
        + 2 * edge_rows * (4 * count + halo_rows) * width,
        tile_count,
        nodes,
        node_grads,
        edges,
        edge_grads,
        pre_local,
        halo_hot,
        near_hot,
        sender_columns,
        receiver_columns,
        from_high,
        from_low,
        upward,
        downward,
        w_edge_in,
        w_edge_out,
        gain_edge,
        w_node_in,
        w_node_out,
        gain_node,
        spaces=[SMEM],
        scratch=[
            pltpu.VMEM((edge_rows, width), F32),
            pltpu.VMEM((edge_rows, width), BF16),
            pltpu.VMEM((edge_rows, width), F32),
            pltpu.VMEM((edge_rows, 128), F32),
            pltpu.VMEM((3 * width, width), F32),
            pltpu.VMEM((4 * width, width), F32),
        ],
    )
    other = across_cores(away)
    members = square_members()
    own, *blocks = call(
        functools.partial(pair_kernel, parts),
        [shaped(16 + halves // members, width, BF16)] * members,
        0,
        keep,
        gains,
        other,
    )
    received = [in_square(block, offset) for offset, block in enumerate(blocks, 1)]
    along_core, along_chip, center = call(
        turn_kernel,
        [
            shaped(3 * slots, width, BF16),
            shaped(3 * slots, width, BF16),
            shaped(2 * slots, width, BF16),
        ],
        10**10,
        passed_along(top, PX, 1),
        middle,
        passed_along(bottom, PX, -1),
    )
    *received, along_core, along_chip = lax.optimization_barrier(
        (*received, along_core, along_chip)
    )
    (sums,) = call(sum_kernel, [like(own)], 0, own, *received)
    gains, mine, along_core, along_chip = joined(
        sums, gains.shape[0], across_cores(along_core), across_chips(along_chip)
    )
    blocks = [mine] + [in_square(mine, offset) for offset in range(1, members)]
    gain_edge_grad = (gains[0] + gains[1]).astype(BF16)
    gain_node_grad = (gains[2] + gains[3]).astype(BF16)
    edges_grad, local_grad = call(
        finish_kernel,
        [shaped(edge_rows, width, BF16), shaped(count, width, F32)],
        square * (edge_rows + 2 * count),
        edge_grads,
        pre_grad,
        sender_sum,
        receiver_sum,
        node_part,
        w_edge_in,
    )
    (nodes_grad,) = call(
        return_kernel,
        [shaped(count, width, BF16)],
        2 * halo_rows * count * width,
        send_list,
        local_grad,
        center,
        along_core,
        along_chip,
        scratch=[pltpu.VMEM((halo_rows, width), BF16)],
    )
    done = (nodes_grad, edges_grad, gain_edge_grad, gain_node_grad)
    for i in range(members):
        blocks[i], *done = lax.optimization_barrier((blocks[i], *done))
    nodes_grad, edges_grad, gain_edge_grad, gain_node_grad = done
    blocks += [across_cores(block) for block in blocks]
    w_edge_in_grad, w_edge_out_grad, w_node_in_grad, w_node_out_grad = placed(
        parts, blocks, width
    )
    return (
        nodes_grad,
        edges_grad,
        w_edge_in_grad,
        w_edge_out_grad,
        gain_edge_grad,
        w_node_in_grad,
        w_node_out_grad,
        gain_node_grad,
    )


def solution(mesh):
    in_specs = (
        P(("groups",) + PX + PY, None),
        P(("groups",) + PX + PY, None),
        P(("groups",) + PX + PY, None),
        P(("groups",) + PX + PY, None),
        P(("groups",) + PX + PY, None),
        P(("groups",) + PX + PY, None),
        P(("groups",) + PX + PY, None),
        P(("groups",) + PX + PY),
        P(),
        P(),
        P(),
        P(),
        P(),
        P(),
    )
    out_specs = (
        P(("groups",) + PX + PY, None),
        P(("groups",) + PX + PY, None),
        P("groups", None),
        P("groups", None),
        P("groups"),
        P("groups", None),
        P("groups", None),
        P("groups"),
    )
    groups, px, py = mesh.devices.shape
    by_core = jax.sharding.Mesh(
        mesh.devices.reshape(groups, px // 2, 2, py // 2, 2), ("groups",) + PX + PY
    )
    return jax.shard_map(
        on_device, mesh=by_core, in_specs=in_specs, out_specs=out_specs, check_vma=False
    )
```

```python
import functools

import jax
import jax.numpy as jnp
from jax import lax
from jax.experimental import pallas as pl
from jax.experimental.pallas import tpu as pltpu
from jax.sharding import PartitionSpec as P

EPS = 1e-05
BF16 = jnp.bfloat16
F32 = jnp.float32
PACKED = 8
VMEM_LIMIT = 24 * 1024 * 1024


CORE = "core"
FAR = "far"
PX = (FAR, "near")
PY = ("side", CORE)
SQUARE = ("near", "side")


def passed_along(array, axis, by):
    size = lax.axis_size(axis)
    return lax.ppermute(array, axis, [(i, (i + by) % size) for i in range(size)])


def chip_neighbour(i, size):
    return (i + 1 if i % 2 else i - 1) % size


def across_chips(array):
    size = lax.axis_size(PY)
    return lax.ppermute(array, PY, [(i, chip_neighbour(i, size)) for i in range(size)])


def to_corner(array, by):
    rows, columns = lax.axis_size(PX), lax.axis_size(PY)
    pairs = [
        (i * columns + j, (i + by) % rows * columns + chip_neighbour(j, columns))
        for i in range(rows)
        for j in range(columns)
    ]
    return lax.ppermute(array, PX + PY, pairs)


def square_members():
    return lax.axis_size(SQUARE)


def place_in_square():
    near, side = SQUARE
    return lax.axis_index(near) * lax.axis_size(side) + lax.axis_index(side)


def in_square(array, offset):
    return lax.ppermute(array, SQUARE, [(i, i ^ offset) for i in range(square_members())])


def tree_sum(terms):
    while len(terms) > 1:
        terms = [terms[i] + terms[i + 1] for i in range(0, len(terms), 2)]
    return terms[0]


def across_cores(array):
    return lax.ppermute(array, CORE, [(0, 1), (1, 0)])


def dot(left, right):
    return jnp.dot(left, right, preferred_element_type=F32)


def dot_tn(left, right):
    return lax.dot_general(left, right, (((0,), (0,)), ((), ())), preferred_element_type=F32)


def dot_nt(left, right):
    return lax.dot_general(left, right, (((1,), (1,)), ((), ())), preferred_element_type=F32)


def sigmoid(value):
    return 0.5 + 0.5 * jnp.tanh(0.5 * value)


def normalize(value):
    centered = value - jnp.mean(value, axis=-1, keepdims=True)
    scale_inv = lax.rsqrt(jnp.mean(centered * centered, axis=-1, keepdims=True) + EPS)
    return centered * scale_inv, scale_inv


def norm_back(normed, scale_inv, gain, upstream):
    scaled = upstream * gain
    inner = (
        scaled
        - jnp.mean(scaled, axis=-1, keepdims=True)
        - normed * jnp.mean(scaled * normed, axis=-1, keepdims=True)
    )
    return inner * scale_inv


def columns_of(ids):
    rows, lanes = ids.shape
    padded = -(-rows // 8) * 8
    if padded > rows:
        ids = jnp.concatenate([ids, jnp.zeros((padded - rows, lanes), ids.dtype)], axis=0)
    return ids.T


def hot_rows(columns, tiles, base, count):
    parts = []
    for tile in tiles:
        column = columns[:, tile : tile + 1] - base
        lanes = lax.broadcasted_iota(jnp.int32, (columns.shape[0], count), 1)
        parts.append(jnp.where(lanes == column, 1.0, 0.0).astype(BF16))
    return jnp.concatenate(parts, axis=0) if len(parts) > 1 else parts[0]


def hot_columns(ids, tiles, base, count):
    parts = []
    for tile in tiles:
        row = ids[tile : tile + 1, :] - base
        subs = lax.broadcasted_iota(jnp.int32, (count, ids.shape[1]), 0)
        parts.append(jnp.where(subs == row, 1.0, 0.0).astype(BF16))
    return jnp.concatenate(parts, axis=1) if len(parts) > 1 else parts[0]


def list_hot(ids, count):
    directions, slots = ids.shape
    wide = jnp.concatenate([ids, jnp.zeros((directions, 128 - slots), ids.dtype)], axis=1)
    columns = wide.T
    parts = []
    for k in range(directions):
        lanes = lax.broadcasted_iota(jnp.int32, (slots, count), 1)
        parts.append(jnp.where(lanes == columns[:slots, k : k + 1], 1.0, 0.0).astype(BF16))
    return jnp.concatenate(parts, axis=0)


def live_rows(count_ref, tile_rows, rows):
    index = lax.broadcasted_iota(jnp.int32, (rows, 1), 0)
    return jnp.where(index < count_ref[0] * tile_rows, 1.0, 0.0)


def fetch_all(sources, targets, sems):
    copies = [
        pltpu.make_async_copy(source, target, sems.at[i])
        for i, (source, target) in enumerate(zip(sources, targets))
    ]
    for copy in copies:
        copy.start()
    return copies


def send_kernel(
    nodes_hbm, list_hbm, up, down, self_out, straight, corner_up, corner_down, nodes, ids, sems
):
    slots = ids.shape[1]
    for copy in fetch_all([list_hbm, nodes_hbm], [ids, nodes], sems):
        copy.wait()
    rows = dot(list_hot(ids[...], nodes.shape[0]), nodes[...]).astype(BF16)

    def block(k):
        return rows[k * slots : (k + 1) * slots]

    up[:slots] = block(6)
    down[:slots] = block(1)

    def store(up_k, down_k, self_k, straight_k, corner_up_k, corner_down_k):
        up[slots:] = block(up_k)
        down[slots:] = block(down_k)
        self_out[...] = block(self_k)
        straight[...] = block(straight_k)
        corner_up[...] = block(corner_up_k)
        corner_down[...] = block(corner_down_k)

    core = lax.axis_index(CORE)

    @pl.when(core == 0)
    def _():
        store(7, 2, 4, 3, 5, 0)

    @pl.when(core == 1)
    def _():
        store(5, 0, 3, 4, 7, 2)


def index_kernel(sources, *refs):
    fetched, refs = refs[:sources], refs[sources:]
    near_rows, halo_rows = refs[:2]
    targets, sems = refs[2:-1], refs[-1]
    senders, receivers = targets[:2]
    copies = fetch_all(fetched, targets, sems)
    for copy in copies[:2]:
        copy.wait()
    tile_rows = senders.shape[1]
    count = near_rows.shape[1] // 2
    by_sender = columns_of(senders[...])
    by_receiver = columns_of(receivers[...])
    for tile in range(senders.shape[0]):
        rows = slice(tile * tile_rows, (tile + 1) * tile_rows)
        near_rows[rows, :count] = hot_rows(by_sender, [tile], 0, count)
        near_rows[rows, count:] = hot_rows(by_receiver, [tile], 0, count)
        halo_rows[rows, :] = hot_rows(by_sender, [tile], count, halo_rows.shape[1])
    for copy in copies[2:]:
        copy.wait()


def local_kernel(
    nodes, edges, senders, receivers, near_rows, w_in, pre, sender_columns, receiver_columns
):
    width = nodes.shape[1]
    tile_rows = senders.shape[1]
    extended = sender_columns.shape[0]
    count = receiver_columns.shape[0]
    sender_ids = senders[...]
    receiver_ids = receivers[...]
    for tile in range(senders.shape[0]):
        rows = slice(tile * tile_rows, (tile + 1) * tile_rows)
        sender_columns[:, rows] = hot_columns(sender_ids, [tile], 0, extended)
        receiver_columns[:, rows] = hot_columns(receiver_ids, [tile], 0, count)
    x = nodes[...]
    table = jnp.concatenate(
        [
            dot(x, w_in[width : 2 * width]).astype(BF16),
            dot(x, w_in[2 * width :]).astype(BF16),
        ],
        axis=0,
    )
    pre[...] = dot(edges[...], w_in[:width]) + dot(near_rows[...], table)


def split_by_core(sums, first, keep_out, away_out):
    half = sums.shape[0] // 2
    core = lax.axis_index(CORE)
    keep_out[first : first + half] = sums[pl.ds(pl.multiple_of(core * half, half), half), :]
    away = sums[pl.ds(pl.multiple_of((1 - core) * half, half), half), :]
    away_out[first : first + half] = away.astype(BF16)


def pack_gains(edge_gain, node_gain):
    edge_high = edge_gain.astype(BF16).astype(F32)
    node_high = node_gain.astype(BF16).astype(F32)
    row = lax.broadcasted_iota(jnp.int32, (PACKED, edge_gain.shape[1]), 0)
    packed = jnp.where(row == 0, edge_high, 0.0)
    packed = jnp.where(row == 1, edge_gain - edge_high, packed)
    packed = jnp.where(row == 2, node_high, packed)
    packed = jnp.where(row == 3, node_gain - node_high, packed)
    return packed.astype(BF16)


def layer_kernel(
    tile_rows,
    count_ref,
    nodes,
    node_grads,
    edges,
    edge_grads,
    pre_local,
    halo_rows,
    near_rows,
    sender_columns,
    receiver_columns,
    from_low,
    from_high,
    from_core,
    straight,
    corner_low,
    corner_high,
    w_in,
    w_out,
    gain_edge,
    w_node_in,
    w_node_out,
    gain_node,
    pre_grad_out,
    sender_out,
    receiver_out,
    node_part_out,
    top_out,
    middle_out,
    bottom_out,
    keep_out,
    away_out,
    gains_out,
    slope_kept,
    hidden_kept,
    normed_kept,
    scale_kept,
    node_sums,
    edge_sums,
):
    count, width = nodes.shape
    edge_rows = edges.shape[0]
    live = live_rows(count_ref, tile_rows, edge_rows)
    slots = straight.shape[0]
    first_core = lax.axis_index(CORE) == 0
    parts = [from_core[i * slots : (i + 1) * slots] for i in range(3)]
    other = [straight[...], corner_low[...], corner_high[...]]
    halo = jnp.concatenate(
        [
            jnp.where(first_core, parts[2], other[2]),
            from_high[:slots],
            jnp.where(first_core, other[2], parts[2]),
            jnp.where(first_core, parts[0], other[0]),
            jnp.where(first_core, other[0], parts[0]),
            jnp.where(first_core, parts[1], other[1]),
            from_low[:slots],
            jnp.where(first_core, other[1], parts[1]),
        ],
        axis=0,
    )
    table = dot(halo, w_in[width : 2 * width]).astype(BF16)
    gain = gain_edge[...].astype(F32)[None, :]
    value = pre_local[...] + dot(halo_rows[...], table)
    sigma = sigmoid(value)
    hidden = (value * sigma).astype(BF16)
    hidden_kept[...] = hidden
    slope_kept[...] = sigma * (1.0 + value * (1.0 - sigma))
    edge_normed, edge_scale = normalize(dot(hidden, w_out[...]))
    normed_kept[...] = edge_normed
    scale_kept[...] = jnp.broadcast_to(edge_scale, (edge_rows, 128))
    message = (live * gain * edge_normed).astype(BF16)
    total = dot(receiver_columns[...], message)
    aggregated = total.astype(BF16)
    x = nodes[...]
    w_first = w_node_in[:width]
    w_second = w_node_in[width:]
    node_pre = dot(x, w_first) + dot(aggregated, w_second)
    sigma = sigmoid(node_pre)
    node_hidden = (node_pre * sigma).astype(BF16)
    normed, scale_inv = normalize(dot(node_hidden, w_node_out[...]))
    upstream = node_grads[...].astype(F32)
    out_grad = norm_back(normed, scale_inv, gain_node[...].astype(F32)[None, :], upstream).astype(BF16)
    slope = sigma * (1.0 + node_pre * (1.0 - sigma))
    pre_grad = (dot_nt(out_grad, w_node_out[...]) * slope).astype(BF16)
    agg_grad = dot_nt(pre_grad, w_second).astype(BF16)
    node_part_out[...] = upstream + dot_nt(pre_grad, w_first)
    node_sums[:width] = dot_tn(x, pre_grad)
    node_sums[width : 2 * width] = dot_tn(aggregated, pre_grad)
    node_sums[2 * width : 3 * width] = dot_tn(node_hidden, out_grad)
    node_gain = jnp.sum(upstream * normed, axis=0, keepdims=True)
    upstream = live * (
        edge_grads[...].astype(F32) + dot(near_rows[:, count:], agg_grad)
    )
    edge_normed = normed_kept[...]
    edge_gain = jnp.sum(upstream * edge_normed, axis=0, keepdims=True)
    out_grad = norm_back(edge_normed, scale_kept[:, :1], gain, upstream).astype(BF16)
    pre_grad = (dot_nt(out_grad, w_out[...]) * slope_kept[...]).astype(BF16)
    pre_grad_out[...] = pre_grad
    sender_total = dot(sender_columns[...], pre_grad)
    receiver_total = dot(receiver_columns[...], pre_grad)
    own = sender_total[:count].astype(BF16)
    away = sender_total[count:].astype(BF16)
    received = receiver_total.astype(BF16)
    sender_out[...] = own
    receiver_out[...] = received
    halo_grad = dot_nt(away, w_in[width : 2 * width]).astype(BF16)
    top_out[...] = halo_grad[: 3 * slots]
    middle_out[...] = halo_grad[3 * slots : 5 * slots]
    bottom_out[...] = halo_grad[5 * slots :]
    edge_sums[:width] = dot_tn(edges[...], pre_grad)
    edge_sums[width : 2 * width] = dot_tn(x, own) + dot_tn(halo, away)
    edge_sums[2 * width : 3 * width] = dot_tn(x, received)
    edge_sums[3 * width : 4 * width] = dot_tn(hidden_kept[...], out_grad)
    split_by_core(edge_sums, 0, keep_out, away_out)
    split_by_core(node_sums, edge_sums.shape[0] // 2, keep_out, away_out)
    gains = pack_gains(edge_gain, node_gain)
    away_out[keep_out.shape[0] :] = gains
    gains_out[...] = gains


def pair_kernel(parts, keep, gains, other, *outs):
    rows = keep.shape[0]
    packed = gains.shape[0]
    members = len(outs)
    both = gains[...].astype(F32) + other[rows : rows + packed].astype(F32)
    summed = pack_gains(both[0:1] + both[1:2], both[2:3] + both[3:4])
    me = place_in_square()
    for offset, out in enumerate(outs):
        owner = me ^ offset
        out[:packed] = summed
        first, at = 0, packed
        for part in parts:
            step = part // members
            source = pl.ds(pl.multiple_of(first + owner * step, 16), step)
            out[at : at + step] = (keep[source, :] + other[source, :].astype(F32)).astype(BF16)
            first, at = first + part, at + step


def add_packed(values):
    packed = PACKED
    gains = values[:packed]
    return pack_gains(gains[0:1] + gains[1:2], gains[2:3] + gains[3:4])


def sum_kernel(*refs):
    sums_out = refs[-1]
    sums = tree_sum([block[...].astype(F32) for block in refs[:-1]])
    sums_out[...] = sums.astype(BF16)
    sums_out[:PACKED] = add_packed(sums)


def join_kernel(own, other, sums_out):
    sums = own[...].astype(F32) + other[...].astype(F32)
    sums_out[...] = sums.astype(BF16)
    sums_out[:PACKED] = add_packed(sums)


def whole_kernel(own, other, gains_out, mine):
    packed = gains_out.shape[0]
    sums = own[...].astype(F32) + other[...].astype(F32)
    gains_out[...] = sums[:packed]
    mine[...] = sums[packed:].astype(BF16)


def place_kernel(parts, *refs):
    count = 2 * len(parts)
    sems, wholes = refs[-1], refs[-1 - len(parts) : -1]
    outs = refs[-1 - len(parts) - count : -1 - len(parts)]
    blocks = refs[: -1 - len(parts) - count]
    members = len(blocks) // 2
    core = lax.axis_index(CORE)
    me = place_in_square()
    for position, block in enumerate(blocks):
        half = core if position < members else 1 - core
        owner = me ^ (position % members)
        at = 0
        for part, whole in zip(parts, wholes):
            step = part // members
            row = pl.multiple_of(half * part + owner * step, 16)
            whole[pl.ds(row, step), :] = block[at : at + step]
            at += step
    copies = []
    for i, whole in enumerate(wholes):
        cut = outs[2 * i].shape[0]
        copies.append(pltpu.make_async_copy(whole.at[:cut], outs[2 * i], sems.at[2 * i]))
        copies.append(pltpu.make_async_copy(whole.at[cut:], outs[2 * i + 1], sems.at[2 * i + 1]))
    for copy in copies:
        copy.start()
    for copy in copies:
        copy.wait()


def finish_kernel(
    edge_grads, pre_grad, sender_sum, receiver_sum, node_part, w_in, edges_grad, local_grad
):
    width = w_in.shape[1]
    edges_grad[...] = (
        edge_grads[...].astype(F32) + dot_nt(pre_grad[...], w_in[:width])
    ).astype(BF16)
    local_grad[...] = (
        node_part[...]
        + dot_nt(sender_sum[...], w_in[width : 2 * width])
        + dot_nt(receiver_sum[...], w_in[2 * width :])
    )


def turn_kernel(top, middle, bottom, along_core, along_chip, center):
    slots = middle.shape[0] // 2

    def turn(up, down):
        up[:slots] = top[:slots]
        up[slots : 2 * slots] = middle[:slots]
        up[2 * slots :] = bottom[:slots]
        down[:slots] = top[2 * slots :]
        down[slots : 2 * slots] = middle[slots:]
        down[2 * slots :] = bottom[2 * slots :]

    core = lax.axis_index(CORE)

    @pl.when(core == 0)
    def _():
        turn(along_core, along_chip)

    @pl.when(core == 1)
    def _():
        turn(along_chip, along_core)

    center[:slots] = top[slots : 2 * slots]
    center[slots:] = bottom[slots : 2 * slots]


def return_kernel(send_list, local_grad, center, along_core, along_chip, nodes_grad, returned):
    slots = send_list.shape[1]

    def fill(up, down):
        for k, (source, i) in enumerate(
            [
                (up, 0),
                (center, 0),
                (down, 0),
                (up, 1),
                (down, 1),
                (up, 2),
                (center, 1),
                (down, 2),
            ]
        ):
            returned[k * slots : (k + 1) * slots] = source[i * slots : (i + 1) * slots]

    core = lax.axis_index(CORE)

    @pl.when(core == 0)
    def _():
        fill(along_chip, along_core)

    @pl.when(core == 1)
    def _():
        fill(along_core, along_chip)

    hot = list_hot(send_list[...], local_grad.shape[0])
    nodes_grad[...] = (local_grad[...] + dot_tn(hot, returned[...])).astype(BF16)


SMEM = pltpu.SMEM
VMEM = pltpu.VMEM
HBM = pltpu.HBM


def call(body, outs, flops, *operands, spaces=(), out_space=VMEM, scratch=()):
    moved = sum(x.size * x.dtype.itemsize for x in operands)
    moved += sum(x.size * jnp.dtype(x.dtype).itemsize for x in outs)
    spaces = list(spaces) + [VMEM] * (len(operands) - len(spaces))
    out_spaces = out_space if isinstance(out_space, list) else [out_space] * len(outs)
    operands = [
        pltpu.with_memory_space_constraint(x, HBM) if space is HBM else x
        for x, space in zip(operands, spaces)
    ]
    return pl.pallas_call(
        body,
        out_shape=outs,
        in_specs=[pl.BlockSpec(memory_space=space) for space in spaces],
        out_specs=[pl.BlockSpec(memory_space=space) for space in out_spaces],
        scratch_shapes=list(scratch),
        compiler_params=pltpu.CompilerParams(vmem_limit_bytes=VMEM_LIMIT),
        cost_estimate=pl.CostEstimate(flops=flops, bytes_accessed=moved, transcendentals=0),
    )(*operands)


def like(array):
    return jax.ShapeDtypeStruct(array.shape, array.dtype)


def shaped(rows, columns, dtype):
    return jax.ShapeDtypeStruct((rows, columns), dtype)


def placed(parts, blocks, width):
    return call(
        functools.partial(place_kernel, parts),
        [
            shaped(3 * width, width, BF16),
            shaped(width, width, BF16),
            shaped(2 * width, width, BF16),
            shaped(width, width, BF16),
        ],
        0,
        *blocks,
        out_space=HBM,
        scratch=[pltpu.VMEM((2 * part, width), BF16) for part in parts]
        + [pltpu.SemaphoreType.DMA((2 * len(parts),))],
    )


def joined(sums, packed, *beside):
    rows, width = sums.shape
    size = lax.axis_size(FAR)
    distance = 1
    while True:
        other = lax.ppermute(sums, FAR, [(i, i ^ distance) for i in range(size)])
        distance *= 2
        if distance == size:
            break
        (sums,) = call(join_kernel, [like(sums)], 0, sums, other)
    other, *beside = lax.optimization_barrier((other, *beside))
    gains, mine = call(
        whole_kernel,
        [shaped(packed, width, F32), shaped(rows - packed, width, BF16)],
        0,
        sums,
        other,
    )
    return gains, mine, *beside


def on_device(
    nodes,
    edges,
    edge_grads,
    node_grads,
    send_list,
    senders,
    receivers,
    tile_count,
    w_edge_in,
    w_edge_out,
    gain_edge,
    w_node_in,
    w_node_out,
    gain_node,
):
    count, width = nodes.shape
    slots = send_list.shape[1]
    halo_rows = 8 * slots
    edge_rows = edges.shape[0]
    tile_rows = senders.shape[1]
    square = 2 * width * width
    up, down, own_rows, straight, corner_up, corner_down, nodes, send_list = call(
        send_kernel,
        [shaped(2 * slots, width, BF16)] * 2
        + [shaped(slots, width, BF16)] * 4
        + [like(nodes), like(send_list)],
        2 * halo_rows * count * width,
        nodes,
        send_list,
        spaces=[HBM, HBM],
        scratch=[pltpu.SemaphoreType.DMA((2,))],
    )
    from_low = passed_along(up, PX, 1)
    from_high = passed_along(down, PX, -1)
    straight = across_chips(straight)
    corner_low = to_corner(corner_up, 1)
    corner_high = to_corner(corner_down, -1)
    fetched = [
        senders,
        receivers,
        edges,
        w_edge_in,
        w_edge_out,
        gain_edge,
        w_node_in,
        w_node_out,
        gain_node,
        node_grads,
        edge_grads,
    ]
    near_hot, halo_hot, *fetched = call(
        functools.partial(index_kernel, len(fetched)),
        [
            shaped(edge_rows, 2 * count, BF16),
            shaped(edge_rows, halo_rows, BF16),
        ]
        + [like(x) for x in fetched],
        0,
        *fetched,
        spaces=[HBM] * len(fetched),
        scratch=[pltpu.SemaphoreType.DMA((len(fetched),))],
    )
    (
        senders,
        receivers,
        edges,
        w_edge_in,
        w_edge_out,
        gain_edge,
        w_node_in,
        w_node_out,
        gain_node,
        node_grads,
        edge_grads,
    ) = fetched
    from_low, from_high, near_hot = lax.optimization_barrier((from_low, from_high, near_hot))
    from_core = across_cores(
        jnp.concatenate([own_rows, from_low[slots:], from_high[slots:]])
    )
    pre_local, sender_columns, receiver_columns = call(
        local_kernel,
        [
            shaped(edge_rows, width, F32),
            shaped(count + halo_rows, edge_rows, BF16),
            shaped(count, edge_rows, BF16),
        ],
        square * (2 * count + edge_rows) + 4 * edge_rows * count * width,
        nodes,
        edges,
        senders,
        receivers,
        near_hot,
        w_edge_in,
    )
    parts = (2 * width, 3 * width // 2)
    halves = sum(parts)
    pre_grad, sender_sum, receiver_sum, node_part, top, middle, bottom, keep, away, gains = call(
        functools.partial(layer_kernel, tile_rows),
        [
            shaped(edge_rows, width, BF16),
            shaped(count, width, BF16),
            shaped(count, width, BF16),
            shaped(count, width, F32),
            shaped(3 * slots, width, BF16),
            shaped(2 * slots, width, BF16),
            shaped(3 * slots, width, BF16),
            shaped(halves, width, F32),
            shaped(halves + PACKED, width, BF16),
            shaped(PACKED, width, BF16),
        ],
        square * (6 * edge_rows + 11 * count + 2 * halo_rows)
        + 2 * edge_rows * (4 * count + halo_rows) * width,
        tile_count,
        nodes,
        node_grads,
        edges,
        edge_grads,
        pre_local,
        halo_hot,
        near_hot,
        sender_columns,
        receiver_columns,
        from_low,
        from_high,
        from_core,
        straight,
        corner_low,
        corner_high,
        w_edge_in,
        w_edge_out,
        gain_edge,
        w_node_in,
        w_node_out,
        gain_node,
        spaces=[SMEM],
        scratch=[
            pltpu.VMEM((edge_rows, width), F32),
            pltpu.VMEM((edge_rows, width), BF16),
            pltpu.VMEM((edge_rows, width), F32),
            pltpu.VMEM((edge_rows, 128), F32),
            pltpu.VMEM((3 * width, width), F32),
            pltpu.VMEM((4 * width, width), F32),
        ],
    )
    other = across_cores(away)
    members = square_members()
    own, *blocks = call(
        functools.partial(pair_kernel, parts),
        [shaped(PACKED + halves // members, width, BF16)] * members,
        0,
        keep,
        gains,
        other,
    )
    received = [in_square(block, offset) for offset, block in enumerate(blocks, 1)]
    along_core, along_chip, center = call(
        turn_kernel,
        [
            shaped(3 * slots, width, BF16),
            shaped(3 * slots, width, BF16),
            shaped(2 * slots, width, BF16),
        ],
        10**10,
        passed_along(top, PX, 1),
        middle,
        passed_along(bottom, PX, -1),
    )
    *received, along_core, along_chip = lax.optimization_barrier(
        (*received, along_core, along_chip)
    )
    (sums,) = call(sum_kernel, [like(own)], 0, own, *received)
    gains, mine, along_core, along_chip = joined(
        sums, gains.shape[0], across_cores(along_core), across_chips(along_chip)
    )
    blocks = [mine] + [in_square(mine, offset) for offset in range(1, members)]
    gain_edge_grad = (gains[0] + gains[1]).astype(BF16)
    gain_node_grad = (gains[2] + gains[3]).astype(BF16)
    edges_grad, local_grad = call(
        finish_kernel,
        [shaped(edge_rows, width, BF16), shaped(count, width, F32)],
        square * (edge_rows + 2 * count),
        edge_grads,
        pre_grad,
        sender_sum,
        receiver_sum,
        node_part,
        w_edge_in,
    )
    (nodes_grad,) = call(
        return_kernel,
        [shaped(count, width, BF16)],
        2 * halo_rows * count * width,
        send_list,
        local_grad,
        center,
        along_core,
        along_chip,
        scratch=[pltpu.VMEM((halo_rows, width), BF16)],
    )
    done = (nodes_grad, edges_grad, gain_edge_grad, gain_node_grad)
    for i in range(members):
        blocks[i], *done = lax.optimization_barrier((blocks[i], *done))
    nodes_grad, edges_grad, gain_edge_grad, gain_node_grad = done
    blocks += [across_cores(block) for block in blocks]
    w_edge_in_grad, w_edge_out_grad, w_node_in_grad, w_node_out_grad = placed(
        parts, blocks, width
    )
    return (
        nodes_grad,
        edges_grad,
        w_edge_in_grad,
        w_edge_out_grad,
        gain_edge_grad,
        w_node_in_grad,
        w_node_out_grad,
        gain_node_grad,
    )


def solution(mesh):
    in_specs = (
        P(("groups",) + PX + PY, None),
        P(("groups",) + PX + PY, None),
        P(("groups",) + PX + PY, None),
        P(("groups",) + PX + PY, None),
        P(("groups",) + PX + PY, None),
        P(("groups",) + PX + PY, None),
        P(("groups",) + PX + PY, None),
        P(("groups",) + PX + PY),
        P(),
        P(),
        P(),
        P(),
        P(),
        P(),
    )
    out_specs = (
        P(("groups",) + PX + PY, None),
        P(("groups",) + PX + PY, None),
        P("groups", None),
        P("groups", None),
        P("groups"),
        P("groups", None),
        P("groups", None),
        P("groups"),
    )
    groups, px, py = mesh.devices.shape
    by_core = jax.sharding.Mesh(
        mesh.devices.reshape(groups, px // 2, 2, py // 2, 2), ("groups",) + PX + PY
    )
    return jax.shard_map(
        on_device, mesh=by_core, in_specs=in_specs, out_specs=out_specs, check_vma=False
    )
```

```python
import functools

import jax
import jax.numpy as jnp
from jax import lax
from jax.experimental import pallas as pl
from jax.experimental.pallas import tpu as pltpu
from jax.sharding import PartitionSpec as P

EPS = 1e-05
BF16 = jnp.bfloat16
F32 = jnp.float32
PACKED = 8
VMEM_LIMIT = 24 * 1024 * 1024


CORE = "core"
FAR = "far"
NEAR = "near"
PX = (FAR, NEAR)
PY = ("side", CORE)
SQUARE = (NEAR, "side")


def other_neighbour(i, size):
    return (i + 1 if i % 2 else i - 1) % size


def in_pair(array, axis):
    return lax.ppermute(array, axis, [(i, i ^ 1) for i in range(lax.axis_size(axis))])


def out_of_pair(array, axis):
    size = lax.axis_size(axis)
    return lax.ppermute(array, axis, [(i, other_neighbour(i, size)) for i in range(size)])


def square_members():
    return lax.axis_size(SQUARE)


def place_in_square():
    near, side = SQUARE
    return lax.axis_index(near) * lax.axis_size(side) + lax.axis_index(side)


def in_square(array, offset):
    return lax.ppermute(array, SQUARE, [(i, i ^ offset) for i in range(square_members())])


def tree_sum(terms):
    while len(terms) > 1:
        terms = [terms[i] + terms[i + 1] for i in range(0, len(terms), 2)]
    return terms[0]


def across_cores(array):
    return in_pair(array, CORE)


def by_pair(axis, up, down, inner, outer):
    first = lax.axis_index(axis) == 0

    @pl.when(first)
    def _():
        inner[...] = up
        outer[...] = down

    @pl.when(jnp.logical_not(first))
    def _():
        inner[...] = down
        outer[...] = up


def from_pair(axis, inner, outer):
    first = lax.axis_index(axis) == 0
    return jnp.where(first, outer, inner), jnp.where(first, inner, outer)


def dot(left, right):
    return jnp.dot(left, right, preferred_element_type=F32)


def dot_tn(left, right):
    return lax.dot_general(left, right, (((0,), (0,)), ((), ())), preferred_element_type=F32)


def dot_nt(left, right):
    return lax.dot_general(left, right, (((1,), (1,)), ((), ())), preferred_element_type=F32)


def sigmoid(value):
    return 0.5 + 0.5 * jnp.tanh(0.5 * value)


def normalize(value):
    centered = value - jnp.mean(value, axis=-1, keepdims=True)
    scale_inv = lax.rsqrt(jnp.mean(centered * centered, axis=-1, keepdims=True) + EPS)
    return centered * scale_inv, scale_inv


def norm_back(normed, scale_inv, gain, upstream):
    scaled = upstream * gain
    inner = (
        scaled
        - jnp.mean(scaled, axis=-1, keepdims=True)
        - normed * jnp.mean(scaled * normed, axis=-1, keepdims=True)
    )
    return inner * scale_inv


def columns_of(ids):
    rows, lanes = ids.shape
    padded = -(-rows // 8) * 8
    if padded > rows:
        ids = jnp.concatenate([ids, jnp.zeros((padded - rows, lanes), ids.dtype)], axis=0)
    return ids.T


def hot_rows(columns, tiles, base, count):
    parts = []
    for tile in tiles:
        column = columns[:, tile : tile + 1] - base
        lanes = lax.broadcasted_iota(jnp.int32, (columns.shape[0], count), 1)
        parts.append(jnp.where(lanes == column, 1.0, 0.0).astype(BF16))
    return jnp.concatenate(parts, axis=0) if len(parts) > 1 else parts[0]


def hot_columns(ids, tiles, base, count):
    parts = []
    for tile in tiles:
        row = ids[tile : tile + 1, :] - base
        subs = lax.broadcasted_iota(jnp.int32, (count, ids.shape[1]), 0)
        parts.append(jnp.where(subs == row, 1.0, 0.0).astype(BF16))
    return jnp.concatenate(parts, axis=1) if len(parts) > 1 else parts[0]


def list_hot(ids, count):
    directions, slots = ids.shape
    wide = jnp.concatenate([ids, jnp.zeros((directions, 128 - slots), ids.dtype)], axis=1)
    columns = wide.T
    parts = []
    for k in range(directions):
        lanes = lax.broadcasted_iota(jnp.int32, (slots, count), 1)
        parts.append(jnp.where(lanes == columns[:slots, k : k + 1], 1.0, 0.0).astype(BF16))
    return jnp.concatenate(parts, axis=0)


def live_rows(count_ref, tile_rows, rows):
    index = lax.broadcasted_iota(jnp.int32, (rows, 1), 0)
    return jnp.where(index < count_ref[0] * tile_rows, 1.0, 0.0)


def fetch_all(sources, targets, sems):
    copies = [
        pltpu.make_async_copy(source, target, sems.at[i])
        for i, (source, target) in enumerate(zip(sources, targets))
    ]
    for copy in copies:
        copy.start()
    return copies


def send_kernel(nodes_hbm, list_hbm, inner, outer, middle, nodes, send_list, sems):
    slots = send_list.shape[1]
    for copy in fetch_all([list_hbm, nodes_hbm], [send_list, nodes], sems):
        copy.wait()
    rows = dot(list_hot(send_list[...], nodes.shape[0]), nodes[...]).astype(BF16)
    by_pair(NEAR, rows[5 * slots :], rows[: 3 * slots], inner, outer)
    middle[...] = rows[3 * slots : 5 * slots]


def corner_kernel(inner, outer, middle, along_core, along_chip, straight):
    slots = middle.shape[0] // 2
    low, high = from_pair(NEAR, inner[...], outer[...])
    up = jnp.concatenate([high[2 * slots :], middle[slots:], low[2 * slots :]], axis=0)
    down = jnp.concatenate([high[:slots], middle[:slots], low[:slots]], axis=0)
    by_pair(CORE, up, down, along_core, along_chip)
    straight[:slots] = high[slots : 2 * slots]
    straight[slots:] = low[slots : 2 * slots]


def index_kernel(sources, *refs):
    fetched, refs = refs[:sources], refs[sources:]
    near_rows, halo_rows = refs[:2]
    targets, sems = refs[2:-1], refs[-1]
    senders, receivers = targets[:2]
    copies = fetch_all(fetched, targets, sems)
    for copy in copies[:2]:
        copy.wait()
    tile_rows = senders.shape[1]
    count = near_rows.shape[1] // 2
    by_sender = columns_of(senders[...])
    by_receiver = columns_of(receivers[...])
    for tile in range(senders.shape[0]):
        rows = slice(tile * tile_rows, (tile + 1) * tile_rows)
        near_rows[rows, :count] = hot_rows(by_sender, [tile], 0, count)
        near_rows[rows, count:] = hot_rows(by_receiver, [tile], 0, count)
        halo_rows[rows, :] = hot_rows(by_sender, [tile], count, halo_rows.shape[1])
    for copy in copies[2:]:
        copy.wait()


def local_kernel(
    nodes, edges, senders, receivers, near_rows, w_in, pre, sender_columns, receiver_columns
):
    width = nodes.shape[1]
    tile_rows = senders.shape[1]
    extended = sender_columns.shape[0]
    count = receiver_columns.shape[0]
    sender_ids = senders[...]
    receiver_ids = receivers[...]
    for tile in range(senders.shape[0]):
        rows = slice(tile * tile_rows, (tile + 1) * tile_rows)
        sender_columns[:, rows] = hot_columns(sender_ids, [tile], 0, extended)
        receiver_columns[:, rows] = hot_columns(receiver_ids, [tile], 0, count)
    x = nodes[...]
    table = jnp.concatenate(
        [
            dot(x, w_in[width : 2 * width]).astype(BF16),
            dot(x, w_in[2 * width :]).astype(BF16),
        ],
        axis=0,
    )
    pre[...] = dot(edges[...], w_in[:width]) + dot(near_rows[...], table)


def split_by_core(sums, first, keep_out, away_out):
    half = sums.shape[0] // 2
    core = lax.axis_index(CORE)
    keep_out[first : first + half] = sums[pl.ds(pl.multiple_of(core * half, half), half), :]
    away = sums[pl.ds(pl.multiple_of((1 - core) * half, half), half), :]
    away_out[first : first + half] = away.astype(BF16)


def pack_gains(edge_gain, node_gain):
    edge_high = edge_gain.astype(BF16).astype(F32)
    node_high = node_gain.astype(BF16).astype(F32)
    row = lax.broadcasted_iota(jnp.int32, (PACKED, edge_gain.shape[1]), 0)
    packed = jnp.where(row == 0, edge_high, 0.0)
    packed = jnp.where(row == 1, edge_gain - edge_high, packed)
    packed = jnp.where(row == 2, node_high, packed)
    packed = jnp.where(row == 3, node_gain - node_high, packed)
    return packed.astype(BF16)


def layer_kernel(
    tile_rows,
    count_ref,
    nodes,
    node_grads,
    edges,
    edge_grads,
    pre_local,
    halo_rows,
    near_rows,
    sender_columns,
    receiver_columns,
    straight,
    along_core,
    along_chip,
    w_in,
    w_out,
    gain_edge,
    w_node_in,
    w_node_out,
    gain_node,
    pre_grad_out,
    sender_out,
    receiver_out,
    node_part_out,
    inner_out,
    outer_out,
    middle_out,
    keep_out,
    away_out,
    gains_out,
    slope_kept,
    hidden_kept,
    normed_kept,
    scale_kept,
    node_sums,
    edge_sums,
):
    count, width = nodes.shape
    edge_rows = edges.shape[0]
    live = live_rows(count_ref, tile_rows, edge_rows)
    slots = straight.shape[0] // 2
    up, down = from_pair(CORE, along_core[...], along_chip[...])
    halo = jnp.concatenate(
        [
            down[:slots],
            straight[:slots],
            up[:slots],
            down[slots : 2 * slots],
            up[slots : 2 * slots],
            down[2 * slots :],
            straight[slots:],
            up[2 * slots :],
        ],
        axis=0,
    )
    table = dot(halo, w_in[width : 2 * width]).astype(BF16)
    gain = gain_edge[...].astype(F32)[None, :]
    value = pre_local[...] + dot(halo_rows[...], table)
    sigma = sigmoid(value)
    hidden = (value * sigma).astype(BF16)
    hidden_kept[...] = hidden
    slope_kept[...] = sigma * (1.0 + value * (1.0 - sigma))
    edge_normed, edge_scale = normalize(dot(hidden, w_out[...]))
    normed_kept[...] = edge_normed
    scale_kept[...] = jnp.broadcast_to(edge_scale, (edge_rows, 128))
    message = (live * gain * edge_normed).astype(BF16)
    total = dot(receiver_columns[...], message)
    aggregated = total.astype(BF16)
    x = nodes[...]
    w_first = w_node_in[:width]
    w_second = w_node_in[width:]
    node_pre = dot(x, w_first) + dot(aggregated, w_second)
    sigma = sigmoid(node_pre)
    node_hidden = (node_pre * sigma).astype(BF16)
    normed, scale_inv = normalize(dot(node_hidden, w_node_out[...]))
    upstream = node_grads[...].astype(F32)
    out_grad = norm_back(normed, scale_inv, gain_node[...].astype(F32)[None, :], upstream).astype(BF16)
    slope = sigma * (1.0 + node_pre * (1.0 - sigma))
    pre_grad = (dot_nt(out_grad, w_node_out[...]) * slope).astype(BF16)
    agg_grad = dot_nt(pre_grad, w_second).astype(BF16)
    node_part_out[...] = upstream + dot_nt(pre_grad, w_first)
    node_sums[:width] = dot_tn(x, pre_grad)
    node_sums[width : 2 * width] = dot_tn(aggregated, pre_grad)
    node_sums[2 * width : 3 * width] = dot_tn(node_hidden, out_grad)
    node_gain = jnp.sum(upstream * normed, axis=0, keepdims=True)
    upstream = live * (
        edge_grads[...].astype(F32) + dot(near_rows[:, count:], agg_grad)
    )
    edge_normed = normed_kept[...]
    edge_gain = jnp.sum(upstream * edge_normed, axis=0, keepdims=True)
    out_grad = norm_back(edge_normed, scale_kept[:, :1], gain, upstream).astype(BF16)
    pre_grad = (dot_nt(out_grad, w_out[...]) * slope_kept[...]).astype(BF16)
    pre_grad_out[...] = pre_grad
    sender_total = dot(sender_columns[...], pre_grad)
    receiver_total = dot(receiver_columns[...], pre_grad)
    own = sender_total[:count].astype(BF16)
    away = sender_total[count:].astype(BF16)
    received = receiver_total.astype(BF16)
    sender_out[...] = own
    receiver_out[...] = received
    halo_grad = dot_nt(away, w_in[width : 2 * width]).astype(BF16)
    by_pair(NEAR, halo_grad[: 3 * slots], halo_grad[5 * slots :], inner_out, outer_out)
    middle_out[...] = halo_grad[3 * slots : 5 * slots]
    edge_sums[:width] = dot_tn(edges[...], pre_grad)
    edge_sums[width : 2 * width] = dot_tn(x, own) + dot_tn(halo, away)
    edge_sums[2 * width : 3 * width] = dot_tn(x, received)
    edge_sums[3 * width : 4 * width] = dot_tn(hidden_kept[...], out_grad)
    split_by_core(edge_sums, 0, keep_out, away_out)
    split_by_core(node_sums, edge_sums.shape[0] // 2, keep_out, away_out)
    gains = pack_gains(edge_gain, node_gain)
    away_out[keep_out.shape[0] :] = gains
    gains_out[...] = gains


def pair_kernel(parts, keep, gains, other, *outs):
    rows = keep.shape[0]
    packed = gains.shape[0]
    members = len(outs)
    both = gains[...].astype(F32) + other[rows : rows + packed].astype(F32)
    summed = pack_gains(both[0:1] + both[1:2], both[2:3] + both[3:4])
    me = place_in_square()
    for offset, out in enumerate(outs):
        owner = me ^ offset
        out[:packed] = summed
        first, at = 0, packed
        for part in parts:
            step = part // members
            source = pl.ds(pl.multiple_of(first + owner * step, 16), step)
            out[at : at + step] = (keep[source, :] + other[source, :].astype(F32)).astype(BF16)
            first, at = first + part, at + step


def add_packed(values):
    packed = PACKED
    gains = values[:packed]
    return pack_gains(gains[0:1] + gains[1:2], gains[2:3] + gains[3:4])


def sum_kernel(*refs):
    sums_out = refs[-1]
    sums = tree_sum([block[...].astype(F32) for block in refs[:-1]])
    sums_out[...] = sums.astype(BF16)
    sums_out[:PACKED] = add_packed(sums)


def join_kernel(own, other, sums_out):
    sums = own[...].astype(F32) + other[...].astype(F32)
    sums_out[...] = sums.astype(BF16)
    sums_out[:PACKED] = add_packed(sums)


def whole_kernel(own, other, gains_out, mine):
    packed = gains_out.shape[0]
    sums = own[...].astype(F32) + other[...].astype(F32)
    gains_out[...] = sums[:packed]
    mine[...] = sums[packed:].astype(BF16)


def place_kernel(parts, *refs):
    count = 2 * len(parts)
    sems, wholes = refs[-1], refs[-1 - len(parts) : -1]
    outs = refs[-1 - len(parts) - count : -1 - len(parts)]
    blocks = refs[: -1 - len(parts) - count]
    members = len(blocks) // 2
    core = lax.axis_index(CORE)
    me = place_in_square()
    for position, block in enumerate(blocks):
        half = core if position < members else 1 - core
        owner = me ^ (position % members)
        at = 0
        for part, whole in zip(parts, wholes):
            step = part // members
            row = pl.multiple_of(half * part + owner * step, 16)
            whole[pl.ds(row, step), :] = block[at : at + step]
            at += step
    copies = []
    for i, whole in enumerate(wholes):
        cut = outs[2 * i].shape[0]
        copies.append(pltpu.make_async_copy(whole.at[:cut], outs[2 * i], sems.at[2 * i]))
        copies.append(pltpu.make_async_copy(whole.at[cut:], outs[2 * i + 1], sems.at[2 * i + 1]))
    for copy in copies:
        copy.start()
    for copy in copies:
        copy.wait()


def finish_kernel(
    edge_grads, pre_grad, sender_sum, receiver_sum, node_part, w_in, edges_grad, local_grad
):
    width = w_in.shape[1]
    edges_grad[...] = (
        edge_grads[...].astype(F32) + dot_nt(pre_grad[...], w_in[:width])
    ).astype(BF16)
    local_grad[...] = (
        node_part[...]
        + dot_nt(sender_sum[...], w_in[width : 2 * width])
        + dot_nt(receiver_sum[...], w_in[2 * width :])
    )


def turn_kernel(inner, outer, middle, along_core, along_chip, center):
    slots = middle.shape[0] // 2
    top, bottom = from_pair(NEAR, inner[...], outer[...])
    up = jnp.concatenate([top[:slots], middle[:slots], bottom[:slots]], axis=0)
    down = jnp.concatenate([top[2 * slots :], middle[slots:], bottom[2 * slots :]], axis=0)
    by_pair(CORE, up, down, along_core, along_chip)
    center[:slots] = top[slots : 2 * slots]
    center[slots:] = bottom[slots : 2 * slots]


def return_kernel(send_list, local_grad, center, along_core, along_chip, nodes_grad):
    slots = send_list.shape[1]
    up, down = from_pair(CORE, along_core[...], along_chip[...])
    returned = jnp.concatenate(
        [
            up[:slots],
            center[:slots],
            down[:slots],
            up[slots : 2 * slots],
            down[slots : 2 * slots],
            up[2 * slots :],
            center[slots:],
            down[2 * slots :],
        ],
        axis=0,
    )
    hot = list_hot(send_list[...], local_grad.shape[0])
    nodes_grad[...] = (local_grad[...] + dot_tn(hot, returned)).astype(BF16)


SMEM = pltpu.SMEM
VMEM = pltpu.VMEM
HBM = pltpu.HBM


def call(body, outs, flops, *operands, spaces=(), out_space=VMEM, scratch=()):
    moved = sum(x.size * x.dtype.itemsize for x in operands)
    moved += sum(x.size * jnp.dtype(x.dtype).itemsize for x in outs)
    spaces = list(spaces) + [VMEM] * (len(operands) - len(spaces))
    out_spaces = out_space if isinstance(out_space, list) else [out_space] * len(outs)
    operands = [
        pltpu.with_memory_space_constraint(x, HBM) if space is HBM else x
        for x, space in zip(operands, spaces)
    ]
    return pl.pallas_call(
        body,
        out_shape=outs,
        in_specs=[pl.BlockSpec(memory_space=space) for space in spaces],
        out_specs=[pl.BlockSpec(memory_space=space) for space in out_spaces],
        scratch_shapes=list(scratch),
        compiler_params=pltpu.CompilerParams(vmem_limit_bytes=VMEM_LIMIT),
        cost_estimate=pl.CostEstimate(flops=flops, bytes_accessed=moved, transcendentals=0),
    )(*operands)


def like(array):
    return jax.ShapeDtypeStruct(array.shape, array.dtype)


def shaped(rows, columns, dtype):
    return jax.ShapeDtypeStruct((rows, columns), dtype)


def placed(parts, blocks, width):
    return call(
        functools.partial(place_kernel, parts),
        [
            shaped(3 * width, width, BF16),
            shaped(width, width, BF16),
            shaped(2 * width, width, BF16),
            shaped(width, width, BF16),
        ],
        0,
        *blocks,
        out_space=HBM,
        scratch=[pltpu.VMEM((2 * part, width), BF16) for part in parts]
        + [pltpu.SemaphoreType.DMA((2 * len(parts),))],
    )


def joined(sums, packed, *beside):
    rows, width = sums.shape
    size = lax.axis_size(FAR)
    distance = 1
    while True:
        other = lax.ppermute(sums, FAR, [(i, i ^ distance) for i in range(size)])
        distance *= 2
        if distance == size:
            break
        (sums,) = call(join_kernel, [like(sums)], 0, sums, other)
    other, *beside = lax.optimization_barrier((other, *beside))
    gains, mine = call(
        whole_kernel,
        [shaped(packed, width, F32), shaped(rows - packed, width, BF16)],
        0,
        sums,
        other,
    )
    return gains, mine, *beside


def on_device(
    nodes,
    edges,
    edge_grads,
    node_grads,
    send_list,
    senders,
    receivers,
    tile_count,
    w_edge_in,
    w_edge_out,
    gain_edge,
    w_node_in,
    w_node_out,
    gain_node,
):
    count, width = nodes.shape
    slots = send_list.shape[1]
    halo_rows = 8 * slots
    edge_rows = edges.shape[0]
    tile_rows = senders.shape[1]
    square = 2 * width * width
    inner, outer, middle, nodes, send_list = call(
        send_kernel,
        [
            shaped(3 * slots, width, BF16),
            shaped(3 * slots, width, BF16),
            shaped(2 * slots, width, BF16),
            like(nodes),
            like(send_list),
        ],
        2 * halo_rows * count * width,
        nodes,
        send_list,
        spaces=[HBM, HBM],
        scratch=[pltpu.SemaphoreType.DMA((2,))],
    )
    inner = in_pair(inner, PX)
    outer = out_of_pair(outer, PX)
    fetched = [
        senders,
        receivers,
        edges,
        w_edge_in,
        w_edge_out,
        gain_edge,
        w_node_in,
        w_node_out,
        gain_node,
        node_grads,
        edge_grads,
    ]
    near_hot, halo_hot, *fetched = call(
        functools.partial(index_kernel, len(fetched)),
        [
            shaped(edge_rows, 2 * count, BF16),
            shaped(edge_rows, halo_rows, BF16),
        ]
        + [like(x) for x in fetched],
        0,
        *fetched,
        spaces=[HBM] * len(fetched),
        scratch=[pltpu.SemaphoreType.DMA((len(fetched),))],
    )
    (
        senders,
        receivers,
        edges,
        w_edge_in,
        w_edge_out,
        gain_edge,
        w_node_in,
        w_node_out,
        gain_node,
        node_grads,
        edge_grads,
    ) = fetched
    inner, outer, near_hot = lax.optimization_barrier((inner, outer, near_hot))
    along_core, along_chip, straight = call(
        corner_kernel,
        [
            shaped(3 * slots, width, BF16),
            shaped(3 * slots, width, BF16),
            shaped(2 * slots, width, BF16),
        ],
        0,
        inner,
        outer,
        middle,
    )
    along_chip = out_of_pair(along_chip, PY)
    along_core = across_cores(along_core)
    pre_local, sender_columns, receiver_columns = call(
        local_kernel,
        [
            shaped(edge_rows, width, F32),
            shaped(count + halo_rows, edge_rows, BF16),
            shaped(count, edge_rows, BF16),
        ],
        square * (2 * count + edge_rows) + 4 * edge_rows * count * width,
        nodes,
        edges,
        senders,
        receivers,
        near_hot,
        w_edge_in,
    )
    parts = (2 * width, 3 * width // 2)
    halves = sum(parts)
    pre_grad, sender_sum, receiver_sum, node_part, inner, outer, middle, keep, away, gains = call(
        functools.partial(layer_kernel, tile_rows),
        [
            shaped(edge_rows, width, BF16),
            shaped(count, width, BF16),
            shaped(count, width, BF16),
            shaped(count, width, F32),
            shaped(3 * slots, width, BF16),
            shaped(3 * slots, width, BF16),
            shaped(2 * slots, width, BF16),
            shaped(halves, width, F32),
            shaped(halves + PACKED, width, BF16),
            shaped(PACKED, width, BF16),
        ],
        square * (6 * edge_rows + 11 * count + 2 * halo_rows)
        + 2 * edge_rows * (4 * count + halo_rows) * width,
        tile_count,
        nodes,
        node_grads,
        edges,
        edge_grads,
        pre_local,
        halo_hot,
        near_hot,
        sender_columns,
        receiver_columns,
        straight,
        along_core,
        along_chip,
        w_edge_in,
        w_edge_out,
        gain_edge,
        w_node_in,
        w_node_out,
        gain_node,
        spaces=[SMEM],
        scratch=[
            pltpu.VMEM((edge_rows, width), F32),
            pltpu.VMEM((edge_rows, width), BF16),
            pltpu.VMEM((edge_rows, width), F32),
            pltpu.VMEM((edge_rows, 128), F32),
            pltpu.VMEM((3 * width, width), F32),
            pltpu.VMEM((4 * width, width), F32),
        ],
    )
    other = across_cores(away)
    members = square_members()
    own, *blocks = call(
        functools.partial(pair_kernel, parts),
        [shaped(PACKED + halves // members, width, BF16)] * members,
        0,
        keep,
        gains,
        other,
    )
    received = [in_square(block, offset) for offset, block in enumerate(blocks, 1)]
    along_core, along_chip, center = call(
        turn_kernel,
        [
            shaped(3 * slots, width, BF16),
            shaped(3 * slots, width, BF16),
            shaped(2 * slots, width, BF16),
        ],
        10**10,
        in_pair(inner, PX),
        out_of_pair(outer, PX),
        middle,
    )
    *received, along_core, along_chip = lax.optimization_barrier(
        (*received, along_core, along_chip)
    )
    (sums,) = call(sum_kernel, [like(own)], 0, own, *received)
    gains, mine, along_core, along_chip = joined(
        sums, gains.shape[0], across_cores(along_core), out_of_pair(along_chip, PY)
    )
    blocks = [mine] + [in_square(mine, offset) for offset in range(1, members)]
    gain_edge_grad = (gains[0] + gains[1]).astype(BF16)
    gain_node_grad = (gains[2] + gains[3]).astype(BF16)
    edges_grad, local_grad = call(
        finish_kernel,
        [shaped(edge_rows, width, BF16), shaped(count, width, F32)],
        square * (edge_rows + 2 * count),
        edge_grads,
        pre_grad,
        sender_sum,
        receiver_sum,
        node_part,
        w_edge_in,
    )
    (nodes_grad,) = call(
        return_kernel,
        [shaped(count, width, BF16)],
        2 * halo_rows * count * width,
        send_list,
        local_grad,
        center,
        along_core,
        along_chip,
    )
    done = (nodes_grad, edges_grad, gain_edge_grad, gain_node_grad)
    for i in range(members):
        blocks[i], *done = lax.optimization_barrier((blocks[i], *done))
    nodes_grad, edges_grad, gain_edge_grad, gain_node_grad = done
    blocks += [across_cores(block) for block in blocks]
    w_edge_in_grad, w_edge_out_grad, w_node_in_grad, w_node_out_grad = placed(
        parts, blocks, width
    )
    return (
        nodes_grad,
        edges_grad,
        w_edge_in_grad,
        w_edge_out_grad,
        gain_edge_grad,
        w_node_in_grad,
        w_node_out_grad,
        gain_node_grad,
    )


def solution(mesh):
    in_specs = (
        P(("groups",) + PX + PY, None),
        P(("groups",) + PX + PY, None),
        P(("groups",) + PX + PY, None),
        P(("groups",) + PX + PY, None),
        P(("groups",) + PX + PY, None),
        P(("groups",) + PX + PY, None),
        P(("groups",) + PX + PY, None),
        P(("groups",) + PX + PY),
        P(),
        P(),
        P(),
        P(),
        P(),
        P(),
    )
    out_specs = (
        P(("groups",) + PX + PY, None),
        P(("groups",) + PX + PY, None),
        P("groups", None),
        P("groups", None),
        P("groups"),
        P("groups", None),
        P("groups", None),
        P("groups"),
    )
    groups, px, py = mesh.devices.shape
    by_core = jax.sharding.Mesh(
        mesh.devices.reshape(groups, px // 2, 2, py // 2, 2), ("groups",) + PX + PY
    )
    return jax.shard_map(
        on_device, mesh=by_core, in_specs=in_specs, out_specs=out_specs, check_vma=False
    )
```

```python
import functools

import jax
import jax.numpy as jnp
from jax import lax
from jax.experimental import pallas as pl
from jax.experimental.pallas import tpu as pltpu
from jax.sharding import PartitionSpec as P

EPS = 1e-05
BF16 = jnp.bfloat16
F32 = jnp.float32
PACKED = 8
VMEM_LIMIT = 24 * 1024 * 1024


CORE = "core"
FAR = "far"
NEAR = "near"
PX = (FAR, NEAR)
PY = ("side", CORE)
SQUARE = (NEAR, "side")


def other_neighbour(i, size):
    return (i + 1 if i % 2 else i - 1) % size


def in_pair(array, axis):
    return lax.ppermute(array, axis, [(i, i ^ 1) for i in range(lax.axis_size(axis))])


def out_of_pair(array, axis):
    size = lax.axis_size(axis)
    return lax.ppermute(array, axis, [(i, other_neighbour(i, size)) for i in range(size)])


def square_members():
    return lax.axis_size(SQUARE)


def place_in_square():
    near, side = SQUARE
    return lax.axis_index(near) * lax.axis_size(side) + lax.axis_index(side)


def in_square(array, offset):
    return lax.ppermute(array, SQUARE, [(i, i ^ offset) for i in range(square_members())])


def tree_sum(terms):
    while len(terms) > 1:
        terms = [terms[i] + terms[i + 1] for i in range(0, len(terms), 2)]
    return terms[0]


def across_cores(array):
    return in_pair(array, CORE)


def by_pair(axis, up, down, inner, outer):
    first = lax.axis_index(axis) == 0

    @pl.when(first)
    def _():
        inner[...] = up
        outer[...] = down

    @pl.when(jnp.logical_not(first))
    def _():
        inner[...] = down
        outer[...] = up


def from_pair(axis, inner, outer):
    first = lax.axis_index(axis) == 0
    return jnp.where(first, outer, inner), jnp.where(first, inner, outer)


def dot(left, right):
    return jnp.dot(left, right, preferred_element_type=F32)


def dot_tn(left, right):
    return lax.dot_general(left, right, (((0,), (0,)), ((), ())), preferred_element_type=F32)


def dot_nt(left, right):
    return lax.dot_general(left, right, (((1,), (1,)), ((), ())), preferred_element_type=F32)


def sigmoid(value):
    return 0.5 + 0.5 * jnp.tanh(0.5 * value)


def normalize(value):
    centered = value - jnp.mean(value, axis=-1, keepdims=True)
    scale_inv = lax.rsqrt(jnp.mean(centered * centered, axis=-1, keepdims=True) + EPS)
    return centered * scale_inv, scale_inv


def norm_back(normed, scale_inv, gain, upstream):
    scaled = upstream * gain
    inner = (
        scaled
        - jnp.mean(scaled, axis=-1, keepdims=True)
        - normed * jnp.mean(scaled * normed, axis=-1, keepdims=True)
    )
    return inner * scale_inv


def columns_of(ids):
    rows, lanes = ids.shape
    padded = -(-rows // 8) * 8
    if padded > rows:
        ids = jnp.concatenate([ids, jnp.zeros((padded - rows, lanes), ids.dtype)], axis=0)
    return ids.T


def hot_rows(columns, tiles, base, count):
    parts = []
    for tile in tiles:
        column = columns[:, tile : tile + 1] - base
        lanes = lax.broadcasted_iota(jnp.int32, (columns.shape[0], count), 1)
        parts.append(jnp.where(lanes == column, 1.0, 0.0).astype(BF16))
    return jnp.concatenate(parts, axis=0) if len(parts) > 1 else parts[0]


def hot_columns(ids, tiles, base, count):
    parts = []
    for tile in tiles:
        row = ids[tile : tile + 1, :] - base
        subs = lax.broadcasted_iota(jnp.int32, (count, ids.shape[1]), 0)
        parts.append(jnp.where(subs == row, 1.0, 0.0).astype(BF16))
    return jnp.concatenate(parts, axis=1) if len(parts) > 1 else parts[0]


def list_hot(ids, count):
    directions, slots = ids.shape
    wide = jnp.concatenate([ids, jnp.zeros((directions, 128 - slots), ids.dtype)], axis=1)
    columns = wide.T
    parts = []
    for k in range(directions):
        lanes = lax.broadcasted_iota(jnp.int32, (slots, count), 1)
        parts.append(jnp.where(lanes == columns[:slots, k : k + 1], 1.0, 0.0).astype(BF16))
    return jnp.concatenate(parts, axis=0)


def live_rows(count_ref, tile_rows, rows):
    index = lax.broadcasted_iota(jnp.int32, (rows, 1), 0)
    return jnp.where(index < count_ref[0] * tile_rows, 1.0, 0.0)


def fetch_all(sources, targets, sems):
    copies = [
        pltpu.make_async_copy(source, target, sems.at[i])
        for i, (source, target) in enumerate(zip(sources, targets))
    ]
    for copy in copies:
        copy.start()
    return copies


def send_kernel(nodes_hbm, list_hbm, inner, outer, middle, nodes, send_list, sems):
    slots = send_list.shape[1]
    for copy in fetch_all([list_hbm, nodes_hbm], [send_list, nodes], sems):
        copy.wait()
    rows = dot(list_hot(send_list[...], nodes.shape[0]), nodes[...]).astype(BF16)
    by_pair(NEAR, rows[5 * slots :], rows[: 3 * slots], inner, outer)
    middle[...] = rows[3 * slots : 5 * slots]


def corner_kernel(inner, outer, middle, along_core, along_chip, straight):
    slots = middle.shape[0] // 2
    low, high = from_pair(NEAR, inner[...], outer[...])
    up = jnp.concatenate([high[2 * slots :], middle[slots:], low[2 * slots :]], axis=0)
    down = jnp.concatenate([high[:slots], middle[:slots], low[:slots]], axis=0)
    by_pair(CORE, up, down, along_core, along_chip)
    straight[:slots] = high[slots : 2 * slots]
    straight[slots:] = low[slots : 2 * slots]


def index_kernel(sources, *refs):
    fetched, refs = refs[:sources], refs[sources:]
    near_rows, halo_rows = refs[:2]
    targets, sems = refs[2:-1], refs[-1]
    senders, receivers = targets[:2]
    copies = fetch_all(fetched, targets, sems)
    for copy in copies[:2]:
        copy.wait()
    tile_rows = senders.shape[1]
    count = near_rows.shape[1] // 2
    by_sender = columns_of(senders[...])
    by_receiver = columns_of(receivers[...])
    for tile in range(senders.shape[0]):
        rows = slice(tile * tile_rows, (tile + 1) * tile_rows)
        near_rows[rows, :count] = hot_rows(by_sender, [tile], 0, count)
        near_rows[rows, count:] = hot_rows(by_receiver, [tile], 0, count)
        halo_rows[rows, :] = hot_rows(by_sender, [tile], count, halo_rows.shape[1])
    for copy in copies[2:]:
        copy.wait()


def local_kernel(
    nodes, edges, senders, receivers, near_rows, w_in, pre, sender_columns, receiver_columns
):
    width = nodes.shape[1]
    tile_rows = senders.shape[1]
    extended = sender_columns.shape[0]
    count = receiver_columns.shape[0]
    sender_ids = senders[...]
    receiver_ids = receivers[...]
    for tile in range(senders.shape[0]):
        rows = slice(tile * tile_rows, (tile + 1) * tile_rows)
        sender_columns[:, rows] = hot_columns(sender_ids, [tile], 0, extended)
        receiver_columns[:, rows] = hot_columns(receiver_ids, [tile], 0, count)
    x = nodes[...]
    table = jnp.concatenate(
        [
            dot(x, w_in[width : 2 * width]).astype(BF16),
            dot(x, w_in[2 * width :]).astype(BF16),
        ],
        axis=0,
    )
    pre[...] = dot(edges[...], w_in[:width]) + dot(near_rows[...], table)


def split_by_core(sums, first, keep_out, away_out):
    half = sums.shape[0] // 2
    core = lax.axis_index(CORE)
    keep_out[first : first + half] = sums[pl.ds(pl.multiple_of(core * half, half), half), :]
    away = sums[pl.ds(pl.multiple_of((1 - core) * half, half), half), :]
    away_out[first : first + half] = away.astype(BF16)


def pack_gains(edge_gain, node_gain):
    edge_high = edge_gain.astype(BF16).astype(F32)
    node_high = node_gain.astype(BF16).astype(F32)
    row = lax.broadcasted_iota(jnp.int32, (PACKED, edge_gain.shape[1]), 0)
    packed = jnp.where(row == 0, edge_high, 0.0)
    packed = jnp.where(row == 1, edge_gain - edge_high, packed)
    packed = jnp.where(row == 2, node_high, packed)
    packed = jnp.where(row == 3, node_gain - node_high, packed)
    return packed.astype(BF16)


def layer_kernel(
    tile_rows,
    count_ref,
    nodes,
    node_grads,
    edges,
    edge_grads,
    pre_local,
    halo_rows,
    near_rows,
    sender_columns,
    receiver_columns,
    straight,
    along_core,
    along_chip,
    w_in,
    w_out,
    gain_edge,
    w_node_in,
    w_node_out,
    gain_node,
    pre_grad_out,
    sender_out,
    receiver_out,
    node_part_out,
    inner_out,
    outer_out,
    middle_out,
    keep_out,
    away_out,
    gains_out,
    slope_kept,
    hidden_kept,
    normed_kept,
    scale_kept,
    node_sums,
    edge_sums,
):
    count, width = nodes.shape
    edge_rows = edges.shape[0]
    live = live_rows(count_ref, tile_rows, edge_rows)
    slots = straight.shape[0] // 2
    up, down = from_pair(CORE, along_core[...], along_chip[...])
    halo = jnp.concatenate(
        [
            down[:slots],
            straight[:slots],
            up[:slots],
            down[slots : 2 * slots],
            up[slots : 2 * slots],
            down[2 * slots :],
            straight[slots:],
            up[2 * slots :],
        ],
        axis=0,
    )
    table = dot(halo, w_in[width : 2 * width]).astype(BF16)
    gain = gain_edge[...].astype(F32)[None, :]
    value = pre_local[...] + dot(halo_rows[...], table)
    sigma = sigmoid(value)
    hidden = (value * sigma).astype(BF16)
    hidden_kept[...] = hidden
    slope_kept[...] = sigma * (1.0 + value * (1.0 - sigma))
    edge_normed, edge_scale = normalize(dot(hidden, w_out[...]))
    normed_kept[...] = edge_normed
    scale_kept[...] = jnp.broadcast_to(edge_scale, (edge_rows, 128))
    message = (live * gain * edge_normed).astype(BF16)
    total = dot(receiver_columns[...], message)
    aggregated = total.astype(BF16)
    x = nodes[...]
    w_first = w_node_in[:width]
    w_second = w_node_in[width:]
    node_pre = dot(x, w_first) + dot(aggregated, w_second)
    sigma = sigmoid(node_pre)
    node_hidden = (node_pre * sigma).astype(BF16)
    normed, scale_inv = normalize(dot(node_hidden, w_node_out[...]))
    upstream = node_grads[...].astype(F32)
    out_grad = norm_back(normed, scale_inv, gain_node[...].astype(F32)[None, :], upstream).astype(BF16)
    slope = sigma * (1.0 + node_pre * (1.0 - sigma))
    pre_grad = (dot_nt(out_grad, w_node_out[...]) * slope).astype(BF16)
    agg_grad = dot_nt(pre_grad, w_second).astype(BF16)
    node_part_out[...] = upstream + dot_nt(pre_grad, w_first)
    node_sums[:width] = dot_tn(x, pre_grad)
    node_sums[width : 2 * width] = dot_tn(aggregated, pre_grad)
    node_sums[2 * width : 3 * width] = dot_tn(node_hidden, out_grad)
    node_gain = jnp.sum(upstream * normed, axis=0, keepdims=True)
    upstream = live * (
        edge_grads[...].astype(F32) + dot(near_rows[:, count:], agg_grad)
    )
    edge_normed = normed_kept[...]
    edge_gain = jnp.sum(upstream * edge_normed, axis=0, keepdims=True)
    out_grad = norm_back(edge_normed, scale_kept[:, :1], gain, upstream).astype(BF16)
    pre_grad = (dot_nt(out_grad, w_out[...]) * slope_kept[...]).astype(BF16)
    pre_grad_out[...] = pre_grad
    sender_total = dot(sender_columns[...], pre_grad)
    receiver_total = dot(receiver_columns[...], pre_grad)
    own = sender_total[:count].astype(BF16)
    away = sender_total[count:].astype(BF16)
    received = receiver_total.astype(BF16)
    sender_out[...] = own
    receiver_out[...] = received
    halo_grad = dot_nt(away, w_in[width : 2 * width]).astype(BF16)
    by_pair(NEAR, halo_grad[: 3 * slots], halo_grad[5 * slots :], inner_out, outer_out)
    middle_out[...] = halo_grad[3 * slots : 5 * slots]
    edge_sums[:width] = dot_tn(edges[...], pre_grad)
    edge_sums[width : 2 * width] = dot_tn(x, own) + dot_tn(halo, away)
    edge_sums[2 * width : 3 * width] = dot_tn(x, received)
    edge_sums[3 * width : 4 * width] = dot_tn(hidden_kept[...], out_grad)
    split_by_core(edge_sums, 0, keep_out, away_out)
    split_by_core(node_sums, edge_sums.shape[0] // 2, keep_out, away_out)
    gains = pack_gains(edge_gain, node_gain)
    away_out[keep_out.shape[0] :] = gains
    gains_out[...] = gains


def pair_kernel(parts, keep, gains, other, *outs):
    rows = keep.shape[0]
    packed = gains.shape[0]
    members = len(outs)
    both = gains[...].astype(F32) + other[rows : rows + packed].astype(F32)
    summed = pack_gains(both[0:1] + both[1:2], both[2:3] + both[3:4])
    me = place_in_square()
    for offset, out in enumerate(outs):
        owner = me ^ offset
        out[:packed] = summed
        first, at = 0, packed
        for part in parts:
            step = part // members
            source = pl.ds(pl.multiple_of(first + owner * step, 16), step)
            out[at : at + step] = (keep[source, :] + other[source, :].astype(F32)).astype(BF16)
            first, at = first + part, at + step


def add_packed(values):
    packed = PACKED
    gains = values[:packed]
    return pack_gains(gains[0:1] + gains[1:2], gains[2:3] + gains[3:4])


def sum_kernel(*refs):
    sums_out = refs[-1]
    sums = tree_sum([block[...].astype(F32) for block in refs[:-1]])
    sums_out[...] = sums.astype(BF16)
    sums_out[:PACKED] = add_packed(sums)


def join_kernel(own, other, sums_out):
    sums = own[...].astype(F32) + other[...].astype(F32)
    sums_out[...] = sums.astype(BF16)
    sums_out[:PACKED] = add_packed(sums)


def whole_kernel(own, other, gains_out, mine):
    packed = gains_out.shape[0]
    sums = own[...].astype(F32) + other[...].astype(F32)
    gains_out[...] = sums[:packed]
    mine[...] = sums[packed:].astype(BF16)


def place_kernel(parts, *refs):
    count = 2 * len(parts)
    sems, wholes = refs[-1], refs[-1 - len(parts) : -1]
    outs = refs[-1 - len(parts) - count : -1 - len(parts)]
    blocks = refs[: -1 - len(parts) - count]
    members = len(blocks) // 2
    core = lax.axis_index(CORE)
    me = place_in_square()
    for position, block in enumerate(blocks):
        half = core if position < members else 1 - core
        owner = me ^ (position % members)
        at = 0
        for part, whole in zip(parts, wholes):
            step = part // members
            row = pl.multiple_of(half * part + owner * step, 16)
            whole[pl.ds(row, step), :] = block[at : at + step]
            at += step
    copies = []
    for i, whole in enumerate(wholes):
        cut = outs[2 * i].shape[0]
        copies.append(pltpu.make_async_copy(whole.at[:cut], outs[2 * i], sems.at[2 * i]))
        copies.append(pltpu.make_async_copy(whole.at[cut:], outs[2 * i + 1], sems.at[2 * i + 1]))
    for copy in copies:
        copy.start()
    for copy in copies:
        copy.wait()


def finish_kernel(
    edge_grads, pre_grad, sender_sum, receiver_sum, node_part, w_in, edges_grad, local_grad
):
    width = w_in.shape[1]
    edges_grad[...] = (
        edge_grads[...].astype(F32) + dot_nt(pre_grad[...], w_in[:width])
    ).astype(BF16)
    local_grad[...] = (
        node_part[...]
        + dot_nt(sender_sum[...], w_in[width : 2 * width])
        + dot_nt(receiver_sum[...], w_in[2 * width :])
    )


def turn_kernel(inner, outer, middle, along_core, along_chip, center):
    slots = middle.shape[0] // 2
    top, bottom = from_pair(NEAR, inner[...], outer[...])
    up = jnp.concatenate([top[:slots], middle[:slots], bottom[:slots]], axis=0)
    down = jnp.concatenate([top[2 * slots :], middle[slots:], bottom[2 * slots :]], axis=0)
    by_pair(CORE, up, down, along_core, along_chip)
    center[:slots] = top[slots : 2 * slots]
    center[slots:] = bottom[slots : 2 * slots]


def return_kernel(send_list, local_grad, center, along_core, along_chip, nodes_grad):
    slots = send_list.shape[1]
    up, down = from_pair(CORE, along_core[...], along_chip[...])
    returned = jnp.concatenate(
        [
            up[:slots],
            center[:slots],
            down[:slots],
            up[slots : 2 * slots],
            down[slots : 2 * slots],
            up[2 * slots :],
            center[slots:],
            down[2 * slots :],
        ],
        axis=0,
    )
    hot = list_hot(send_list[...], local_grad.shape[0])
    nodes_grad[...] = (local_grad[...] + dot_tn(hot, returned)).astype(BF16)


SMEM = pltpu.SMEM
VMEM = pltpu.VMEM
HBM = pltpu.HBM


def call(body, outs, flops, *operands, spaces=(), out_space=VMEM, scratch=(), after=()):
    if after:
        first, rest = len(operands), len(operands) + len(after)
        inner = body

        def body(*refs):
            inner(*refs[:first], *refs[rest:])

        operands = operands + tuple(after)
    moved = sum(x.size * x.dtype.itemsize for x in operands)
    moved += sum(x.size * jnp.dtype(x.dtype).itemsize for x in outs)
    spaces = list(spaces) + [VMEM] * (len(operands) - len(spaces))
    out_spaces = out_space if isinstance(out_space, list) else [out_space] * len(outs)
    operands = [
        pltpu.with_memory_space_constraint(x, HBM) if space is HBM else x
        for x, space in zip(operands, spaces)
    ]
    return pl.pallas_call(
        body,
        out_shape=outs,
        in_specs=[pl.BlockSpec(memory_space=space) for space in spaces],
        out_specs=[pl.BlockSpec(memory_space=space) for space in out_spaces],
        scratch_shapes=list(scratch),
        compiler_params=pltpu.CompilerParams(vmem_limit_bytes=VMEM_LIMIT),
        cost_estimate=pl.CostEstimate(flops=flops, bytes_accessed=moved, transcendentals=0),
    )(*operands)


def like(array):
    return jax.ShapeDtypeStruct(array.shape, array.dtype)


def shaped(rows, columns, dtype):
    return jax.ShapeDtypeStruct((rows, columns), dtype)


def placed(parts, blocks, width):
    return call(
        functools.partial(place_kernel, parts),
        [
            shaped(3 * width, width, BF16),
            shaped(width, width, BF16),
            shaped(2 * width, width, BF16),
            shaped(width, width, BF16),
        ],
        0,
        *blocks,
        out_space=HBM,
        scratch=[pltpu.VMEM((2 * part, width), BF16) for part in parts]
        + [pltpu.SemaphoreType.DMA((2 * len(parts),))],
    )


def joined(sums, packed, *beside):
    rows, width = sums.shape
    size = lax.axis_size(FAR)
    distance = 1
    while True:
        other = lax.ppermute(sums, FAR, [(i, i ^ distance) for i in range(size)])
        distance *= 2
        if distance == size:
            break
        (sums,) = call(join_kernel, [like(sums)], 0, sums, other)
    other, *beside = lax.optimization_barrier((other, *beside))
    gains, mine = call(
        whole_kernel,
        [shaped(packed, width, F32), shaped(rows - packed, width, BF16)],
        0,
        sums,
        other,
    )
    return gains, mine, *beside


def on_device(
    nodes,
    edges,
    edge_grads,
    node_grads,
    send_list,
    senders,
    receivers,
    tile_count,
    w_edge_in,
    w_edge_out,
    gain_edge,
    w_node_in,
    w_node_out,
    gain_node,
):
    count, width = nodes.shape
    slots = send_list.shape[1]
    halo_rows = 8 * slots
    edge_rows = edges.shape[0]
    tile_rows = senders.shape[1]
    square = 2 * width * width
    inner, outer, middle, nodes, send_list = call(
        send_kernel,
        [
            shaped(3 * slots, width, BF16),
            shaped(3 * slots, width, BF16),
            shaped(2 * slots, width, BF16),
            like(nodes),
            like(send_list),
        ],
        2 * halo_rows * count * width,
        nodes,
        send_list,
        spaces=[HBM, HBM],
        scratch=[pltpu.SemaphoreType.DMA((2,))],
    )
    inner = in_pair(inner, PX)
    outer = out_of_pair(outer, PX)
    fetched = [
        senders,
        receivers,
        edges,
        w_edge_in,
        w_edge_out,
        gain_edge,
        w_node_in,
        w_node_out,
        gain_node,
        node_grads,
        edge_grads,
    ]
    near_hot, halo_hot, *fetched = call(
        functools.partial(index_kernel, len(fetched)),
        [
            shaped(edge_rows, 2 * count, BF16),
            shaped(edge_rows, halo_rows, BF16),
        ]
        + [like(x) for x in fetched],
        0,
        *fetched,
        spaces=[HBM] * len(fetched),
        scratch=[pltpu.SemaphoreType.DMA((len(fetched),))],
    )
    (
        senders,
        receivers,
        edges,
        w_edge_in,
        w_edge_out,
        gain_edge,
        w_node_in,
        w_node_out,
        gain_node,
        node_grads,
        edge_grads,
    ) = fetched
    inner, outer, near_hot = lax.optimization_barrier((inner, outer, near_hot))
    along_core, along_chip, straight = call(
        corner_kernel,
        [
            shaped(3 * slots, width, BF16),
            shaped(3 * slots, width, BF16),
            shaped(2 * slots, width, BF16),
        ],
        0,
        inner,
        outer,
        middle,
    )
    along_chip = out_of_pair(along_chip, PY)
    along_core = across_cores(along_core)
    pre_local, sender_columns, receiver_columns = call(
        local_kernel,
        [
            shaped(edge_rows, width, F32),
            shaped(count + halo_rows, edge_rows, BF16),
            shaped(count, edge_rows, BF16),
        ],
        square * (2 * count + edge_rows) + 4 * edge_rows * count * width,
        nodes,
        edges,
        senders,
        receivers,
        near_hot,
        w_edge_in,
    )
    parts = (2 * width, 3 * width // 2)
    halves = sum(parts)
    pre_grad, sender_sum, receiver_sum, node_part, inner, outer, middle, keep, away, gains = call(
        functools.partial(layer_kernel, tile_rows),
        [
            shaped(edge_rows, width, BF16),
            shaped(count, width, BF16),
            shaped(count, width, BF16),
            shaped(count, width, F32),
            shaped(3 * slots, width, BF16),
            shaped(3 * slots, width, BF16),
            shaped(2 * slots, width, BF16),
            shaped(halves, width, F32),
            shaped(halves + PACKED, width, BF16),
            shaped(PACKED, width, BF16),
        ],
        square * (6 * edge_rows + 11 * count + 2 * halo_rows)
        + 2 * edge_rows * (4 * count + halo_rows) * width,
        tile_count,
        nodes,
        node_grads,
        edges,
        edge_grads,
        pre_local,
        halo_hot,
        near_hot,
        sender_columns,
        receiver_columns,
        straight,
        along_core,
        along_chip,
        w_edge_in,
        w_edge_out,
        gain_edge,
        w_node_in,
        w_node_out,
        gain_node,
        spaces=[SMEM],
        scratch=[
            pltpu.VMEM((edge_rows, width), F32),
            pltpu.VMEM((edge_rows, width), BF16),
            pltpu.VMEM((edge_rows, width), F32),
            pltpu.VMEM((edge_rows, 128), F32),
            pltpu.VMEM((3 * width, width), F32),
            pltpu.VMEM((4 * width, width), F32),
        ],
    )
    other = across_cores(away)
    members = square_members()
    own, *blocks = call(
        functools.partial(pair_kernel, parts),
        [shaped(PACKED + halves // members, width, BF16)] * members,
        0,
        keep,
        gains,
        other,
    )
    received = [in_square(block, offset) for offset, block in enumerate(blocks, 1)]
    (sums,) = call(sum_kernel, [like(own)], 0, own, *received)
    edges_grad, local_grad = call(
        finish_kernel,
        [shaped(edge_rows, width, BF16), shaped(count, width, F32)],
        square * (edge_rows + 2 * count),
        edge_grads,
        pre_grad,
        sender_sum,
        receiver_sum,
        node_part,
        w_edge_in,
    )
    along_core, along_chip, center = call(
        turn_kernel,
        [
            shaped(3 * slots, width, BF16),
            shaped(3 * slots, width, BF16),
            shaped(2 * slots, width, BF16),
        ],
        10**10,
        in_pair(inner, PX),
        out_of_pair(outer, PX),
        middle,
        after=[sums],
    )
    gains, mine, along_core, along_chip = joined(
        sums, gains.shape[0], across_cores(along_core), out_of_pair(along_chip, PY)
    )
    blocks = [mine] + [in_square(mine, offset) for offset in range(1, members)]
    gain_edge_grad = (gains[0] + gains[1]).astype(BF16)
    gain_node_grad = (gains[2] + gains[3]).astype(BF16)
    (nodes_grad,) = call(
        return_kernel,
        [shaped(count, width, BF16)],
        2 * halo_rows * count * width,
        send_list,
        local_grad,
        center,
        along_core,
        along_chip,
    )
    done = (nodes_grad, edges_grad, gain_edge_grad, gain_node_grad)
    for i in range(members):
        blocks[i], *done = lax.optimization_barrier((blocks[i], *done))
    nodes_grad, edges_grad, gain_edge_grad, gain_node_grad = done
    blocks += [across_cores(block) for block in blocks]
    w_edge_in_grad, w_edge_out_grad, w_node_in_grad, w_node_out_grad = placed(
        parts, blocks, width
    )
    return (
        nodes_grad,
        edges_grad,
        w_edge_in_grad,
        w_edge_out_grad,
        gain_edge_grad,
        w_node_in_grad,
        w_node_out_grad,
        gain_node_grad,
    )


def solution(mesh):
    in_specs = (
        P(("groups",) + PX + PY, None),
        P(("groups",) + PX + PY, None),
        P(("groups",) + PX + PY, None),
        P(("groups",) + PX + PY, None),
        P(("groups",) + PX + PY, None),
        P(("groups",) + PX + PY, None),
        P(("groups",) + PX + PY, None),
        P(("groups",) + PX + PY),
        P(),
        P(),
        P(),
        P(),
        P(),
        P(),
    )
    out_specs = (
        P(("groups",) + PX + PY, None),
        P(("groups",) + PX + PY, None),
        P("groups", None),
        P("groups", None),
        P("groups"),
        P("groups", None),
        P("groups", None),
        P("groups"),
    )
    groups, px, py = mesh.devices.shape
    by_core = jax.sharding.Mesh(
        mesh.devices.reshape(groups, px // 2, 2, py // 2, 2), ("groups",) + PX + PY
    )
    return jax.shard_map(
        on_device, mesh=by_core, in_specs=in_specs, out_specs=out_specs, check_vma=False
    )
```

```python
import functools

import jax
import jax.numpy as jnp
from jax import lax
from jax.experimental import pallas as pl
from jax.experimental.pallas import tpu as pltpu
from jax.sharding import PartitionSpec as P

EPS = 1e-05
BF16 = jnp.bfloat16
F32 = jnp.float32
PACKED = 8
VMEM_LIMIT = 24 * 1024 * 1024


CORE = "core"
FAR = "far"
NEAR = "near"
PX = (FAR, NEAR)
PY = ("side", CORE)
SQUARE = (NEAR, "side")


def other_neighbour(i, size):
    return (i + 1 if i % 2 else i - 1) % size


def in_pair(array, axis):
    return lax.ppermute(array, axis, [(i, i ^ 1) for i in range(lax.axis_size(axis))])


def out_of_pair(array, axis):
    size = lax.axis_size(axis)
    return lax.ppermute(array, axis, [(i, other_neighbour(i, size)) for i in range(size)])


def square_members():
    return lax.axis_size(SQUARE)


def place_in_square():
    near, side = SQUARE
    return lax.axis_index(near) * lax.axis_size(side) + lax.axis_index(side)


def in_square(array, offset):
    return lax.ppermute(array, SQUARE, [(i, i ^ offset) for i in range(square_members())])


def tree_sum(terms):
    while len(terms) > 1:
        terms = [terms[i] + terms[i + 1] for i in range(0, len(terms), 2)]
    return terms[0]


def across_cores(array):
    return in_pair(array, CORE)


def by_pair(axis, up, down, inner, outer):
    first = lax.axis_index(axis) == 0

    @pl.when(first)
    def _():
        inner[...] = up
        outer[...] = down

    @pl.when(jnp.logical_not(first))
    def _():
        inner[...] = down
        outer[...] = up


def from_pair(axis, inner, outer):
    first = lax.axis_index(axis) == 0
    return jnp.where(first, outer, inner), jnp.where(first, inner, outer)


def dot(left, right):
    return jnp.dot(left, right, preferred_element_type=F32)


def dot_tn(left, right):
    return lax.dot_general(left, right, (((0,), (0,)), ((), ())), preferred_element_type=F32)


def dot_nt(left, right):
    return lax.dot_general(left, right, (((1,), (1,)), ((), ())), preferred_element_type=F32)


def sigmoid(value):
    return 0.5 + 0.5 * jnp.tanh(0.5 * value)


def normalize(value):
    centered = value - jnp.mean(value, axis=-1, keepdims=True)
    scale_inv = lax.rsqrt(jnp.mean(centered * centered, axis=-1, keepdims=True) + EPS)
    return centered * scale_inv, scale_inv


def norm_back(normed, scale_inv, gain, upstream):
    scaled = upstream * gain
    inner = (
        scaled
        - jnp.mean(scaled, axis=-1, keepdims=True)
        - normed * jnp.mean(scaled * normed, axis=-1, keepdims=True)
    )
    return inner * scale_inv


def columns_of(ids):
    rows, lanes = ids.shape
    padded = -(-rows // 8) * 8
    if padded > rows:
        ids = jnp.concatenate([ids, jnp.zeros((padded - rows, lanes), ids.dtype)], axis=0)
    return ids.T


def hot_rows(columns, tiles, base, count):
    parts = []
    for tile in tiles:
        column = columns[:, tile : tile + 1] - base
        lanes = lax.broadcasted_iota(jnp.int32, (columns.shape[0], count), 1)
        parts.append(jnp.where(lanes == column, 1.0, 0.0).astype(BF16))
    return jnp.concatenate(parts, axis=0) if len(parts) > 1 else parts[0]


def hot_columns(ids, tiles, base, count):
    parts = []
    for tile in tiles:
        row = ids[tile : tile + 1, :] - base
        subs = lax.broadcasted_iota(jnp.int32, (count, ids.shape[1]), 0)
        parts.append(jnp.where(subs == row, 1.0, 0.0).astype(BF16))
    return jnp.concatenate(parts, axis=1) if len(parts) > 1 else parts[0]


def list_hot(ids, count):
    directions, slots = ids.shape
    wide = jnp.concatenate([ids, jnp.zeros((directions, 128 - slots), ids.dtype)], axis=1)
    columns = wide.T
    parts = []
    for k in range(directions):
        lanes = lax.broadcasted_iota(jnp.int32, (slots, count), 1)
        parts.append(jnp.where(lanes == columns[:slots, k : k + 1], 1.0, 0.0).astype(BF16))
    return jnp.concatenate(parts, axis=0)


def live_rows(count_ref, tile_rows, rows):
    index = lax.broadcasted_iota(jnp.int32, (rows, 1), 0)
    return jnp.where(index < count_ref[0] * tile_rows, 1.0, 0.0)


def fetch_all(sources, targets, sems):
    copies = [
        pltpu.make_async_copy(source, target, sems.at[i])
        for i, (source, target) in enumerate(zip(sources, targets))
    ]
    for copy in copies:
        copy.start()
    return copies


def send_kernel(nodes_hbm, list_hbm, outer, inner, middle, nodes, send_list, sems):
    slots = send_list.shape[1]
    for copy in fetch_all([list_hbm, nodes_hbm], [send_list, nodes], sems):
        copy.wait()
    rows = dot(list_hot(send_list[...], nodes.shape[0]), nodes[...]).astype(BF16)
    by_pair(NEAR, rows[5 * slots :], rows[: 3 * slots], inner, outer)
    middle[...] = rows[3 * slots : 5 * slots]


def corner_kernel(outer, inner, middle, along_core, along_chip, straight):
    slots = middle.shape[0] // 2
    low, high = from_pair(NEAR, inner[...], outer[...])
    up = jnp.concatenate([high[2 * slots :], middle[slots:], low[2 * slots :]], axis=0)
    down = jnp.concatenate([high[:slots], middle[:slots], low[:slots]], axis=0)
    by_pair(CORE, up, down, along_core, along_chip)
    straight[:slots] = high[slots : 2 * slots]
    straight[slots:] = low[slots : 2 * slots]


def index_kernel(sources, *refs):
    fetched, refs = refs[:sources], refs[sources:]
    near_rows, halo_rows = refs[:2]
    targets, sems = refs[2:-1], refs[-1]
    senders, receivers = targets[:2]
    copies = fetch_all(fetched, targets, sems)
    for copy in copies[:2]:
        copy.wait()
    tile_rows = senders.shape[1]
    count = near_rows.shape[1] // 2
    by_sender = columns_of(senders[...])
    by_receiver = columns_of(receivers[...])
    for tile in range(senders.shape[0]):
        rows = slice(tile * tile_rows, (tile + 1) * tile_rows)
        near_rows[rows, :count] = hot_rows(by_sender, [tile], 0, count)
        near_rows[rows, count:] = hot_rows(by_receiver, [tile], 0, count)
        halo_rows[rows, :] = hot_rows(by_sender, [tile], count, halo_rows.shape[1])
    for copy in copies[2:]:
        copy.wait()


def local_kernel(
    nodes, edges, senders, receivers, near_rows, w_in, pre, sender_columns, receiver_columns
):
    width = nodes.shape[1]
    tile_rows = senders.shape[1]
    extended = sender_columns.shape[0]
    count = receiver_columns.shape[0]
    sender_ids = senders[...]
    receiver_ids = receivers[...]
    for tile in range(senders.shape[0]):
        rows = slice(tile * tile_rows, (tile + 1) * tile_rows)
        sender_columns[:, rows] = hot_columns(sender_ids, [tile], 0, extended)
        receiver_columns[:, rows] = hot_columns(receiver_ids, [tile], 0, count)
    x = nodes[...]
    table = jnp.concatenate(
        [
            dot(x, w_in[width : 2 * width]).astype(BF16),
            dot(x, w_in[2 * width :]).astype(BF16),
        ],
        axis=0,
    )
    pre[...] = dot(edges[...], w_in[:width]) + dot(near_rows[...], table)


def split_by_core(sums, first, keep_out, away_out):
    half = sums.shape[0] // 2
    core = lax.axis_index(CORE)
    keep_out[first : first + half] = sums[pl.ds(pl.multiple_of(core * half, half), half), :]
    away = sums[pl.ds(pl.multiple_of((1 - core) * half, half), half), :]
    away_out[first : first + half] = away.astype(BF16)


def pack_gains(edge_gain, node_gain):
    edge_high = edge_gain.astype(BF16).astype(F32)
    node_high = node_gain.astype(BF16).astype(F32)
    row = lax.broadcasted_iota(jnp.int32, (PACKED, edge_gain.shape[1]), 0)
    packed = jnp.where(row == 0, edge_high, 0.0)
    packed = jnp.where(row == 1, edge_gain - edge_high, packed)
    packed = jnp.where(row == 2, node_high, packed)
    packed = jnp.where(row == 3, node_gain - node_high, packed)
    return packed.astype(BF16)


def layer_kernel(
    tile_rows,
    count_ref,
    nodes,
    node_grads,
    edges,
    edge_grads,
    pre_local,
    halo_rows,
    near_rows,
    sender_columns,
    receiver_columns,
    straight,
    along_core,
    along_chip,
    w_in,
    w_out,
    gain_edge,
    w_node_in,
    w_node_out,
    gain_node,
    pre_grad_out,
    sender_out,
    receiver_out,
    node_part_out,
    inner_out,
    outer_out,
    middle_out,
    keep_out,
    away_out,
    gains_out,
    slope_kept,
    hidden_kept,
    normed_kept,
    scale_kept,
    node_sums,
    edge_sums,
):
    count, width = nodes.shape
    edge_rows = edges.shape[0]
    live = live_rows(count_ref, tile_rows, edge_rows)
    slots = straight.shape[0] // 2
    up, down = from_pair(CORE, along_core[...], along_chip[...])
    halo = jnp.concatenate(
        [
            down[:slots],
            straight[:slots],
            up[:slots],
            down[slots : 2 * slots],
            up[slots : 2 * slots],
            down[2 * slots :],
            straight[slots:],
            up[2 * slots :],
        ],
        axis=0,
    )
    table = dot(halo, w_in[width : 2 * width]).astype(BF16)
    gain = gain_edge[...].astype(F32)[None, :]
    value = pre_local[...] + dot(halo_rows[...], table)
    sigma = sigmoid(value)
    hidden = (value * sigma).astype(BF16)
    hidden_kept[...] = hidden
    slope_kept[...] = sigma * (1.0 + value * (1.0 - sigma))
    edge_normed, edge_scale = normalize(dot(hidden, w_out[...]))
    normed_kept[...] = edge_normed
    scale_kept[...] = jnp.broadcast_to(edge_scale, (edge_rows, 128))
    message = (live * gain * edge_normed).astype(BF16)
    total = dot(receiver_columns[...], message)
    aggregated = total.astype(BF16)
    x = nodes[...]
    w_first = w_node_in[:width]
    w_second = w_node_in[width:]
    node_pre = dot(x, w_first) + dot(aggregated, w_second)
    sigma = sigmoid(node_pre)
    node_hidden = (node_pre * sigma).astype(BF16)
    normed, scale_inv = normalize(dot(node_hidden, w_node_out[...]))
    upstream = node_grads[...].astype(F32)
    out_grad = norm_back(normed, scale_inv, gain_node[...].astype(F32)[None, :], upstream).astype(BF16)
    slope = sigma * (1.0 + node_pre * (1.0 - sigma))
    pre_grad = (dot_nt(out_grad, w_node_out[...]) * slope).astype(BF16)
    agg_grad = dot_nt(pre_grad, w_second).astype(BF16)
    node_part_out[...] = upstream + dot_nt(pre_grad, w_first)
    node_sums[:width] = dot_tn(x, pre_grad)
    node_sums[width : 2 * width] = dot_tn(aggregated, pre_grad)
    node_sums[2 * width : 3 * width] = dot_tn(node_hidden, out_grad)
    node_gain = jnp.sum(upstream * normed, axis=0, keepdims=True)
    upstream = live * (
        edge_grads[...].astype(F32) + dot(near_rows[:, count:], agg_grad)
    )
    edge_normed = normed_kept[...]
    edge_gain = jnp.sum(upstream * edge_normed, axis=0, keepdims=True)
    out_grad = norm_back(edge_normed, scale_kept[:, :1], gain, upstream).astype(BF16)
    pre_grad = (dot_nt(out_grad, w_out[...]) * slope_kept[...]).astype(BF16)
    pre_grad_out[...] = pre_grad
    sender_total = dot(sender_columns[...], pre_grad)
    receiver_total = dot(receiver_columns[...], pre_grad)
    own = sender_total[:count].astype(BF16)
    away = sender_total[count:].astype(BF16)
    received = receiver_total.astype(BF16)
    sender_out[...] = own
    receiver_out[...] = received
    halo_grad = dot_nt(away, w_in[width : 2 * width]).astype(BF16)
    by_pair(NEAR, halo_grad[: 3 * slots], halo_grad[5 * slots :], inner_out, outer_out)
    middle_out[...] = halo_grad[3 * slots : 5 * slots]
    edge_sums[:width] = dot_tn(edges[...], pre_grad)
    edge_sums[width : 2 * width] = dot_tn(x, own) + dot_tn(halo, away)
    edge_sums[2 * width : 3 * width] = dot_tn(x, received)
    edge_sums[3 * width : 4 * width] = dot_tn(hidden_kept[...], out_grad)
    split_by_core(edge_sums, 0, keep_out, away_out)
    split_by_core(node_sums, edge_sums.shape[0] // 2, keep_out, away_out)
    gains = pack_gains(edge_gain, node_gain)
    away_out[keep_out.shape[0] :] = gains
    gains_out[...] = gains


def pair_kernel(parts, keep, gains, other, *outs):
    rows = keep.shape[0]
    packed = gains.shape[0]
    members = len(outs)
    both = gains[...].astype(F32) + other[rows : rows + packed].astype(F32)
    summed = pack_gains(both[0:1] + both[1:2], both[2:3] + both[3:4])
    me = place_in_square()
    for offset, out in enumerate(reversed(outs)):
        owner = me ^ offset
        out[:packed] = summed
        first, at = 0, packed
        for part in parts:
            step = part // members
            source = pl.ds(pl.multiple_of(first + owner * step, 16), step)
            out[at : at + step] = (keep[source, :] + other[source, :].astype(F32)).astype(BF16)
            first, at = first + part, at + step


def add_packed(values):
    packed = PACKED
    gains = values[:packed]
    return pack_gains(gains[0:1] + gains[1:2], gains[2:3] + gains[3:4])


def copy_kernel(source, target):
    target[...] = source[...]


def sum_kernel(*refs):
    sums_out = refs[-1]
    sums = tree_sum([block[...].astype(F32) for block in refs[:-1]])
    sums_out[...] = sums.astype(BF16)
    sums_out[:PACKED] = add_packed(sums)


def join_kernel(own, other, sums_out):
    sums = own[...].astype(F32) + other[...].astype(F32)
    sums_out[...] = sums.astype(BF16)
    sums_out[:PACKED] = add_packed(sums)


def whole_kernel(own, other, gains_out, mine):
    packed = gains_out.shape[0]
    sums = own[...].astype(F32) + other[...].astype(F32)
    gains_out[...] = sums[:packed]
    mine[...] = sums[packed:].astype(BF16)


def place_kernel(parts, *refs):
    count = 2 * len(parts)
    sems, wholes = refs[-1], refs[-1 - len(parts) : -1]
    outs = refs[-1 - len(parts) - count : -1 - len(parts)]
    blocks = refs[: -1 - len(parts) - count]
    members = len(blocks) // 2
    core = lax.axis_index(CORE)
    me = place_in_square()
    for position, block in enumerate(blocks):
        half = core if position < members else 1 - core
        owner = me ^ (position % members)
        at = 0
        for part, whole in zip(parts, wholes):
            step = part // members
            row = pl.multiple_of(half * part + owner * step, 16)
            whole[pl.ds(row, step), :] = block[at : at + step]
            at += step
    copies = []
    for i, whole in enumerate(wholes):
        cut = outs[2 * i].shape[0]
        copies.append(pltpu.make_async_copy(whole.at[:cut], outs[2 * i], sems.at[2 * i]))
        copies.append(pltpu.make_async_copy(whole.at[cut:], outs[2 * i + 1], sems.at[2 * i + 1]))
    for copy in copies:
        copy.start()
    for copy in copies:
        copy.wait()


def finish_kernel(
    edge_grads, pre_grad, sender_sum, receiver_sum, node_part, w_in, edges_grad, local_grad
):
    width = w_in.shape[1]
    edges_grad[...] = (
        edge_grads[...].astype(F32) + dot_nt(pre_grad[...], w_in[:width])
    ).astype(BF16)
    local_grad[...] = (
        node_part[...]
        + dot_nt(sender_sum[...], w_in[width : 2 * width])
        + dot_nt(receiver_sum[...], w_in[2 * width :])
    )


def turn_kernel(inner, outer, middle, along_core, along_chip, center):
    slots = middle.shape[0] // 2
    top, bottom = from_pair(NEAR, inner[...], outer[...])
    up = jnp.concatenate([top[:slots], middle[:slots], bottom[:slots]], axis=0)
    down = jnp.concatenate([top[2 * slots :], middle[slots:], bottom[2 * slots :]], axis=0)
    by_pair(CORE, up, down, along_core, along_chip)
    center[:slots] = top[slots : 2 * slots]
    center[slots:] = bottom[slots : 2 * slots]


def return_kernel(send_list, local_grad, center, along_core, along_chip, nodes_grad):
    slots = send_list.shape[1]
    up, down = from_pair(CORE, along_core[...], along_chip[...])
    returned = jnp.concatenate(
        [
            up[:slots],
            center[:slots],
            down[:slots],
            up[slots : 2 * slots],
            down[slots : 2 * slots],
            up[2 * slots :],
            center[slots:],
            down[2 * slots :],
        ],
        axis=0,
    )
    hot = list_hot(send_list[...], local_grad.shape[0])
    nodes_grad[...] = (local_grad[...] + dot_tn(hot, returned)).astype(BF16)


SMEM = pltpu.SMEM
VMEM = pltpu.VMEM
HBM = pltpu.HBM


def call(body, outs, flops, *operands, spaces=(), out_space=VMEM, scratch=(), after=()):
    if after:
        first, rest = len(operands), len(operands) + len(after)
        inner = body

        def body(*refs):
            inner(*refs[:first], *refs[rest:])

        operands = operands + tuple(after)
    moved = sum(x.size * x.dtype.itemsize for x in operands)
    moved += sum(x.size * jnp.dtype(x.dtype).itemsize for x in outs)
    spaces = list(spaces) + [VMEM] * (len(operands) - len(spaces))
    out_spaces = out_space if isinstance(out_space, list) else [out_space] * len(outs)
    operands = [
        pltpu.with_memory_space_constraint(x, HBM) if space is HBM else x
        for x, space in zip(operands, spaces)
    ]
    return pl.pallas_call(
        body,
        out_shape=outs,
        in_specs=[pl.BlockSpec(memory_space=space) for space in spaces],
        out_specs=[pl.BlockSpec(memory_space=space) for space in out_spaces],
        scratch_shapes=list(scratch),
        compiler_params=pltpu.CompilerParams(vmem_limit_bytes=VMEM_LIMIT),
        cost_estimate=pl.CostEstimate(flops=flops, bytes_accessed=moved, transcendentals=0),
    )(*operands)


def like(array):
    return jax.ShapeDtypeStruct(array.shape, array.dtype)


def shaped(rows, columns, dtype):
    return jax.ShapeDtypeStruct((rows, columns), dtype)


def placed(parts, blocks, width):
    return call(
        functools.partial(place_kernel, parts),
        [
            shaped(3 * width, width, BF16),
            shaped(width, width, BF16),
            shaped(2 * width, width, BF16),
            shaped(width, width, BF16),
        ],
        0,
        *blocks,
        out_space=HBM,
        scratch=[pltpu.VMEM((2 * part, width), BF16) for part in parts]
        + [pltpu.SemaphoreType.DMA((2 * len(parts),))],
    )


def joined(sums, packed, *beside):
    rows, width = sums.shape
    size = lax.axis_size(FAR)
    distance = 1
    while True:
        other = lax.ppermute(sums, FAR, [(i, i ^ distance) for i in range(size)])
        distance *= 2
        if distance == size:
            break
        (sums,) = call(join_kernel, [like(sums)], 0, sums, other)
    other, *beside = lax.optimization_barrier((other, *beside))
    gains, mine = call(
        whole_kernel,
        [shaped(packed, width, F32), shaped(rows - packed, width, BF16)],
        0,
        sums,
        other,
    )
    return gains, mine, *beside


def on_device(
    nodes,
    edges,
    edge_grads,
    node_grads,
    send_list,
    senders,
    receivers,
    tile_count,
    w_edge_in,
    w_edge_out,
    gain_edge,
    w_node_in,
    w_node_out,
    gain_node,
):
    count, width = nodes.shape
    slots = send_list.shape[1]
    halo_rows = 8 * slots
    edge_rows = edges.shape[0]
    tile_rows = senders.shape[1]
    square = 2 * width * width
    outer, inner, middle, nodes, send_list = call(
        send_kernel,
        [
            shaped(3 * slots, width, BF16),
            shaped(3 * slots, width, BF16),
            shaped(2 * slots, width, BF16),
            like(nodes),
            like(send_list),
        ],
        2 * halo_rows * count * width,
        nodes,
        send_list,
        spaces=[HBM, HBM],
        scratch=[pltpu.SemaphoreType.DMA((2,))],
    )
    outer = out_of_pair(outer, PX)
    inner = in_pair(inner, PX)
    fetched = [
        senders,
        receivers,
        edges,
        w_edge_in,
        w_edge_out,
        gain_edge,
        w_node_in,
        w_node_out,
        gain_node,
        node_grads,
        edge_grads,
    ]
    near_hot, halo_hot, *fetched = call(
        functools.partial(index_kernel, len(fetched)),
        [
            shaped(edge_rows, 2 * count, BF16),
            shaped(edge_rows, halo_rows, BF16),
        ]
        + [like(x) for x in fetched],
        0,
        *fetched,
        spaces=[HBM] * len(fetched),
        scratch=[pltpu.SemaphoreType.DMA((len(fetched),))],
    )
    (
        senders,
        receivers,
        edges,
        w_edge_in,
        w_edge_out,
        gain_edge,
        w_node_in,
        w_node_out,
        gain_node,
        node_grads,
        edge_grads,
    ) = fetched
    outer, inner, near_hot = lax.optimization_barrier((outer, inner, near_hot))
    along_core, along_chip, straight = call(
        corner_kernel,
        [
            shaped(3 * slots, width, BF16),
            shaped(3 * slots, width, BF16),
            shaped(2 * slots, width, BF16),
        ],
        0,
        outer,
        inner,
        middle,
    )
    along_chip = out_of_pair(along_chip, PY)
    along_core = across_cores(along_core)
    pre_local, sender_columns, receiver_columns = call(
        local_kernel,
        [
            shaped(edge_rows, width, F32),
            shaped(count + halo_rows, edge_rows, BF16),
            shaped(count, edge_rows, BF16),
        ],
        square * (2 * count + edge_rows) + 4 * edge_rows * count * width,
        nodes,
        edges,
        senders,
        receivers,
        near_hot,
        w_edge_in,
    )
    parts = (2 * width, 3 * width // 2)
    halves = sum(parts)
    pre_grad, sender_sum, receiver_sum, node_part, inner, outer, middle, keep, away, gains = call(
        functools.partial(layer_kernel, tile_rows),
        [
            shaped(edge_rows, width, BF16),
            shaped(count, width, BF16),
            shaped(count, width, BF16),
            shaped(count, width, F32),
            shaped(3 * slots, width, BF16),
            shaped(3 * slots, width, BF16),
            shaped(2 * slots, width, BF16),
            shaped(halves, width, F32),
            shaped(halves + PACKED, width, BF16),
            shaped(PACKED, width, BF16),
        ],
        square * (6 * edge_rows + 11 * count + 2 * halo_rows)
        + 2 * edge_rows * (4 * count + halo_rows) * width,
        tile_count,
        nodes,
        node_grads,
        edges,
        edge_grads,
        pre_local,
        halo_hot,
        near_hot,
        sender_columns,
        receiver_columns,
        straight,
        along_core,
        along_chip,
        w_edge_in,
        w_edge_out,
        gain_edge,
        w_node_in,
        w_node_out,
        gain_node,
        spaces=[SMEM],
        scratch=[
            pltpu.VMEM((edge_rows, width), F32),
            pltpu.VMEM((edge_rows, width), BF16),
            pltpu.VMEM((edge_rows, width), F32),
            pltpu.VMEM((edge_rows, 128), F32),
            pltpu.VMEM((3 * width, width), F32),
            pltpu.VMEM((4 * width, width), F32),
        ],
    )
    other = across_cores(away)
    members = square_members()
    *blocks, own = call(
        functools.partial(pair_kernel, parts),
        [shaped(PACKED + halves // members, width, BF16)] * members,
        0,
        keep,
        gains,
        other,
    )
    received = [in_square(block, members - 1 - i) for i, block in enumerate(blocks)]
    outer = out_of_pair(outer, PX)
    (inner,) = call(copy_kernel, [like(inner)], 10**9, in_pair(inner, PX))
    *received, inner = lax.optimization_barrier((*received, inner))
    (sums,) = call(sum_kernel, [like(own)], 0, *received, own)
    edges_grad, local_grad = call(
        finish_kernel,
        [shaped(edge_rows, width, BF16), shaped(count, width, F32)],
        square * (edge_rows + 2 * count),
        edge_grads,
        pre_grad,
        sender_sum,
        receiver_sum,
        node_part,
        w_edge_in,
    )
    along_core, along_chip, center = call(
        turn_kernel,
        [
            shaped(3 * slots, width, BF16),
            shaped(3 * slots, width, BF16),
            shaped(2 * slots, width, BF16),
        ],
        10**10,
        inner,
        outer,
        middle,
        after=[sums],
    )
    gains, mine, along_core, along_chip = joined(
        sums, gains.shape[0], across_cores(along_core), out_of_pair(along_chip, PY)
    )
    blocks = [mine] + [in_square(mine, offset) for offset in range(1, members)]
    gain_edge_grad = (gains[0] + gains[1]).astype(BF16)
    gain_node_grad = (gains[2] + gains[3]).astype(BF16)
    (nodes_grad,) = call(
        return_kernel,
        [shaped(count, width, BF16)],
        2 * halo_rows * count * width,
        send_list,
        local_grad,
        center,
        along_core,
        along_chip,
    )
    done = (nodes_grad, edges_grad, gain_edge_grad, gain_node_grad)
    for i in range(members):
        blocks[i], *done = lax.optimization_barrier((blocks[i], *done))
    nodes_grad, edges_grad, gain_edge_grad, gain_node_grad = done
    blocks += [across_cores(block) for block in blocks]
    w_edge_in_grad, w_edge_out_grad, w_node_in_grad, w_node_out_grad = placed(
        parts, blocks, width
    )
    return (
        nodes_grad,
        edges_grad,
        w_edge_in_grad,
        w_edge_out_grad,
        gain_edge_grad,
        w_node_in_grad,
        w_node_out_grad,
        gain_node_grad,
    )


def solution(mesh):
    in_specs = (
        P(("groups",) + PX + PY, None),
        P(("groups",) + PX + PY, None),
        P(("groups",) + PX + PY, None),
        P(("groups",) + PX + PY, None),
        P(("groups",) + PX + PY, None),
        P(("groups",) + PX + PY, None),
        P(("groups",) + PX + PY, None),
        P(("groups",) + PX + PY),
        P(),
        P(),
        P(),
        P(),
        P(),
        P(),
    )
    out_specs = (
        P(("groups",) + PX + PY, None),
        P(("groups",) + PX + PY, None),
        P("groups", None),
        P("groups", None),
        P("groups"),
        P("groups", None),
        P("groups", None),
        P("groups"),
    )
    groups, px, py = mesh.devices.shape
    by_core = jax.sharding.Mesh(
        mesh.devices.reshape(groups, px // 2, 2, py // 2, 2), ("groups",) + PX + PY
    )
    return jax.shard_map(
        on_device, mesh=by_core, in_specs=in_specs, out_specs=out_specs, check_vma=False
    )
```

```python
import functools

import jax
import jax.numpy as jnp
from jax import lax
from jax.experimental import pallas as pl
from jax.experimental.pallas import tpu as pltpu
from jax.sharding import PartitionSpec as P

EPS = 1e-05
BF16 = jnp.bfloat16
F32 = jnp.float32
PACKED = 8
VMEM_LIMIT = 24 * 1024 * 1024


CORE = "core"
FAR = "far"
NEAR = "near"
PX = (FAR, NEAR)
PY = ("side", CORE)
SQUARE = (NEAR, "side")


def other_neighbour(i, size):
    return (i + 1 if i % 2 else i - 1) % size


def in_pair(array, axis):
    return lax.ppermute(array, axis, [(i, i ^ 1) for i in range(lax.axis_size(axis))])


def out_of_pair(array, axis):
    size = lax.axis_size(axis)
    return lax.ppermute(array, axis, [(i, other_neighbour(i, size)) for i in range(size)])


def square_members():
    return lax.axis_size(SQUARE)


def place_in_square():
    near, side = SQUARE
    return lax.axis_index(near) * lax.axis_size(side) + lax.axis_index(side)


def in_square(array, offset):
    return lax.ppermute(array, SQUARE, [(i, i ^ offset) for i in range(square_members())])


def tree_sum(terms):
    while len(terms) > 1:
        terms = [terms[i] + terms[i + 1] for i in range(0, len(terms), 2)]
    return terms[0]


def across_cores(array):
    return in_pair(array, CORE)


def by_pair(axis, up, down, inner, outer):
    first = lax.axis_index(axis) == 0

    @pl.when(first)
    def _():
        inner[...] = up
        outer[...] = down

    @pl.when(jnp.logical_not(first))
    def _():
        inner[...] = down
        outer[...] = up


def from_pair(axis, inner, outer):
    first = lax.axis_index(axis) == 0
    return jnp.where(first, outer, inner), jnp.where(first, inner, outer)


def dot(left, right):
    return jnp.dot(left, right, preferred_element_type=F32)


def dot_tn(left, right):
    return lax.dot_general(left, right, (((0,), (0,)), ((), ())), preferred_element_type=F32)


def dot_nt(left, right):
    return lax.dot_general(left, right, (((1,), (1,)), ((), ())), preferred_element_type=F32)


def sigmoid(value):
    return 0.5 + 0.5 * jnp.tanh(0.5 * value)


def normalize(value):
    centered = value - jnp.mean(value, axis=-1, keepdims=True)
    scale_inv = lax.rsqrt(jnp.mean(centered * centered, axis=-1, keepdims=True) + EPS)
    return centered * scale_inv, scale_inv


def norm_back(normed, scale_inv, gain, upstream):
    scaled = upstream * gain
    inner = (
        scaled
        - jnp.mean(scaled, axis=-1, keepdims=True)
        - normed * jnp.mean(scaled * normed, axis=-1, keepdims=True)
    )
    return inner * scale_inv


def columns_of(ids):
    rows, lanes = ids.shape
    padded = -(-rows // 8) * 8
    if padded > rows:
        ids = jnp.concatenate([ids, jnp.zeros((padded - rows, lanes), ids.dtype)], axis=0)
    return ids.T


def hot_rows(columns, tiles, base, count):
    parts = []
    for tile in tiles:
        column = columns[:, tile : tile + 1] - base
        lanes = lax.broadcasted_iota(jnp.int32, (columns.shape[0], count), 1)
        parts.append(jnp.where(lanes == column, 1.0, 0.0).astype(BF16))
    return jnp.concatenate(parts, axis=0) if len(parts) > 1 else parts[0]


def hot_columns(ids, tiles, base, count):
    parts = []
    for tile in tiles:
        row = ids[tile : tile + 1, :] - base
        subs = lax.broadcasted_iota(jnp.int32, (count, ids.shape[1]), 0)
        parts.append(jnp.where(subs == row, 1.0, 0.0).astype(BF16))
    return jnp.concatenate(parts, axis=1) if len(parts) > 1 else parts[0]


def list_hot(ids, count):
    directions, slots = ids.shape
    wide = jnp.concatenate([ids, jnp.zeros((directions, 128 - slots), ids.dtype)], axis=1)
    columns = wide.T
    parts = []
    for k in range(directions):
        lanes = lax.broadcasted_iota(jnp.int32, (slots, count), 1)
        parts.append(jnp.where(lanes == columns[:slots, k : k + 1], 1.0, 0.0).astype(BF16))
    return jnp.concatenate(parts, axis=0)


def live_rows(count_ref, tile_rows, rows):
    index = lax.broadcasted_iota(jnp.int32, (rows, 1), 0)
    return jnp.where(index < count_ref[0] * tile_rows, 1.0, 0.0)


def fetch_all(sources, targets, sems):
    copies = [
        pltpu.make_async_copy(source, target, sems.at[i])
        for i, (source, target) in enumerate(zip(sources, targets))
    ]
    for copy in copies:
        copy.start()
    return copies


def send_kernel(nodes_hbm, list_hbm, inner, outer, middle, nodes, send_list, sems):
    slots = send_list.shape[1]
    list_copy, nodes_copy = fetch_all([list_hbm, nodes_hbm], [send_list, nodes], sems)
    list_copy.wait()
    hot = list_hot(send_list[...], nodes.shape[0])
    nodes_copy.wait()
    rows = dot(hot, nodes[...]).astype(BF16)
    by_pair(NEAR, rows[5 * slots :], rows[: 3 * slots], inner, outer)
    middle[...] = rows[3 * slots : 5 * slots]


def corner_kernel(inner, outer, middle, along_core, along_chip, straight):
    slots = middle.shape[0] // 2
    low, high = from_pair(NEAR, inner[...], outer[...])
    up = jnp.concatenate([high[2 * slots :], middle[slots:], low[2 * slots :]], axis=0)
    down = jnp.concatenate([high[:slots], middle[:slots], low[:slots]], axis=0)
    by_pair(CORE, up, down, along_core, along_chip)
    straight[:slots] = high[slots : 2 * slots]
    straight[slots:] = low[slots : 2 * slots]


def index_kernel(sources, *refs):
    fetched, refs = refs[:sources], refs[sources:]
    near_rows, halo_rows = refs[:2]
    targets, sems = refs[2:-1], refs[-1]
    senders, receivers = targets[:2]
    copies = fetch_all(fetched, targets, sems)
    for copy in copies[:2]:
        copy.wait()
    tile_rows = senders.shape[1]
    count = near_rows.shape[1] // 2
    by_sender = columns_of(senders[...])
    by_receiver = columns_of(receivers[...])
    for tile in range(senders.shape[0]):
        rows = slice(tile * tile_rows, (tile + 1) * tile_rows)
        near_rows[rows, :count] = hot_rows(by_sender, [tile], 0, count)
        near_rows[rows, count:] = hot_rows(by_receiver, [tile], 0, count)
        halo_rows[rows, :] = hot_rows(by_sender, [tile], count, halo_rows.shape[1])
    for copy in copies[2:]:
        copy.wait()


def local_kernel(
    nodes, edges, senders, receivers, near_rows, w_in, pre, sender_columns, receiver_columns
):
    width = nodes.shape[1]
    tile_rows = senders.shape[1]
    extended = sender_columns.shape[0]
    count = receiver_columns.shape[0]
    sender_ids = senders[...]
    receiver_ids = receivers[...]
    for tile in range(senders.shape[0]):
        rows = slice(tile * tile_rows, (tile + 1) * tile_rows)
        sender_columns[:, rows] = hot_columns(sender_ids, [tile], 0, extended)
        receiver_columns[:, rows] = hot_columns(receiver_ids, [tile], 0, count)
    x = nodes[...]
    table = jnp.concatenate(
        [
            dot(x, w_in[width : 2 * width]).astype(BF16),
            dot(x, w_in[2 * width :]).astype(BF16),
        ],
        axis=0,
    )
    pre[...] = dot(edges[...], w_in[:width]) + dot(near_rows[...], table)


def split_by_core(sums, first, keep_out, away_out):
    half = sums.shape[0] // 2
    core = lax.axis_index(CORE)
    keep_out[first : first + half] = sums[pl.ds(pl.multiple_of(core * half, half), half), :]
    away = sums[pl.ds(pl.multiple_of((1 - core) * half, half), half), :]
    away_out[first : first + half] = away.astype(BF16)


def pack_gains(edge_gain, node_gain):
    edge_high = edge_gain.astype(BF16).astype(F32)
    node_high = node_gain.astype(BF16).astype(F32)
    row = lax.broadcasted_iota(jnp.int32, (PACKED, edge_gain.shape[1]), 0)
    packed = jnp.where(row == 0, edge_high, 0.0)
    packed = jnp.where(row == 1, edge_gain - edge_high, packed)
    packed = jnp.where(row == 2, node_high, packed)
    packed = jnp.where(row == 3, node_gain - node_high, packed)
    return packed.astype(BF16)


def layer_kernel(
    tile_rows,
    count_ref,
    nodes,
    node_grads,
    edges,
    edge_grads,
    pre_local,
    halo_rows,
    near_rows,
    sender_columns,
    receiver_columns,
    straight,
    along_core,
    along_chip,
    w_in,
    w_out,
    gain_edge,
    w_node_in,
    w_node_out,
    gain_node,
    pre_grad_out,
    sender_out,
    receiver_out,
    node_part_out,
    inner_out,
    outer_out,
    middle_out,
    keep_out,
    away_out,
    gains_out,
    slope_kept,
    hidden_kept,
    normed_kept,
    scale_kept,
    node_sums,
    edge_sums,
):
    count, width = nodes.shape
    edge_rows = edges.shape[0]
    live = live_rows(count_ref, tile_rows, edge_rows)
    slots = straight.shape[0] // 2
    up, down = from_pair(CORE, along_core[...], along_chip[...])
    halo = jnp.concatenate(
        [
            down[:slots],
            straight[:slots],
            up[:slots],
            down[slots : 2 * slots],
            up[slots : 2 * slots],
            down[2 * slots :],
            straight[slots:],
            up[2 * slots :],
        ],
        axis=0,
    )
    table = dot(halo, w_in[width : 2 * width]).astype(BF16)
    gain = gain_edge[...].astype(F32)[None, :]
    value = pre_local[...] + dot(halo_rows[...], table)
    sigma = sigmoid(value)
    hidden = (value * sigma).astype(BF16)
    hidden_kept[...] = hidden
    slope_kept[...] = sigma * (1.0 + value * (1.0 - sigma))
    edge_normed, edge_scale = normalize(dot(hidden, w_out[...]))
    normed_kept[...] = edge_normed
    scale_kept[...] = jnp.broadcast_to(edge_scale, (edge_rows, 128))
    message = (live * gain * edge_normed).astype(BF16)
    total = dot(receiver_columns[...], message)
    aggregated = total.astype(BF16)
    x = nodes[...]
    w_first = w_node_in[:width]
    w_second = w_node_in[width:]
    node_pre = dot(x, w_first) + dot(aggregated, w_second)
    sigma = sigmoid(node_pre)
    node_hidden = (node_pre * sigma).astype(BF16)
    normed, scale_inv = normalize(dot(node_hidden, w_node_out[...]))
    upstream = node_grads[...].astype(F32)
    out_grad = norm_back(normed, scale_inv, gain_node[...].astype(F32)[None, :], upstream).astype(BF16)
    slope = sigma * (1.0 + node_pre * (1.0 - sigma))
    pre_grad = (dot_nt(out_grad, w_node_out[...]) * slope).astype(BF16)
    agg_grad = dot_nt(pre_grad, w_second).astype(BF16)
    node_part_out[...] = upstream + dot_nt(pre_grad, w_first)
    node_sums[:width] = dot_tn(x, pre_grad)
    node_sums[width : 2 * width] = dot_tn(aggregated, pre_grad)
    node_sums[2 * width : 3 * width] = dot_tn(node_hidden, out_grad)
    node_gain = jnp.sum(upstream * normed, axis=0, keepdims=True)
    upstream = live * (
        edge_grads[...].astype(F32) + dot(near_rows[:, count:], agg_grad)
    )
    edge_normed = normed_kept[...]
    edge_gain = jnp.sum(upstream * edge_normed, axis=0, keepdims=True)
    out_grad = norm_back(edge_normed, scale_kept[:, :1], gain, upstream).astype(BF16)
    pre_grad = (dot_nt(out_grad, w_out[...]) * slope_kept[...]).astype(BF16)
    pre_grad_out[...] = pre_grad
    sender_total = dot(sender_columns[...], pre_grad)
    receiver_total = dot(receiver_columns[...], pre_grad)
    own = sender_total[:count].astype(BF16)
    away = sender_total[count:].astype(BF16)
    received = receiver_total.astype(BF16)
    sender_out[...] = own
    receiver_out[...] = received
    halo_grad = dot_nt(away, w_in[width : 2 * width]).astype(BF16)
    by_pair(NEAR, halo_grad[: 3 * slots], halo_grad[5 * slots :], inner_out, outer_out)
    middle_out[...] = halo_grad[3 * slots : 5 * slots]
    edge_sums[:width] = dot_tn(edges[...], pre_grad)
    edge_sums[width : 2 * width] = dot_tn(x, own) + dot_tn(halo, away)
    edge_sums[2 * width : 3 * width] = dot_tn(x, received)
    edge_sums[3 * width : 4 * width] = dot_tn(hidden_kept[...], out_grad)
    split_by_core(edge_sums, 0, keep_out, away_out)
    split_by_core(node_sums, edge_sums.shape[0] // 2, keep_out, away_out)
    gains = pack_gains(edge_gain, node_gain)
    away_out[keep_out.shape[0] :] = gains
    gains_out[...] = gains


def pair_kernel(parts, keep, gains, other, *outs):
    rows = keep.shape[0]
    packed = gains.shape[0]
    members = len(outs)
    both = gains[...].astype(F32) + other[rows : rows + packed].astype(F32)
    summed = pack_gains(both[0:1] + both[1:2], both[2:3] + both[3:4])
    me = place_in_square()
    for offset, out in enumerate(reversed(outs)):
        owner = me ^ offset
        out[:packed] = summed
        first, at = 0, packed
        for part in parts:
            step = part // members
            source = pl.ds(pl.multiple_of(first + owner * step, 16), step)
            out[at : at + step] = (keep[source, :] + other[source, :].astype(F32)).astype(BF16)
            first, at = first + part, at + step


def add_packed(values):
    packed = PACKED
    gains = values[:packed]
    return pack_gains(gains[0:1] + gains[1:2], gains[2:3] + gains[3:4])


def copy_kernel(source, target):
    target[...] = source[...]


def sum_kernel(*refs):
    sums_out = refs[-1]
    sums = tree_sum([block[...].astype(F32) for block in refs[:-1]])
    sums_out[...] = sums.astype(BF16)
    sums_out[:PACKED] = add_packed(sums)


def join_kernel(own, other, sums_out):
    sums = own[...].astype(F32) + other[...].astype(F32)
    sums_out[...] = sums.astype(BF16)
    sums_out[:PACKED] = add_packed(sums)


def whole_kernel(own, other, gains_out, mine):
    packed = gains_out.shape[0]
    sums = own[...].astype(F32) + other[...].astype(F32)
    gains_out[...] = sums[:packed]
    mine[...] = sums[packed:].astype(BF16)


def place_kernel(parts, *refs):
    count = 2 * len(parts)
    sems, wholes = refs[-1], refs[-1 - len(parts) : -1]
    outs = refs[-1 - len(parts) - count : -1 - len(parts)]
    blocks = refs[: -1 - len(parts) - count]
    members = len(blocks) // 2
    core = lax.axis_index(CORE)
    me = place_in_square()
    copies = []
    at = 0
    for i, (part, whole) in enumerate(zip(parts, wholes)):
        step = part // members
        for position, block in enumerate(blocks):
            half = core if position < members else 1 - core
            owner = me ^ (position % members)
            row = pl.multiple_of(half * part + owner * step, 16)
            whole[pl.ds(row, step), :] = block[at : at + step]
        at += step
        cut = outs[2 * i].shape[0]
        copies += [
            pltpu.make_async_copy(whole.at[:cut], outs[2 * i], sems.at[2 * i]),
            pltpu.make_async_copy(whole.at[cut:], outs[2 * i + 1], sems.at[2 * i + 1]),
        ]
        for copy in copies[-2:]:
            copy.start()
    for copy in copies:
        copy.wait()


def finish_kernel(
    edge_grads, pre_grad, sender_sum, receiver_sum, node_part, w_in, edges_grad, local_grad
):
    width = w_in.shape[1]
    edges_grad[...] = (
        edge_grads[...].astype(F32) + dot_nt(pre_grad[...], w_in[:width])
    ).astype(BF16)
    local_grad[...] = (
        node_part[...]
        + dot_nt(sender_sum[...], w_in[width : 2 * width])
        + dot_nt(receiver_sum[...], w_in[2 * width :])
    )


def turn_kernel(inner, outer, middle, along_core, along_chip, center):
    slots = middle.shape[0] // 2
    top, bottom = from_pair(NEAR, inner[...], outer[...])
    up = jnp.concatenate([top[:slots], middle[:slots], bottom[:slots]], axis=0)
    down = jnp.concatenate([top[2 * slots :], middle[slots:], bottom[2 * slots :]], axis=0)
    by_pair(CORE, up, down, along_core, along_chip)
    center[:slots] = top[slots : 2 * slots]
    center[slots:] = bottom[slots : 2 * slots]


def return_kernel(send_list, local_grad, center, along_core, along_chip, nodes_grad):
    slots = send_list.shape[1]
    up, down = from_pair(CORE, along_core[...], along_chip[...])
    returned = jnp.concatenate(
        [
            up[:slots],
            center[:slots],
            down[:slots],
            up[slots : 2 * slots],
            down[slots : 2 * slots],
            up[2 * slots :],
            center[slots:],
            down[2 * slots :],
        ],
        axis=0,
    )
    hot = list_hot(send_list[...], local_grad.shape[0])
    nodes_grad[...] = (local_grad[...] + dot_tn(hot, returned)).astype(BF16)


SMEM = pltpu.SMEM
VMEM = pltpu.VMEM
HBM = pltpu.HBM


def call(body, outs, flops, *operands, spaces=(), out_space=VMEM, scratch=(), after=()):
    if after:
        first, rest = len(operands), len(operands) + len(after)
        inner = body

        def body(*refs):
            inner(*refs[:first], *refs[rest:])

        operands = operands + tuple(after)
    moved = sum(x.size * x.dtype.itemsize for x in operands)
    moved += sum(x.size * jnp.dtype(x.dtype).itemsize for x in outs)
    spaces = list(spaces) + [VMEM] * (len(operands) - len(spaces))
    out_spaces = out_space if isinstance(out_space, list) else [out_space] * len(outs)
    operands = [
        pltpu.with_memory_space_constraint(x, HBM) if space is HBM else x
        for x, space in zip(operands, spaces)
    ]
    return pl.pallas_call(
        body,
        out_shape=outs,
        in_specs=[pl.BlockSpec(memory_space=space) for space in spaces],
        out_specs=[pl.BlockSpec(memory_space=space) for space in out_spaces],
        scratch_shapes=list(scratch),
        compiler_params=pltpu.CompilerParams(vmem_limit_bytes=VMEM_LIMIT),
        cost_estimate=pl.CostEstimate(flops=flops, bytes_accessed=moved, transcendentals=0),
    )(*operands)


def like(array):
    return jax.ShapeDtypeStruct(array.shape, array.dtype)


def shaped(rows, columns, dtype):
    return jax.ShapeDtypeStruct((rows, columns), dtype)


def placed(parts, blocks, width):
    return call(
        functools.partial(place_kernel, parts),
        [
            shaped(3 * width, width, BF16),
            shaped(width, width, BF16),
            shaped(2 * width, width, BF16),
            shaped(width, width, BF16),
        ],
        0,
        *blocks,
        out_space=HBM,
        scratch=[pltpu.VMEM((2 * part, width), BF16) for part in parts]
        + [pltpu.SemaphoreType.DMA((2 * len(parts),))],
    )


def joined(sums, packed, *beside):
    rows, width = sums.shape
    size = lax.axis_size(FAR)
    distance = 1
    while True:
        other = lax.ppermute(sums, FAR, [(i, i ^ distance) for i in range(size)])
        distance *= 2
        if distance == size:
            break
        (sums,) = call(join_kernel, [like(sums)], 0, sums, other)
    other, *beside = lax.optimization_barrier((other, *beside))
    gains, mine = call(
        whole_kernel,
        [shaped(packed, width, F32), shaped(rows - packed, width, BF16)],
        0,
        sums,
        other,
    )
    return gains, mine, *beside


def on_device(
    nodes,
    edges,
    edge_grads,
    node_grads,
    send_list,
    senders,
    receivers,
    tile_count,
    w_edge_in,
    w_edge_out,
    gain_edge,
    w_node_in,
    w_node_out,
    gain_node,
):
    count, width = nodes.shape
    slots = send_list.shape[1]
    halo_rows = 8 * slots
    edge_rows = edges.shape[0]
    tile_rows = senders.shape[1]
    square = 2 * width * width
    inner, outer, middle, nodes, send_list = call(
        send_kernel,
        [
            shaped(3 * slots, width, BF16),
            shaped(3 * slots, width, BF16),
            shaped(2 * slots, width, BF16),
            like(nodes),
            like(send_list),
        ],
        2 * halo_rows * count * width,
        nodes,
        send_list,
        spaces=[HBM, HBM],
        scratch=[pltpu.SemaphoreType.DMA((2,))],
    )
    inner = in_pair(inner, PX)
    outer = out_of_pair(outer, PX)
    fetched = [
        senders,
        receivers,
        edges,
        w_edge_in,
        w_edge_out,
        gain_edge,
        w_node_in,
        w_node_out,
        gain_node,
        node_grads,
        edge_grads,
    ]
    near_hot, halo_hot, *fetched = call(
        functools.partial(index_kernel, len(fetched)),
        [
            shaped(edge_rows, 2 * count, BF16),
            shaped(edge_rows, halo_rows, BF16),
        ]
        + [like(x) for x in fetched],
        0,
        *fetched,
        spaces=[HBM] * len(fetched),
        scratch=[pltpu.SemaphoreType.DMA((len(fetched),))],
    )
    (
        senders,
        receivers,
        edges,
        w_edge_in,
        w_edge_out,
        gain_edge,
        w_node_in,
        w_node_out,
        gain_node,
        node_grads,
        edge_grads,
    ) = fetched
    inner, outer, near_hot = lax.optimization_barrier((inner, outer, near_hot))
    along_core, along_chip, straight = call(
        corner_kernel,
        [
            shaped(3 * slots, width, BF16),
            shaped(3 * slots, width, BF16),
            shaped(2 * slots, width, BF16),
        ],
        0,
        inner,
        outer,
        middle,
    )
    along_chip = out_of_pair(along_chip, PY)
    along_core = across_cores(along_core)
    pre_local, sender_columns, receiver_columns = call(
        local_kernel,
        [
            shaped(edge_rows, width, F32),
            shaped(count + halo_rows, edge_rows, BF16),
            shaped(count, edge_rows, BF16),
        ],
        square * (2 * count + edge_rows) + 4 * edge_rows * count * width,
        nodes,
        edges,
        senders,
        receivers,
        near_hot,
        w_edge_in,
    )
    parts = (2 * width, 3 * width // 2)
    halves = sum(parts)
    pre_grad, sender_sum, receiver_sum, node_part, inner, outer, middle, keep, away, gains = call(
        functools.partial(layer_kernel, tile_rows),
        [
            shaped(edge_rows, width, BF16),
            shaped(count, width, BF16),
            shaped(count, width, BF16),
            shaped(count, width, F32),
            shaped(3 * slots, width, BF16),
            shaped(3 * slots, width, BF16),
            shaped(2 * slots, width, BF16),
            shaped(halves, width, F32),
            shaped(halves + PACKED, width, BF16),
            shaped(PACKED, width, BF16),
        ],
        square * (6 * edge_rows + 11 * count + 2 * halo_rows)
        + 2 * edge_rows * (4 * count + halo_rows) * width,
        tile_count,
        nodes,
        node_grads,
        edges,
        edge_grads,
        pre_local,
        halo_hot,
        near_hot,
        sender_columns,
        receiver_columns,
        straight,
        along_core,
        along_chip,
        w_edge_in,
        w_edge_out,
        gain_edge,
        w_node_in,
        w_node_out,
        gain_node,
        spaces=[SMEM],
        scratch=[
            pltpu.VMEM((edge_rows, width), F32),
            pltpu.VMEM((edge_rows, width), BF16),
            pltpu.VMEM((edge_rows, width), F32),
            pltpu.VMEM((edge_rows, 128), F32),
            pltpu.VMEM((3 * width, width), F32),
            pltpu.VMEM((4 * width, width), F32),
        ],
    )
    other = across_cores(away)
    members = square_members()
    *blocks, own = call(
        functools.partial(pair_kernel, parts),
        [shaped(PACKED + halves // members, width, BF16)] * members,
        0,
        keep,
        gains,
        other,
    )
    received = [in_square(block, members - 1 - i) for i, block in enumerate(blocks)]
    outer = out_of_pair(outer, PX)
    (inner,) = call(copy_kernel, [like(inner)], 10**9, in_pair(inner, PX))
    *received, inner = lax.optimization_barrier((*received, inner))
    (sums,) = call(sum_kernel, [like(own)], 0, *received, own)
    edges_grad, local_grad = call(
        finish_kernel,
        [shaped(edge_rows, width, BF16), shaped(count, width, F32)],
        square * (edge_rows + 2 * count),
        edge_grads,
        pre_grad,
        sender_sum,
        receiver_sum,
        node_part,
        w_edge_in,
    )
    along_core, along_chip, center = call(
        turn_kernel,
        [
            shaped(3 * slots, width, BF16),
            shaped(3 * slots, width, BF16),
            shaped(2 * slots, width, BF16),
        ],
        10**10,
        inner,
        outer,
        middle,
        after=[sums],
    )
    gains, mine, along_core, along_chip = joined(
        sums, gains.shape[0], across_cores(along_core), out_of_pair(along_chip, PY)
    )
    blocks = [mine] + [in_square(mine, offset) for offset in range(1, members)]
    gain_edge_grad = (gains[0] + gains[1]).astype(BF16)
    gain_node_grad = (gains[2] + gains[3]).astype(BF16)
    (nodes_grad,) = call(
        return_kernel,
        [shaped(count, width, BF16)],
        2 * halo_rows * count * width,
        send_list,
        local_grad,
        center,
        along_core,
        along_chip,
    )
    done = (nodes_grad, edges_grad, gain_edge_grad, gain_node_grad)
    for i in range(members):
        blocks[i], *done = lax.optimization_barrier((blocks[i], *done))
    nodes_grad, edges_grad, gain_edge_grad, gain_node_grad = done
    blocks += [across_cores(block) for block in blocks]
    w_edge_in_grad, w_edge_out_grad, w_node_in_grad, w_node_out_grad = placed(
        parts, blocks, width
    )
    return (
        nodes_grad,
        edges_grad,
        w_edge_in_grad,
        w_edge_out_grad,
        gain_edge_grad,
        w_node_in_grad,
        w_node_out_grad,
        gain_node_grad,
    )


def solution(mesh):
    in_specs = (
        P(("groups",) + PX + PY, None),
        P(("groups",) + PX + PY, None),
        P(("groups",) + PX + PY, None),
        P(("groups",) + PX + PY, None),
        P(("groups",) + PX + PY, None),
        P(("groups",) + PX + PY, None),
        P(("groups",) + PX + PY, None),
        P(("groups",) + PX + PY),
        P(),
        P(),
        P(),
        P(),
        P(),
        P(),
    )
    out_specs = (
        P(("groups",) + PX + PY, None),
        P(("groups",) + PX + PY, None),
        P("groups", None),
        P("groups", None),
        P("groups"),
        P("groups", None),
        P("groups", None),
        P("groups"),
    )
    groups, px, py = mesh.devices.shape
    by_core = jax.sharding.Mesh(
        mesh.devices.reshape(groups, px // 2, 2, py // 2, 2), ("groups",) + PX + PY
    )
    return jax.shard_map(
        on_device, mesh=by_core, in_specs=in_specs, out_specs=out_specs, check_vma=False
    )
```

```python
import functools

import jax
import jax.numpy as jnp
from jax import lax
from jax.experimental import pallas as pl
from jax.experimental.pallas import tpu as pltpu
from jax.sharding import PartitionSpec as P

EPS = 1e-05
BF16 = jnp.bfloat16
F32 = jnp.float32
PACKED = 8
VMEM_LIMIT = 24 * 1024 * 1024


CORE = "core"
FAR = "far"
NEAR = "near"
PX = (FAR, NEAR)
PY = ("side", CORE)
SQUARE = (NEAR, "side")


def other_neighbour(i, size):
    return (i + 1 if i % 2 else i - 1) % size


def in_pair(array, axis):
    return lax.ppermute(array, axis, [(i, i ^ 1) for i in range(lax.axis_size(axis))])


def out_of_pair(array, axis):
    size = lax.axis_size(axis)
    return lax.ppermute(array, axis, [(i, other_neighbour(i, size)) for i in range(size)])


def square_members():
    return lax.axis_size(SQUARE)


def place_in_square():
    near, side = SQUARE
    return lax.axis_index(near) * lax.axis_size(side) + lax.axis_index(side)


def in_square(array, offset):
    return lax.ppermute(array, SQUARE, [(i, i ^ offset) for i in range(square_members())])


def tree_sum(terms):
    while len(terms) > 1:
        terms = [terms[i] + terms[i + 1] for i in range(0, len(terms), 2)]
    return terms[0]


def across_cores(array):
    return in_pair(array, CORE)


def by_pair(axis, up, down, inner, outer):
    first = lax.axis_index(axis) == 0

    @pl.when(first)
    def _():
        inner[...] = up
        outer[...] = down

    @pl.when(jnp.logical_not(first))
    def _():
        inner[...] = down
        outer[...] = up


def from_pair(axis, inner, outer):
    first = lax.axis_index(axis) == 0
    return jnp.where(first, outer, inner), jnp.where(first, inner, outer)


def dot(left, right):
    return jnp.dot(left, right, preferred_element_type=F32)


def dot_tn(left, right):
    return lax.dot_general(left, right, (((0,), (0,)), ((), ())), preferred_element_type=F32)


def dot_nt(left, right):
    return lax.dot_general(left, right, (((1,), (1,)), ((), ())), preferred_element_type=F32)


def sigmoid(value):
    return 0.5 + 0.5 * jnp.tanh(0.5 * value)


def normalize(value):
    centered = value - jnp.mean(value, axis=-1, keepdims=True)
    scale_inv = lax.rsqrt(jnp.mean(centered * centered, axis=-1, keepdims=True) + EPS)
    return centered * scale_inv, scale_inv


def norm_back(normed, scale_inv, gain, upstream):
    scaled = upstream * gain
    inner = (
        scaled
        - jnp.mean(scaled, axis=-1, keepdims=True)
        - normed * jnp.mean(scaled * normed, axis=-1, keepdims=True)
    )
    return inner * scale_inv


def columns_of(ids):
    rows, lanes = ids.shape
    padded = -(-rows // 8) * 8
    if padded > rows:
        ids = jnp.concatenate([ids, jnp.zeros((padded - rows, lanes), ids.dtype)], axis=0)
    return ids.T


def hot_rows(columns, tiles, base, count):
    parts = []
    for tile in tiles:
        column = columns[:, tile : tile + 1] - base
        lanes = lax.broadcasted_iota(jnp.int32, (columns.shape[0], count), 1)
        parts.append(jnp.where(lanes == column, 1.0, 0.0).astype(BF16))
    return jnp.concatenate(parts, axis=0) if len(parts) > 1 else parts[0]


def hot_columns(ids, tiles, base, count):
    parts = []
    for tile in tiles:
        row = ids[tile : tile + 1, :] - base
        subs = lax.broadcasted_iota(jnp.int32, (count, ids.shape[1]), 0)
        parts.append(jnp.where(subs == row, 1.0, 0.0).astype(BF16))
    return jnp.concatenate(parts, axis=1) if len(parts) > 1 else parts[0]


def list_hot(ids, count):
    directions, slots = ids.shape
    wide = jnp.concatenate([ids, jnp.zeros((directions, 128 - slots), ids.dtype)], axis=1)
    columns = wide.T
    parts = []
    for k in range(directions):
        lanes = lax.broadcasted_iota(jnp.int32, (slots, count), 1)
        parts.append(jnp.where(lanes == columns[:slots, k : k + 1], 1.0, 0.0).astype(BF16))
    return jnp.concatenate(parts, axis=0)


def live_rows(count_ref, tile_rows, rows):
    index = lax.broadcasted_iota(jnp.int32, (rows, 1), 0)
    return jnp.where(index < count_ref[0] * tile_rows, 1.0, 0.0)


def fetch_all(sources, targets, sems):
    copies = [
        pltpu.make_async_copy(source, target, sems.at[i])
        for i, (source, target) in enumerate(zip(sources, targets))
    ]
    for copy in copies:
        copy.start()
    return copies


def send_kernel(nodes_hbm, list_hbm, inner, outer, middle, nodes, send_list, sems):
    slots = send_list.shape[1]
    list_copy, nodes_copy = fetch_all([list_hbm, nodes_hbm], [send_list, nodes], sems)
    list_copy.wait()
    hot = list_hot(send_list[...], nodes.shape[0])
    nodes_copy.wait()
    rows = dot(hot, nodes[...]).astype(BF16)
    by_pair(NEAR, rows[5 * slots :], rows[: 3 * slots], inner, outer)
    middle[...] = rows[3 * slots : 5 * slots]


def corner_kernel(inner, outer, middle, along_core, along_chip, straight):
    slots = middle.shape[0] // 2
    low, high = from_pair(NEAR, inner[...], outer[...])
    up = jnp.concatenate([high[2 * slots :], middle[slots:], low[2 * slots :]], axis=0)
    down = jnp.concatenate([high[:slots], middle[:slots], low[:slots]], axis=0)
    by_pair(CORE, up, down, along_core, along_chip)
    straight[:slots] = high[slots : 2 * slots]
    straight[slots:] = low[slots : 2 * slots]


def index_kernel(sources, *refs):
    fetched, refs = refs[:sources], refs[sources:]
    near_rows, halo_rows = refs[:2]
    targets, sems = refs[2:-1], refs[-1]
    senders, receivers = targets[:2]
    copies = fetch_all(fetched, targets, sems)
    for copy in copies[:2]:
        copy.wait()
    tile_rows = senders.shape[1]
    count = near_rows.shape[1] // 2
    by_sender = columns_of(senders[...])
    by_receiver = columns_of(receivers[...])
    for tile in range(senders.shape[0]):
        rows = slice(tile * tile_rows, (tile + 1) * tile_rows)
        near_rows[rows, :count] = hot_rows(by_sender, [tile], 0, count)
        near_rows[rows, count:] = hot_rows(by_receiver, [tile], 0, count)
        halo_rows[rows, :] = hot_rows(by_sender, [tile], count, halo_rows.shape[1])
    for copy in copies[2:]:
        copy.wait()


def local_kernel(
    nodes, edges, senders, receivers, near_rows, w_in, pre, sender_columns, receiver_columns
):
    width = nodes.shape[1]
    tile_rows = senders.shape[1]
    extended = sender_columns.shape[0]
    count = receiver_columns.shape[0]
    sender_ids = senders[...]
    receiver_ids = receivers[...]
    for tile in range(senders.shape[0]):
        rows = slice(tile * tile_rows, (tile + 1) * tile_rows)
        sender_columns[:, rows] = hot_columns(sender_ids, [tile], 0, extended)
        receiver_columns[:, rows] = hot_columns(receiver_ids, [tile], 0, count)
    x = nodes[...]
    table = jnp.concatenate(
        [
            dot(x, w_in[width : 2 * width]).astype(BF16),
            dot(x, w_in[2 * width :]).astype(BF16),
        ],
        axis=0,
    )
    pre[...] = dot(edges[...], w_in[:width]) + dot(near_rows[...], table)


def split_by_core(sums, first, keep_out, away_out):
    half = sums.shape[0] // 2
    core = lax.axis_index(CORE)
    keep_out[first : first + half] = sums[pl.ds(pl.multiple_of(core * half, half), half), :]
    away = sums[pl.ds(pl.multiple_of((1 - core) * half, half), half), :]
    away_out[first : first + half] = away.astype(BF16)


def pack_gains(edge_gain, node_gain):
    edge_high = edge_gain.astype(BF16).astype(F32)
    node_high = node_gain.astype(BF16).astype(F32)
    row = lax.broadcasted_iota(jnp.int32, (PACKED, edge_gain.shape[1]), 0)
    packed = jnp.where(row == 0, edge_high, 0.0)
    packed = jnp.where(row == 1, edge_gain - edge_high, packed)
    packed = jnp.where(row == 2, node_high, packed)
    packed = jnp.where(row == 3, node_gain - node_high, packed)
    return packed.astype(BF16)


def layer_kernel(
    tile_rows,
    count_ref,
    nodes,
    node_grads,
    edges,
    edge_grads,
    pre_local,
    halo_rows,
    near_rows,
    sender_columns,
    receiver_columns,
    straight,
    along_core,
    along_chip,
    w_in,
    w_out,
    gain_edge,
    w_node_in,
    w_node_out,
    gain_node,
    pre_grad_out,
    sender_out,
    receiver_out,
    node_part_out,
    inner_out,
    outer_out,
    middle_out,
    keep_out,
    away_out,
    gains_out,
    slope_kept,
    hidden_kept,
    normed_kept,
    scale_kept,
    node_sums,
    edge_sums,
):
    count, width = nodes.shape
    edge_rows = edges.shape[0]
    live = live_rows(count_ref, tile_rows, edge_rows)
    slots = straight.shape[0] // 2
    up, down = from_pair(CORE, along_core[...], along_chip[...])
    halo = jnp.concatenate(
        [
            down[:slots],
            straight[:slots],
            up[:slots],
            down[slots : 2 * slots],
            up[slots : 2 * slots],
            down[2 * slots :],
            straight[slots:],
            up[2 * slots :],
        ],
        axis=0,
    )
    table = dot(halo, w_in[width : 2 * width]).astype(BF16)
    gain = gain_edge[...].astype(F32)[None, :]
    value = pre_local[...] + dot(halo_rows[...], table)
    sigma = sigmoid(value)
    hidden = (value * sigma).astype(BF16)
    hidden_kept[...] = hidden
    slope_kept[...] = sigma * (1.0 + value * (1.0 - sigma))
    edge_normed, edge_scale = normalize(dot(hidden, w_out[...]))
    normed_kept[...] = edge_normed
    scale_kept[...] = jnp.broadcast_to(edge_scale, (edge_rows, 128))
    message = (live * gain * edge_normed).astype(BF16)
    total = dot(receiver_columns[...], message)
    aggregated = total.astype(BF16)
    x = nodes[...]
    w_first = w_node_in[:width]
    w_second = w_node_in[width:]
    node_pre = dot(x, w_first) + dot(aggregated, w_second)
    sigma = sigmoid(node_pre)
    node_hidden = (node_pre * sigma).astype(BF16)
    normed, scale_inv = normalize(dot(node_hidden, w_node_out[...]))
    upstream = node_grads[...].astype(F32)
    out_grad = norm_back(normed, scale_inv, gain_node[...].astype(F32)[None, :], upstream).astype(BF16)
    slope = sigma * (1.0 + node_pre * (1.0 - sigma))
    pre_grad = (dot_nt(out_grad, w_node_out[...]) * slope).astype(BF16)
    agg_grad = dot_nt(pre_grad, w_second).astype(BF16)
    node_part_out[...] = upstream + dot_nt(pre_grad, w_first)
    node_sums[:width] = dot_tn(x, pre_grad)
    node_sums[width : 2 * width] = dot_tn(aggregated, pre_grad)
    node_sums[2 * width : 3 * width] = dot_tn(node_hidden, out_grad)
    node_gain = jnp.sum(upstream * normed, axis=0, keepdims=True)
    upstream = live * (
        edge_grads[...].astype(F32) + dot(near_rows[:, count:], agg_grad)
    )
    edge_normed = normed_kept[...]
    edge_gain = jnp.sum(upstream * edge_normed, axis=0, keepdims=True)
    out_grad = norm_back(edge_normed, scale_kept[:, :1], gain, upstream).astype(BF16)
    pre_grad = (dot_nt(out_grad, w_out[...]) * slope_kept[...]).astype(BF16)
    pre_grad_out[...] = pre_grad
    sender_total = dot(sender_columns[...], pre_grad)
    receiver_total = dot(receiver_columns[...], pre_grad)
    own = sender_total[:count].astype(BF16)
    away = sender_total[count:].astype(BF16)
    received = receiver_total.astype(BF16)
    sender_out[...] = own
    receiver_out[...] = received
    halo_grad = dot_nt(away, w_in[width : 2 * width]).astype(BF16)
    by_pair(NEAR, halo_grad[: 3 * slots], halo_grad[5 * slots :], inner_out, outer_out)
    middle_out[...] = halo_grad[3 * slots : 5 * slots]
    edge_sums[:width] = dot_tn(edges[...], pre_grad)
    edge_sums[width : 2 * width] = dot_tn(x, own) + dot_tn(halo, away)
    edge_sums[2 * width : 3 * width] = dot_tn(x, received)
    edge_sums[3 * width : 4 * width] = dot_tn(hidden_kept[...], out_grad)
    split_by_core(edge_sums, 0, keep_out, away_out)
    split_by_core(node_sums, edge_sums.shape[0] // 2, keep_out, away_out)
    gains = pack_gains(edge_gain, node_gain)
    away_out[keep_out.shape[0] :] = gains
    gains_out[...] = gains


def pair_kernel(parts, keep, gains, other, inner, *outs):
    rows = keep.shape[0]
    packed = gains.shape[0]
    members = len(outs)
    both = gains[...].astype(F32) + other[rows : rows + packed].astype(F32)
    summed = pack_gains(both[0:1] + both[1:2], both[2:3] + both[3:4])
    me = place_in_square()
    for offset, out in enumerate(reversed(outs)):
        owner = me ^ offset
        at = 0
        if offset == lax.axis_size(SQUARE[1]):
            at = inner.shape[0]
            out[:at] = inner[...]
        out[at : at + packed] = summed
        first, at = 0, at + packed
        for part in parts:
            step = part // members
            source = pl.ds(pl.multiple_of(first + owner * step, 16), step)
            out[at : at + step] = (keep[source, :] + other[source, :].astype(F32)).astype(BF16)
            first, at = first + part, at + step


def add_packed(values):
    packed = PACKED
    gains = values[:packed]
    return pack_gains(gains[0:1] + gains[1:2], gains[2:3] + gains[3:4])


def sum_kernel(*refs):
    sums_out = refs[-1]
    rows = sums_out.shape[0]
    sums = tree_sum([block[block.shape[0] - rows :].astype(F32) for block in refs[:-1]])
    sums_out[...] = sums.astype(BF16)
    sums_out[:PACKED] = add_packed(sums)


def join_kernel(own, other, sums_out):
    sums = own[...].astype(F32) + other[...].astype(F32)
    sums_out[...] = sums.astype(BF16)
    sums_out[:PACKED] = add_packed(sums)


def whole_kernel(own, other, gains_out, mine):
    packed = gains_out.shape[0]
    sums = own[...].astype(F32) + other[...].astype(F32)
    gains_out[...] = sums[:packed]
    mine[...] = sums[packed:].astype(BF16)


def place_kernel(parts, *refs):
    count = 2 * len(parts)
    sems, wholes = refs[-1], refs[-1 - len(parts) : -1]
    outs = refs[-1 - len(parts) - count : -1 - len(parts)]
    blocks = refs[: -1 - len(parts) - count]
    members = len(blocks) // 2
    core = lax.axis_index(CORE)
    me = place_in_square()
    copies = []
    at = 0
    for i, (part, whole) in enumerate(zip(parts, wholes)):
        step = part // members
        for position, block in enumerate(blocks):
            half = core if position < members else 1 - core
            owner = me ^ (position % members)
            row = pl.multiple_of(half * part + owner * step, 16)
            whole[pl.ds(row, step), :] = block[at : at + step]
        at += step
        cut = outs[2 * i].shape[0]
        copies += [
            pltpu.make_async_copy(whole.at[:cut], outs[2 * i], sems.at[2 * i]),
            pltpu.make_async_copy(whole.at[cut:], outs[2 * i + 1], sems.at[2 * i + 1]),
        ]
        for copy in copies[-2:]:
            copy.start()
    for copy in copies:
        copy.wait()


def finish_kernel(
    edge_grads, pre_grad, sender_sum, receiver_sum, node_part, w_in, edges_grad, local_grad
):
    width = w_in.shape[1]
    edges_grad[...] = (
        edge_grads[...].astype(F32) + dot_nt(pre_grad[...], w_in[:width])
    ).astype(BF16)
    local_grad[...] = (
        node_part[...]
        + dot_nt(sender_sum[...], w_in[width : 2 * width])
        + dot_nt(receiver_sum[...], w_in[2 * width :])
    )


def turn_kernel(inner, outer, middle, along_core, along_chip, center):
    slots = middle.shape[0] // 2
    top, bottom = from_pair(NEAR, inner[: outer.shape[0]], outer[...])
    up = jnp.concatenate([top[:slots], middle[:slots], bottom[:slots]], axis=0)
    down = jnp.concatenate([top[2 * slots :], middle[slots:], bottom[2 * slots :]], axis=0)
    by_pair(CORE, up, down, along_core, along_chip)
    center[:slots] = top[slots : 2 * slots]
    center[slots:] = bottom[slots : 2 * slots]


def return_kernel(send_list, local_grad, center, along_core, along_chip, nodes_grad):
    slots = send_list.shape[1]
    up, down = from_pair(CORE, along_core[...], along_chip[...])
    returned = jnp.concatenate(
        [
            up[:slots],
            center[:slots],
            down[:slots],
            up[slots : 2 * slots],
            down[slots : 2 * slots],
            up[2 * slots :],
            center[slots:],
            down[2 * slots :],
        ],
        axis=0,
    )
    hot = list_hot(send_list[...], local_grad.shape[0])
    nodes_grad[...] = (local_grad[...] + dot_tn(hot, returned)).astype(BF16)


SMEM = pltpu.SMEM
VMEM = pltpu.VMEM
HBM = pltpu.HBM


def call(body, outs, flops, *operands, spaces=(), out_space=VMEM, scratch=(), after=()):
    if after:
        first, rest = len(operands), len(operands) + len(after)
        inner = body

        def body(*refs):
            inner(*refs[:first], *refs[rest:])

        operands = operands + tuple(after)
    moved = sum(x.size * x.dtype.itemsize for x in operands)
    moved += sum(x.size * jnp.dtype(x.dtype).itemsize for x in outs)
    spaces = list(spaces) + [VMEM] * (len(operands) - len(spaces))
    out_spaces = out_space if isinstance(out_space, list) else [out_space] * len(outs)
    operands = [
        pltpu.with_memory_space_constraint(x, HBM) if space is HBM else x
        for x, space in zip(operands, spaces)
    ]
    return pl.pallas_call(
        body,
        out_shape=outs,
        in_specs=[pl.BlockSpec(memory_space=space) for space in spaces],
        out_specs=[pl.BlockSpec(memory_space=space) for space in out_spaces],
        scratch_shapes=list(scratch),
        compiler_params=pltpu.CompilerParams(vmem_limit_bytes=VMEM_LIMIT),
        cost_estimate=pl.CostEstimate(flops=flops, bytes_accessed=moved, transcendentals=0),
    )(*operands)


def like(array):
    return jax.ShapeDtypeStruct(array.shape, array.dtype)


def shaped(rows, columns, dtype):
    return jax.ShapeDtypeStruct((rows, columns), dtype)


def placed(parts, blocks, width):
    return call(
        functools.partial(place_kernel, parts),
        [
            shaped(3 * width, width, BF16),
            shaped(width, width, BF16),
            shaped(2 * width, width, BF16),
            shaped(width, width, BF16),
        ],
        0,
        *blocks,
        out_space=HBM,
        scratch=[pltpu.VMEM((2 * part, width), BF16) for part in parts]
        + [pltpu.SemaphoreType.DMA((2 * len(parts),))],
    )


def joined(sums, packed, *beside):
    rows, width = sums.shape
    size = lax.axis_size(FAR)
    distance = 1
    while True:
        other = lax.ppermute(sums, FAR, [(i, i ^ distance) for i in range(size)])
        distance *= 2
        if distance == size:
            break
        (sums,) = call(join_kernel, [like(sums)], 0, sums, other)
    other, *beside = lax.optimization_barrier((other, *beside))
    gains, mine = call(
        whole_kernel,
        [shaped(packed, width, F32), shaped(rows - packed, width, BF16)],
        0,
        sums,
        other,
    )
    return gains, mine, *beside


def on_device(
    nodes,
    edges,
    edge_grads,
    node_grads,
    send_list,
    senders,
    receivers,
    tile_count,
    w_edge_in,
    w_edge_out,
    gain_edge,
    w_node_in,
    w_node_out,
    gain_node,
):
    count, width = nodes.shape
    slots = send_list.shape[1]
    halo_rows = 8 * slots
    edge_rows = edges.shape[0]
    tile_rows = senders.shape[1]
    square = 2 * width * width
    inner, outer, middle, nodes, send_list = call(
        send_kernel,
        [
            shaped(3 * slots, width, BF16),
            shaped(3 * slots, width, BF16),
            shaped(2 * slots, width, BF16),
            like(nodes),
            like(send_list),
        ],
        2 * halo_rows * count * width,
        nodes,
        send_list,
        spaces=[HBM, HBM],
        scratch=[pltpu.SemaphoreType.DMA((2,))],
    )
    inner = in_pair(inner, PX)
    outer = out_of_pair(outer, PX)
    fetched = [
        senders,
        receivers,
        edges,
        w_edge_in,
        w_edge_out,
        gain_edge,
        w_node_in,
        w_node_out,
        gain_node,
        node_grads,
        edge_grads,
    ]
    near_hot, halo_hot, *fetched = call(
        functools.partial(index_kernel, len(fetched)),
        [
            shaped(edge_rows, 2 * count, BF16),
            shaped(edge_rows, halo_rows, BF16),
        ]
        + [like(x) for x in fetched],
        0,
        *fetched,
        spaces=[HBM] * len(fetched),
        scratch=[pltpu.SemaphoreType.DMA((len(fetched),))],
    )
    (
        senders,
        receivers,
        edges,
        w_edge_in,
        w_edge_out,
        gain_edge,
        w_node_in,
        w_node_out,
        gain_node,
        node_grads,
        edge_grads,
    ) = fetched
    inner, outer, near_hot = lax.optimization_barrier((inner, outer, near_hot))
    along_core, along_chip, straight = call(
        corner_kernel,
        [
            shaped(3 * slots, width, BF16),
            shaped(3 * slots, width, BF16),
            shaped(2 * slots, width, BF16),
        ],
        0,
        inner,
        outer,
        middle,
    )
    along_chip = out_of_pair(along_chip, PY)
    along_core = across_cores(along_core)
    pre_local, sender_columns, receiver_columns = call(
        local_kernel,
        [
            shaped(edge_rows, width, F32),
            shaped(count + halo_rows, edge_rows, BF16),
            shaped(count, edge_rows, BF16),
        ],
        square * (2 * count + edge_rows) + 4 * edge_rows * count * width,
        nodes,
        edges,
        senders,
        receivers,
        near_hot,
        w_edge_in,
    )
    parts = (2 * width, 3 * width // 2)
    halves = sum(parts)
    pre_grad, sender_sum, receiver_sum, node_part, inner, outer, middle, keep, away, gains = call(
        functools.partial(layer_kernel, tile_rows),
        [
            shaped(edge_rows, width, BF16),
            shaped(count, width, BF16),
            shaped(count, width, BF16),
            shaped(count, width, F32),
            shaped(3 * slots, width, BF16),
            shaped(3 * slots, width, BF16),
            shaped(2 * slots, width, BF16),
            shaped(halves, width, F32),
            shaped(halves + PACKED, width, BF16),
            shaped(PACKED, width, BF16),
        ],
        square * (6 * edge_rows + 11 * count + 2 * halo_rows)
        + 2 * edge_rows * (4 * count + halo_rows) * width,
        tile_count,
        nodes,
        node_grads,
        edges,
        edge_grads,
        pre_local,
        halo_hot,
        near_hot,
        sender_columns,
        receiver_columns,
        straight,
        along_core,
        along_chip,
        w_edge_in,
        w_edge_out,
        gain_edge,
        w_node_in,
        w_node_out,
        gain_node,
        spaces=[SMEM],
        scratch=[
            pltpu.VMEM((edge_rows, width), F32),
            pltpu.VMEM((edge_rows, width), BF16),
            pltpu.VMEM((edge_rows, width), F32),
            pltpu.VMEM((edge_rows, 128), F32),
            pltpu.VMEM((3 * width, width), F32),
            pltpu.VMEM((4 * width, width), F32),
        ],
    )
    other = across_cores(away)
    members = square_members()
    block_rows = PACKED + halves // members
    paired = lax.axis_size(SQUARE[1])
    *blocks, own = call(
        functools.partial(pair_kernel, parts),
        [
            shaped(block_rows + (3 * slots if offset == paired else 0), width, BF16)
            for offset in reversed(range(members))
        ],
        0,
        keep,
        gains,
        other,
        inner,
    )
    received = [in_square(block, members - 1 - i) for i, block in enumerate(blocks)]
    inner = received[members - 1 - paired]
    outer = out_of_pair(outer, PX)
    (sums,) = call(sum_kernel, [like(own)], 0, *received, own)
    edges_grad, local_grad = call(
        finish_kernel,
        [shaped(edge_rows, width, BF16), shaped(count, width, F32)],
        square * (edge_rows + 2 * count),
        edge_grads,
        pre_grad,
        sender_sum,
        receiver_sum,
        node_part,
        w_edge_in,
    )
    along_core, along_chip, center = call(
        turn_kernel,
        [
            shaped(3 * slots, width, BF16),
            shaped(3 * slots, width, BF16),
            shaped(2 * slots, width, BF16),
        ],
        10**10,
        inner,
        outer,
        middle,
        after=[sums],
    )
    gains, mine, along_core, along_chip = joined(
        sums, gains.shape[0], across_cores(along_core), out_of_pair(along_chip, PY)
    )
    blocks = [mine] + [in_square(mine, offset) for offset in range(1, members)]
    gain_edge_grad = (gains[0] + gains[1]).astype(BF16)
    gain_node_grad = (gains[2] + gains[3]).astype(BF16)
    (nodes_grad,) = call(
        return_kernel,
        [shaped(count, width, BF16)],
        2 * halo_rows * count * width,
        send_list,
        local_grad,
        center,
        along_core,
        along_chip,
    )
    done = (nodes_grad, edges_grad, gain_edge_grad, gain_node_grad)
    for i in range(members):
        blocks[i], *done = lax.optimization_barrier((blocks[i], *done))
    nodes_grad, edges_grad, gain_edge_grad, gain_node_grad = done
    blocks += [across_cores(block) for block in blocks]
    w_edge_in_grad, w_edge_out_grad, w_node_in_grad, w_node_out_grad = placed(
        parts, blocks, width
    )
    return (
        nodes_grad,
        edges_grad,
        w_edge_in_grad,
        w_edge_out_grad,
        gain_edge_grad,
        w_node_in_grad,
        w_node_out_grad,
        gain_node_grad,
    )


def solution(mesh):
    in_specs = (
        P(("groups",) + PX + PY, None),
        P(("groups",) + PX + PY, None),
        P(("groups",) + PX + PY, None),
        P(("groups",) + PX + PY, None),
        P(("groups",) + PX + PY, None),
        P(("groups",) + PX + PY, None),
        P(("groups",) + PX + PY, None),
        P(("groups",) + PX + PY),
        P(),
        P(),
        P(),
        P(),
        P(),
        P(),
    )
    out_specs = (
        P(("groups",) + PX + PY, None),
        P(("groups",) + PX + PY, None),
        P("groups", None),
        P("groups", None),
        P("groups"),
        P("groups", None),
        P("groups", None),
        P("groups"),
    )
    groups, px, py = mesh.devices.shape
    by_core = jax.sharding.Mesh(
        mesh.devices.reshape(groups, px // 2, 2, py // 2, 2), ("groups",) + PX + PY
    )
    return jax.shard_map(
        on_device, mesh=by_core, in_specs=in_specs, out_specs=out_specs, check_vma=False
    )
```

```python
import functools

import jax
import jax.numpy as jnp
from jax import lax
from jax.experimental import pallas as pl
from jax.experimental.pallas import tpu as pltpu
from jax.sharding import PartitionSpec as P

EPS = 1e-05
BF16 = jnp.bfloat16
F32 = jnp.float32
PACKED = 8
VMEM_LIMIT = 24 * 1024 * 1024


CORE = "core"
FAR = "far"
NEAR = "near"
PX = (FAR, NEAR)
PY = ("side", CORE)
SQUARE = (NEAR, "side")


def other_neighbour(i, size):
    return (i + 1 if i % 2 else i - 1) % size


def in_pair(array, axis):
    return lax.ppermute(array, axis, [(i, i ^ 1) for i in range(lax.axis_size(axis))])


def out_of_pair(array, axis):
    size = lax.axis_size(axis)
    return lax.ppermute(array, axis, [(i, other_neighbour(i, size)) for i in range(size)])


def square_members():
    return lax.axis_size(SQUARE)


def place_in_square():
    near, side = SQUARE
    return lax.axis_index(near) * lax.axis_size(side) + lax.axis_index(side)


def in_square(array, offset):
    return lax.ppermute(array, SQUARE, [(i, i ^ offset) for i in range(square_members())])


def tree_sum(terms):
    while len(terms) > 1:
        terms = [terms[i] + terms[i + 1] for i in range(0, len(terms), 2)]
    return terms[0]


def across_cores(array):
    return in_pair(array, CORE)


def by_pair(axis, up, down, inner, outer):
    first = lax.axis_index(axis) == 0

    @pl.when(first)
    def _():
        inner[...] = up
        outer[...] = down

    @pl.when(jnp.logical_not(first))
    def _():
        inner[...] = down
        outer[...] = up


def from_pair(axis, inner, outer):
    first = lax.axis_index(axis) == 0
    return jnp.where(first, outer, inner), jnp.where(first, inner, outer)


def dot(left, right):
    return jnp.dot(left, right, preferred_element_type=F32)


def dot_tn(left, right):
    return lax.dot_general(left, right, (((0,), (0,)), ((), ())), preferred_element_type=F32)


def dot_nt(left, right):
    return lax.dot_general(left, right, (((1,), (1,)), ((), ())), preferred_element_type=F32)


def sigmoid(value):
    return 0.5 + 0.5 * jnp.tanh(0.5 * value)


def normalize(value):
    centered = value - jnp.mean(value, axis=-1, keepdims=True)
    scale_inv = lax.rsqrt(jnp.mean(centered * centered, axis=-1, keepdims=True) + EPS)
    return centered * scale_inv, scale_inv


def norm_back(normed, scale_inv, gain, upstream):
    scaled = upstream * gain
    inner = (
        scaled
        - jnp.mean(scaled, axis=-1, keepdims=True)
        - normed * jnp.mean(scaled * normed, axis=-1, keepdims=True)
    )
    return inner * scale_inv


def columns_of(ids):
    rows, lanes = ids.shape
    padded = -(-rows // 8) * 8
    if padded > rows:
        ids = jnp.concatenate([ids, jnp.zeros((padded - rows, lanes), ids.dtype)], axis=0)
    return ids.T


def hot_rows(columns, tiles, base, count):
    parts = []
    for tile in tiles:
        column = columns[:, tile : tile + 1] - base
        lanes = lax.broadcasted_iota(jnp.int32, (columns.shape[0], count), 1)
        parts.append(jnp.where(lanes == column, 1.0, 0.0).astype(BF16))
    return jnp.concatenate(parts, axis=0) if len(parts) > 1 else parts[0]


def hot_columns(ids, tiles, base, count):
    parts = []
    for tile in tiles:
        row = ids[tile : tile + 1, :] - base
        subs = lax.broadcasted_iota(jnp.int32, (count, ids.shape[1]), 0)
        parts.append(jnp.where(subs == row, 1.0, 0.0).astype(BF16))
    return jnp.concatenate(parts, axis=1) if len(parts) > 1 else parts[0]


def list_hot(ids, count):
    directions, slots = ids.shape
    wide = jnp.concatenate([ids, jnp.zeros((directions, 128 - slots), ids.dtype)], axis=1)
    columns = wide.T
    parts = []
    for k in range(directions):
        lanes = lax.broadcasted_iota(jnp.int32, (slots, count), 1)
        parts.append(jnp.where(lanes == columns[:slots, k : k + 1], 1.0, 0.0).astype(BF16))
    return jnp.concatenate(parts, axis=0)


def live_rows(count_ref, tile_rows, rows):
    index = lax.broadcasted_iota(jnp.int32, (rows, 1), 0)
    return jnp.where(index < count_ref[0] * tile_rows, 1.0, 0.0)


def fetch_all(sources, targets, sems):
    copies = [
        pltpu.make_async_copy(source, target, sems.at[i])
        for i, (source, target) in enumerate(zip(sources, targets))
    ]
    for copy in copies:
        copy.start()
    return copies


def send_kernel(nodes_hbm, list_hbm, inner, outer, middle, nodes, send_list, sems):
    slots = send_list.shape[1]
    list_copy, nodes_copy = fetch_all([list_hbm, nodes_hbm], [send_list, nodes], sems)
    list_copy.wait()
    hot = list_hot(send_list[...], nodes.shape[0])
    nodes_copy.wait()
    rows = dot(hot, nodes[...]).astype(BF16)
    by_pair(NEAR, rows[5 * slots :], rows[: 3 * slots], inner, outer)
    middle[...] = rows[3 * slots : 5 * slots]


def corner_kernel(inner, outer, middle, along_core, along_chip, straight):
    slots = middle.shape[0] // 2
    low, high = from_pair(NEAR, inner[...], outer[...])
    up = jnp.concatenate([high[2 * slots :], middle[slots:], low[2 * slots :]], axis=0)
    down = jnp.concatenate([high[:slots], middle[:slots], low[:slots]], axis=0)
    by_pair(CORE, up, down, along_core, along_chip)
    straight[:slots] = high[slots : 2 * slots]
    straight[slots:] = low[slots : 2 * slots]


def index_kernel(sources, *refs):
    fetched, refs = refs[:sources], refs[sources:]
    near_rows, halo_rows = refs[:2]
    targets, sems = refs[2:-1], refs[-1]
    senders, receivers = targets[:2]
    copies = fetch_all(fetched, targets, sems)
    for copy in copies[:2]:
        copy.wait()
    tile_rows = senders.shape[1]
    count = near_rows.shape[1] // 2
    by_sender = columns_of(senders[...])
    by_receiver = columns_of(receivers[...])
    for tile in range(senders.shape[0]):
        rows = slice(tile * tile_rows, (tile + 1) * tile_rows)
        near_rows[rows, :count] = hot_rows(by_sender, [tile], 0, count)
        near_rows[rows, count:] = hot_rows(by_receiver, [tile], 0, count)
        halo_rows[rows, :] = hot_rows(by_sender, [tile], count, halo_rows.shape[1])
    for copy in copies[2:]:
        copy.wait()


def local_kernel(
    nodes, edges, senders, receivers, near_rows, w_in, pre, sender_columns, receiver_columns
):
    width = nodes.shape[1]
    tile_rows = senders.shape[1]
    extended = sender_columns.shape[0]
    count = receiver_columns.shape[0]
    sender_ids = senders[...]
    receiver_ids = receivers[...]
    for tile in range(senders.shape[0]):
        rows = slice(tile * tile_rows, (tile + 1) * tile_rows)
        sender_columns[:, rows] = hot_columns(sender_ids, [tile], 0, extended)
        receiver_columns[:, rows] = hot_columns(receiver_ids, [tile], 0, count)
    x = nodes[...]
    table = jnp.concatenate(
        [
            dot(x, w_in[width : 2 * width]).astype(BF16),
            dot(x, w_in[2 * width :]).astype(BF16),
        ],
        axis=0,
    )
    pre[...] = dot(edges[...], w_in[:width]) + dot(near_rows[...], table)


def split_by_core(sums, first, keep_out, away_out):
    half = sums.shape[0] // 2
    core = lax.axis_index(CORE)
    keep_out[first : first + half] = sums[pl.ds(pl.multiple_of(core * half, half), half), :]
    away = sums[pl.ds(pl.multiple_of((1 - core) * half, half), half), :]
    away_out[first : first + half] = away.astype(BF16)


def pack_gains(edge_gain, node_gain):
    edge_high = edge_gain.astype(BF16).astype(F32)
    node_high = node_gain.astype(BF16).astype(F32)
    row = lax.broadcasted_iota(jnp.int32, (PACKED, edge_gain.shape[1]), 0)
    packed = jnp.where(row == 0, edge_high, 0.0)
    packed = jnp.where(row == 1, edge_gain - edge_high, packed)
    packed = jnp.where(row == 2, node_high, packed)
    packed = jnp.where(row == 3, node_gain - node_high, packed)
    return packed.astype(BF16)


def layer_kernel(
    tile_rows,
    count_ref,
    nodes,
    node_grads,
    edges,
    edge_grads,
    pre_local,
    halo_rows,
    near_rows,
    sender_columns,
    receiver_columns,
    straight,
    along_core,
    along_chip,
    w_in,
    w_out,
    gain_edge,
    w_node_in,
    w_node_out,
    gain_node,
    pre_grad_out,
    sender_out,
    receiver_out,
    node_part_out,
    inner_out,
    outer_out,
    middle_out,
    keep_out,
    away_out,
    gains_out,
    slope_kept,
    hidden_kept,
    normed_kept,
    scale_kept,
    node_sums,
    edge_sums,
):
    count, width = nodes.shape
    edge_rows = edges.shape[0]
    live = live_rows(count_ref, tile_rows, edge_rows)
    slots = straight.shape[0] // 2
    up, down = from_pair(CORE, along_core[...], along_chip[...])
    halo = jnp.concatenate(
        [
            down[:slots],
            straight[:slots],
            up[:slots],
            down[slots : 2 * slots],
            up[slots : 2 * slots],
            down[2 * slots :],
            straight[slots:],
            up[2 * slots :],
        ],
        axis=0,
    )
    table = dot(halo, w_in[width : 2 * width]).astype(BF16)
    gain = gain_edge[...].astype(F32)[None, :]
    value = pre_local[...] + dot(halo_rows[...], table)
    sigma = sigmoid(value)
    hidden = (value * sigma).astype(BF16)
    hidden_kept[...] = hidden
    slope_kept[...] = sigma * (1.0 + value * (1.0 - sigma))
    edge_normed, edge_scale = normalize(dot(hidden, w_out[...]))
    normed_kept[...] = edge_normed
    scale_kept[...] = jnp.broadcast_to(edge_scale, (edge_rows, 128))
    message = (live * gain * edge_normed).astype(BF16)
    total = dot(receiver_columns[...], message)
    aggregated = total.astype(BF16)
    x = nodes[...]
    w_first = w_node_in[:width]
    w_second = w_node_in[width:]
    node_pre = dot(x, w_first) + dot(aggregated, w_second)
    sigma = sigmoid(node_pre)
    node_hidden = (node_pre * sigma).astype(BF16)
    normed, scale_inv = normalize(dot(node_hidden, w_node_out[...]))
    upstream = node_grads[...].astype(F32)
    out_grad = norm_back(normed, scale_inv, gain_node[...].astype(F32)[None, :], upstream).astype(BF16)
    slope = sigma * (1.0 + node_pre * (1.0 - sigma))
    pre_grad = (dot_nt(out_grad, w_node_out[...]) * slope).astype(BF16)
    agg_grad = dot_nt(pre_grad, w_second).astype(BF16)
    node_part_out[...] = upstream + dot_nt(pre_grad, w_first)
    node_sums[:width] = dot_tn(x, pre_grad)
    node_sums[width : 2 * width] = dot_tn(aggregated, pre_grad)
    node_sums[2 * width : 3 * width] = dot_tn(node_hidden, out_grad)
    node_gain = jnp.sum(upstream * normed, axis=0, keepdims=True)
    upstream = live * (
        edge_grads[...].astype(F32) + dot(near_rows[:, count:], agg_grad)
    )
    edge_normed = normed_kept[...]
    edge_gain = jnp.sum(upstream * edge_normed, axis=0, keepdims=True)
    out_grad = norm_back(edge_normed, scale_kept[:, :1], gain, upstream).astype(BF16)
    pre_grad = (dot_nt(out_grad, w_out[...]) * slope_kept[...]).astype(BF16)
    pre_grad_out[...] = pre_grad
    sender_total = dot(sender_columns[...], pre_grad)
    receiver_total = dot(receiver_columns[...], pre_grad)
    own = sender_total[:count].astype(BF16)
    away = sender_total[count:].astype(BF16)
    received = receiver_total.astype(BF16)
    sender_out[...] = own
    receiver_out[...] = received
    halo_grad = dot_nt(away, w_in[width : 2 * width]).astype(BF16)
    by_pair(NEAR, halo_grad[: 3 * slots], halo_grad[5 * slots :], inner_out, outer_out)
    middle_out[...] = halo_grad[3 * slots : 5 * slots]
    edge_sums[:width] = dot_tn(edges[...], pre_grad)
    edge_sums[width : 2 * width] = dot_tn(x, own) + dot_tn(halo, away)
    edge_sums[2 * width : 3 * width] = dot_tn(x, received)
    edge_sums[3 * width : 4 * width] = dot_tn(hidden_kept[...], out_grad)
    split_by_core(edge_sums, 0, keep_out, away_out)
    split_by_core(node_sums, edge_sums.shape[0] // 2, keep_out, away_out)
    gains = pack_gains(edge_gain, node_gain)
    away_out[keep_out.shape[0] :] = gains
    gains_out[...] = gains


def pair_kernel(parts, keep, gains, other, *outs):
    rows = keep.shape[0]
    packed = gains.shape[0]
    members = len(outs)
    both = gains[...].astype(F32) + other[rows : rows + packed].astype(F32)
    summed = pack_gains(both[0:1] + both[1:2], both[2:3] + both[3:4])
    me = place_in_square()
    for offset, out in enumerate(reversed(outs)):
        owner = me ^ offset
        out[:packed] = summed
        first, at = 0, packed
        for part in parts:
            step = part // members
            source = pl.ds(pl.multiple_of(first + owner * step, 16), step)
            out[at : at + step] = (keep[source, :] + other[source, :].astype(F32)).astype(BF16)
            first, at = first + part, at + step


def add_packed(values):
    packed = PACKED
    gains = values[:packed]
    return pack_gains(gains[0:1] + gains[1:2], gains[2:3] + gains[3:4])


def sum_kernel(*refs):
    sums_out = refs[-1]
    sums = tree_sum([block[...].astype(F32) for block in refs[:-1]])
    sums_out[...] = sums.astype(BF16)
    sums_out[:PACKED] = add_packed(sums)


def join_kernel(own, other, sums_out):
    sums = own[...].astype(F32) + other[...].astype(F32)
    sums_out[...] = sums.astype(BF16)
    sums_out[:PACKED] = add_packed(sums)


def whole_kernel(own, other, gains_out, mine):
    packed = gains_out.shape[0]
    sums = own[...].astype(F32) + other[...].astype(F32)
    gains_out[...] = sums[:packed]
    mine[...] = sums[packed:].astype(BF16)


def place_kernel(parts, *refs):
    count = 2 * len(parts)
    sems, wholes = refs[-1], refs[-1 - len(parts) : -1]
    outs = refs[-1 - len(parts) - count : -1 - len(parts)]
    blocks = refs[: -1 - len(parts) - count]
    members = len(blocks) // 2
    core = lax.axis_index(CORE)
    me = place_in_square()
    copies = []
    at = 0
    for i, (part, whole) in enumerate(zip(parts, wholes)):
        step = part // members
        for position, block in enumerate(blocks):
            half = core if position < members else 1 - core
            owner = me ^ (position % members)
            row = pl.multiple_of(half * part + owner * step, 16)
            whole[pl.ds(row, step), :] = block[at : at + step]
        at += step
        cut = outs[2 * i].shape[0]
        copies += [
            pltpu.make_async_copy(whole.at[:cut], outs[2 * i], sems.at[2 * i]),
            pltpu.make_async_copy(whole.at[cut:], outs[2 * i + 1], sems.at[2 * i + 1]),
        ]
        for copy in copies[-2:]:
            copy.start()
    for copy in copies:
        copy.wait()


def finish_kernel(
    edge_grads, pre_grad, sender_sum, receiver_sum, node_part, w_in, edges_grad, local_grad
):
    width = w_in.shape[1]
    edges_grad[...] = (
        edge_grads[...].astype(F32) + dot_nt(pre_grad[...], w_in[:width])
    ).astype(BF16)
    local_grad[...] = (
        node_part[...]
        + dot_nt(sender_sum[...], w_in[width : 2 * width])
        + dot_nt(receiver_sum[...], w_in[2 * width :])
    )


def turn_kernel(inner, outer, middle, along_core, along_chip, center):
    slots = middle.shape[0] // 2
    top, bottom = from_pair(NEAR, inner[...], outer[...])
    up = jnp.concatenate([top[:slots], middle[:slots], bottom[:slots]], axis=0)
    down = jnp.concatenate([top[2 * slots :], middle[slots:], bottom[2 * slots :]], axis=0)
    by_pair(CORE, up, down, along_core, along_chip)
    center[:slots] = top[slots : 2 * slots]
    center[slots:] = bottom[slots : 2 * slots]


def return_kernel(send_list, local_grad, center, along_core, along_chip, nodes_grad):
    slots = send_list.shape[1]
    up, down = from_pair(CORE, along_core[...], along_chip[...])
    returned = jnp.concatenate(
        [
            up[:slots],
            center[:slots],
            down[:slots],
            up[slots : 2 * slots],
            down[slots : 2 * slots],
            up[2 * slots :],
            center[slots:],
            down[2 * slots :],
        ],
        axis=0,
    )
    hot = list_hot(send_list[...], local_grad.shape[0])
    nodes_grad[...] = (local_grad[...] + dot_tn(hot, returned)).astype(BF16)


SMEM = pltpu.SMEM
VMEM = pltpu.VMEM
HBM = pltpu.HBM


def call(body, outs, flops, *operands, spaces=(), out_space=VMEM, scratch=(), after=()):
    if after:
        first, rest = len(operands), len(operands) + len(after)
        inner = body

        def body(*refs):
            inner(*refs[:first], *refs[rest:])

        operands = operands + tuple(after)
    moved = sum(x.size * x.dtype.itemsize for x in operands)
    moved += sum(x.size * jnp.dtype(x.dtype).itemsize for x in outs)
    spaces = list(spaces) + [VMEM] * (len(operands) - len(spaces))
    out_spaces = out_space if isinstance(out_space, list) else [out_space] * len(outs)
    operands = [
        pltpu.with_memory_space_constraint(x, HBM) if space is HBM else x
        for x, space in zip(operands, spaces)
    ]
    return pl.pallas_call(
        body,
        out_shape=outs,
        in_specs=[pl.BlockSpec(memory_space=space) for space in spaces],
        out_specs=[pl.BlockSpec(memory_space=space) for space in out_spaces],
        scratch_shapes=list(scratch),
        compiler_params=pltpu.CompilerParams(vmem_limit_bytes=VMEM_LIMIT),
        cost_estimate=pl.CostEstimate(flops=flops, bytes_accessed=moved, transcendentals=0),
    )(*operands)


def like(array):
    return jax.ShapeDtypeStruct(array.shape, array.dtype)


def shaped(rows, columns, dtype):
    return jax.ShapeDtypeStruct((rows, columns), dtype)


def placed(parts, blocks, width):
    return call(
        functools.partial(place_kernel, parts),
        [
            shaped(3 * width, width, BF16),
            shaped(width, width, BF16),
            shaped(2 * width, width, BF16),
            shaped(width, width, BF16),
        ],
        0,
        *blocks,
        out_space=HBM,
        scratch=[pltpu.VMEM((2 * part, width), BF16) for part in parts]
        + [pltpu.SemaphoreType.DMA((2 * len(parts),))],
    )


def joined(sums, packed, *beside):
    rows, width = sums.shape
    size = lax.axis_size(FAR)
    distance = 1
    while True:
        other = lax.ppermute(sums, FAR, [(i, i ^ distance) for i in range(size)])
        distance *= 2
        if distance == size:
            break
        (sums,) = call(join_kernel, [like(sums)], 0, sums, other)
    other, *beside = lax.optimization_barrier((other, *beside))
    gains, mine = call(
        whole_kernel,
        [shaped(packed, width, F32), shaped(rows - packed, width, BF16)],
        0,
        sums,
        other,
    )
    return gains, mine, *beside


def on_device(
    nodes,
    edges,
    edge_grads,
    node_grads,
    send_list,
    senders,
    receivers,
    tile_count,
    w_edge_in,
    w_edge_out,
    gain_edge,
    w_node_in,
    w_node_out,
    gain_node,
):
    count, width = nodes.shape
    slots = send_list.shape[1]
    halo_rows = 8 * slots
    edge_rows = edges.shape[0]
    tile_rows = senders.shape[1]
    square = 2 * width * width
    inner, outer, middle, nodes, send_list = call(
        send_kernel,
        [
            shaped(3 * slots, width, BF16),
            shaped(3 * slots, width, BF16),
            shaped(2 * slots, width, BF16),
            like(nodes),
            like(send_list),
        ],
        2 * halo_rows * count * width,
        nodes,
        send_list,
        spaces=[HBM, HBM],
        scratch=[pltpu.SemaphoreType.DMA((2,))],
    )
    inner = in_pair(inner, PX)
    outer = out_of_pair(outer, PX)
    fetched = [
        senders,
        receivers,
        edges,
        w_edge_in,
        w_edge_out,
        gain_edge,
        w_node_in,
        w_node_out,
        gain_node,
        node_grads,
        edge_grads,
    ]
    near_hot, halo_hot, *fetched = call(
        functools.partial(index_kernel, len(fetched)),
        [
            shaped(edge_rows, 2 * count, BF16),
            shaped(edge_rows, halo_rows, BF16),
        ]
        + [like(x) for x in fetched],
        0,
        *fetched,
        spaces=[HBM] * len(fetched),
        scratch=[pltpu.SemaphoreType.DMA((len(fetched),))],
    )
    (
        senders,
        receivers,
        edges,
        w_edge_in,
        w_edge_out,
        gain_edge,
        w_node_in,
        w_node_out,
        gain_node,
        node_grads,
        edge_grads,
    ) = fetched
    inner, outer, near_hot = lax.optimization_barrier((inner, outer, near_hot))
    along_core, along_chip, straight = call(
        corner_kernel,
        [
            shaped(3 * slots, width, BF16),
            shaped(3 * slots, width, BF16),
            shaped(2 * slots, width, BF16),
        ],
        0,
        inner,
        outer,
        middle,
    )
    along_chip = out_of_pair(along_chip, PY)
    along_core = across_cores(along_core)
    pre_local, sender_columns, receiver_columns = call(
        local_kernel,
        [
            shaped(edge_rows, width, F32),
            shaped(count + halo_rows, edge_rows, BF16),
            shaped(count, edge_rows, BF16),
        ],
        square * (2 * count + edge_rows) + 4 * edge_rows * count * width,
        nodes,
        edges,
        senders,
        receivers,
        near_hot,
        w_edge_in,
    )
    parts = (2 * width, 3 * width // 2)
    halves = sum(parts)
    pre_grad, sender_sum, receiver_sum, node_part, inner, outer, middle, keep, away, gains = call(
        functools.partial(layer_kernel, tile_rows),
        [
            shaped(edge_rows, width, BF16),
            shaped(count, width, BF16),
            shaped(count, width, BF16),
            shaped(count, width, F32),
            shaped(3 * slots, width, BF16),
            shaped(3 * slots, width, BF16),
            shaped(2 * slots, width, BF16),
            shaped(halves, width, F32),
            shaped(halves + PACKED, width, BF16),
            shaped(PACKED, width, BF16),
        ],
        square * (6 * edge_rows + 11 * count + 2 * halo_rows)
        + 2 * edge_rows * (4 * count + halo_rows) * width,
        tile_count,
        nodes,
        node_grads,
        edges,
        edge_grads,
        pre_local,
        halo_hot,
        near_hot,
        sender_columns,
        receiver_columns,
        straight,
        along_core,
        along_chip,
        w_edge_in,
        w_edge_out,
        gain_edge,
        w_node_in,
        w_node_out,
        gain_node,
        spaces=[SMEM],
        scratch=[
            pltpu.VMEM((edge_rows, width), F32),
            pltpu.VMEM((edge_rows, width), BF16),
            pltpu.VMEM((edge_rows, width), F32),
            pltpu.VMEM((edge_rows, 128), F32),
            pltpu.VMEM((3 * width, width), F32),
            pltpu.VMEM((4 * width, width), F32),
        ],
    )
    other = across_cores(away)
    members = square_members()
    *blocks, own = call(
        functools.partial(pair_kernel, parts),
        [shaped(PACKED + halves // members, width, BF16)] * members,
        0,
        keep,
        gains,
        other,
    )
    received = [in_square(block, members - 1 - i) for i, block in enumerate(blocks)]
    (sums,) = call(sum_kernel, [like(own)], 0, *received, own)
    edges_grad, local_grad = call(
        finish_kernel,
        [shaped(edge_rows, width, BF16), shaped(count, width, F32)],
        square * (edge_rows + 2 * count),
        edge_grads,
        pre_grad,
        sender_sum,
        receiver_sum,
        node_part,
        w_edge_in,
    )
    along_core, along_chip, center = call(
        turn_kernel,
        [
            shaped(3 * slots, width, BF16),
            shaped(3 * slots, width, BF16),
            shaped(2 * slots, width, BF16),
        ],
        10**10,
        in_pair(inner, PX),
        out_of_pair(outer, PX),
        middle,
        after=[sums],
    )
    gains, mine, along_core, along_chip = joined(
        sums, gains.shape[0], across_cores(along_core), out_of_pair(along_chip, PY)
    )
    blocks = [mine] + [in_square(mine, offset) for offset in range(1, members)]
    gain_edge_grad = (gains[0] + gains[1]).astype(BF16)
    gain_node_grad = (gains[2] + gains[3]).astype(BF16)
    (nodes_grad,) = call(
        return_kernel,
        [shaped(count, width, BF16)],
        2 * halo_rows * count * width,
        send_list,
        local_grad,
        center,
        along_core,
        along_chip,
    )
    done = (nodes_grad, edges_grad, gain_edge_grad, gain_node_grad)
    for i in range(members):
        blocks[i], *done = lax.optimization_barrier((blocks[i], *done))
    nodes_grad, edges_grad, gain_edge_grad, gain_node_grad = done
    blocks += [across_cores(block) for block in blocks]
    w_edge_in_grad, w_edge_out_grad, w_node_in_grad, w_node_out_grad = placed(
        parts, blocks, width
    )
    return (
        nodes_grad,
        edges_grad,
        w_edge_in_grad,
        w_edge_out_grad,
        gain_edge_grad,
        w_node_in_grad,
        w_node_out_grad,
        gain_node_grad,
    )


def solution(mesh):
    in_specs = (
        P(("groups",) + PX + PY, None),
        P(("groups",) + PX + PY, None),
        P(("groups",) + PX + PY, None),
        P(("groups",) + PX + PY, None),
        P(("groups",) + PX + PY, None),
        P(("groups",) + PX + PY, None),
        P(("groups",) + PX + PY, None),
        P(("groups",) + PX + PY),
        P(),
        P(),
        P(),
        P(),
        P(),
        P(),
    )
    out_specs = (
        P(("groups",) + PX + PY, None),
        P(("groups",) + PX + PY, None),
        P("groups", None),
        P("groups", None),
        P("groups"),
        P("groups", None),
        P("groups", None),
        P("groups"),
    )
    groups, px, py = mesh.devices.shape
    by_core = jax.sharding.Mesh(
        mesh.devices.reshape(groups, px // 2, 2, py // 2, 2), ("groups",) + PX + PY
    )
    return jax.shard_map(
        on_device, mesh=by_core, in_specs=in_specs, out_specs=out_specs, check_vma=False
    )
```
